32 devices in a mesh: dp: 8 (over z, y), seq: 4 (over x, core).
Axes of the slice: x: 2, y: 2, z: 4, core: 2. Of those that a mesh axis runs over, the one named last changes fastest.
Arguments:
- decoder_in: bfloat16 [16, 2048, 512], P('dp', 'seq'), may hold values from -6 to 6
- source_states: bfloat16 [16, 512, 512], P('dp', 'seq'), may hold values from -6 to 6
- source_len: int32 [16], replicated, may hold values from 128 to 512, as said below
- upsample: int32 [16], replicated, may hold values from 2 to 4, as said below
- send_counts: int32 [8], replicated, may hold values from 0 to 1, as said below
- self_query: bfloat16 [512, 512], P('dp', 'seq'), may hold values from -0.25 to 0.25
- self_key: bfloat16 [512, 512], P('dp', 'seq'), may hold values from -0.25 to 0.25
- self_value: bfloat16 [512, 512], P('dp', 'seq'), may hold values from -0.25 to 0.25
- self_output: bfloat16 [512, 512], P('dp', 'seq'), may hold values from -6 to 6
- cross_query: bfloat16 [512, 512], P('dp', 'seq'), may hold values from -0.25 to 0.25
- cross_key: bfloat16 [512, 512], P('dp', 'seq'), may hold values from -0.25 to 0.25
- cross_value: bfloat16 [512, 512], P('dp', 'seq'), may hold values from -0.25 to 0.25
- cross_output: bfloat16 [512, 512], P('dp', 'seq'), may hold values from -3 to 3
- ffn_expand: bfloat16 [512, 2048], P('dp', 'seq'), may hold values from -0.25 to 0.25
- ffn_reduce: bfloat16 [2048, 512], P('dp', 'seq'), may hold values from -0.125 to 0.125
- norm_gains: bfloat16 [3, 512], P(None, 'seq'), may hold values from 0.5 to 1.5
- out_grad: bfloat16 [16, 2048, 512], P('dp', 'seq'), may hold values from -6 to 6
Outputs:
- decoder_out: bfloat16 [16, 2048, 512], P('dp', 'seq')
- grad_decoder: float32 [16, 2048, 512], P('dp', 'seq')
- grad_source: float32 [16, 512, 512], P('dp', 'seq')
- grad_self_query: float32 [512, 512], P('dp', 'seq')
- grad_self_key: float32 [512, 512], P('dp', 'seq')
- grad_self_value: float32 [512, 512], P('dp', 'seq')
- grad_self_output: float32 [512, 512], P('dp', 'seq')
- grad_cross_query: float32 [512, 512], P('dp', 'seq')
- grad_cross_key: float32 [512, 512], P('dp', 'seq')
- grad_cross_value: float32 [512, 512], P('dp', 'seq')
- grad_cross_output: float32 [512, 512], P('dp', 'seq')
- grad_ffn_expand: float32 [512, 2048], P('dp', 'seq')
- grad_ffn_reduce: float32 [2048, 512], P('dp', 'seq')
- grad_norm_gains: float32 [3, 512], P(None, 'seq')
The draws below stay inside these ranges and needn't reach their ends.
Inputs may be any that keep to these rules, and one draw needn't show every extreme that they name: `source_len`: in every group of 2 sentences held by one index of dp on entry, one sentence, drawn from the seed and never the last one where that group's send count is 1, has source length 512 and upsample factor 4. `upsample`: each factor is 2 or 4, and 2 occurs in every draw. Where send_counts[g] is 1, index g of dp hands its last sentence to index (g + 4) mod 8. Indices 0, 3, 4 and 7 always hand one, index 5 never does.
All inputs are finite; a program needn't handle non-finite values.
Results may differ from the reference program's by a relative error of at most 0.02.
Values may be sent and summed in bfloat16 or wider, within the bound.
A program may use at most 192 MiB of HBM per device.

```python
import jax
import jax.numpy as jnp
from jax import lax

D = 512
HEADS = 8
FF = 2048
SENT = 2
SRC = 512
DEC = 2048
NSENT = 16
N_DP = 8


def pick_lengths(key):
    groups = NSENT // SENT
    length_key, factor_key, full_key, count_key = jax.random.split(key, 4)
    lengths = jax.random.randint(length_key, (groups, SENT), SRC // 4, SRC + 1)
    factors = 2 + 2 * jax.random.randint(factor_key, (groups, SENT), 0, 2)
    counts = jax.random.randint(count_key, (groups,), 0, 2)
    group_ids = jnp.arange(groups)
    forced_send = (group_ids == 0) | (group_ids == groups // 2 - 1) | (group_ids == groups // 2) | (group_ids == groups - 1)
    counts = jnp.where(forced_send, 1, jnp.where(group_ids == groups // 2 + 1, 0, counts))
    chosen = jax.random.randint(full_key, (groups,), 0, SENT)
    chosen = jnp.where((counts == 1) & (chosen == SENT - 1), 0, chosen)
    slot_ids = jnp.arange(SENT)[None, :]
    is_full = slot_ids == chosen[:, None]
    first_other = (group_ids[:, None] == 0) & (slot_ids == (chosen[0] + 1) % SENT)
    lengths = jnp.where(is_full, SRC, lengths)
    factors = jnp.where(is_full, 4, jnp.where(first_other, 2, factors))
    return (lengths.reshape(NSENT).astype(jnp.int32), factors.reshape(NSENT).astype(jnp.int32), counts.astype(jnp.int32))


def draw_source_len(key, part):
    return pick_lengths(key)[0]


def draw_upsample(key, part):
    return pick_lengths(key)[1]


def draw_send_counts(key, part):
    return pick_lengths(key)[2]


def raised(array, stream_key, source, target, blocks, factor):
    owner, partner = [(jnp.arange(array.shape[axis_at]) // (array.shape[axis_at] // blocks)).reshape([-1 if axis == axis_at else 1 for axis in range(array.ndim)]) for axis_at in (source, target)]
    chosen = jax.random.permutation(stream_key, blocks)[partner]
    strong = (owner == chosen) | (owner == (partner + blocks // 2) % blocks)
    return jnp.where(strong, factor * array, array)


def level_of(own_key, dims, cuts, low, largest):
    def one(axis_at, blocks):
        steps = jax.random.uniform(jax.random.fold_in(jax.random.fold_in(own_key, 6), axis_at), (blocks,), jnp.float32, low / len(cuts), largest / len(cuts))
        return jnp.repeat(jnp.exp(steps), dims[axis_at] // blocks).reshape((-1,) + (1,) * (len(dims) - axis_at - 1))

    level = one(*cuts[0])
    for cut in cuts[1:]:
        level = level * one(*cut)
    return level


def normal_values(key, shape, width, bound, shards=(), kind=jnp.bfloat16):
    values = width * jax.random.normal(key, shape, jnp.float32)
    if shards:
        values = values * level_of(key, shape, shards, -0.22, 0.18)
    return jnp.clip(values, -bound, bound).astype(kind)


def noise_with(key, extent, scale, most, shards, heavy, kind=jnp.bfloat16):
    values = scale * jax.random.normal(key, extent, jnp.float32)
    if shards:
        values = values * level_of(key, extent, shards, -0.22, 0.18)
    return jnp.clip(raised(values, jax.random.fold_in(key, 3), *heavy), -most, most).astype(kind)


def setup_inputs(seed: int = 0) -> dict:
    arg_keys = jax.random.split(jax.random.key(seed), 18)
    decoder_in = noise_with(arg_keys[0], (NSENT, DEC, D), 1.0, 6.0, ((0, 8), (1, 4)), (0, 2, 8, 2.0))
    source_states = normal_values(arg_keys[1], (NSENT, SRC, D), 1.0, 6.0, ((0, 8), (1, 4)))
    source_len = draw_source_len(jax.random.fold_in(arg_keys[17], 71), 0)
    upsample = draw_upsample(jax.random.fold_in(arg_keys[17], 71), 0)
    send_counts = draw_send_counts(jax.random.fold_in(arg_keys[17], 71), 0)
    self_query = normal_values(arg_keys[5], (D, D), D ** -0.5, 0.25, ((0, 8), (1, 4)))
    self_key = normal_values(arg_keys[6], (D, D), D ** -0.5, 0.25, ((0, 8), (1, 4)))
    self_value = normal_values(arg_keys[7], (D, D), D ** -0.5, 0.25, ((0, 8), (1, 4)))
    self_output = normal_values(arg_keys[8], (D, D), (max(1, 4 * D // DEC)) ** -0.5, 6.0, ((0, 8), (1, 4)))
    cross_query = normal_values(arg_keys[9], (D, D), D ** -0.5, 0.25, ((0, 8), (1, 4)))
    cross_key = normal_values(arg_keys[10], (D, D), D ** -0.5, 0.25, ((0, 8), (1, 4)))
    cross_value = normal_values(arg_keys[11], (D, D), D ** -0.5, 0.25, ((0, 8), (1, 4)))
    cross_output = normal_values(arg_keys[12], (D, D), (max(1, 4 * D // SRC)) ** -0.5, 3.0, ((0, 8), (1, 4)))
    ffn_expand = normal_values(arg_keys[13], (D, FF), D ** -0.5, 0.25, ((0, 8), (1, 4)))
    ffn_reduce = normal_values(arg_keys[14], (FF, D), FF ** -0.5, 0.125, ((0, 8), (1, 4)))
    norm_gains = jnp.clip(1.0 + 0.1 * jax.random.normal(arg_keys[15], (3, D), jnp.float32), 0.5, 1.5).astype(jnp.bfloat16)
    out_grad = normal_values(arg_keys[16], (NSENT, DEC, D), 1.0, 6.0, ((0, 8), (1, 4)))
    return {"decoder_in": decoder_in, "source_states": source_states, "source_len": source_len, "upsample": upsample, "send_counts": send_counts, "self_query": self_query, "self_key": self_key, "self_value": self_value, "self_output": self_output, "cross_query": cross_query, "cross_key": cross_key, "cross_value": cross_value, "cross_output": cross_output, "ffn_expand": ffn_expand, "ffn_reduce": ffn_reduce, "norm_gains": norm_gains, "out_grad": out_grad}


@jax.custom_vjp
def low(v):
    return lax.optimization_barrier(v.astype(jnp.bfloat16)).astype(jnp.float32)

@jax.custom_vjp
def low_back(v):
    return v

def low_keep(v):
    return (low(v), None)

def low_pass(kept, grad):
    return (grad,)

def back_keep(v):
    return (v, None)

def back_low(kept, grad):
    return (low(grad),)
low.defvjp(low_keep, low_pass)
low_back.defvjp(back_keep, back_low)
epsilon = 1e-05
negative = -1000000000.0
highest = lax.Precision.HIGHEST

def rounded_both(values):
    return low(low_back(values))

def matmul(left_side, right_side):
    return jnp.dot(left_side, right_side, precision=highest)

def normalize(values, gain):
    row_mean = lax.optimization_barrier(jnp.mean(values, axis=-1, keepdims=True))
    centred = values - row_mean
    spread = lax.optimization_barrier(jnp.mean(centred * centred, axis=-1, keepdims=True))
    return centred * lax.rsqrt(spread + epsilon) * gain

def attention(queries, key_rows, value_rows, key_mask):
    head_width = D // HEADS
    score_scale = head_width ** (-0.5)

    def split_heads(matrix):
        return jnp.transpose(matrix.reshape(matrix.shape[0], HEADS, head_width), (1, 0, 2))

    def one_head(entries):
        head_query, head_key, head_value = entries
        scores = low_back(matmul(head_query, head_key.T)) * score_scale
        scores = jnp.where(key_mask[None, :], scores, negative)
        row_peak = lax.optimization_barrier(jnp.max(scores, axis=-1, keepdims=True))
        exp_scores = jnp.exp(scores - row_peak)
        probs = exp_scores / lax.optimization_barrier(jnp.sum(exp_scores, axis=-1, keepdims=True))
        return matmul(low(probs), head_value)
    mixed_heads = lax.map(jax.checkpoint(one_head), (split_heads(queries), split_heads(key_rows), split_heads(value_rows)))
    return rounded_both(jnp.transpose(mixed_heads, (1, 0, 2)).reshape(queries.shape[0], D))

def sentence(entries, params):
    inputs, sources, length_src, factor = entries
    query_self, key_self, value_self, output_self, query_cross, key_cross, value_cross, output_cross, expand_weight, reduce_weight, gain_rows = params
    dec_len = length_src * factor
    row_mask = jnp.arange(inputs.shape[0]) < dec_len
    source_mask = jnp.arange(sources.shape[0]) < length_src
    hidden_one = low(normalize(inputs, gain_rows[0]))
    self_q = rounded_both(matmul(hidden_one, query_self))
    self_k = rounded_both(matmul(hidden_one, key_self))
    self_v = rounded_both(matmul(hidden_one, value_self))
    self_mixed = attention(self_q, self_k, self_v, row_mask)
    after_self = inputs + low_back(matmul(self_mixed, output_self))
    hidden_two = low(normalize(after_self, gain_rows[1]))
    cross_q = rounded_both(matmul(hidden_two, query_cross))
    cross_k = rounded_both(matmul(sources, key_cross))
    cross_v = rounded_both(matmul(sources, value_cross))
    cross_mixed = attention(cross_q, cross_k, cross_v, source_mask)
    after_cross = after_self + low_back(matmul(cross_mixed, output_cross))
    hidden_three = low(normalize(after_cross, gain_rows[2]))
    expanded = low_back(matmul(hidden_three, expand_weight))
    activated = low(jax.nn.gelu(expanded, approximate=True))
    final = after_cross + low_back(matmul(activated, reduce_weight))
    return final * row_mask.astype(jnp.float32)[:, None]

def reference(decoder_in, source_states, source_len, upsample, send_counts, self_query, self_key, self_value, self_output, cross_query, cross_key, cross_value, cross_output, ffn_expand, ffn_reduce, norm_gains, out_grad):
    slot_ids = jnp.arange(NSENT, dtype=jnp.int32)
    home_group = slot_ids // SENT
    moved = (slot_ids % SENT == SENT - 1) & (send_counts[home_group] == 1)
    holder = jnp.where(moved, (home_group + N_DP // 2) % N_DP, home_group).astype(jnp.int32)
    dec_lengths = source_len * upsample
    group_tokens = jax.ops.segment_sum(dec_lengths, holder, num_segments=N_DP)
    loss_scale = jnp.float32(DEC) / group_tokens[holder].astype(jnp.float32)
    floats = [member.astype(jnp.float32) for member in (decoder_in, source_states, self_query, self_key, self_value, self_output, cross_query, cross_key, cross_value, cross_output, ffn_expand, ffn_reduce, norm_gains)]

    def forward(inputs, sources, *params):

        def one_sentence(entries):
            return sentence(entries, params)
        return lax.map(jax.checkpoint(one_sentence), (inputs, sources, source_len, upsample))
    result, pullback = jax.vjp(forward, *floats)
    cotangent = out_grad.astype(jnp.float32) * loss_scale[:, None, None]
    gradients = pullback(cotangent)
    return (result.astype(jnp.bfloat16), gradients[0], gradients[1], gradients[2], gradients[3], gradients[4], gradients[5], gradients[6], gradients[7], gradients[8], gradients[9], gradients[10], gradients[11], gradients[12])
```

```python
from functools import partial

import jax
import jax.numpy as jnp
from jax import lax
from jax.experimental import pallas as pl
from jax.experimental.pallas import tpu as pltpu
from jax.sharding import PartitionSpec as P

HEADS = 8
EPSILON = 1e-05
NEGATIVE = -1000000000.0
LOG2E = 1.4426950408889634
LN2 = 0.6931471805599453
GELU_IN = 0.7978845608028654
GELU_CUBE = 0.044715
BLOCK = 256
PAIR = 128

bf16 = jnp.bfloat16
f32 = jnp.float32
VMEM = pltpu.VMEM
VMEM_LIMIT = 60 * 1024 * 1024
PARAMS = pltpu.CompilerParams(vmem_limit_bytes=VMEM_LIMIT)


def dot(left, right):
    return jnp.dot(left, right, preferred_element_type=f32)


def dot_nt(left, right):
    return lax.dot_general(left, right, (((1,), (1,)), ((), ())), preferred_element_type=f32)


def block_at(index, size):
    return pl.ds(pl.multiple_of(index * size, size), size)


def row_mean(values):
    return jnp.mean(values, axis=-1, keepdims=True)


def normalize(values):
    centred = values - row_mean(values)
    inverse = lax.rsqrt(row_mean(centred * centred) + EPSILON)
    return centred * inverse, inverse


def norm_back(upstream, scaled, inverse, gain):
    inner = upstream * gain
    back = inverse * (inner - row_mean(inner) - scaled * row_mean(inner * scaled))
    return back, jnp.sum(upstream * scaled, axis=0, keepdims=True)


def three_parts(column, lane, last):
    high = column.astype(bf16).astype(f32)
    middle = (column - high).astype(bf16).astype(f32)
    low = column - high - middle
    rest = jnp.where(lane == 3, last, 0.0)
    return jnp.where(
        lane == 0, high, jnp.where(lane == 1, middle, jnp.where(lane == 2, low, rest))
    ).astype(bf16)


def one_head(values, first, head):
    zero = jnp.zeros_like(values)
    return jnp.where(first, values, zero) if head == 0 else jnp.where(first, zero, values)


def attend_pair(query, keys, key_extra, values, lane):
    first = lane < 64
    ones = jnp.where(lane == 3, 1.0, 0.0).astype(bf16)
    keys = jnp.concatenate([keys, key_extra], axis=1)
    scores = [
        dot_nt(jnp.concatenate([one_head(query, first, head), ones], axis=1), keys)
        for head in (0, 1)
    ]
    mixed, extras = [], []
    for head in (0, 1):
        peak = jnp.max(scores[head], axis=1, keepdims=True)
        exps = jnp.exp2(scores[head] - peak)
        total = jnp.sum(exps, axis=1, keepdims=True)
        mixed.append(dot(exps.astype(bf16), values) * (1.0 / total))
        extras.append(three_parts(-(peak + jnp.log2(total)), lane, 1.0))
    return jnp.where(first, mixed[0], mixed[1]).astype(bf16), extras


def attend_pair_back(
    query, grad, mixed, query_extra, key_at, value_at, key_columns_at, chunks, lane, add_key, add_value
):
    first = lane < 64
    product = grad.astype(f32) * mixed.astype(f32)
    queries = [one_head(query, first, head) for head in (0, 1)]
    grads = [one_head(grad, first, head) for head in (0, 1)]
    long_queries = [jnp.concatenate([queries[h], query_extra[h]], axis=1) for h in (0, 1)]
    long_grads = []
    for head in (0, 1):
        delta = jnp.sum(one_head(product, first, head), axis=1, keepdims=True)
        long_grads.append(
            jnp.concatenate([grads[head], three_parts(-delta, lane, 0.0)], axis=1)
        )
    both_queries = jnp.concatenate(queries, axis=0)
    both_grads = jnp.concatenate(grads, axis=0)
    query_grads = [jnp.zeros((64, query.shape[0]), f32)] * 2
    for chunk in range(chunks):
        keys, values = key_at(chunk), value_at(chunk)
        probs, score_grads = [], []
        for head in (0, 1):
            prob = jnp.exp2(dot_nt(keys, long_queries[head]))
            score_grad = (prob * dot_nt(values, long_grads[head])).astype(bf16)
            probs.append(prob.astype(bf16))
            score_grads.append(score_grad)
            query_grads[head] = query_grads[head] + dot(key_columns_at(chunk, head), score_grad)
        add_value(chunk, dot(jnp.concatenate(probs, axis=1), both_grads))
        add_key(chunk, dot(jnp.concatenate(score_grads, axis=1), both_queries))
    return (jnp.concatenate(query_grads, axis=0) * 0.125).astype(bf16)


def copy_to(source, target, send, receive, partner):
    return pltpu.make_async_remote_copy(
        src_ref=source,
        dst_ref=target,
        send_sem=send,
        recv_sem=receive,
        device_id=partner,
        device_id_type=pl.DeviceIdType.MESH,
    )


def entry_barrier(partners):
    barrier = pltpu.get_barrier_semaphore()
    for partner in partners:
        pl.semaphore_signal(
            barrier, inc=1, device_id=partner, device_id_type=pl.DeviceIdType.MESH
        )
    pl.semaphore_wait(barrier, len(partners))


class Where:
    def __init__(self, planes):
        group, self.place = lax.axis_index("dp"), lax.axis_index("seq")
        self.group = group
        self.chip, self.core = self.place // 2, self.place % 2
        self.plane, self.side = group // 2, group % 2
        self.planes = planes
        self.other_core = self.at(self.chip, 1 - self.core)
        self.other_chip = self.at(1 - self.chip, self.core)
        self.diagonal = self.at(1 - self.chip, 1 - self.core)
        self.other_side = {"dp": self.plane * 2 + 1 - self.side}
        self.other_planes = [
            {"dp": (self.plane + step) % planes * 2 + self.side} for step in range(1, planes)
        ]

    def at(self, chip, core):
        return {"seq": chip * 2 + core}

    def column(self, step):
        return (self.chip + step // 2) % 2 * 2 + (self.core + step % 2) % 2

    def everyone(self):
        return [self.other_core, self.other_chip, self.diagonal, self.other_side] + self.other_planes


class Semaphores:
    def __init__(self, send, receive):
        self.send, self.receive, self.count = send, receive, 0
        self.sent = []

    def remote(self, source, target, partner):
        at = self.count
        self.count += 1
        copy = copy_to(source, target, self.send.at[at], self.receive.at[at], partner)
        self.sent.append(copy)
        return copy

    def local(self, source, target):
        at = self.count
        self.count += 1
        return pltpu.make_async_copy(source, target, self.send.at[at])


def block_places(where_chip, where_core, rows, offset, index, size):
    per = rows // size
    slot = index // per
    block = (where_chip + slot % 2) % 2 * 2 + (where_core + slot // 2) % 2
    return block * rows + index % per * size + offset


def mask_columns(where_chip, where_core, rows, count, size, length, ref):
    lane = lax.broadcasted_iota(jnp.int32, (size, PAIR), 1)
    offset = lax.broadcasted_iota(jnp.int32, (size, PAIR), 0)

    def step(index, _):
        places = block_places(where_chip, where_core, rows, offset, index, size)
        bias = jnp.where(places < length, 0.0, NEGATIVE)
        ref[block_at(index, size), :] = jnp.where(
            lane < 3, 1.0, jnp.where(lane == 3, bias, 0.0)
        ).astype(bf16)
        return 0

    lax.fori_loop(0, count // size, step, 0)


def open_kernel(
    comm,
    planes,
    deep,
    source_len_ref,
    upsample_ref,
    *refs,
):
    if comm:
        (
            decoder_ref, source_ref, cotangent_ref,
            wq_in, wk_in, wv_in, *later_in, gain_in,
            x_out, source_out, cotangent_out, qkv_out, later_a, later_b, later_c, gain_out,
            q_out, k_out, v_out, mixed_out, extra_out,
            x_ref, qkv_ref, gain_ref, hidden_ref, weight_ref, mask_ref,
            q_ref, k_ref, v_ref, mixed_ref, extra_ref, send, receive,
        ) = refs
    else:
        (
            x_ref, qkv_ref, gain_ref,
            q_out, k_out, v_out, mixed_out, extra_out,
            hidden_ref, weight_ref, mask_ref,
            q_ref, k_ref, v_ref, mixed_ref, extra_ref, send, receive,
        ) = refs
    where = Where(planes)
    place, plane, side, chip, core = where.place, where.plane, where.side, where.chip, where.core
    total, width = x_ref.shape
    pairs = width // PAIR
    own = total // 2
    rows = total // 4
    semaphores = Semaphores(send, receive)
    column = where.column

    if comm:
        group = where.group
        x_slots = [x_ref.at[slot * rows : (slot + 1) * rows] for slot in range(4)]
        few = source_ref.shape[1]
        s_slots = [source_out.at[slot * few : (slot + 1) * few] for slot in range(4)]
        c_slots = [cotangent_out.at[slot * rows : (slot + 1) * rows] for slot in range(2)]
        local_x = semaphores.local(decoder_ref.at[chip], x_slots[0])
        local_gain = semaphores.local(gain_in, gain_ref.at[place])
        mine = qkv_ref.at[place, side, plane]
        local_qkv = [
            semaphores.local(ref, mine.at[at * deep : (at + 1) * deep])
            for at, ref in enumerate((wq_in, wk_in, wv_in))
        ]
        first = [local_x, local_gain, *local_qkv]
        wo_in, wcq_in, wck_in, wcv_in, wco_in, w1_in, w2_in = later_in
        mine_a = later_a.at[place, side, plane]
        mine_b = later_b.at[place, side, plane]
        mine_c = later_c.at[place, side, plane]
        wide = w1_in.shape[1] // PAIR
        local_later = [
            [
                semaphores.local(ref, mine_a.at[at * deep : (at + 1) * deep])
                for at, ref in enumerate((wo_in, wcq_in, wck_in, wcv_in, wco_in))
            ],
            [
                semaphores.local(
                    w1_in.at[:, at * PAIR : (at + 1) * PAIR], mine_b.at[at * deep : (at + 1) * deep]
                )
                for at in range(wide)
            ],
            [semaphores.local(w2_in, mine_c)],
        ]
        local_rest = [
            semaphores.local(source_ref.at[chip], s_slots[0]),
            semaphores.local(cotangent_ref.at[chip], c_slots[0]),
        ]
        for copy in first + local_later[0] + local_later[1] + local_later[2] + local_rest:
            copy.start()
        entry_barrier(where.everyone())

        x_cross = semaphores.remote(decoder_ref.at[1 - chip], x_slots[1], where.other_chip)
        x_core = semaphores.remote(decoder_ref.at[chip], x_slots[2], where.other_core)
        x_pass = semaphores.remote(x_slots[1], x_slots[3], where.other_core)
        s_cross = semaphores.remote(source_ref.at[1 - chip], s_slots[1], where.other_chip)
        s_core = semaphores.remote(source_ref.at[chip], s_slots[2], where.other_core)
        s_pass = semaphores.remote(s_slots[1], s_slots[3], where.other_core)
        c_cross = semaphores.remote(cotangent_ref.at[1 - chip], c_slots[1], where.other_chip)
        gain_sends = [
            semaphores.remote(gain_in, gain_ref.at[place], partner)
            for partner in (where.other_core, where.other_chip, where.diagonal)
        ]
        qkv_planes = [semaphores.remote(mine, mine, partner) for partner in where.other_planes]
        qkv_side = semaphores.remote(
            qkv_ref.at[place, side], qkv_ref.at[place, side], where.other_side
        )
        qkv_core = semaphores.remote(qkv_ref.at[place], qkv_ref.at[place], where.other_core)
        qkv_chip = semaphores.remote(qkv_ref.at[place], qkv_ref.at[place], where.other_chip)
        across = column(2)
        qkv_pass = semaphores.remote(qkv_ref.at[across], qkv_ref.at[across], where.other_core)
        later = []
        for buffer in (later_a, later_b, later_c):
            block = buffer.at[place, side, plane]
            later.append(
                dict(
                    planes=[semaphores.remote(block, block, p) for p in where.other_planes],
                    chip=[
                        semaphores.remote(
                            buffer.at[place, side], buffer.at[place, side], where.other_chip
                        )
                    ],
                    side=[
                        semaphores.remote(
                            buffer.at[at, side], buffer.at[at, side], where.other_side
                        )
                        for at in (place, across)
                    ],
                    core=[
                        semaphores.remote(buffer.at[at], buffer.at[at], where.other_core)
                        for at in (place, across)
                    ],
                )
            )

        def begin(copies):
            for copy in copies:
                copy.start()

        def arrive(copies):
            for copy in copies:
                copy.wait_recv()

        x_cross.start()
        x_core.start()
        for copy in [local_gain, *local_qkv]:
            copy.wait()
        begin(gain_sends)
        begin(qkv_planes)
        begin([s_cross, s_core])
        for copies, piece in zip(local_later, later):
            for copy in copies:
                copy.wait()
            begin(piece["planes"])

    length = source_len_ref[where.group * 2 + chip] * upsample_ref[where.group * 2 + chip]
    mask_columns(chip, core, rows, total, BLOCK, length, mask_ref)

    def hide(slot):
        gain = jnp.concatenate([gain_ref[at, 0:1, :] for at in range(pairs)], axis=1)

        def step(index, _):
            at = block_at(index + slot * (rows // BLOCK), BLOCK)
            scaled, _ = normalize(x_ref[at, :].astype(f32))
            hidden_ref[at, :] = (scaled * gain).astype(bf16)
            return 0

        lax.fori_loop(0, rows // BLOCK, step, 0)

    def take_weights(pair):
        for part in range(3):
            for at in range(8):
                weight_ref[at * 64 : at * 64 + 64, part * PAIR : (part + 1) * PAIR] = qkv_ref[
                    pair, at % 2, at // 2, part * 64 : part * 64 + 64, :
                ]

    def project(pair, slot, count):
        def step(index, _):
            at = block_at(index + slot * (rows // BLOCK), BLOCK)
            both = dot(hidden_ref[at, :], weight_ref[:, PAIR:]).astype(bf16)
            k_ref[pair, at, :] = both[:, :PAIR]
            v_ref[pair, at, :] = both[:, PAIR:]
            return 0

        def query_step(index, _):
            at = block_at(index + slot * (rows // BLOCK), BLOCK)
            query = dot(hidden_ref[at, :], weight_ref[:, :PAIR]) * (0.125 * LOG2E)
            q_ref[pair, at, :] = query.astype(bf16)
            return 0

        lax.fori_loop(0, count * (rows // BLOCK), step, 0)
        if slot < 2:
            lax.fori_loop(0, min(2 - slot, count) * (rows // BLOCK), query_step, 0)

    if comm:
        local_x.wait()
        arrive(gain_sends)
        hide(0)
        arrive([x_core])
        hide(2)
        arrive(qkv_planes)
        qkv_side.start()
        arrive([x_cross])
        x_pass.start()
        hide(1)
        arrive([qkv_side])
        begin([qkv_core, qkv_chip])
        take_weights(place)
        project(place, 0, 1)
        project(place, 2, 1)
        project(place, 1, 1)
        arrive([x_pass])
        hide(3)
        project(place, 3, 1)
    else:
        for slot in range(4):
            hide(slot)
        take_weights(place)
        project(place, 0, 4)

    size = 2 * BLOCK
    blocks = own // size
    lane = lax.broadcasted_iota(jnp.int32, (size, PAIR), 1)

    def outs_of(pair):
        return [
            (q_ref.at[pair], q_out.at[pair]),
            (k_ref.at[pair], k_out.at[pair]),
            (v_ref.at[pair], v_out.at[pair]),
            (mixed_ref.at[pair], mixed_out.at[pair]),
            (extra_ref.at[pair], extra_out.at[pair]),
        ]

    first_out = semaphores.count

    def out_copies(step, pair):
        return [
            pltpu.make_async_copy(source, target, send.at[first_out + step * 5 + at])
            for at, (source, target) in enumerate(outs_of(pair))
        ]

    def when(index, value, todo):
        pl.when(index == value)(todo)

    def step(index, _):
        turn = index // blocks
        pair = column(turn)
        if comm:
            a, b, c = later

            @pl.when(index == 0)
            def _():
                arrive(a["planes"])
                begin(a["chip"])

            @pl.when(index == 1)
            def _():
                arrive(b["planes"])
                begin(b["chip"])
                arrive(c["planes"])
                begin(c["chip"])

            @pl.when(index == 2)
            def _():
                arrive([qkv_core])
                arrive(a["chip"])
                begin(a["side"])

            @pl.when(index == 3)
            def _():
                arrive([qkv_chip])
                qkv_pass.start()
                arrive(b["chip"])
                begin(b["side"])
                local_rest[0].wait()
                arrive([s_cross])
                s_pass.start()
                c_cross.start()

            @pl.when(index == 4)
            def _():
                arrive(c["chip"])
                begin(c["side"])
                arrive(a["side"])
                begin(a["core"])

            @pl.when(index == 6)
            def _():
                arrive([qkv_pass])
                arrive(b["side"])
                begin(b["core"])

        @pl.when((index % blocks == 0) & (index > 0))
        def _():
            take_weights(pair)
            project(pair, 0, 4)

        at = block_at(index % blocks, size)
        mixed, extras = attend_pair(
            q_ref[pair, at, :], k_ref[pair], mask_ref[...], v_ref[pair], lane
        )
        mixed_ref[pair, at, :] = mixed
        extra_ref[pair, 0, at, :] = extras[0]
        extra_ref[pair, 1, at, :] = extras[1]

        @pl.when(index % blocks == blocks - 1)
        def _():
            for copy in out_copies(turn, pair):
                copy.start()

        return 0

    lax.fori_loop(0, pairs * blocks, step, 0)
    if comm:
        x_local = pltpu.make_async_copy(x_ref, x_out, send.at[first_out + 20])
        qkv_local = pltpu.make_async_copy(qkv_ref, qkv_out, send.at[first_out + 21])
        gain_local = pltpu.make_async_copy(gain_ref, gain_out, send.at[first_out + 22])
        for copy in (x_local, qkv_local, gain_local):
            copy.start()
        c = later[2]
        arrive(c["side"])
        begin(c["core"])
        local_rest[1].wait()
        arrive([s_core, s_pass, c_cross])
        for piece in later:
            arrive(piece["core"])
        for copy in semaphores.sent:
            copy.wait_send()
        for copy in (x_local, qkv_local, gain_local):
            copy.wait()
    for turn in range(pairs):
        for copy in out_copies(turn, column(turn)):
            copy.wait()


def whole_weight(ref, blocks, start, count, chunks=1):
    columns, sides, planes = blocks.shape[:3]
    for column in range(columns):
        for side in range(sides):
            for plane in range(planes):
                row = (plane * sides + side) * count
                for chunk in range(chunks):
                    at = (column * chunks + chunk) * PAIR
                    ref[row : row + count, at : at + PAIR] = blocks[
                        column, side, plane, start + chunk * count : start + (chunk + 1) * count, :
                    ]


def middle_kernel(
    planes,
    source_len_ref,
    upsample_ref,
    send_ref,
    x_any,
    mixed_ref,
    cotangent_ref,
    source_ref,
    later_a,
    later_b,
    later_c,
    gain_blocks,
    out_ref,
    grad_mixed_ref,
    grad_self_ref,
    dwo_ref,
    dwcq_ref,
    dwco_ref,
    dw1_ref,
    dw2t_ref,
    dwck_ref,
    dwcv_ref,
    grad_source_ref,
    dgain_ref,
    x_ref,
    wo_ref,
    wcq_ref,
    wck_ref,
    wcv_ref,
    wco_ref,
    w1_ref,
    w2_ref,
    ck_ref,
    cv_ref,
    ckt_ref,
    cextra_ref,
    dck_ref,
    dcv_ref,
    x_sem,
    cm_s,
    extra_s,
    dqt_s,
    dq_s,
    gcm_s,
    qc_s,
):
    rows_own, width = x_ref.shape
    pairs = mixed_ref.shape[0]
    hidden_width = w1_ref.shape[1]
    chunk = 512
    x_copy = pltpu.make_async_copy(x_any.at[:rows_own], x_ref, x_sem)
    x_copy.start()
    where = Where(planes)
    chip, core = where.chip, where.core
    few = source_ref.shape[0]
    deep = width // 8
    for at, ref in enumerate((wo_ref, wcq_ref, wck_ref, wcv_ref, wco_ref)):
        whole_weight(ref, later_a, at * deep, deep)
    whole_weight(w1_ref, later_b, 0, deep, hidden_width // width)
    whole_weight(w2_ref, later_c, 0, hidden_width // 8)
    gain_rows = jnp.concatenate([gain_blocks[at] for at in range(pairs)], axis=1)
    gain_two = gain_rows[1:2, :]
    gain_three = gain_rows[2:3, :]
    lane = lax.broadcasted_iota(jnp.int32, (BLOCK, PAIR), 1)
    offset = lax.broadcasted_iota(jnp.int32, (BLOCK, 1), 0)
    for ref in (dwo_ref, dwcq_ref, dwco_ref, dw1_ref, dw2t_ref, dck_ref, dcv_ref, dgain_ref):
        ref[...] = jnp.zeros(ref.shape, f32)

    dp_size = planes * 2
    group, half_way = where.group, planes
    sentence = group * 2 + chip
    src_len = source_len_ref[sentence]
    dec_len = src_len * upsample_ref[sentence]
    moved = chip * send_ref[group]
    holder = (group + moved * half_way) % dp_size
    partner = (holder + half_way) % dp_size

    def tokens_of(slot):
        return source_len_ref[slot] * upsample_ref[slot]

    tokens = (
        tokens_of(holder * 2)
        + tokens_of(holder * 2 + 1) * (1 - send_ref[holder])
        + tokens_of(partner * 2 + 1) * send_ref[partner]
    )
    loss_scale = jnp.full((1, 1), rows_own * 2, f32) / jnp.full((1, 1), tokens, jnp.int32).astype(f32)
    mask_columns(chip, core, few // 4, few, few // 4, src_len, cextra_ref)

    def source_step(index, _):
        rows = block_at(index, BLOCK)
        source = source_ref[rows, :]
        key_rows = dot(source, wck_ref[...]).astype(bf16)
        value_rows = dot(source, wcv_ref[...]).astype(bf16)
        for pair in range(pairs):
            part = key_rows[:, pair * PAIR : (pair + 1) * PAIR]
            ck_ref[pair, rows, :] = part
            ckt_ref[pair, :, rows] = part.T
            cv_ref[pair, rows, :] = value_rows[:, pair * PAIR : (pair + 1) * PAIR]
        return 0

    lax.fori_loop(0, few // BLOCK, source_step, 0)
    x_copy.wait()

    def step(index, _):
        rows = block_at(index, BLOCK)
        place = block_places(chip, core, rows_own // 2, offset, index, BLOCK)
        counted = jnp.where(place < dec_len, 1.0, 0.0)
        self_rows = jnp.concatenate([mixed_ref[pair, rows, :] for pair in range(pairs)], axis=1)
        after_self = x_ref[rows, :].astype(f32) + dot(self_rows, wo_ref[...])
        scaled_two, inverse_two = normalize(after_self)
        hidden_two = (scaled_two * gain_two).astype(bf16)
        queries = (dot(hidden_two, wcq_ref[...]) * (0.125 * LOG2E)).astype(bf16)
        for pair in range(pairs):
            qc_s[pair] = queries[:, pair * PAIR : (pair + 1) * PAIR]

        def cross(pair, _):
            mixed, extras = attend_pair(
                qc_s[pair], ck_ref[pair], cextra_ref[...], cv_ref[pair], lane
            )
            cm_s[pair] = mixed
            extra_s[2 * pair] = extras[0]
            extra_s[2 * pair + 1] = extras[1]
            return 0

        lax.fori_loop(0, pairs, cross, 0)
        cross_rows = jnp.concatenate([cm_s[pair] for pair in range(pairs)], axis=1)
        after_cross = after_self + dot(cross_rows, wco_ref[...])
        scaled_three, inverse_three = normalize(after_cross)
        hidden_three = (scaled_three * gain_three).astype(bf16)
        grad_final = cotangent_ref[rows, :].astype(f32) * (counted * loss_scale)
        grad_ffn = grad_final.astype(bf16)
        hidden_columns = hidden_three.T
        grad_columns = grad_ffn.T
        final = after_cross
        grad_hidden = jnp.zeros((BLOCK, width), f32)
        for part in range(hidden_width // chunk):
            columns = slice(part * chunk, (part + 1) * chunk)
            expanded = dot(hidden_three, w1_ref[:, columns])
            square = expanded * expanded
            bend = jnp.tanh(GELU_IN * expanded * (1.0 + GELU_CUBE * square))
            half = 0.5 * (1.0 + bend)
            activated = (expanded * half).astype(bf16)
            slope = half + 0.5 * expanded * (1.0 - bend * bend) * (
                GELU_IN * (1.0 + 3.0 * GELU_CUBE * square)
            )
            grad_expanded = (dot_nt(grad_ffn, w2_ref[columns, :]) * slope).astype(bf16)
            final = final + dot(activated, w2_ref[columns, :])
            dw2t_ref[:, columns] += dot(grad_columns, activated)
            dw1_ref[:, columns] += dot(hidden_columns, grad_expanded)
            grad_hidden = grad_hidden + dot_nt(grad_expanded, w1_ref[:, columns])
        out_ref[rows, :] = (final * counted).astype(bf16)
        back, gain_sum = norm_back(grad_hidden, scaled_three, inverse_three, gain_three)
        dgain_ref[2:3, :] += gain_sum
        grad_cross = grad_final + back
        branch = grad_cross.astype(bf16)
        dwco_ref[...] += dot(cross_rows.T, branch)
        grad_mixed = dot_nt(branch, wco_ref[...]).astype(bf16)
        for pair in range(pairs):
            gcm_s[pair] = grad_mixed[:, pair * PAIR : (pair + 1) * PAIR]

        def cross_back(pair, _):
            def add_key(_, value):
                dck_ref[pair] += value

            def add_value(_, value):
                dcv_ref[pair] += value

            extra = cextra_ref[...]
            dqt_s[pair] = attend_pair_back(
                qc_s[pair],
                gcm_s[pair],
                cm_s[pair],
                [extra_s[2 * pair], extra_s[2 * pair + 1]],
                lambda _: jnp.concatenate([ck_ref[pair], extra], axis=1),
                lambda _: jnp.concatenate([cv_ref[pair], extra], axis=1),
                lambda _, head: ckt_ref[pair, 64 * head : 64 * head + 64, :],
                1,
                lane,
                add_key,
                add_value,
            )
            dq_s[pair] = dqt_s[pair].T
            return 0

        lax.fori_loop(0, pairs, cross_back, 0)
        query_grad = jnp.concatenate([dq_s[pair] for pair in range(pairs)], axis=1)
        dwcq_ref[...] += dot(hidden_two.T, query_grad)
        back, gain_sum = norm_back(
            dot_nt(query_grad, wcq_ref[...]), scaled_two, inverse_two, gain_two
        )
        dgain_ref[1:2, :] += gain_sum
        grad_self = grad_cross + back
        grad_self_ref[rows, :] = grad_self
        branch = grad_self.astype(bf16)
        dwo_ref[...] += dot(self_rows.T, branch)
        grad_mixed = dot_nt(branch, wo_ref[...]).astype(bf16)
        for pair in range(pairs):
            grad_mixed_ref[pair, rows, :] = grad_mixed[:, pair * PAIR : (pair + 1) * PAIR]
        return 0

    lax.fori_loop(0, rows_own // BLOCK, step, 0)
    dwck_ref[...] = jnp.zeros(dwck_ref.shape, f32)
    dwcv_ref[...] = jnp.zeros(dwcv_ref.shape, f32)

    def gathered(ref, rows, factor):
        parts = [(ref[pair, rows, :] * factor).astype(bf16) for pair in range(pairs)]
        return jnp.concatenate(parts, axis=1)

    def source_back(index, _):
        rows = block_at(index, BLOCK)
        source_columns = source_ref[rows, :].T
        key_grad = gathered(dck_ref, rows, LN2)
        value_grad = gathered(dcv_ref, rows, 1.0)
        dwck_ref[...] += dot(source_columns, key_grad)
        dwcv_ref[...] += dot(source_columns, value_grad)
        grad_source_ref[rows, :] = dot_nt(key_grad, wck_ref[...]) + dot_nt(
            value_grad, wcv_ref[...]
        )
        return 0

    lax.fori_loop(0, few // BLOCK, source_back, 0)


def self_back_kernel(
    planes,
    source_len_ref,
    upsample_ref,
    q_ref,
    k_ref,
    v_ref,
    mixed_ref,
    grad_ref,
    query_extra_ref,
    dqt_ref,
    dk_ref,
    dv_ref,
    keys_s,
    values_s,
    kt_s,
):
    pairs, rows_own, _ = q_ref.shape
    keys = k_ref.shape[1]
    where = Where(planes)
    sentence = where.group * 2 + where.chip
    length = source_len_ref[sentence] * upsample_ref[sentence]
    extra = values_s.at[:, PAIR:]
    mask_columns(where.chip, where.core, keys // 4, keys, BLOCK, length, extra)
    keys_s[:, PAIR:] = values_s[:, PAIR:]
    size = 2 * BLOCK
    blocks = rows_own // size
    lane = lax.broadcasted_iota(jnp.int32, (size, PAIR), 1)
    chunk = 512

    def step(index, _):
        pair = index // blocks
        rows = block_at(index % blocks, size)

        @pl.when(index % blocks == 0)
        def _():
            dk_ref[pair] = jnp.zeros((keys, PAIR), f32)
            dv_ref[pair] = jnp.zeros((keys, PAIR), f32)
            keys_s[:, :PAIR] = k_ref[pair]
            values_s[:, :PAIR] = v_ref[pair]
            kt_s[...] = k_ref[pair].T

        def part(ref):
            return lambda at: ref[at * chunk : (at + 1) * chunk, :]

        def add_to(ref):
            def add(at, value):
                ref[pair, at * chunk : (at + 1) * chunk, :] += value

            return add

        dqt_ref[pair, :, rows] = attend_pair_back(
            q_ref[pair, rows, :],
            grad_ref[pair, rows, :],
            mixed_ref[pair, rows, :],
            [query_extra_ref[pair, head, rows, :] for head in (0, 1)],
            part(keys_s),
            part(values_s),
            lambda at, head: kt_s[64 * head : 64 * head + 64, at * chunk : (at + 1) * chunk],
            keys // chunk,
            lane,
            add_to(dk_ref),
            add_to(dv_ref),
        )
        return 0

    lax.fori_loop(0, pairs * blocks, step, 0)


def close_kernel(
    own,
    x_ref,
    qkv_ref,
    gain_blocks,
    dqt_ref,
    dk_ref,
    dv_ref,
    grad_self_ref,
    own_ref,
    other_ref,
    dwq_ref,
    dwk_ref,
    dwv_ref,
    dgain_ref,
    wq_ref,
    wk_ref,
    wv_ref,
):
    pairs = dk_ref.shape[0]
    gain = jnp.concatenate([gain_blocks[at, 0:1, :] for at in range(pairs)], axis=1)
    deep = x_ref.shape[1] // 8
    for at, ref in enumerate((wq_ref, wk_ref, wv_ref)):
        whole_weight(ref, qkv_ref, at * deep, deep)
    for ref in (dwq_ref, dwk_ref, dwv_ref, dgain_ref):
        ref[...] = jnp.zeros(ref.shape, f32)

    def gathered(ref, rows, factor):
        parts = [(ref[pair, rows, :] * factor).astype(bf16) for pair in range(pairs)]
        return jnp.concatenate(parts, axis=1)

    def common(rows):
        scaled, inverse = normalize(x_ref[rows, :].astype(f32))
        hidden_columns = (scaled * gain).astype(bf16).T
        key_grad = gathered(dk_ref, rows, LN2)
        value_grad = gathered(dv_ref, rows, 1.0)
        dwk_ref[...] += dot(hidden_columns, key_grad)
        dwv_ref[...] += dot(hidden_columns, value_grad)
        upstream = dot_nt(key_grad, wk_ref[...]) + dot_nt(value_grad, wv_ref[...])
        return scaled, inverse, hidden_columns, upstream

    def own_step(index, _):
        rows = block_at(index, BLOCK)
        scaled, inverse, hidden_columns, upstream = common(rows)
        parts = [dqt_ref[pair, :, rows].T for pair in range(pairs)]
        query_grad = jnp.concatenate(parts, axis=1)
        dwq_ref[...] += dot(hidden_columns, query_grad)
        upstream = upstream + dot_nt(query_grad, wq_ref[...])
        back, gain_sum = norm_back(upstream, scaled, inverse, gain)
        dgain_ref[0:1, :] += gain_sum
        own_ref[rows, :] = grad_self_ref[rows, :] + back
        return 0

    def other_step(index, _):
        rows = block_at(index + own // BLOCK, BLOCK)
        scaled, inverse, _, upstream = common(rows)
        back, gain_sum = norm_back(upstream, scaled, inverse, gain)
        dgain_ref[0:1, :] += gain_sum
        other_ref[block_at(index, BLOCK), :] = back.astype(bf16)
        return 0

    lax.fori_loop(0, own // BLOCK, own_step, 0)
    lax.fori_loop(0, x_ref.shape[0] // BLOCK - own // BLOCK, other_step, 0)


def call(kernel, outs, *operands, scratch=(), smem=0, params=PARAMS, spaces=None, out_space=VMEM):
    spaces = spaces or {}
    return pl.pallas_call(
        kernel,
        out_shape=[jax.ShapeDtypeStruct(shape, kind) for shape, kind in outs],
        in_specs=[
            pl.BlockSpec(memory_space=pltpu.SMEM if at < smem else spaces.get(at, VMEM))
            for at in range(len(operands))
        ],
        out_specs=[pl.BlockSpec(memory_space=out_space)] * len(outs),
        scratch_shapes=list(scratch),
        compiler_params=params,
    )(*operands)


def swapped(value, axis, bit):
    pairs = [(source, source ^ bit) for source in range(lax.axis_size(axis))]
    return lax.ppermute(value, axis, pairs)


def as_blocks(weight, chunks=1):
    height, width = weight.shape
    deep = height // 8
    cut = weight.reshape(4, 2, deep, 4, chunks, PAIR).transpose(3, 1, 0, 4, 2, 5)
    return cut.reshape(4, 2, 4, chunks * deep, PAIR)


def gather_plain(arguments, seq_size, dp_size):
    (decoder_in, source_states, out_grad, narrow, ffn_expand, ffn_reduce, gain_block) = arguments
    chip = lax.axis_index("seq") // 2
    rows_dec = decoder_in.shape[1]
    own = 2 * rows_dec
    outgoing = jnp.concatenate([decoder_in[1 - chip], source_states[1 - chip]], axis=0)
    arrived = swapped(outgoing, "seq", 2)
    own_rows = jnp.concatenate(
        [decoder_in[chip], arrived[:rows_dec], source_states[chip], arrived[rows_dec:]], axis=0
    )
    other_rows = swapped(own_rows, "seq", 1)
    x_all = jnp.concatenate([own_rows[:own], other_rows[:own]], axis=0)
    source_all = jnp.concatenate([own_rows[own:], other_rows[own:]], axis=0)
    cotangent = jnp.concatenate([out_grad[chip], swapped(out_grad[1 - chip], "seq", 2)], axis=0)

    def whole(weight):
        weight = lax.all_gather(weight, "seq", axis=1, tiled=True)
        return lax.all_gather(weight, "dp", axis=0, tiled=True)

    blocks = [as_blocks(whole(weight)) for weight in narrow]
    qkv = jnp.concatenate(blocks[:3], axis=3)
    later_a = jnp.concatenate(blocks[3:], axis=3)
    later_b = as_blocks(whole(ffn_expand), ffn_expand.shape[1] // PAIR)
    later_c = as_blocks(whole(ffn_reduce))
    gains = lax.all_gather(gain_block, "seq", axis=0)
    return x_all, source_all, cotangent, qkv, later_a, later_b, later_c, gains


def body(
    decoder_in,
    source_states,
    source_len,
    upsample,
    send_counts,
    self_query,
    self_key,
    self_value,
    self_output,
    cross_query,
    cross_key,
    cross_value,
    cross_output,
    ffn_expand,
    ffn_reduce,
    norm_gains,
    out_grad,
):
    both = ("dp", "seq")
    seq_size = lax.axis_size("seq")
    dp_size = lax.axis_size("dp")
    devices = dp_size * seq_size
    planes = dp_size // 2
    place = lax.axis_index("seq")
    chip = place // 2
    home_count, rows_dec, width = decoder_in.shape
    rows_src = source_states.shape[1]
    pairs = width // PAIR
    own = 2 * rows_dec
    total = 4 * rows_dec
    deep = self_query.shape[0]
    deep_two = ffn_reduce.shape[0]
    wide = ffn_expand.shape[1] // PAIR
    hidden_width = wide * PAIR * seq_size
    gain_block = jnp.pad(norm_gains.astype(f32), ((0, 5), (0, 0)))
    all_src = 4 * rows_src
    comm = dp_size == 8

    def pair_rows(rows):
        return (pairs, rows, PAIR)

    narrow = (self_query, self_key, self_value, self_output)
    narrow += (cross_query, cross_key, cross_value, cross_output)
    rows_outs = [
        (pair_rows(own), bf16),
        (pair_rows(total), bf16),
        (pair_rows(total), bf16),
        (pair_rows(own), bf16),
        ((pairs, 2, own, PAIR), bf16),
    ]
    buffers = [VMEM(shape, kind) for shape, kind in rows_outs]
    work = [
        VMEM((total, width), bf16),
        VMEM((width, 3 * PAIR), bf16),
        VMEM((total, PAIR), bf16),
        *buffers,
    ]
    semaphores = [pltpu.SemaphoreType.DMA((96,)), pltpu.SemaphoreType.DMA((96,))]
    if comm:
        cut = (seq_size, 2, planes)
        gathered = [
            ((total, width), bf16),
            ((all_src, width), bf16),
            ((own, width), bf16),
            (cut + (3 * deep, PAIR), bf16),
            (cut + (5 * deep, PAIR), bf16),
            (cut + (wide * deep, PAIR), bf16),
            (cut + (deep_two, PAIR), bf16),
            ((seq_size, 8, PAIR), f32),
        ]
        operands = (source_len, upsample, decoder_in, source_states, out_grad)
        operands += (*narrow, ffn_expand, ffn_reduce, gain_block)
        (
            x_all, source_all, cotangent, qkv, later_a, later_b, later_c, gains,
            q, k, v, mixed, query_extra,
        ) = call(
            partial(open_kernel, True, planes, deep),
            gathered + rows_outs,
            *operands,
            scratch=[
                VMEM((total, width), bf16),
                VMEM(cut + (3 * deep, PAIR), bf16),
                VMEM((seq_size, 8, PAIR), f32),
                *work,
                *semaphores,
            ],
            smem=2,
            spaces={at: pl.ANY for at in range(2, len(operands))},
            out_space=pl.ANY,
            params=pltpu.CompilerParams(
                vmem_limit_bytes=VMEM_LIMIT, collective_id=0, has_side_effects=True
            ),
        )
    else:
        x_all, source_all, cotangent, qkv, later_a, later_b, later_c, gains = gather_plain(
            (decoder_in, source_states, out_grad, narrow, ffn_expand, ffn_reduce, gain_block),
            seq_size,
            dp_size,
        )
        q, k, v, mixed, query_extra = call(
            partial(open_kernel, False, planes, deep),
            rows_outs,
            source_len,
            upsample,
            x_all,
            qkv,
            gains,
            scratch=[*work, *semaphores],
            smem=2,
            out_space=pl.ANY,
        )
    square = ((width, width), f32)
    (
        out_rows,
        grad_mixed,
        grad_self,
        dwo,
        dwcq,
        dwco,
        dw1,
        dw2t,
        dwck,
        dwcv,
        grad_source,
        dgain,
    ) = call(
        partial(middle_kernel, planes),
        [
            ((own, width), bf16),
            (pair_rows(own), bf16),
            ((own, width), f32),
            square,
            square,
            square,
            ((width, hidden_width), f32),
            ((width, hidden_width), f32),
            square,
            square,
            ((all_src, width), f32),
            ((8, width), f32),
        ],
        source_len,
        upsample,
        send_counts,
        x_all,
        mixed,
        cotangent,
        source_all,
        later_a,
        later_b,
        later_c,
        gains,
        scratch=[
            VMEM((own, width), bf16),
            *[VMEM((width, width), bf16)] * 5,
            VMEM((width, hidden_width), bf16),
            VMEM((hidden_width, width), bf16),
            VMEM(pair_rows(all_src), bf16),
            VMEM(pair_rows(all_src), bf16),
            VMEM((pairs, PAIR, all_src), bf16),
            VMEM((all_src, PAIR), bf16),
            VMEM(pair_rows(all_src), f32),
            VMEM(pair_rows(all_src), f32),
            pltpu.SemaphoreType.DMA,
            VMEM((pairs, BLOCK, PAIR), bf16),
            VMEM((2 * pairs, BLOCK, PAIR), bf16),
            VMEM((pairs, PAIR, BLOCK), bf16),
            VMEM((pairs, BLOCK, PAIR), bf16),
            VMEM((pairs, BLOCK, PAIR), bf16),
            VMEM((pairs, BLOCK, PAIR), bf16),
        ],
        smem=3,
        spaces={3: pl.ANY},
    )
    dqt, dk, dv = call(
        partial(self_back_kernel, planes),
        [
            ((pairs, PAIR, own), bf16),
            (pair_rows(total), f32),
            (pair_rows(total), f32),
        ],
        source_len,
        upsample,
        q,
        k,
        v,
        mixed,
        grad_mixed,
        query_extra,
        scratch=[VMEM((total, 2 * PAIR), bf16)] * 2 + [VMEM((PAIR, total), bf16)],
        smem=2,
    )
    own_grad, other_grad, dwq, dwk, dwv, dgain_one = call(
        partial(close_kernel, own),
        [
            ((own, width), f32),
            ((total - own, width), bf16),
            square,
            square,
            square,
            ((8, width), f32),
        ],
        x_all,
        qkv,
        gains,
        dqt,
        dk,
        dv,
        grad_self,
        scratch=[VMEM((width, width), bf16)] * 3,
    )

    half_src = all_src // 2
    crossing = jnp.concatenate([other_grad, grad_source[half_src:].astype(bf16)], axis=0)
    returned = swapped(crossing, "seq", 1).astype(f32)
    grad_rows = own_grad + returned[:own]
    source_rows = grad_source[:half_src] + returned[own:]
    homeward = jnp.concatenate(
        [out_rows[rows_dec:], grad_rows[rows_dec:].astype(bf16), source_rows[rows_src:].astype(bf16)],
        axis=0,
    )
    came = swapped(homeward, "seq", 2)

    def both_sentences(mine, theirs):
        return jnp.where(chip == 0, jnp.stack([mine, theirs]), jnp.stack([theirs, mine]))

    decoder_out = both_sentences(out_rows[:rows_dec], came[:rows_dec])
    grad_decoder = both_sentences(grad_rows[:rows_dec], came[rows_dec : 2 * rows_dec].astype(f32))
    grad_src = both_sentences(source_rows[:rows_src], came[2 * rows_dec :].astype(f32))

    def shares(grad, depth, columns):
        parts = grad.reshape(dp_size, depth, seq_size, columns).swapaxes(1, 2)
        return parts.reshape(dp_size, seq_size, depth * columns // PAIR, PAIR)

    dgains = jnp.stack([dgain_one[0], dgain[1], dgain[2]])
    dgains = jnp.concatenate([dgains, jnp.zeros((13, width), f32)], axis=0)
    dgains = dgains.reshape(1, 16, seq_size, PAIR).swapaxes(1, 2)
    dgains = jnp.broadcast_to(dgains, (dp_size, seq_size, 16, PAIR))
    dw2_parts = dw2t.reshape(seq_size, PAIR, dp_size, deep_two).transpose(2, 0, 1, 3)
    dw2_parts = dw2_parts.reshape(dp_size, seq_size, deep_two, PAIR)
    grads = [shares(grad, deep, PAIR) for grad in (dwq, dwk, dwv, dwo, dwcq, dwck, dwcv, dwco)]
    grads += [shares(dw1, deep, wide * PAIR), dw2_parts, dgains]
    grads = jnp.concatenate([grad.astype(bf16) for grad in grads], axis=2)
    total = lax.psum_scatter(
        grads.reshape(devices, -1, PAIR), both, scatter_dimension=0, tiled=True
    )[0].astype(f32)
    outs = [total[at * deep : (at + 1) * deep] for at in range(8)]
    start = 8 * deep
    outs.append(total[start : start + wide * deep].reshape(deep, wide * PAIR))
    start += wide * deep
    outs.append(total[start : start + deep_two].reshape(PAIR, deep_two).T)
    start += deep_two
    outs.append(total[start : start + 3])
    return (decoder_out, grad_decoder, grad_src, *outs)


def solution(mesh):
    rows = P("dp", "seq", None)
    weight = P("dp", "seq")
    placed = (rows, rows, P(), P(), P()) + (weight,) * 10 + (P(None, "seq"), rows)
    return jax.shard_map(
        body,
        mesh=mesh,
        in_specs=placed,
        out_specs=(rows, rows, rows) + (weight,) * 10 + (P(None, "seq"),),
        check_vma=False,
    )
```

```python
from functools import partial

import jax
import jax.numpy as jnp
from jax import lax
from jax.experimental import pallas as pl
from jax.experimental.pallas import tpu as pltpu
from jax.sharding import PartitionSpec as P

HEADS = 8
EPSILON = 1e-05
NEGATIVE = -1000000000.0
LOG2E = 1.4426950408889634
LN2 = 0.6931471805599453
GELU_IN = 0.7978845608028654
GELU_CUBE = 0.044715
BLOCK = 256
PAIR = 128

bf16 = jnp.bfloat16
f32 = jnp.float32
VMEM = pltpu.VMEM
VMEM_LIMIT = 60 * 1024 * 1024
PARAMS = pltpu.CompilerParams(vmem_limit_bytes=VMEM_LIMIT)


def dot(left, right):
    return jnp.dot(left, right, preferred_element_type=f32)


def dot_nt(left, right):
    return lax.dot_general(left, right, (((1,), (1,)), ((), ())), preferred_element_type=f32)


def block_at(index, size):
    return pl.ds(pl.multiple_of(index * size, size), size)


def row_mean(values):
    return jnp.mean(values, axis=-1, keepdims=True)


def normalize(values):
    centred = values - row_mean(values)
    inverse = lax.rsqrt(row_mean(centred * centred) + EPSILON)
    return centred * inverse, inverse


def norm_back(upstream, scaled, inverse, gain):
    inner = upstream * gain
    back = inverse * (inner - row_mean(inner) - scaled * row_mean(inner * scaled))
    return back, jnp.sum(upstream * scaled, axis=0, keepdims=True)


def three_parts(column, lane, last):
    high = column.astype(bf16).astype(f32)
    middle = (column - high).astype(bf16).astype(f32)
    low = column - high - middle
    rest = jnp.where(lane == 3, last, 0.0)
    return jnp.where(
        lane == 0, high, jnp.where(lane == 1, middle, jnp.where(lane == 2, low, rest))
    ).astype(bf16)


def one_head(values, first, head):
    zero = jnp.zeros_like(values)
    return jnp.where(first, values, zero) if head == 0 else jnp.where(first, zero, values)


def attend_pair(query, keys, key_extra, values, lane):
    first = lane < 64
    ones = jnp.where(lane == 3, 1.0, 0.0).astype(bf16)
    keys = jnp.concatenate([keys, key_extra], axis=1)
    scores = [
        dot_nt(jnp.concatenate([one_head(query, first, head), ones], axis=1), keys)
        for head in (0, 1)
    ]
    mixed, extras = [], []
    for head in (0, 1):
        peak = jnp.max(scores[head], axis=1, keepdims=True)
        exps = jnp.exp2(scores[head] - peak)
        total = jnp.sum(exps, axis=1, keepdims=True)
        mixed.append(dot(exps.astype(bf16), values) * (1.0 / total))
        extras.append(three_parts(-(peak + jnp.log2(total)), lane, 1.0))
    return jnp.where(first, mixed[0], mixed[1]).astype(bf16), extras


def attend_pair_back(
    query, grad, mixed, query_extra, key_at, value_at, key_columns_at, chunks, lane, add_key, add_value
):
    first = lane < 64
    product = grad.astype(f32) * mixed.astype(f32)
    queries = [one_head(query, first, head) for head in (0, 1)]
    grads = [one_head(grad, first, head) for head in (0, 1)]
    long_queries = [jnp.concatenate([queries[h], query_extra[h]], axis=1) for h in (0, 1)]
    long_grads = []
    for head in (0, 1):
        delta = jnp.sum(one_head(product, first, head), axis=1, keepdims=True)
        long_grads.append(
            jnp.concatenate([grads[head], three_parts(-delta, lane, 0.0)], axis=1)
        )
    both_queries = jnp.concatenate(queries, axis=0)
    both_grads = jnp.concatenate(grads, axis=0)
    query_grads = [jnp.zeros((64, query.shape[0]), f32)] * 2
    for chunk in range(chunks):
        keys, values = key_at(chunk), value_at(chunk)
        probs, score_grads = [], []
        for head in (0, 1):
            prob = jnp.exp2(dot_nt(keys, long_queries[head]))
            score_grad = (prob * dot_nt(values, long_grads[head])).astype(bf16)
            probs.append(prob.astype(bf16))
            score_grads.append(score_grad)
            query_grads[head] = query_grads[head] + dot(key_columns_at(chunk, head), score_grad)
        add_value(chunk, dot(jnp.concatenate(probs, axis=1), both_grads))
        add_key(chunk, dot(jnp.concatenate(score_grads, axis=1), both_queries))
    return (jnp.concatenate(query_grads, axis=0) * 0.125).astype(bf16)


def copy_to(source, target, send, receive, partner):
    return pltpu.make_async_remote_copy(
        src_ref=source,
        dst_ref=target,
        send_sem=send,
        recv_sem=receive,
        device_id=partner,
        device_id_type=pl.DeviceIdType.MESH,
    )


def entry_barrier(partners):
    barrier = pltpu.get_barrier_semaphore()
    for partner in partners:
        pl.semaphore_signal(
            barrier, inc=1, device_id=partner, device_id_type=pl.DeviceIdType.MESH
        )
    pl.semaphore_wait(barrier, len(partners))


class Where:
    def __init__(self, planes):
        group, self.place = lax.axis_index("dp"), lax.axis_index("seq")
        self.group = group
        self.chip, self.core = self.place // 2, self.place % 2
        self.plane, self.side = group // 2, group % 2
        self.planes = planes
        self.other_core = self.at(self.chip, 1 - self.core)
        self.other_chip = self.at(1 - self.chip, self.core)
        self.diagonal = self.at(1 - self.chip, 1 - self.core)
        self.other_side = {"dp": self.plane * 2 + 1 - self.side}
        self.other_planes = [
            {"dp": (self.plane + step) % planes * 2 + self.side} for step in range(1, planes)
        ]

    def at(self, chip, core):
        return {"seq": chip * 2 + core}

    def column(self, step):
        return (self.chip + step // 2) % 2 * 2 + (self.core + step % 2) % 2

    def everyone(self):
        return [self.other_core, self.other_chip, self.diagonal, self.other_side] + self.other_planes


class Semaphores:
    def __init__(self, send, receive):
        self.send, self.receive, self.count = send, receive, 0
        self.sent = []

    def remote(self, source, target, partner):
        at = self.count
        self.count += 1
        copy = copy_to(source, target, self.send.at[at], self.receive.at[at], partner)
        self.sent.append(copy)
        return copy

    def local(self, source, target):
        at = self.count
        self.count += 1
        return pltpu.make_async_copy(source, target, self.send.at[at])


def block_places(where_chip, where_core, rows, offset, index, size):
    per = rows // size
    slot = index // per
    block = (where_chip + slot % 2) % 2 * 2 + (where_core + slot // 2) % 2
    return block * rows + index % per * size + offset


def mask_columns(where_chip, where_core, rows, count, size, length, ref):
    lane = lax.broadcasted_iota(jnp.int32, (size, PAIR), 1)
    offset = lax.broadcasted_iota(jnp.int32, (size, PAIR), 0)

    def step(index, _):
        places = block_places(where_chip, where_core, rows, offset, index, size)
        bias = jnp.where(places < length, 0.0, NEGATIVE)
        ref[block_at(index, size), :] = jnp.where(
            lane < 3, 1.0, jnp.where(lane == 3, bias, 0.0)
        ).astype(bf16)
        return 0

    lax.fori_loop(0, count // size, step, 0)


def open_kernel(
    comm,
    planes,
    deep,
    source_len_ref,
    upsample_ref,
    *refs,
):
    if comm:
        (
            decoder_ref, source_ref, cotangent_ref,
            wq_in, wk_in, wv_in, *later_in, gain_in,
            x_out, source_out, cotangent_out, qkv_out, later_a, later_b, later_c, gain_out,
            q_out, k_out, v_out, mixed_out, extra_out,
            x_ref, qkv_ref, gain_ref, hidden_ref, weight_ref, mask_ref,
            q_ref, k_ref, v_ref, mixed_ref, extra_ref, send, receive,
        ) = refs
    else:
        (
            x_ref, qkv_ref, gain_ref,
            q_out, k_out, v_out, mixed_out, extra_out,
            hidden_ref, weight_ref, mask_ref,
            q_ref, k_ref, v_ref, mixed_ref, extra_ref, send, receive,
        ) = refs
    where = Where(planes)
    place, plane, side, chip, core = where.place, where.plane, where.side, where.chip, where.core
    total, width = x_ref.shape
    pairs = width // PAIR
    own = total // 2
    rows = total // 4
    semaphores = Semaphores(send, receive)
    column = where.column

    if comm:
        group = where.group
        x_slots = [x_ref.at[slot * rows : (slot + 1) * rows] for slot in range(4)]
        few = source_ref.shape[1]
        s_slots = [source_out.at[slot * few : (slot + 1) * few] for slot in range(4)]
        c_slots = [cotangent_out.at[slot * rows : (slot + 1) * rows] for slot in range(2)]
        local_x = semaphores.local(decoder_ref.at[chip], x_slots[0])
        local_gain = semaphores.local(gain_in, gain_ref.at[place])
        mine = qkv_ref.at[place, side, plane]
        local_qkv = [
            semaphores.local(ref, mine.at[at * deep : (at + 1) * deep])
            for at, ref in enumerate((wq_in, wk_in, wv_in))
        ]
        first = [local_x, local_gain, *local_qkv]
        wo_in, wcq_in, wck_in, wcv_in, wco_in, w1_in, w2_in = later_in
        mine_a = later_a.at[place, side, plane]
        mine_b = later_b.at[place, side, plane]
        mine_c = later_c.at[place, side, plane]
        wide = w1_in.shape[1] // PAIR
        local_later = [
            [
                semaphores.local(ref, mine_a.at[at * deep : (at + 1) * deep])
                for at, ref in enumerate((wo_in, wcq_in, wck_in, wcv_in, wco_in))
            ],
            [
                semaphores.local(
                    w1_in.at[:, at * PAIR : (at + 1) * PAIR], mine_b.at[at * deep : (at + 1) * deep]
                )
                for at in range(wide)
            ],
            [semaphores.local(w2_in, mine_c)],
        ]
        local_rest = [
            semaphores.local(source_ref.at[chip], s_slots[0]),
            semaphores.local(cotangent_ref.at[chip], c_slots[0]),
        ]
        for copy in first + local_later[0] + local_later[1] + local_later[2] + local_rest:
            copy.start()
        entry_barrier(where.everyone())

        x_cross = semaphores.remote(decoder_ref.at[1 - chip], x_slots[1], where.other_chip)
        x_core = semaphores.remote(decoder_ref.at[chip], x_slots[2], where.other_core)
        x_pass = semaphores.remote(x_slots[1], x_slots[3], where.other_core)
        s_cross = semaphores.remote(source_ref.at[1 - chip], s_slots[1], where.other_chip)
        s_core = semaphores.remote(source_ref.at[chip], s_slots[2], where.other_core)
        s_pass = semaphores.remote(s_slots[1], s_slots[3], where.other_core)
        c_cross = semaphores.remote(cotangent_ref.at[1 - chip], c_slots[1], where.other_chip)
        gain_sends = [
            semaphores.remote(gain_in, gain_ref.at[place], partner)
            for partner in (where.other_core, where.other_chip, where.diagonal)
        ]
        qkv_planes = [semaphores.remote(mine, mine, partner) for partner in where.other_planes]
        qkv_side = semaphores.remote(
            qkv_ref.at[place, side], qkv_ref.at[place, side], where.other_side
        )
        qkv_core = semaphores.remote(qkv_ref.at[place], qkv_ref.at[place], where.other_core)
        qkv_chip = semaphores.remote(qkv_ref.at[place], qkv_ref.at[place], where.other_chip)
        across = column(2)
        qkv_pass = semaphores.remote(qkv_ref.at[across], qkv_ref.at[across], where.other_core)
        later = []
        for buffer in (later_a, later_b, later_c):
            block = buffer.at[place, side, plane]
            later.append(
                dict(
                    planes=[semaphores.remote(block, block, p) for p in where.other_planes],
                    chip=[
                        semaphores.remote(
                            buffer.at[place, side], buffer.at[place, side], where.other_chip
                        )
                    ],
                    side=[
                        semaphores.remote(
                            buffer.at[at, side], buffer.at[at, side], where.other_side
                        )
                        for at in (place, across)
                    ],
                    core=[
                        semaphores.remote(buffer.at[at], buffer.at[at], where.other_core)
                        for at in (place, across)
                    ],
                )
            )

        def begin(copies):
            for copy in copies:
                copy.start()

        def arrive(copies):
            for copy in copies:
                copy.wait_recv()

        x_cross.start()
        x_core.start()
        for copy in [local_gain, *local_qkv]:
            copy.wait()
        begin(gain_sends)
        begin(qkv_planes)
        begin([s_cross, s_core])
        for copies, piece in zip(local_later, later):
            for copy in copies:
                copy.wait()
            begin(piece["planes"])

    length = source_len_ref[where.group * 2 + chip] * upsample_ref[where.group * 2 + chip]
    mask_columns(chip, core, rows, total, BLOCK, length, mask_ref)

    def hide(slot):
        gain = jnp.concatenate([gain_ref[at, 0:1, :] for at in range(pairs)], axis=1)

        def step(index, _):
            at = block_at(index + slot * (rows // BLOCK), BLOCK)
            scaled, _ = normalize(x_ref[at, :].astype(f32))
            hidden_ref[at, :] = (scaled * gain).astype(bf16)
            return 0

        lax.fori_loop(0, rows // BLOCK, step, 0)

    def take_weights(pair):
        for part in range(3):
            for at in range(8):
                weight_ref[at * 64 : at * 64 + 64, part * PAIR : (part + 1) * PAIR] = qkv_ref[
                    pair, at % 2, at // 2, part * 64 : part * 64 + 64, :
                ]

    def project(pair, slot, count):
        def step(index, _):
            at = block_at(index + slot * (rows // BLOCK), BLOCK)
            both = dot(hidden_ref[at, :], weight_ref[:, PAIR:]).astype(bf16)
            k_ref[pair, at, :] = both[:, :PAIR]
            v_ref[pair, at, :] = both[:, PAIR:]
            return 0

        def query_step(index, _):
            at = block_at(index + slot * (rows // BLOCK), BLOCK)
            query = dot(hidden_ref[at, :], weight_ref[:, :PAIR]) * (0.125 * LOG2E)
            q_ref[pair, at, :] = query.astype(bf16)
            return 0

        lax.fori_loop(0, count * (rows // BLOCK), step, 0)
        if slot < 2:
            lax.fori_loop(0, min(2 - slot, count) * (rows // BLOCK), query_step, 0)

    if comm:
        local_x.wait()
        arrive(gain_sends)
        hide(0)
        arrive([x_core])
        hide(2)
        arrive(qkv_planes)
        qkv_side.start()
        arrive([x_cross])
        x_pass.start()
        hide(1)
        arrive([qkv_side])
        begin([qkv_core, qkv_chip])
        take_weights(place)
        project(place, 0, 1)
        project(place, 2, 1)
        project(place, 1, 1)
        arrive([x_pass])
        hide(3)
        project(place, 3, 1)
    else:
        for slot in range(4):
            hide(slot)
        take_weights(place)
        project(place, 0, 4)

    size = 2 * BLOCK
    blocks = own // size
    lane = lax.broadcasted_iota(jnp.int32, (size, PAIR), 1)

    def outs_of(pair):
        return [
            (q_ref.at[pair], q_out.at[pair]),
            (k_ref.at[pair], k_out.at[pair]),
            (v_ref.at[pair], v_out.at[pair]),
            (mixed_ref.at[pair], mixed_out.at[pair]),
            (extra_ref.at[pair], extra_out.at[pair]),
        ]

    first_out = semaphores.count

    def out_copies(step, pair):
        return [
            pltpu.make_async_copy(source, target, send.at[first_out + step * 5 + at])
            for at, (source, target) in enumerate(outs_of(pair))
        ]

    def when(index, value, todo):
        pl.when(index == value)(todo)

    def step(index, _):
        turn = index // blocks
        pair = column(turn)
        if comm:
            a, b, c = later

            @pl.when(index == 0)
            def _():
                arrive(a["planes"])
                begin(a["chip"])

            @pl.when(index == 1)
            def _():
                arrive(b["planes"])
                begin(b["chip"])
                arrive(c["planes"])
                begin(c["chip"])

            @pl.when(index == 2)
            def _():
                arrive([qkv_core])
                arrive(a["chip"])
                begin(a["side"])

            @pl.when(index == 3)
            def _():
                arrive([qkv_chip])
                qkv_pass.start()
                arrive(b["chip"])
                begin(b["side"])
                local_rest[0].wait()
                arrive([s_cross])
                s_pass.start()
                c_cross.start()

            @pl.when(index == 4)
            def _():
                arrive(c["chip"])
                begin(c["side"])
                arrive(a["side"])
                begin(a["core"])

            @pl.when(index == 6)
            def _():
                arrive([qkv_pass])
                arrive(b["side"])
                begin(b["core"])

        @pl.when((index % blocks == 0) & (index > 0))
        def _():
            take_weights(pair)
            project(pair, 0, 4)

        at = block_at(index % blocks, size)
        mixed, extras = attend_pair(
            q_ref[pair, at, :], k_ref[pair], mask_ref[...], v_ref[pair], lane
        )
        mixed_ref[pair, at, :] = mixed
        extra_ref[pair, 0, at, :] = extras[0]
        extra_ref[pair, 1, at, :] = extras[1]

        @pl.when(index % blocks == blocks - 1)
        def _():
            for copy in out_copies(turn, pair):
                copy.start()

        return 0

    lax.fori_loop(0, pairs * blocks, step, 0)
    if comm:
        x_local = pltpu.make_async_copy(x_ref, x_out, send.at[first_out + 20])
        qkv_local = pltpu.make_async_copy(qkv_ref, qkv_out, send.at[first_out + 21])
        gain_local = pltpu.make_async_copy(gain_ref, gain_out, send.at[first_out + 22])
        for copy in (x_local, qkv_local, gain_local):
            copy.start()
        c = later[2]
        arrive(c["side"])
        begin(c["core"])
        local_rest[1].wait()
        arrive([s_core, s_pass, c_cross])
        for piece in later:
            arrive(piece["core"])
        for copy in semaphores.sent:
            copy.wait_send()
        for copy in (x_local, qkv_local, gain_local):
            copy.wait()
    for turn in range(pairs):
        for copy in out_copies(turn, column(turn)):
            copy.wait()


def whole_weight(ref, blocks, start, count, chunks=1):
    columns, sides, planes = blocks.shape[:3]
    for column in range(columns):
        for side in range(sides):
            for plane in range(planes):
                row = (plane * sides + side) * count
                for chunk in range(chunks):
                    at = (column * chunks + chunk) * PAIR
                    ref[row : row + count, at : at + PAIR] = blocks[
                        column, side, plane, start + chunk * count : start + (chunk + 1) * count, :
                    ]


def to_blocks(blocks, start, count, ref, chunks=1):
    columns, sides, planes = blocks.shape[:3]
    for column in range(columns):
        for side in range(sides):
            for plane in range(planes):
                row = (plane * sides + side) * count
                for chunk in range(chunks):
                    at = (column * chunks + chunk) * PAIR
                    blocks[
                        column, side, plane, start + chunk * count : start + (chunk + 1) * count, :
                    ] = ref[row : row + count, at : at + PAIR].astype(bf16)


def middle_kernel(
    planes,
    source_len_ref,
    upsample_ref,
    send_ref,
    x_any,
    mixed_ref,
    cotangent_ref,
    source_ref,
    later_a,
    later_b,
    later_c,
    gain_blocks,
    out_ref,
    grad_mixed_ref,
    grad_self_ref,
    part_a,
    part_b,
    part_c,
    grad_source_ref,
    dgain_ref,
    dwo_ref,
    dwcq_ref,
    dwco_ref,
    dw1_ref,
    dw2t_ref,
    dwck_ref,
    dwcv_ref,
    x_ref,
    wo_ref,
    wcq_ref,
    wck_ref,
    wcv_ref,
    wco_ref,
    w1_ref,
    w2_ref,
    ck_ref,
    cv_ref,
    ckt_ref,
    cextra_ref,
    dck_ref,
    dcv_ref,
    x_sem,
    cm_s,
    extra_s,
    dqt_s,
    dq_s,
    gcm_s,
    qc_s,
):
    rows_own, width = x_ref.shape
    pairs = mixed_ref.shape[0]
    hidden_width = w1_ref.shape[1]
    chunk = 512
    x_copy = pltpu.make_async_copy(x_any.at[:rows_own], x_ref, x_sem)
    x_copy.start()
    where = Where(planes)
    chip, core = where.chip, where.core
    few = source_ref.shape[0]
    deep = width // 8
    for at, ref in enumerate((wo_ref, wcq_ref, wck_ref, wcv_ref, wco_ref)):
        whole_weight(ref, later_a, at * deep, deep)
    whole_weight(w1_ref, later_b, 0, deep, hidden_width // width)
    whole_weight(w2_ref, later_c, 0, hidden_width // 8)
    gain_rows = jnp.concatenate([gain_blocks[at] for at in range(pairs)], axis=1)
    gain_two = gain_rows[1:2, :]
    gain_three = gain_rows[2:3, :]
    lane = lax.broadcasted_iota(jnp.int32, (BLOCK, PAIR), 1)
    offset = lax.broadcasted_iota(jnp.int32, (BLOCK, 1), 0)
    for ref in (dwo_ref, dwcq_ref, dwco_ref, dw1_ref, dw2t_ref, dck_ref, dcv_ref, dgain_ref):
        ref[...] = jnp.zeros(ref.shape, f32)

    dp_size = planes * 2
    group, half_way = where.group, planes
    sentence = group * 2 + chip
    src_len = source_len_ref[sentence]
    dec_len = src_len * upsample_ref[sentence]
    moved = chip * send_ref[group]
    holder = (group + moved * half_way) % dp_size
    partner = (holder + half_way) % dp_size

    def tokens_of(slot):
        return source_len_ref[slot] * upsample_ref[slot]

    tokens = (
        tokens_of(holder * 2)
        + tokens_of(holder * 2 + 1) * (1 - send_ref[holder])
        + tokens_of(partner * 2 + 1) * send_ref[partner]
    )
    loss_scale = jnp.full((1, 1), rows_own * 2, f32) / jnp.full((1, 1), tokens, jnp.int32).astype(f32)
    mask_columns(chip, core, few // 4, few, few // 4, src_len, cextra_ref)

    def source_step(index, _):
        rows = block_at(index, BLOCK)
        source = source_ref[rows, :]
        key_rows = dot(source, wck_ref[...]).astype(bf16)
        value_rows = dot(source, wcv_ref[...]).astype(bf16)
        for pair in range(pairs):
            part = key_rows[:, pair * PAIR : (pair + 1) * PAIR]
            ck_ref[pair, rows, :] = part
            ckt_ref[pair, :, rows] = part.T
            cv_ref[pair, rows, :] = value_rows[:, pair * PAIR : (pair + 1) * PAIR]
        return 0

    lax.fori_loop(0, few // BLOCK, source_step, 0)
    x_copy.wait()

    def step(index, _):
        rows = block_at(index, BLOCK)
        place = block_places(chip, core, rows_own // 2, offset, index, BLOCK)
        counted = jnp.where(place < dec_len, 1.0, 0.0)
        self_rows = jnp.concatenate([mixed_ref[pair, rows, :] for pair in range(pairs)], axis=1)
        after_self = x_ref[rows, :].astype(f32) + dot(self_rows, wo_ref[...])
        scaled_two, inverse_two = normalize(after_self)
        hidden_two = (scaled_two * gain_two).astype(bf16)
        queries = (dot(hidden_two, wcq_ref[...]) * (0.125 * LOG2E)).astype(bf16)
        for pair in range(pairs):
            qc_s[pair] = queries[:, pair * PAIR : (pair + 1) * PAIR]

        def cross(pair, _):
            mixed, extras = attend_pair(
                qc_s[pair], ck_ref[pair], cextra_ref[...], cv_ref[pair], lane
            )
            cm_s[pair] = mixed
            extra_s[2 * pair] = extras[0]
            extra_s[2 * pair + 1] = extras[1]
            return 0

        lax.fori_loop(0, pairs, cross, 0)
        cross_rows = jnp.concatenate([cm_s[pair] for pair in range(pairs)], axis=1)
        after_cross = after_self + dot(cross_rows, wco_ref[...])
        scaled_three, inverse_three = normalize(after_cross)
        hidden_three = (scaled_three * gain_three).astype(bf16)
        grad_final = cotangent_ref[rows, :].astype(f32) * (counted * loss_scale)
        grad_ffn = grad_final.astype(bf16)
        hidden_columns = hidden_three.T
        grad_columns = grad_ffn.T
        final = after_cross
        grad_hidden = jnp.zeros((BLOCK, width), f32)
        for part in range(hidden_width // chunk):
            columns = slice(part * chunk, (part + 1) * chunk)
            expanded = dot(hidden_three, w1_ref[:, columns])
            square = expanded * expanded
            bend = jnp.tanh(GELU_IN * expanded * (1.0 + GELU_CUBE * square))
            half = 0.5 * (1.0 + bend)
            activated = (expanded * half).astype(bf16)
            slope = half + 0.5 * expanded * (1.0 - bend * bend) * (
                GELU_IN * (1.0 + 3.0 * GELU_CUBE * square)
            )
            grad_expanded = (dot_nt(grad_ffn, w2_ref[columns, :]) * slope).astype(bf16)
            final = final + dot(activated, w2_ref[columns, :])
            dw2t_ref[:, columns] += dot(grad_columns, activated)
            dw1_ref[:, columns] += dot(hidden_columns, grad_expanded)
            grad_hidden = grad_hidden + dot_nt(grad_expanded, w1_ref[:, columns])
        out_ref[rows, :] = (final * counted).astype(bf16)
        back, gain_sum = norm_back(grad_hidden, scaled_three, inverse_three, gain_three)
        dgain_ref[2:3, :] += gain_sum
        grad_cross = grad_final + back
        branch = grad_cross.astype(bf16)
        dwco_ref[...] += dot(cross_rows.T, branch)
        grad_mixed = dot_nt(branch, wco_ref[...]).astype(bf16)
        for pair in range(pairs):
            gcm_s[pair] = grad_mixed[:, pair * PAIR : (pair + 1) * PAIR]

        def cross_back(pair, _):
            def add_key(_, value):
                dck_ref[pair] += value

            def add_value(_, value):
                dcv_ref[pair] += value

            extra = cextra_ref[...]
            dqt_s[pair] = attend_pair_back(
                qc_s[pair],
                gcm_s[pair],
                cm_s[pair],
                [extra_s[2 * pair], extra_s[2 * pair + 1]],
                lambda _: jnp.concatenate([ck_ref[pair], extra], axis=1),
                lambda _: jnp.concatenate([cv_ref[pair], extra], axis=1),
                lambda _, head: ckt_ref[pair, 64 * head : 64 * head + 64, :],
                1,
                lane,
                add_key,
                add_value,
            )
            dq_s[pair] = dqt_s[pair].T
            return 0

        lax.fori_loop(0, pairs, cross_back, 0)
        query_grad = jnp.concatenate([dq_s[pair] for pair in range(pairs)], axis=1)
        dwcq_ref[...] += dot(hidden_two.T, query_grad)
        back, gain_sum = norm_back(
            dot_nt(query_grad, wcq_ref[...]), scaled_two, inverse_two, gain_two
        )
        dgain_ref[1:2, :] += gain_sum
        grad_self = grad_cross + back
        grad_self_ref[rows, :] = grad_self
        branch = grad_self.astype(bf16)
        dwo_ref[...] += dot(self_rows.T, branch)
        grad_mixed = dot_nt(branch, wo_ref[...]).astype(bf16)
        for pair in range(pairs):
            grad_mixed_ref[pair, rows, :] = grad_mixed[:, pair * PAIR : (pair + 1) * PAIR]
        return 0

    lax.fori_loop(0, rows_own // BLOCK, step, 0)
    dwck_ref[...] = jnp.zeros(dwck_ref.shape, f32)
    dwcv_ref[...] = jnp.zeros(dwcv_ref.shape, f32)

    def gathered(ref, rows, factor):
        parts = [(ref[pair, rows, :] * factor).astype(bf16) for pair in range(pairs)]
        return jnp.concatenate(parts, axis=1)

    def source_back(index, _):
        rows = block_at(index, BLOCK)
        source_columns = source_ref[rows, :].T
        key_grad = gathered(dck_ref, rows, LN2)
        value_grad = gathered(dcv_ref, rows, 1.0)
        dwck_ref[...] += dot(source_columns, key_grad)
        dwcv_ref[...] += dot(source_columns, value_grad)
        grad_source_ref[rows, :] = (
            dot_nt(key_grad, wck_ref[...]) + dot_nt(value_grad, wcv_ref[...])
        ).astype(bf16)
        return 0

    lax.fori_loop(0, few // BLOCK, source_back, 0)
    for at, ref in enumerate((dwo_ref, dwcq_ref, dwck_ref, dwcv_ref, dwco_ref)):
        to_blocks(part_a, at * deep, deep, ref)
    to_blocks(part_b, 0, deep, dw1_ref, hidden_width // width)
    deep_two = hidden_width // 8
    for column in range(4):
        for side in range(2):
            for plane in range(4):
                for half in range(2):
                    at = (plane * 2 + side) * deep_two + half * PAIR
                    part_c[column, side, plane, half * PAIR : (half + 1) * PAIR, :] = dw2t_ref[
                        column * PAIR : (column + 1) * PAIR, at : at + PAIR
                    ].astype(bf16)


def last_kernel(comm, planes, source_len_ref, upsample_ref, *refs):
    (q_any, k_any, v_any, mixed_any, grad_any, extra_any) = refs[:6]
    (x_any, qkv_any, gain_any, grad_self_any, dgain_any) = refs[6:11]
    refs = refs[11:]
    if comm:
        (part_a, part_b, part_c, source_any, rows_any) = refs[:5]
        (decoder_out, grad_out, source_out, *weight_outs, gain_out) = refs[5:19]
        refs = refs[19:]
    else:
        (own_out, other_out, part_out, gain_out) = refs[:4]
        refs = refs[4:]
    (
        q_s, k_s, v_s, mixed_s, grad_s, extra_s, x_s, qkv_s, gain_s, grad_self_s, dgain_s,
        dk_s, dv_s, keys_s, values_s, kt_s, hidden_s, total_s, dkv_s, dq_s, weight_s,
        part_s, load, send, receive,
    ) = refs[:25]
    refs = refs[25:]
    where = Where(planes)
    chip, core, side, plane = where.chip, where.core, where.side, where.plane
    total, width = x_s.shape
    own = total // 2
    rows = total // 4
    pairs = width // PAIR
    deep = width // 8
    chunk = 512
    size = 512
    blocks = own // size
    lane = lax.broadcasted_iota(jnp.int32, (size, PAIR), 1)
    semaphores = Semaphores(send, receive)
    sentence = where.group * 2 + chip
    length = source_len_ref[sentence] * upsample_ref[sentence]

    def turn_pair(turn):
        return where.column(pairs - 1 - turn)

    def turn_loads(turn):
        pair, slot = turn_pair(turn), turn % 2
        return [
            pltpu.make_async_copy(source.at[pair], target.at[slot], load.at[slot, at])
            for at, (source, target) in enumerate(
                (
                    (q_any, q_s),
                    (k_any, k_s),
                    (v_any, v_s),
                    (mixed_any, mixed_s),
                    (grad_any, grad_s),
                    (extra_any, extra_s),
                )
            )
        ]

    for copy in turn_loads(0):
        copy.start()
    common = [
        semaphores.local(source, target)
        for source, target in (
            (x_any, x_s),
            (qkv_any, qkv_s),
            (gain_any, gain_s),
            (dgain_any, dgain_s),
            (grad_self_any, grad_self_s),
        )
    ]
    for copy in common:
        copy.start()

    def begin(copies):
        for copy in copies:
            copy.start()

    def arrive(copies):
        for copy in copies:
            copy.wait_recv()

    if comm:
        (
            keep_a, keep_b, keep_c, core_a, core_b, core_c, far_a, far_b, far_c,
            near_a, near_b, near_c, planes_a, planes_b, planes_c,
            land_q, far_q, planes_q, gain_send, gain_land, gain_far, gain_planes, grads_send,
            grads_land, cross_send, cross_land, stage, source_s, source_land, source_far, stage_s,
        ) = refs
        place, across = where.place, where.column(2)
        pieces = []
        for part, keep, land, far, near, land_planes, side_first in (
            (part_a, keep_a, core_a, far_a, near_a, planes_a, True),
            (part_b, keep_b, core_b, far_b, near_b, planes_b, False),
            (part_c, keep_c, core_c, far_c, near_c, planes_c, True),
        ):
            piece = dict(keep=keep, land=land, far=far, near=near, planes=land_planes)
            piece["load"] = [
                semaphores.local(part.at[place], keep.at[0]),
                semaphores.local(part.at[across], keep.at[1]),
            ]
            piece["core"] = [
                semaphores.remote(part.at[where.column(1)], land.at[0], where.other_core),
                semaphores.remote(part.at[where.column(3)], land.at[1], where.other_core),
            ]
            if side_first:
                piece["far"] = [
                    semaphores.remote(keep.at[at, 1 - side], far.at[at], where.other_side)
                    for at in (0, 1)
                ]
                piece["near"] = [semaphores.remote(keep.at[1, side], near, where.other_chip)]
            else:
                piece["far"] = [
                    semaphores.remote(keep.at[1, at], far.at[at], where.other_chip)
                    for at in (0, 1)
                ]
                piece["near"] = [semaphores.remote(keep.at[0, 1 - side], near, where.other_side)]
            piece["last"] = [
                semaphores.remote(
                    keep.at[0, side, (plane + step) % planes],
                    land_planes.at[step - 1],
                    where.other_planes[step - 1],
                )
                for step in range(1, planes)
            ]
            piece["side_first"] = side_first
            pieces.append(piece)
        a, b, c = pieces
        owners = (where.diagonal, where.other_chip, where.other_core)
        send_q = [
            semaphores.remote(part_s.at[turn], land_q.at[turn], owners[turn]) for turn in range(3)
        ]
        side_q = semaphores.remote(part_s.at[3, 1 - side], far_q, where.other_side)
        plane_q = [
            semaphores.remote(
                part_s.at[3, side, (plane + step) % planes],
                planes_q.at[step - 1],
                where.other_planes[step - 1],
            )
            for step in range(1, planes)
        ]
        gain_group = [
            semaphores.remote(gain_send.at[where.column(3 - turn)], gain_land.at[turn], owners[turn])
            for turn in range(3)
        ]
        gain_side = semaphores.remote(gain_land.at[3], gain_far, where.other_side)
        gain_last = [
            semaphores.remote(
                gain_planes.at[plane], gain_planes.at[plane], where.other_planes[step - 1]
            )
            for step in range(1, planes)
        ]
        rows_local = semaphores.local(rows_any.at[:rows], decoder_out.at[chip])
        rows_cross = semaphores.remote(rows_any.at[rows:], decoder_out.at[chip], where.other_chip)
        few = source_any.shape[0] // 4
        source_local = semaphores.local(source_any.at[: 2 * few], source_s)
        source_core = semaphores.remote(source_any.at[2 * few :], source_land, where.other_core)
        source_cross = semaphores.remote(source_s.at[few:], source_far, where.other_chip)
        grads_core = [
            semaphores.remote(grads_send.at[at], grads_land.at[at], where.other_core)
            for at in range(2)
        ]
        grads_cross = [
            semaphores.remote(cross_send.at[at], cross_land.at[at], where.other_chip)
            for at in range(rows // BLOCK)
        ]
        stage_out = [
            semaphores.local(stage.at[at], grad_out.at[chip if at == 0 else 1 - chip])
            for at in range(2)
        ]
        source_outs = [
            semaphores.local(stage_s.at[at], source_out.at[chip if at == 0 else 1 - chip])
            for at in range(2)
        ]
        for piece in pieces:
            begin(piece["load"])
        begin([rows_local, source_local])
        entry_barrier(where.everyone())
        for piece in pieces:
            begin(piece["core"])
        begin([source_core, rows_cross])

        def add_in(ref, land):
            def add(at, _):
                ref[at] = (ref[at].astype(f32) + land[at].astype(f32)).astype(bf16)
                return 0

            lax.fori_loop(0, planes, add, 0)

        def add_core(piece):
            for copy in piece["load"]:
                copy.wait()
            arrive(piece["core"])
            for at in (0, 1):
                for half in (0, 1):
                    add_in(piece["keep"].at[at, half], piece["land"].at[at, half])
            begin(piece["far"])

        def add_far(piece):
            arrive(piece["far"])
            for at in (0, 1):
                if piece["side_first"]:
                    add_in(piece["keep"].at[at, side], piece["far_land"].at[at])
                else:
                    add_in(piece["keep"].at[0, at], piece["far_land"].at[at])
            begin(piece["near"])

        def add_near(piece):
            arrive(piece["near"])
            add_in(piece["keep"].at[0, side], piece["near_land"])
            begin(piece["last"])

        def finish(piece):
            arrive(piece["last"])
            value = piece["keep"][0, side, plane].astype(f32)
            for step in range(planes - 1):
                value = value + piece["planes"][step].astype(f32)
            return value

        for piece, far, near in ((a, far_a, near_a), (b, far_b, near_b), (c, far_c, near_c)):
            piece["far_land"], piece["near_land"] = far, near

    mask_columns(chip, core, rows, total, BLOCK, length, values_s.at[:, PAIR:])
    keys_s[:, PAIR:] = values_s[:, PAIR:]
    for copy in common:
        copy.wait()
    gain = jnp.concatenate([gain_s[at, 0:1, :] for at in range(pairs)], axis=1)

    def hide(index, _):
        at = block_at(index, BLOCK)
        scaled, _ = normalize(x_s[at, :].astype(f32))
        hidden_s[:, at] = (scaled * gain).astype(bf16).T
        return 0

    lax.fori_loop(0, total // BLOCK, hide, 0)

    def take_weights(turn, pair):
        for part in range(3):
            for at in range(8):
                weight_s[turn, at * 64 : at * 64 + 64, part * PAIR : (part + 1) * PAIR] = qkv_s[
                    pair, at % 2, at // 2, part * 64 : part * 64 + 64, :
                ]

    def upstream(turns, at, own_rows):
        value = None
        for turn in turns:
            term = dot_nt(dkv_s[turn, at, :], weight_s[turn, :, PAIR:])
            if own_rows:
                term = term + dot_nt(dq_s[turn, at, :], weight_s[turn, :, :PAIR])
            value = term if value is None else value + term
        return value

    def step(index, _):
        turn = index // blocks
        pair, slot = turn_pair(turn), turn % 2
        at = block_at(index % blocks, size)
        if comm:

            @pl.when(index == 1)
            def _():
                add_core(a)
                add_core(b)
                source_local.wait()
                arrive([source_core])
                for half in range(2):
                    r = slice(half * few, (half + 1) * few)
                    value = source_s[r, :].astype(f32) + source_land[r, :].astype(f32)
                    source_s[r, :] = value.astype(bf16)
                    if half == 0:
                        stage_s[0] = value
                begin([source_cross, source_outs[0]])

            @pl.when(index == 3)
            def _():
                add_far(a)
                add_core(c)

            @pl.when(index == 4)
            def _():
                add_far(b)

            @pl.when(index == 5)
            def _():
                add_near(a)
                add_far(c)

            @pl.when(index == 6)
            def _():
                add_near(b)

            @pl.when(index == 7)
            def _():
                add_near(c)

        @pl.when(index % blocks == 0)
        def _():
            for copy in turn_loads(turn):
                copy.wait()

            @pl.when(turn + 1 < pairs)
            def _():
                for copy in turn_loads(turn + 1):
                    copy.start()

            dk_s[...] = jnp.zeros(dk_s.shape, f32)
            dv_s[...] = jnp.zeros(dv_s.shape, f32)
            keys_s[:, :PAIR] = k_s[slot]
            values_s[:, :PAIR] = v_s[slot]
            kt_s[...] = k_s[slot].T
            take_weights(turn, pair)

        def part(ref):
            return lambda part: ref[part * chunk : (part + 1) * chunk, :]

        def add_to(ref):
            def add(part, value):
                ref[part * chunk : (part + 1) * chunk, :] += value

            return add

        query_grad = attend_pair_back(
            q_s[slot, at, :],
            grad_s[slot, at, :],
            mixed_s[slot, at, :],
            [extra_s[slot, head, at, :] for head in (0, 1)],
            part(keys_s),
            part(values_s),
            lambda part, head: kt_s[64 * head : 64 * head + 64, part * chunk : (part + 1) * chunk],
            total // chunk,
            lane,
            add_to(dk_s),
            add_to(dv_s),
        )
        dq_s[turn, at, :] = query_grad.T

        @pl.when(index % blocks == blocks - 1)
        def _():
            dkv_s[turn, :, :PAIR] = (dk_s[...] * LN2).astype(bf16)
            dkv_s[turn, :, PAIR:] = dv_s[...].astype(bf16)
            both = dot(hidden_s[...], dkv_s[turn]).astype(bf16)
            query = dot(hidden_s[:, :own], dq_s[turn]).astype(bf16)
            for at in range(8):
                r = slice(at * deep, (at + 1) * deep)
                for part, value in enumerate(
                    (query[r, :], both[r, :PAIR], both[r, PAIR:])
                ):
                    part_s[turn, at % 2, at // 2, part * deep : (part + 1) * deep, :] = value

        if comm:
            for sent in range(3):

                @pl.when(index == sent * blocks + blocks - 1)
                def _():
                    send_q[sent].start()

        @pl.when(index == (pairs - 1) * blocks - 1)
        def _():
            def early(row, _):
                r = block_at(row, BLOCK)
                total_s[r, :] = upstream(range(pairs - 1), r, True)
                return 0

            def early_other(row, _):
                r = block_at(row, BLOCK)
                total_s[r, :] = upstream(range(pairs - 1), r, False)
                return 0

            lax.fori_loop(0, own // BLOCK, early, 0)
            lax.fori_loop(own // BLOCK, total // BLOCK, early_other, 0)

        return 0

    lax.fori_loop(0, pairs * blocks, step, 0)

    def row_back(row, own_rows):
        r = block_at(row, BLOCK)
        scaled, inverse = normalize(x_s[r, :].astype(f32))
        value = total_s[r, :] + upstream([pairs - 1], r, own_rows)
        back, gain_sum = norm_back(value, scaled, inverse, gain)
        dgain_s[0:1, :] += gain_sum
        return r, back

    per = rows // BLOCK
    if not comm:

        def own_step(row, _):
            r, back = row_back(row, True)
            grad_self_s[r, :] += back
            return 0

        def other_step(row, _):
            r, back = row_back(row, False)
            total_s[r, :] = back
            return 0

        lax.fori_loop(0, 2 * per, own_step, 0)
        lax.fori_loop(2 * per, 4 * per, other_step, 0)
        own_out[...] = grad_self_s[...]
        other_out[...] = total_s[own:, :].astype(bf16)
        for turn in range(pairs):
            part_out[turn_pair(turn)] = part_s[turn]
        gain_out[...] = dgain_s[...]
        return

    def add_q(at, _):
        for half in range(2):
            value = part_s[3, half, at].astype(f32)
            for turn in range(3):
                value = value + land_q[turn, half, at].astype(f32)
            part_s[3, half, at] = value.astype(bf16)
        return 0

    def other_rows(slot):
        def other_step(row, _):
            _, back = row_back(slot * per + row, False)
            grads_send[slot - 2, block_at(row, BLOCK), :] = back.astype(bf16)
            return 0

        lax.fori_loop(0, per, other_step, 0)
        grads_core[slot - 2].start()

    other_rows(3)
    arrive(send_q)
    lax.fori_loop(0, planes, add_q, 0)
    side_q.start()
    other_rows(2)
    arrive([grads_core[1]])
    for row in range(per):
        r, back = row_back(per + row, True)
        value = back + grad_self_s[r, :] + grads_land[1, row * BLOCK : (row + 1) * BLOCK, :].astype(f32)
        cross_send[row] = value.astype(bf16)
        grads_cross[row].start()
    arrive([side_q])
    add_in(part_s.at[3, side], far_q)
    begin(plane_q)
    arrive([grads_core[0]])
    for row in range(per):
        r, back = row_back(row, True)
        r_own = slice(row * BLOCK, (row + 1) * BLOCK)
        stage[0, r_own, :] = back + grad_self_s[r, :] + grads_land[0, r_own, :].astype(f32)
    stage_out[0].start()

    for at in range(pairs):
        gain_send[at] = dgain_s[:, at * PAIR : (at + 1) * PAIR]
    begin(gain_group)
    sums = [finish(piece) for piece in pieces]
    arrive(gain_group)
    gain_land[3] = gain_send[place] + gain_land[0] + gain_land[1] + gain_land[2]
    gain_side.start()
    for at in range(5):
        weight_outs[3 + at][...] = sums[0][at * deep : (at + 1) * deep, :]
    for at in range(sums[1].shape[0] // deep):
        weight_outs[8][:, at * PAIR : (at + 1) * PAIR] = sums[1][at * deep : (at + 1) * deep, :]
    for at in range(sums[2].shape[0] // PAIR):
        r = slice(at * PAIR, (at + 1) * PAIR)
        weight_outs[9][r, :] = sums[2][r, :].T
    arrive([source_cross])
    stage_s[1] = source_far[...].astype(f32)
    source_outs[1].start()
    arrive([gain_side])
    gain_planes[plane] = gain_land[3] + gain_far[...]
    begin(gain_last)
    arrive(plane_q)
    value = part_s[3, side, plane].astype(f32)
    for at in range(planes - 1):
        value = value + planes_q[at].astype(f32)
    for at in range(3):
        weight_outs[at][...] = value[at * deep : (at + 1) * deep, :]
    for row in range(per):
        arrive([grads_cross[row]])
        stage[1, row * BLOCK : (row + 1) * BLOCK, :] = cross_land[row].astype(f32)
    stage_out[1].start()
    arrive(gain_last)
    value = gain_planes[0]
    for at in range(1, planes):
        value = value + gain_planes[at]
    gain_out[...] = value
    arrive([rows_cross])
    for copy in [rows_local, *stage_out, *source_outs]:
        copy.wait()
    for copy in semaphores.sent:
        copy.wait_send()


def call(kernel, outs, *operands, scratch=(), smem=0, params=PARAMS, spaces=None, out_space=VMEM, out_spaces=None):
    spaces = spaces or {}
    out_spaces = out_spaces or {}
    return pl.pallas_call(
        kernel,
        out_shape=[jax.ShapeDtypeStruct(shape, kind) for shape, kind in outs],
        in_specs=[
            pl.BlockSpec(memory_space=pltpu.SMEM if at < smem else spaces.get(at, VMEM))
            for at in range(len(operands))
        ],
        out_specs=[
            pl.BlockSpec(memory_space=out_spaces.get(at, out_space)) for at in range(len(outs))
        ],
        scratch_shapes=list(scratch),
        compiler_params=params,
    )(*operands)


def swapped(value, axis, bit):
    pairs = [(source, source ^ bit) for source in range(lax.axis_size(axis))]
    return lax.ppermute(value, axis, pairs)


def as_blocks(weight, chunks=1):
    height, width = weight.shape
    deep = height // 8
    cut = weight.reshape(4, 2, deep, 4, chunks, PAIR).transpose(3, 1, 0, 4, 2, 5)
    return cut.reshape(4, 2, 4, chunks * deep, PAIR)


def from_blocks(blocks, chunks=1):
    height = blocks.shape[3] // chunks
    cut = blocks.reshape(4, 2, 4, chunks, height, PAIR).transpose(2, 1, 4, 0, 3, 5)
    return cut.reshape(8 * height, 4 * chunks * PAIR)


def gather_plain(arguments, seq_size, dp_size):
    (decoder_in, source_states, out_grad, narrow, ffn_expand, ffn_reduce, gain_block) = arguments
    chip = lax.axis_index("seq") // 2
    rows_dec = decoder_in.shape[1]
    own = 2 * rows_dec
    outgoing = jnp.concatenate([decoder_in[1 - chip], source_states[1 - chip]], axis=0)
    arrived = swapped(outgoing, "seq", 2)
    own_rows = jnp.concatenate(
        [decoder_in[chip], arrived[:rows_dec], source_states[chip], arrived[rows_dec:]], axis=0
    )
    other_rows = swapped(own_rows, "seq", 1)
    x_all = jnp.concatenate([own_rows[:own], other_rows[:own]], axis=0)
    source_all = jnp.concatenate([own_rows[own:], other_rows[own:]], axis=0)
    cotangent = jnp.concatenate([out_grad[chip], swapped(out_grad[1 - chip], "seq", 2)], axis=0)

    def whole(weight):
        weight = lax.all_gather(weight, "seq", axis=1, tiled=True)
        return lax.all_gather(weight, "dp", axis=0, tiled=True)

    blocks = [as_blocks(whole(weight)) for weight in narrow]
    qkv = jnp.concatenate(blocks[:3], axis=3)
    later_a = jnp.concatenate(blocks[3:], axis=3)
    later_b = as_blocks(whole(ffn_expand), ffn_expand.shape[1] // PAIR)
    later_c = as_blocks(whole(ffn_reduce))
    gains = lax.all_gather(gain_block, "seq", axis=0)
    return x_all, source_all, cotangent, qkv, later_a, later_b, later_c, gains


def body(
    decoder_in,
    source_states,
    source_len,
    upsample,
    send_counts,
    self_query,
    self_key,
    self_value,
    self_output,
    cross_query,
    cross_key,
    cross_value,
    cross_output,
    ffn_expand,
    ffn_reduce,
    norm_gains,
    out_grad,
):
    seq_size = lax.axis_size("seq")
    dp_size = lax.axis_size("dp")
    planes = dp_size // 2
    place = lax.axis_index("seq")
    chip = place // 2
    home_count, rows_dec, width = decoder_in.shape
    rows_src = source_states.shape[1]
    pairs = width // PAIR
    own = 2 * rows_dec
    total = 4 * rows_dec
    deep = self_query.shape[0]
    deep_two = ffn_reduce.shape[0]
    wide = ffn_expand.shape[1] // PAIR
    hidden_width = wide * PAIR * seq_size
    gain_block = jnp.pad(norm_gains.astype(f32), ((0, 5), (0, 0)))
    all_src = 4 * rows_src
    comm = dp_size == 8

    def pair_rows(rows):
        return (pairs, rows, PAIR)

    narrow = (self_query, self_key, self_value, self_output)
    narrow += (cross_query, cross_key, cross_value, cross_output)
    rows_outs = [
        (pair_rows(own), bf16),
        (pair_rows(total), bf16),
        (pair_rows(total), bf16),
        (pair_rows(own), bf16),
        ((pairs, 2, own, PAIR), bf16),
    ]
    buffers = [VMEM(shape, kind) for shape, kind in rows_outs]
    work = [
        VMEM((total, width), bf16),
        VMEM((width, 3 * PAIR), bf16),
        VMEM((total, PAIR), bf16),
        *buffers,
    ]
    semaphores = [pltpu.SemaphoreType.DMA((96,)), pltpu.SemaphoreType.DMA((96,))]
    if comm:
        cut = (seq_size, 2, planes)
        gathered = [
            ((total, width), bf16),
            ((all_src, width), bf16),
            ((own, width), bf16),
            (cut + (3 * deep, PAIR), bf16),
            (cut + (5 * deep, PAIR), bf16),
            (cut + (wide * deep, PAIR), bf16),
            (cut + (deep_two, PAIR), bf16),
            ((seq_size, 8, PAIR), f32),
        ]
        operands = (source_len, upsample, decoder_in, source_states, out_grad)
        operands += (*narrow, ffn_expand, ffn_reduce, gain_block)
        (
            x_all, source_all, cotangent, qkv, later_a, later_b, later_c, gains,
            q, k, v, mixed, query_extra,
        ) = call(
            partial(open_kernel, True, planes, deep),
            gathered + rows_outs,
            *operands,
            scratch=[
                VMEM((total, width), bf16),
                VMEM(cut + (3 * deep, PAIR), bf16),
                VMEM((seq_size, 8, PAIR), f32),
                *work,
                *semaphores,
            ],
            smem=2,
            spaces={at: pl.ANY for at in range(2, len(operands))},
            out_space=pl.ANY,
            params=pltpu.CompilerParams(
                vmem_limit_bytes=VMEM_LIMIT, collective_id=0, has_side_effects=True
            ),
        )
    else:
        x_all, source_all, cotangent, qkv, later_a, later_b, later_c, gains = gather_plain(
            (decoder_in, source_states, out_grad, narrow, ffn_expand, ffn_reduce, gain_block),
            seq_size,
            dp_size,
        )
        q, k, v, mixed, query_extra = call(
            partial(open_kernel, False, planes, deep),
            rows_outs,
            source_len,
            upsample,
            x_all,
            qkv,
            gains,
            scratch=[*work, *semaphores],
            smem=2,
            out_space=pl.ANY,
        )
    square = VMEM((width, width), f32)
    parts = [
        ((seq_size, 2, 4, 5 * width // 8, PAIR), bf16),
        ((seq_size, 2, 4, hidden_width // 8, PAIR), bf16),
        ((seq_size, 2, 4, hidden_width // 8, PAIR), bf16),
    ]
    out_rows, grad_mixed, grad_self, part_a, part_b, part_c, grad_source, dgain = call(
        partial(middle_kernel, planes),
        [
            ((own, width), bf16),
            (pair_rows(own), bf16),
            ((own, width), f32),
            *parts,
            ((all_src, width), bf16),
            ((8, width), f32),
        ],
        source_len,
        upsample,
        send_counts,
        x_all,
        mixed,
        cotangent,
        source_all,
        later_a,
        later_b,
        later_c,
        gains,
        scratch=[
            *[square] * 3,
            *[VMEM((width, hidden_width), f32)] * 2,
            *[square] * 2,
            VMEM((own, width), bf16),
            *[VMEM((width, width), bf16)] * 5,
            VMEM((width, hidden_width), bf16),
            VMEM((hidden_width, width), bf16),
            VMEM(pair_rows(all_src), bf16),
            VMEM(pair_rows(all_src), bf16),
            VMEM((pairs, PAIR, all_src), bf16),
            VMEM((all_src, PAIR), bf16),
            VMEM(pair_rows(all_src), f32),
            VMEM(pair_rows(all_src), f32),
            pltpu.SemaphoreType.DMA,
            VMEM((pairs, BLOCK, PAIR), bf16),
            VMEM((2 * pairs, BLOCK, PAIR), bf16),
            VMEM((pairs, PAIR, BLOCK), bf16),
            VMEM((pairs, BLOCK, PAIR), bf16),
            VMEM((pairs, BLOCK, PAIR), bf16),
            VMEM((pairs, BLOCK, PAIR), bf16),
        ],
        smem=3,
        spaces={3: pl.ANY},
    )
    part_q = ((seq_size, 2, 4, 3 * width // 8, PAIR), bf16)
    operands = (source_len, upsample, q, k, v, mixed, grad_mixed, query_extra)
    operands += (x_all, qkv, gains, grad_self, dgain)
    work = [
        VMEM((2, own, PAIR), bf16),
        VMEM((2, total, PAIR), bf16),
        VMEM((2, total, PAIR), bf16),
        VMEM((2, own, PAIR), bf16),
        VMEM((2, own, PAIR), bf16),
        VMEM((2, 2, own, PAIR), bf16),
        VMEM((total, width), bf16),
        VMEM(qkv.shape, bf16),
        VMEM(gains.shape, f32),
        VMEM((own, width), f32),
        VMEM((8, width), f32),
        VMEM((total, PAIR), f32),
        VMEM((total, PAIR), f32),
        VMEM((total, 2 * PAIR), bf16),
        VMEM((total, 2 * PAIR), bf16),
        VMEM((PAIR, total), bf16),
        VMEM((width, total), bf16),
        VMEM((total, width), f32),
        VMEM((pairs, total, 2 * PAIR), bf16),
        VMEM((pairs, own, PAIR), bf16),
        VMEM((pairs, width, 3 * PAIR), bf16),
        VMEM(*part_q),
        pltpu.SemaphoreType.DMA((2, 6)),
        *semaphores,
    ]
    everywhere = {at: pl.ANY for at in range(2, 18)}
    if comm:
        heights = [shape[3] for shape, _ in parts]

        def per_piece(lead):
            return [VMEM((*lead, height, PAIR), bf16) for height in heights]

        work += [
            *per_piece((2, 2, planes)),
            *per_piece((2, 2, planes)),
            *per_piece((2, planes)),
            *per_piece((planes,)),
            *per_piece((planes - 1,)),
            VMEM((3, 2, planes, 3 * deep, PAIR), bf16),
            VMEM((planes, 3 * deep, PAIR), bf16),
            VMEM((planes - 1, 3 * deep, PAIR), bf16),
            VMEM((pairs, 8, PAIR), f32),
            VMEM((4, 8, PAIR), f32),
            VMEM((8, PAIR), f32),
            VMEM((planes, 8, PAIR), f32),
            VMEM((2, rows_dec, width), bf16),
            VMEM((2, rows_dec, width), bf16),
            VMEM((rows_dec // BLOCK, BLOCK, width), bf16),
            VMEM((rows_dec // BLOCK, BLOCK, width), bf16),
            VMEM((2, rows_dec, width), f32),
            VMEM((2 * rows_src, width), bf16),
            VMEM((2 * rows_src, width), bf16),
            VMEM((rows_src, width), bf16),
            VMEM((2, rows_src, width), f32),
        ]
        small = ((deep, PAIR), f32)
        outs = call(
            partial(last_kernel, True, planes),
            [
                (decoder_in.shape, bf16),
                (decoder_in.shape, f32),
                (source_states.shape, f32),
                *[small] * 8,
                (ffn_expand.shape, f32),
                (ffn_reduce.shape, f32),
                ((8, PAIR), f32),
            ],
            *operands,
            part_a,
            part_b,
            part_c,
            grad_source,
            out_rows,
            scratch=work,
            smem=2,
            spaces=everywhere,
            out_spaces={at: pl.ANY for at in range(3)},
            params=pltpu.CompilerParams(
                vmem_limit_bytes=VMEM_LIMIT, collective_id=1, has_side_effects=True
            ),
        )
        (decoder_out, grad_decoder, grad_src, dwq, dwk, dwv, *rest, dw1, dw2, dgains) = outs
        dwo, dwcq, dwck, dwcv, dwco = rest
    else:
        own_grad, other_grad, part_qkv, dgains = call(
            partial(last_kernel, False, planes),
            [((own, width), f32), ((own, width), bf16), part_q, ((8, width), f32)],
            *operands,
            scratch=work,
            smem=2,
            spaces=everywhere,
        )
        crossing = jnp.concatenate([other_grad, grad_source[2 * rows_src :]], axis=0)
        returned = swapped(crossing, "seq", 1).astype(f32)
        grad_rows = own_grad + returned[:own]
        source_rows = grad_source[: 2 * rows_src].astype(f32) + returned[own:]
        homeward = [grad_rows[rows_dec:].astype(bf16), source_rows[rows_src:].astype(bf16)]
        came = swapped(jnp.concatenate([out_rows[rows_dec:], *homeward], axis=0), "seq", 2)

        def both_sentences(mine, theirs):
            theirs = theirs.astype(mine.dtype)
            return jnp.where(chip == 0, jnp.stack([mine, theirs]), jnp.stack([theirs, mine]))

        decoder_out = both_sentences(out_rows[:rows_dec], came[:rows_dec])
        grad_decoder = both_sentences(grad_rows[:rows_dec], came[rows_dec : 2 * rows_dec])
        grad_src = both_sentences(source_rows[:rows_src], came[2 * rows_dec :])

        def summed(blocks, start, count, chunks=1):
            grad = from_blocks(blocks[:, :, :, start : start + chunks * count], chunks)
            grad = lax.psum_scatter(grad.astype(f32), "dp", scatter_dimension=0, tiled=True)
            return lax.psum_scatter(grad, "seq", scatter_dimension=1, tiled=True)

        step = width // 8
        dwq, dwk, dwv = [summed(part_qkv, at * step, step) for at in range(3)]
        dwo, dwcq, dwck, dwcv, dwco = [summed(part_a, at * step, step) for at in range(5)]
        dw1 = summed(part_b, 0, step, hidden_width // width)
        tall = part_c.reshape(seq_size, 2, 4, hidden_width // 8 // PAIR, PAIR, PAIR)
        dw2 = summed(tall.swapaxes(4, 5).reshape(part_c.shape), 0, hidden_width // 8)
        dgains = lax.psum(dgains, "dp")
        dgains = lax.psum_scatter(dgains, "seq", scatter_dimension=1, tiled=True)
    return (
        decoder_out,
        grad_decoder,
        grad_src,
        dwq,
        dwk,
        dwv,
        dwo,
        dwcq,
        dwck,
        dwcv,
        dwco,
        dw1,
        dw2,
        dgains[:3],
    )


def solution(mesh):
    rows = P("dp", "seq", None)
    weight = P("dp", "seq")
    placed = (rows, rows, P(), P(), P()) + (weight,) * 10 + (P(None, "seq"), rows)
    return jax.shard_map(
        body,
        mesh=mesh,
        in_specs=placed,
        out_specs=(rows, rows, rows) + (weight,) * 10 + (P(None, "seq"),),
        check_vma=False,
    )
```

```python
from functools import partial

import jax
import jax.numpy as jnp
from jax import lax
from jax.experimental import pallas as pl
from jax.experimental.pallas import tpu as pltpu
from jax.sharding import PartitionSpec as P

HEADS = 8
EPSILON = 1e-05
NEGATIVE = -1000000000.0
LOG2E = 1.4426950408889634
LN2 = 0.6931471805599453
GELU_IN = 0.7978845608028654
GELU_CUBE = 0.044715
BLOCK = 256
PAIR = 128

bf16 = jnp.bfloat16
f32 = jnp.float32
VMEM = pltpu.VMEM
VMEM_LIMIT = 60 * 1024 * 1024
PARAMS = pltpu.CompilerParams(vmem_limit_bytes=VMEM_LIMIT)


def dot(left, right):
    return jnp.dot(left, right, preferred_element_type=f32)


def dot_nt(left, right):
    return lax.dot_general(left, right, (((1,), (1,)), ((), ())), preferred_element_type=f32)


def block_at(index, size):
    return pl.ds(pl.multiple_of(index * size, size), size)


def row_mean(values):
    return jnp.mean(values, axis=-1, keepdims=True)


def normalize(values):
    centred = values - row_mean(values)
    inverse = lax.rsqrt(row_mean(centred * centred) + EPSILON)
    return centred * inverse, inverse


def norm_back(upstream, scaled, inverse, gain):
    inner = upstream * gain
    back = inverse * (inner - row_mean(inner) - scaled * row_mean(inner * scaled))
    return back, jnp.sum(upstream * scaled, axis=0, keepdims=True)


def three_parts(column, lane, last):
    high = column.astype(bf16).astype(f32)
    middle = (column - high).astype(bf16).astype(f32)
    low = column - high - middle
    rest = jnp.where(lane == 3, last, 0.0)
    return jnp.where(
        lane == 0, high, jnp.where(lane == 1, middle, jnp.where(lane == 2, low, rest))
    ).astype(bf16)


def one_head(values, first, head):
    zero = jnp.zeros_like(values)
    return jnp.where(first, values, zero) if head == 0 else jnp.where(first, zero, values)


def attend_pair(query, keys, key_extra, values, lane):
    first = lane < 64
    ones = jnp.where(lane == 3, 1.0, 0.0).astype(bf16)
    keys = jnp.concatenate([keys, key_extra], axis=1)
    scores = [
        dot_nt(jnp.concatenate([one_head(query, first, head), ones], axis=1), keys)
        for head in (0, 1)
    ]
    mixed, extras = [], []
    for head in (0, 1):
        peak = jnp.max(scores[head], axis=1, keepdims=True)
        exps = jnp.exp2(scores[head] - peak)
        total = jnp.sum(exps, axis=1, keepdims=True)
        mixed.append(dot(exps.astype(bf16), values) * (1.0 / total))
        extras.append(three_parts(-(peak + jnp.log2(total)), lane, 1.0))
    return jnp.where(first, mixed[0], mixed[1]).astype(bf16), extras


def attend_pair_back(
    query, grad, mixed, query_extra, key_at, value_at, key_columns_at, chunks, lane, add_key, add_value
):
    first = lane < 64
    product = grad.astype(f32) * mixed.astype(f32)
    queries = [one_head(query, first, head) for head in (0, 1)]
    grads = [one_head(grad, first, head) for head in (0, 1)]
    long_queries = [jnp.concatenate([queries[h], query_extra[h]], axis=1) for h in (0, 1)]
    long_grads = []
    for head in (0, 1):
        delta = jnp.sum(one_head(product, first, head), axis=1, keepdims=True)
        long_grads.append(
            jnp.concatenate([grads[head], three_parts(-delta, lane, 0.0)], axis=1)
        )
    both_queries = jnp.concatenate(queries, axis=0)
    both_grads = jnp.concatenate(grads, axis=0)
    query_grads = [jnp.zeros((64, query.shape[0]), f32)] * 2
    for chunk in range(chunks):
        keys, values = key_at(chunk), value_at(chunk)
        probs, score_grads = [], []
        for head in (0, 1):
            prob = jnp.exp2(dot_nt(keys, long_queries[head]))
            score_grad = (prob * dot_nt(values, long_grads[head])).astype(bf16)
            probs.append(prob.astype(bf16))
            score_grads.append(score_grad)
            query_grads[head] = query_grads[head] + dot(key_columns_at(chunk, head), score_grad)
        add_value(chunk, dot(jnp.concatenate(probs, axis=1), both_grads))
        add_key(chunk, dot(jnp.concatenate(score_grads, axis=1), both_queries))
    return (jnp.concatenate(query_grads, axis=0) * 0.125).astype(bf16)


def copy_to(source, target, send, receive, partner):
    return pltpu.make_async_remote_copy(
        src_ref=source,
        dst_ref=target,
        send_sem=send,
        recv_sem=receive,
        device_id=partner,
        device_id_type=pl.DeviceIdType.MESH,
    )


def greet(partners):
    for partner in partners:
        pl.semaphore_signal(
            pltpu.get_barrier_semaphore(),
            inc=1,
            device_id=partner,
            device_id_type=pl.DeviceIdType.MESH,
        )


def await_greetings(partners):
    pl.semaphore_wait(pltpu.get_barrier_semaphore(), len(partners))


class Where:
    def __init__(self, planes):
        group, self.place = lax.axis_index("dp"), lax.axis_index("seq")
        self.group = group
        self.chip, self.core = self.place // 2, self.place % 2
        self.plane, self.side = group // 2, group % 2
        self.planes = planes
        self.other_core = self.at(self.chip, 1 - self.core)
        self.other_chip = self.at(1 - self.chip, self.core)
        self.diagonal = self.at(1 - self.chip, 1 - self.core)
        self.other_side = {"dp": self.plane * 2 + 1 - self.side}
        self.other_planes = [
            {"dp": (self.plane + step) % planes * 2 + self.side} for step in range(1, planes)
        ]

    def at(self, chip, core):
        return {"seq": chip * 2 + core}

    def column(self, step):
        return (self.chip + step // 2) % 2 * 2 + (self.core + step % 2) % 2

    def everyone(self):
        return [self.other_core, self.other_chip, self.diagonal, self.other_side] + self.other_planes


class Semaphores:
    def __init__(self, send, receive):
        self.send, self.receive, self.count = send, receive, 0
        self.sent = []

    def remote(self, source, target, partner):
        at = self.count
        self.count += 1
        copy = copy_to(source, target, self.send.at[at], self.receive.at[at], partner)
        self.sent.append(copy)
        return copy

    def local(self, source, target):
        at = self.count
        self.count += 1
        return pltpu.make_async_copy(source, target, self.send.at[at])


def block_places(where_chip, where_core, rows, offset, index, size):
    per = rows // size
    slot = index // per
    block = (where_chip + slot % 2) % 2 * 2 + (where_core + slot // 2) % 2
    return block * rows + index % per * size + offset


def mask_columns(where_chip, where_core, rows, count, size, length, ref):
    lane = lax.broadcasted_iota(jnp.int32, (size, PAIR), 1)
    offset = lax.broadcasted_iota(jnp.int32, (size, PAIR), 0)

    def step(index, _):
        places = block_places(where_chip, where_core, rows, offset, index, size)
        bias = jnp.where(places < length, 0.0, NEGATIVE)
        ref[block_at(index, size), :] = jnp.where(
            lane < 3, 1.0, jnp.where(lane == 3, bias, 0.0)
        ).astype(bf16)
        return 0

    lax.fori_loop(0, count // size, step, 0)


def open_kernel(
    comm,
    planes,
    deep,
    source_len_ref,
    upsample_ref,
    *refs,
):
    if comm:
        (
            decoder_ref, source_ref, cotangent_ref,
            wq_in, wk_in, wv_in, *later_in, gain_in,
            x_out, source_out, cotangent_out, qkv_out, later_a, later_b, later_c, gain_out,
            q_out, k_out, v_out, mixed_out, extra_out,
            x_ref, qkv_ref, gain_ref, hidden_ref, weight_ref, mask_ref,
            q_ref, k_ref, v_ref, mixed_ref, extra_ref, send, receive,
            stage_a, stage_b, stage_c, stage_s, gain_block,
        ) = refs
    else:
        (
            x_ref, qkv_ref, gain_ref,
            q_out, k_out, v_out, mixed_out, extra_out,
            hidden_ref, weight_ref, mask_ref,
            q_ref, k_ref, v_ref, mixed_ref, extra_ref, send, receive,
        ) = refs
    where = Where(planes)
    place, plane, side, chip, core = where.place, where.plane, where.side, where.chip, where.core
    total, width = x_ref.shape
    pairs = width // PAIR
    own = total // 2
    rows = total // 4
    semaphores = Semaphores(send, receive)
    column = where.column

    if comm:
        group = where.group
        x_slots = [x_ref.at[slot * rows : (slot + 1) * rows] for slot in range(4)]
        few = source_ref.shape[1]
        s_slots = [source_out.at[slot * few : (slot + 1) * few] for slot in range(4)]
        local_x = semaphores.local(decoder_ref.at[chip], x_slots[0])
        mine = qkv_ref.at[place, side, plane]
        local_qkv = [
            semaphores.local(ref, mine.at[at * deep : (at + 1) * deep])
            for at, ref in enumerate((wq_in, wk_in, wv_in))
        ]
        first = [local_x, *local_qkv]
        wo_in, wcq_in, wck_in, wcv_in, wco_in, w1_in, w2_in = later_in
        mine_a = later_a.at[place, side, plane]
        mine_b = later_b.at[place, side, plane]
        mine_c = later_c.at[place, side, plane]
        wide = w1_in.shape[1] // PAIR
        local_later = [
            [
                semaphores.local(ref, stage_a.at[at * deep : (at + 1) * deep])
                for at, ref in enumerate((wo_in, wcq_in, wck_in, wcv_in, wco_in))
            ],
            [
                semaphores.local(
                    w1_in.at[:, at * PAIR : (at + 1) * PAIR], stage_b.at[at * deep : (at + 1) * deep]
                )
                for at in range(wide)
            ],
            [semaphores.local(w2_in, stage_c)],
        ]
        stores = [
            semaphores.local(stage_a, mine_a),
            semaphores.local(stage_b, mine_b),
            semaphores.local(stage_c, mine_c),
        ]
        source_load = semaphores.local(source_ref.at[chip], stage_s)
        source_store = semaphores.local(stage_s, s_slots[0])
        greet(where.everyone())
        gain_block[...] = jnp.zeros(gain_block.shape, f32)
        gain_block[0 : gain_in.shape[0], :] = gain_in[...].astype(f32)
        gain_ref[place] = gain_block[...]
        for copy in first + local_later[0] + local_later[1] + local_later[2] + [source_load]:
            copy.start()
        await_greetings(where.everyone())

        x_cross = semaphores.remote(decoder_ref.at[1 - chip], x_slots[1], where.other_chip)
        x_core = semaphores.remote(decoder_ref.at[chip], x_slots[2], where.other_core)
        x_pass = semaphores.remote(x_slots[1], x_slots[3], where.other_core)
        s_cross = semaphores.remote(source_ref.at[1 - chip], s_slots[1], where.other_chip)
        s_core = semaphores.remote(source_ref.at[chip], s_slots[2], where.other_core)
        s_pass = semaphores.remote(s_slots[1], s_slots[3], where.other_core)
        c_cross = semaphores.remote(cotangent_ref.at[1 - chip], cotangent_out, where.other_chip)
        gain_sends = [
            semaphores.remote(gain_block, gain_ref.at[place], partner)
            for partner in (where.other_core, where.other_chip, where.diagonal)
        ]
        qkv_planes = [semaphores.remote(mine, mine, partner) for partner in where.other_planes]
        qkv_side = semaphores.remote(
            qkv_ref.at[place, side], qkv_ref.at[place, side], where.other_side
        )
        qkv_core = semaphores.remote(qkv_ref.at[place], qkv_ref.at[place], where.other_core)
        qkv_chip = semaphores.remote(qkv_ref.at[place], qkv_ref.at[place], where.other_chip)
        across = column(2)
        qkv_pass = semaphores.remote(qkv_ref.at[across], qkv_ref.at[across], where.other_core)
        later = []
        for buffer, stage in ((later_a, stage_a), (later_b, stage_b), (later_c, stage_c)):
            block = buffer.at[place, side, plane]
            mine_side, across_side = buffer.at[place, side], buffer.at[across, side]
            if buffer is later_c:
                first = [semaphores.remote(stage, block, where.other_chip)]
                far = buffer.at[across, side, plane]
                second = [
                    semaphores.remote(stage, block, where.other_side),
                    semaphores.remote(far, far, where.other_side),
                ]
                others = [buffer.at[at, 1 - side, plane] for at in (place, across)]
                kept = [(stage, block), (far, far)] + [(one, one) for one in others]
            else:
                first = [semaphores.remote(mine_side, mine_side, where.other_chip)]
                second = [
                    semaphores.remote(one, one, where.other_side)
                    for one in (mine_side, across_side)
                ]
                kept = [(stage, block)]
            later.append(
                dict(
                    planes=[
                        semaphores.remote(one, other, partner)
                        for one, other in kept
                        for partner in where.other_planes
                    ],
                    first=first,
                    second=second,
                    core=[
                        semaphores.remote(buffer.at[at], buffer.at[at], where.other_core)
                        for at in (place, across)
                    ],
                )
            )

        def begin(copies):
            for copy in copies:
                copy.start()

        def arrive(copies):
            for copy in copies:
                copy.wait_recv()

        begin(gain_sends)
        for copy in local_qkv:
            copy.wait()
        begin(qkv_planes)
        x_cross.start()
        x_core.start()
        begin([s_core])
        for copies in local_later:
            for copy in copies:
                copy.wait()
        source_load.wait()
        begin([*stores, source_store])
        a, b, c = later
        begin(c["first"])
        begin(a["planes"])
        begin(b["planes"])

    length = source_len_ref[where.group * 2 + chip] * upsample_ref[where.group * 2 + chip]
    mask_columns(chip, core, rows, total, BLOCK, length, mask_ref)

    def hide(slot):
        gain = jnp.concatenate([gain_ref[at, 0:1, :] for at in range(pairs)], axis=1)

        def step(index, _):
            at = block_at(index + slot * (rows // BLOCK), BLOCK)
            scaled, _ = normalize(x_ref[at, :].astype(f32))
            hidden_ref[at, :] = (scaled * gain).astype(bf16)
            return 0

        lax.fori_loop(0, rows // BLOCK, step, 0)

    def take_weights(pair):
        for part in range(3):
            for at in range(8):
                weight_ref[at * 64 : at * 64 + 64, part * PAIR : (part + 1) * PAIR] = qkv_ref[
                    pair, at % 2, at // 2, part * 64 : part * 64 + 64, :
                ]

    def project(pair, slot, count):
        def step(index, _):
            at = block_at(index + slot * (rows // BLOCK), BLOCK)
            both = dot(hidden_ref[at, :], weight_ref[:, PAIR:]).astype(bf16)
            k_ref[pair, at, :] = both[:, :PAIR]
            v_ref[pair, at, :] = both[:, PAIR:]
            return 0

        def query_step(index, _):
            at = block_at(index + slot * (rows // BLOCK), BLOCK)
            query = dot(hidden_ref[at, :], weight_ref[:, :PAIR]) * (0.125 * LOG2E)
            q_ref[pair, at, :] = query.astype(bf16)
            return 0

        lax.fori_loop(0, count * (rows // BLOCK), step, 0)
        if slot < 2:
            lax.fori_loop(0, min(2 - slot, count) * (rows // BLOCK), query_step, 0)

    if comm:
        local_x.wait()
        arrive(gain_sends)
        hide(0)
        arrive([x_core])
        hide(2)
        arrive(qkv_planes)
        qkv_side.start()
        arrive([qkv_side])
        begin([qkv_core])
        take_weights(place)
        project(place, 0, 1)
        project(place, 2, 1)
        arrive([x_cross])
        x_pass.start()
        arrive(a["planes"])
        for copy in [*stores, source_store]:
            copy.wait()
        begin(a["first"])
        arrive(c["first"])
        begin(c["second"])
        begin([qkv_chip])
        hide(1)
        project(place, 1, 1)
        arrive([x_pass])
        hide(3)
        project(place, 3, 1)
    else:
        for slot in range(4):
            hide(slot)
        take_weights(place)
        project(place, 0, 4)

    size = 2 * BLOCK
    blocks = own // size
    lane = lax.broadcasted_iota(jnp.int32, (size, PAIR), 1)

    def outs_of(pair):
        return [
            (q_ref.at[pair], q_out.at[pair]),
            (k_ref.at[pair], k_out.at[pair]),
            (v_ref.at[pair], v_out.at[pair]),
            (mixed_ref.at[pair], mixed_out.at[pair]),
            (extra_ref.at[pair], extra_out.at[pair]),
        ]

    first_out = semaphores.count

    def out_copies(step, pair):
        return [
            pltpu.make_async_copy(source, target, send.at[first_out + step * 5 + at])
            for at, (source, target) in enumerate(outs_of(pair))
        ]

    def when(index, value, todo):
        pl.when(index == value)(todo)

    def step(index, _):
        turn = index // blocks
        pair = column(turn)
        if comm:
            @pl.when(index == 1)
            def _():
                arrive(c["second"])
                begin(c["planes"])
                arrive(b["planes"])
                begin(b["first"])
                begin([s_cross, c_cross])

            @pl.when(index == 2)
            def _():
                arrive([qkv_core])
                arrive(a["first"])
                begin(a["second"])

            @pl.when(index == 4)
            def _():
                arrive([qkv_chip])
                qkv_pass.start()

            @pl.when(index == 5)
            def _():
                arrive(b["first"])
                begin(b["second"])
                arrive(a["second"])
                begin(a["core"])

            @pl.when(index == 6)
            def _():
                arrive([qkv_pass])
                arrive([s_cross])
                s_pass.start()

            @pl.when(index == 7)
            def _():
                arrive(c["planes"])
                begin(c["core"])

        @pl.when((index % blocks == 0) & (index > 0))
        def _():
            take_weights(pair)
            project(pair, 0, 4)

        at = block_at(index % blocks, size)
        mixed, extras = attend_pair(
            q_ref[pair, at, :], k_ref[pair], mask_ref[...], v_ref[pair], lane
        )
        mixed_ref[pair, at, :] = mixed
        extra_ref[pair, 0, at, :] = extras[0]
        extra_ref[pair, 1, at, :] = extras[1]

        @pl.when(index % blocks == blocks - 1)
        def _():
            for copy in out_copies(turn, pair):
                copy.start()

        return 0

    lax.fori_loop(0, pairs * blocks, step, 0)
    if comm:
        x_local = pltpu.make_async_copy(x_ref, x_out, send.at[first_out + 20])
        qkv_local = pltpu.make_async_copy(qkv_ref, qkv_out, send.at[first_out + 21])
        gain_local = pltpu.make_async_copy(gain_ref, gain_out, send.at[first_out + 22])
        for copy in (x_local, qkv_local, gain_local):
            copy.start()
        arrive(b["second"])
        begin(b["core"])
        arrive([s_core, s_pass, c_cross])
        for piece in later:
            arrive(piece["core"])
        for copy in semaphores.sent:
            copy.wait_send()
        for copy in (x_local, qkv_local, gain_local):
            copy.wait()
    for turn in range(pairs):
        for copy in out_copies(turn, column(turn)):
            copy.wait()


def whole_weight(ref, blocks, start, count, chunks=1):
    columns, sides, planes = blocks.shape[:3]
    for column in range(columns):
        for side in range(sides):
            for plane in range(planes):
                row = (plane * sides + side) * count
                for chunk in range(chunks):
                    at = (column * chunks + chunk) * PAIR
                    ref[row : row + count, at : at + PAIR] = blocks[
                        column, side, plane, start + chunk * count : start + (chunk + 1) * count, :
                    ]


def to_blocks(blocks, start, count, ref, chunks=1):
    columns, sides, planes = blocks.shape[:3]
    for column in range(columns):
        for side in range(sides):
            for plane in range(planes):
                row = (plane * sides + side) * count
                for chunk in range(chunks):
                    at = (column * chunks + chunk) * PAIR
                    blocks[
                        column, side, plane, start + chunk * count : start + (chunk + 1) * count, :
                    ] = ref[row : row + count, at : at + PAIR].astype(bf16)


def middle_kernel(
    planes,
    source_len_ref,
    upsample_ref,
    send_ref,
    x_any,
    mixed_ref,
    cotangent_any,
    cotangent_far,
    source_ref,
    later_a,
    later_b,
    later_c,
    gain_blocks,
    out_ref,
    grad_mixed_ref,
    grad_self_ref,
    part_a,
    part_b,
    part_c,
    grad_source_ref,
    dgain_ref,
    dwo_ref,
    dwcq_ref,
    dwco_ref,
    dw1_ref,
    dw2t_ref,
    dwck_ref,
    dwcv_ref,
    x_ref,
    wo_ref,
    wcq_ref,
    wck_ref,
    wcv_ref,
    wco_ref,
    w1_ref,
    w2_ref,
    ck_ref,
    cv_ref,
    ckt_ref,
    cextra_ref,
    dck_ref,
    dcv_ref,
    x_sem,
    cotangent_ref,
    cm_s,
    extra_s,
    dqt_s,
    dq_s,
    gcm_s,
    qc_s,
):
    rows_own, width = x_ref.shape
    pairs = mixed_ref.shape[0]
    hidden_width = w1_ref.shape[1]
    chunk = 512
    where = Where(planes)
    chip, core = where.chip, where.core
    half = rows_own // 2
    loads = [
        pltpu.make_async_copy(source, target, x_sem.at[at])
        for at, (source, target) in enumerate(
            (
                (x_any.at[:rows_own], x_ref),
                (cotangent_any.at[chip], cotangent_ref.at[:half]),
                (cotangent_far, cotangent_ref.at[half:]),
            )
        )
    ]
    for copy in loads:
        copy.start()
    few = source_ref.shape[0]
    deep = width // 8
    for at, ref in enumerate((wo_ref, wcq_ref, wck_ref, wcv_ref, wco_ref)):
        whole_weight(ref, later_a, at * deep, deep)
    whole_weight(w1_ref, later_b, 0, deep, hidden_width // width)
    whole_weight(w2_ref, later_c, 0, hidden_width // 8)
    gain_rows = jnp.concatenate([gain_blocks[at] for at in range(pairs)], axis=1)
    gain_two = gain_rows[1:2, :]
    gain_three = gain_rows[2:3, :]
    lane = lax.broadcasted_iota(jnp.int32, (BLOCK, PAIR), 1)
    offset = lax.broadcasted_iota(jnp.int32, (BLOCK, 1), 0)
    for ref in (dwo_ref, dwcq_ref, dwco_ref, dw1_ref, dw2t_ref, dck_ref, dcv_ref, dgain_ref):
        ref[...] = jnp.zeros(ref.shape, f32)

    dp_size = planes * 2
    group, half_way = where.group, planes
    sentence = group * 2 + chip
    src_len = source_len_ref[sentence]
    dec_len = src_len * upsample_ref[sentence]
    moved = chip * send_ref[group]
    holder = (group + moved * half_way) % dp_size
    partner = (holder + half_way) % dp_size

    def tokens_of(slot):
        return source_len_ref[slot] * upsample_ref[slot]

    tokens = (
        tokens_of(holder * 2)
        + tokens_of(holder * 2 + 1) * (1 - send_ref[holder])
        + tokens_of(partner * 2 + 1) * send_ref[partner]
    )
    loss_scale = jnp.full((1, 1), rows_own * 2, f32) / jnp.full((1, 1), tokens, jnp.int32).astype(f32)
    mask_columns(chip, core, few // 4, few, few // 4, src_len, cextra_ref)

    def source_step(index, _):
        rows = block_at(index, BLOCK)
        source = source_ref[rows, :]
        key_rows = dot(source, wck_ref[...]).astype(bf16)
        value_rows = dot(source, wcv_ref[...]).astype(bf16)
        for pair in range(pairs):
            part = key_rows[:, pair * PAIR : (pair + 1) * PAIR]
            ck_ref[pair, rows, :] = part
            ckt_ref[pair, :, rows] = part.T
            cv_ref[pair, rows, :] = value_rows[:, pair * PAIR : (pair + 1) * PAIR]
        return 0

    lax.fori_loop(0, few // BLOCK, source_step, 0)
    for copy in loads:
        copy.wait()

    def step(index, _):
        rows = block_at(index, BLOCK)
        place = block_places(chip, core, rows_own // 2, offset, index, BLOCK)
        counted = jnp.where(place < dec_len, 1.0, 0.0)
        self_rows = jnp.concatenate([mixed_ref[pair, rows, :] for pair in range(pairs)], axis=1)
        after_self = x_ref[rows, :].astype(f32) + dot(self_rows, wo_ref[...])
        scaled_two, inverse_two = normalize(after_self)
        hidden_two = (scaled_two * gain_two).astype(bf16)
        queries = (dot(hidden_two, wcq_ref[...]) * (0.125 * LOG2E)).astype(bf16)
        for pair in range(pairs):
            qc_s[pair] = queries[:, pair * PAIR : (pair + 1) * PAIR]

        def cross(pair, _):
            mixed, extras = attend_pair(
                qc_s[pair], ck_ref[pair], cextra_ref[...], cv_ref[pair], lane
            )
            cm_s[pair] = mixed
            extra_s[2 * pair] = extras[0]
            extra_s[2 * pair + 1] = extras[1]
            return 0

        lax.fori_loop(0, pairs, cross, 0)
        cross_rows = jnp.concatenate([cm_s[pair] for pair in range(pairs)], axis=1)
        after_cross = after_self + dot(cross_rows, wco_ref[...])
        scaled_three, inverse_three = normalize(after_cross)
        hidden_three = (scaled_three * gain_three).astype(bf16)
        grad_final = cotangent_ref[rows, :].astype(f32) * (counted * loss_scale)
        grad_ffn = grad_final.astype(bf16)
        hidden_columns = hidden_three.T
        grad_columns = grad_ffn.T
        final = after_cross
        grad_hidden = jnp.zeros((BLOCK, width), f32)
        for part in range(hidden_width // chunk):
            columns = slice(part * chunk, (part + 1) * chunk)
            expanded = dot(hidden_three, w1_ref[:, columns])
            square = expanded * expanded
            bend = jnp.tanh(GELU_IN * expanded * (1.0 + GELU_CUBE * square))
            half = 0.5 * (1.0 + bend)
            activated = (expanded * half).astype(bf16)
            slope = half + 0.5 * expanded * (1.0 - bend * bend) * (
                GELU_IN * (1.0 + 3.0 * GELU_CUBE * square)
            )
            grad_expanded = (dot_nt(grad_ffn, w2_ref[columns, :]) * slope).astype(bf16)
            final = final + dot(activated, w2_ref[columns, :])
            dw2t_ref[:, columns] += dot(grad_columns, activated)
            dw1_ref[:, columns] += dot(hidden_columns, grad_expanded)
            grad_hidden = grad_hidden + dot_nt(grad_expanded, w1_ref[:, columns])
        out_ref[rows, :] = (final * counted).astype(bf16)
        back, gain_sum = norm_back(grad_hidden, scaled_three, inverse_three, gain_three)
        dgain_ref[2:3, :] += gain_sum
        grad_cross = grad_final + back
        branch = grad_cross.astype(bf16)
        dwco_ref[...] += dot(cross_rows.T, branch)
        grad_mixed = dot_nt(branch, wco_ref[...]).astype(bf16)
        for pair in range(pairs):
            gcm_s[pair] = grad_mixed[:, pair * PAIR : (pair + 1) * PAIR]

        def cross_back(pair, _):
            def add_key(_, value):
                dck_ref[pair] += value

            def add_value(_, value):
                dcv_ref[pair] += value

            extra = cextra_ref[...]
            dqt_s[pair] = attend_pair_back(
                qc_s[pair],
                gcm_s[pair],
                cm_s[pair],
                [extra_s[2 * pair], extra_s[2 * pair + 1]],
                lambda _: jnp.concatenate([ck_ref[pair], extra], axis=1),
                lambda _: jnp.concatenate([cv_ref[pair], extra], axis=1),
                lambda _, head: ckt_ref[pair, 64 * head : 64 * head + 64, :],
                1,
                lane,
                add_key,
                add_value,
            )
            dq_s[pair] = dqt_s[pair].T
            return 0

        lax.fori_loop(0, pairs, cross_back, 0)
        query_grad = jnp.concatenate([dq_s[pair] for pair in range(pairs)], axis=1)
        dwcq_ref[...] += dot(hidden_two.T, query_grad)
        back, gain_sum = norm_back(
            dot_nt(query_grad, wcq_ref[...]), scaled_two, inverse_two, gain_two
        )
        dgain_ref[1:2, :] += gain_sum
        grad_self = grad_cross + back
        grad_self_ref[rows, :] = grad_self
        branch = grad_self.astype(bf16)
        dwo_ref[...] += dot(self_rows.T, branch)
        grad_mixed = dot_nt(branch, wo_ref[...]).astype(bf16)
        for pair in range(pairs):
            grad_mixed_ref[pair, rows, :] = grad_mixed[:, pair * PAIR : (pair + 1) * PAIR]
        return 0

    lax.fori_loop(0, rows_own // BLOCK, step, 0)
    dwck_ref[...] = jnp.zeros(dwck_ref.shape, f32)
    dwcv_ref[...] = jnp.zeros(dwcv_ref.shape, f32)

    def gathered(ref, rows, factor):
        parts = [(ref[pair, rows, :] * factor).astype(bf16) for pair in range(pairs)]
        return jnp.concatenate(parts, axis=1)

    def source_back(index, _):
        rows = block_at(index, BLOCK)
        source_columns = source_ref[rows, :].T
        key_grad = gathered(dck_ref, rows, LN2)
        value_grad = gathered(dcv_ref, rows, 1.0)
        dwck_ref[...] += dot(source_columns, key_grad)
        dwcv_ref[...] += dot(source_columns, value_grad)
        grad_source_ref[rows, :] = (
            dot_nt(key_grad, wck_ref[...]) + dot_nt(value_grad, wcv_ref[...])
        ).astype(bf16)
        return 0

    lax.fori_loop(0, few // BLOCK, source_back, 0)
    for at, ref in enumerate((dwo_ref, dwcq_ref, dwck_ref, dwcv_ref, dwco_ref)):
        to_blocks(part_a, at * deep, deep, ref)
    to_blocks(part_b, 0, deep, dw1_ref, hidden_width // width)
    deep_two = hidden_width // 8
    for column in range(4):
        for side in range(2):
            for plane in range(4):
                for half in range(2):
                    at = (plane * 2 + side) * deep_two + half * PAIR
                    part_c[column, side, plane, half * PAIR : (half + 1) * PAIR, :] = dw2t_ref[
                        column * PAIR : (column + 1) * PAIR, at : at + PAIR
                    ].astype(bf16)


def last_kernel(comm, planes, source_len_ref, upsample_ref, *refs):
    (q_any, k_any, v_any, mixed_any, grad_any, extra_any) = refs[:6]
    (x_any, qkv_any, gain_any, grad_self_any, dgain_any) = refs[6:11]
    refs = refs[11:]
    if comm:
        (part_a, part_b, part_c, source_any, rows_any) = refs[:5]
        (rows_land, grad_out, cross_land, source_out, source_far) = refs[5:10]
        (*weight_outs, gain_out) = refs[10:21]
        refs = refs[21:]
    else:
        (own_out, other_out, part_out, gain_out) = refs[:4]
        refs = refs[4:]
    (
        q_s, k_s, v_s, mixed_s, grad_s, extra_s, x_s, qkv_s, gain_s, grad_self_s, dgain_s,
        dk_s, dv_s, keys_s, values_s, kt_s, hidden_s, total_s, dkv_s, dq_s, weight_s,
        part_s, load, send, receive,
    ) = refs[:25]
    refs = refs[25:]
    where = Where(planes)
    chip, core, side, plane = where.chip, where.core, where.side, where.plane
    total, width = x_s.shape
    own = total // 2
    rows = total // 4
    pairs = width // PAIR
    deep = width // 8
    chunk = 512
    size = 512
    blocks = own // size
    lane = lax.broadcasted_iota(jnp.int32, (size, PAIR), 1)
    semaphores = Semaphores(send, receive)
    sentence = where.group * 2 + chip
    length = source_len_ref[sentence] * upsample_ref[sentence]

    def turn_pair(turn):
        return where.column(pairs - 1 - turn)

    def turn_loads(turn):
        pair, slot = turn_pair(turn), turn % 2
        return [
            pltpu.make_async_copy(source.at[pair], target.at[slot], load.at[slot, at])
            for at, (source, target) in enumerate(
                (
                    (q_any, q_s),
                    (k_any, k_s),
                    (v_any, v_s),
                    (mixed_any, mixed_s),
                    (grad_any, grad_s),
                    (extra_any, extra_s),
                )
            )
        ]

    for copy in turn_loads(0):
        copy.start()
    common = [
        semaphores.local(source, target)
        for source, target in (
            (x_any, x_s),
            (qkv_any, qkv_s),
            (gain_any, gain_s),
            (dgain_any, dgain_s),
            (grad_self_any, grad_self_s),
        )
    ]
    for copy in common:
        copy.start()

    def begin(copies):
        for copy in copies:
            copy.start()

    def arrive(copies):
        for copy in copies:
            copy.wait_recv()

    if comm:
        (
            keep_a, keep_b, keep_c, core_a, core_b, core_c, far_a, far_b, far_c,
            near_a, near_b, near_c, planes_a, planes_b, planes_c,
            land_q, far_q, planes_q, gain_send, gain_land, gain_far, gain_planes, grads_send,
            grads_land, cross_send, stage, source_s, source_land, stage_s,
        ) = refs
        place, across = where.place, where.column(2)
        pieces = []
        for part, keep, land, far_land, near_land, land_planes, order in (
            (part_a, keep_a, core_a, far_a, near_a, planes_a, "yxz"),
            (part_b, keep_b, core_b, far_b, near_b, planes_b, "yzx"),
            (part_c, keep_c, core_c, far_c, near_c, planes_c, "xyz"),
        ):
            piece = dict(keep=keep, land=land, order=order)
            piece.update(far_land=far_land, near_land=near_land, planes=land_planes)
            piece["load"] = [
                semaphores.local(part.at[place], keep.at[0]),
                semaphores.local(part.at[across], keep.at[1]),
            ]
            piece["core"] = [
                semaphores.remote(part.at[where.column(1)], land.at[0], where.other_core),
                semaphores.remote(part.at[where.column(3)], land.at[1], where.other_core),
            ]
            if order[0] == "y":
                piece["far"] = [
                    semaphores.remote(keep.at[at, 1 - side], far_land.at[at], where.other_side)
                    for at in (0, 1)
                ]
            else:
                piece["far"] = [
                    semaphores.remote(keep.at[1, at], far_land.at[at], where.other_chip)
                    for at in (0, 1)
                ]
            if order == "yzx":
                near = (keep.at[1, side, plane], near_land.at[0], where.other_chip)
            elif order == "yxz":
                near = (keep.at[1, side], near_land, where.other_chip)
            else:
                near = (keep.at[0, 1 - side], near_land, where.other_side)
            piece["near"] = [semaphores.remote(*near)]
            piece["last"] = [
                semaphores.remote(
                    keep.at[at, side, (plane + step) % planes],
                    land_planes.at[at, step - 1],
                    where.other_planes[step - 1],
                )
                for at in ((0, 1) if order == "yzx" else (0,))
                for step in range(1, planes)
            ]
            pieces.append(piece)
        a, b, c = pieces
        owners = (where.diagonal, where.other_chip, where.other_core)
        hops = (where.other_core, where.other_chip, where.other_core)
        send_q = [
            semaphores.remote(part_s.at[turn], land_q.at[turn], hops[turn]) for turn in range(3)
        ]
        side_q = semaphores.remote(part_s.at[3, 1 - side], far_q, where.other_side)
        plane_q = [
            semaphores.remote(
                part_s.at[3, side, (plane + step) % planes],
                planes_q.at[step - 1],
                where.other_planes[step - 1],
            )
            for step in range(1, planes)
        ]
        gain_group = [
            semaphores.remote(gain_send.at[where.column(3 - turn)], gain_land.at[turn], owners[turn])
            for turn in range(3)
        ]
        gain_side = semaphores.remote(gain_land.at[3], gain_far, where.other_side)
        gain_last = [
            semaphores.remote(
                gain_planes.at[plane], gain_planes.at[plane], where.other_planes[step - 1]
            )
            for step in range(1, planes)
        ]
        rows_cross = semaphores.remote(rows_any.at[rows:], rows_land, where.other_chip)
        few = source_any.shape[0] // 4
        source_local = semaphores.local(source_any.at[: 2 * few], source_s)
        source_core = semaphores.remote(source_any.at[2 * few :], source_land, where.other_core)
        source_cross = semaphores.remote(source_s.at[few:], source_far, where.other_chip)
        grads_core = [
            semaphores.remote(grads_send.at[at], grads_land.at[at], where.other_core)
            for at in range(2)
        ]
        grads_cross = [
            semaphores.remote(cross_send.at[at], cross_land.at[at], where.other_chip)
            for at in range(rows // BLOCK)
        ]
        stage_out = semaphores.local(stage, grad_out)
        source_own = semaphores.local(stage_s, source_out)
        for piece in pieces:
            begin(piece["load"])
        begin([source_local])
        greet(where.everyone())

        def add_in(ref, land):
            def add(at, _):
                ref[at] = (ref[at].astype(f32) + land[at].astype(f32)).astype(bf16)
                return 0

            lax.fori_loop(0, planes, add, 0)

        def add_core(piece):
            for copy in piece["load"]:
                copy.wait()
            arrive(piece["core"])
            for at in (0, 1):
                for half in (0, 1):
                    add_in(piece["keep"].at[at, half], piece["land"].at[at, half])
            begin(piece["far"])

        def add_far(piece):
            arrive(piece["far"])
            for at in (0, 1):
                if piece["order"][0] == "y":
                    add_in(piece["keep"].at[at, side], piece["far_land"].at[at])
                else:
                    add_in(piece["keep"].at[0, at], piece["far_land"].at[at])
            begin(piece["last" if piece["order"] == "yzx" else "near"])

        def add_near(piece):
            arrive(piece["near"])
            add_in(piece["keep"].at[0, side], piece["near_land"])
            begin(piece["last"])

        def over_planes(piece, at):
            value = piece["keep"][at, side, plane].astype(f32)
            for step in range(planes - 1):
                value = value + piece["planes"][at, step].astype(f32)
            return value

        def add_planes(piece):
            arrive(piece["last"])
            for at in (0, 1):
                piece["keep"][at, side, plane] = over_planes(piece, at).astype(bf16)
            begin(piece["near"])

        def finish(piece):
            if piece["order"] == "yzx":
                arrive(piece["near"])
                return piece["keep"][0, side, plane].astype(f32) + piece["near_land"][0].astype(f32)
            arrive(piece["last"])
            return over_planes(piece, 0)

    mask_columns(chip, core, rows, total, BLOCK, length, values_s.at[:, PAIR:])
    keys_s[:, PAIR:] = values_s[:, PAIR:]
    for copy in common:
        copy.wait()
    gain = jnp.concatenate([gain_s[at, 0:1, :] for at in range(pairs)], axis=1)

    def hide(index, _):
        at = block_at(index, BLOCK)
        scaled, _ = normalize(x_s[at, :].astype(f32))
        hidden_s[:, at] = (scaled * gain).astype(bf16).T
        return 0

    lax.fori_loop(0, total // BLOCK, hide, 0)
    if comm:
        await_greetings(where.everyone())
        for piece in pieces:
            begin(piece["core"])
        begin([source_core, rows_cross])

    def take_weights(turn, pair):
        for part in range(3):
            for at in range(8):
                weight_s[turn, at * 64 : at * 64 + 64, part * PAIR : (part + 1) * PAIR] = qkv_s[
                    pair, at % 2, at // 2, part * 64 : part * 64 + 64, :
                ]

    def upstream(turns, at, own_rows):
        value = None
        for turn in turns:
            term = dot_nt(dkv_s[turn, at, :], weight_s[turn, :, PAIR:])
            if own_rows:
                term = term + dot_nt(dq_s[turn, at, :], weight_s[turn, :, :PAIR])
            value = term if value is None else value + term
        return value

    def step(index, _):
        turn = index // blocks
        pair, slot = turn_pair(turn), turn % 2
        at = block_at(index % blocks, size)
        if comm:

            @pl.when(index == 1)
            def _():
                add_core(a)
                add_core(c)
                add_core(b)
                source_local.wait()
                arrive([source_core])
                for half in range(2):
                    r = slice(half * few, (half + 1) * few)
                    value = source_s[r, :].astype(f32) + source_land[r, :].astype(f32)
                    source_s[r, :] = value.astype(bf16)
                    if half == 0:
                        stage_s[...] = value
                begin([source_cross, source_own])

            @pl.when(index == 3)
            def _():
                add_far(a)
                add_far(c)

            @pl.when(index == 4)
            def _():
                arrive([send_q[0]])
                for half in range(2):
                    add_in(part_s.at[1, half], land_q.at[0, half])
                send_q[1].start()

            @pl.when(index == 5)
            def _():
                add_far(b)
                add_near(a)

            @pl.when(index == 6)
            def _():
                add_near(c)

            @pl.when(index == 7)
            def _():
                add_planes(b)

        @pl.when(index % blocks == 0)
        def _():
            for copy in turn_loads(turn):
                copy.wait()

            @pl.when(turn + 1 < pairs)
            def _():
                for copy in turn_loads(turn + 1):
                    copy.start()

            dk_s[...] = jnp.zeros(dk_s.shape, f32)
            dv_s[...] = jnp.zeros(dv_s.shape, f32)
            keys_s[:, :PAIR] = k_s[slot]
            values_s[:, :PAIR] = v_s[slot]
            kt_s[...] = k_s[slot].T
            take_weights(turn, pair)

        def part(ref):
            return lambda part: ref[part * chunk : (part + 1) * chunk, :]

        def add_to(ref):
            def add(part, value):
                ref[part * chunk : (part + 1) * chunk, :] += value

            return add

        query_grad = attend_pair_back(
            q_s[slot, at, :],
            grad_s[slot, at, :],
            mixed_s[slot, at, :],
            [extra_s[slot, head, at, :] for head in (0, 1)],
            part(keys_s),
            part(values_s),
            lambda part, head: kt_s[64 * head : 64 * head + 64, part * chunk : (part + 1) * chunk],
            total // chunk,
            lane,
            add_to(dk_s),
            add_to(dv_s),
        )
        dq_s[turn, at, :] = query_grad.T

        @pl.when(index % blocks == blocks - 1)
        def _():
            dkv_s[turn, :, :PAIR] = (dk_s[...] * LN2).astype(bf16)
            dkv_s[turn, :, PAIR:] = dv_s[...].astype(bf16)
            both = dot(hidden_s[...], dkv_s[turn]).astype(bf16)
            query = dot(hidden_s[:, :own], dq_s[turn]).astype(bf16)
            for at in range(8):
                r = slice(at * deep, (at + 1) * deep)
                for part, value in enumerate(
                    (query[r, :], both[r, :PAIR], both[r, PAIR:])
                ):
                    part_s[turn, at % 2, at // 2, part * deep : (part + 1) * deep, :] = value

        if comm:
            for sent in (0, 2):

                @pl.when(index == sent * blocks + blocks - 1)
                def _():
                    send_q[sent].start()

        @pl.when(index == (pairs - 1) * blocks - 1)
        def _():
            def early(row, _):
                r = block_at(row, BLOCK)
                total_s[r, :] = upstream(range(pairs - 1), r, True)
                return 0

            def early_other(row, _):
                r = block_at(row, BLOCK)
                total_s[r, :] = upstream(range(pairs - 1), r, False)
                return 0

            lax.fori_loop(0, own // BLOCK, early, 0)
            lax.fori_loop(own // BLOCK, total // BLOCK, early_other, 0)

        return 0

    lax.fori_loop(0, pairs * blocks, step, 0)

    def row_back(row, own_rows):
        r = block_at(row, BLOCK)
        scaled, inverse = normalize(x_s[r, :].astype(f32))
        value = total_s[r, :] + upstream([pairs - 1], r, own_rows)
        back, gain_sum = norm_back(value, scaled, inverse, gain)
        dgain_s[0:1, :] += gain_sum
        return r, back

    per = rows // BLOCK
    if not comm:

        def own_step(row, _):
            r, back = row_back(row, True)
            grad_self_s[r, :] += back
            return 0

        def other_step(row, _):
            r, back = row_back(row, False)
            total_s[r, :] = back
            return 0

        lax.fori_loop(0, 2 * per, own_step, 0)
        lax.fori_loop(2 * per, 4 * per, other_step, 0)
        own_out[...] = grad_self_s[...]
        other_out[...] = total_s[own:, :].astype(bf16)
        for turn in range(pairs):
            part_out[turn_pair(turn)] = part_s[turn]
        gain_out[...] = dgain_s[...]
        return

    def add_q(at, _):
        for half in range(2):
            value = part_s[3, half, at].astype(f32)
            for turn in (1, 2):
                value = value + land_q[turn, half, at].astype(f32)
            part_s[3, half, at] = value.astype(bf16)
        return 0

    def other_rows(slot):
        def other_step(row, _):
            _, back = row_back(slot * per + row, False)
            grads_send[slot - 2, block_at(row, BLOCK), :] = back.astype(bf16)
            return 0

        lax.fori_loop(0, per, other_step, 0)
        grads_core[slot - 2].start()

    other_rows(3)
    arrive(send_q[1:])
    lax.fori_loop(0, planes, add_q, 0)
    side_q.start()
    other_rows(2)

    def own_rows(row, _):
        r, back = row_back(row, True)
        total_s[r, :] = back + grad_self_s[r, :]
        return 0

    lax.fori_loop(0, 2 * per, own_rows, 0)
    for at in range(pairs):
        gain_send[at] = dgain_s[:, at * PAIR : (at + 1) * PAIR]
    begin(gain_group)
    arrive([grads_core[1]])
    for row in range(per):
        r = slice(row * BLOCK, (row + 1) * BLOCK)
        value = total_s[rows + row * BLOCK : rows + (row + 1) * BLOCK, :]
        cross_send[row] = (value + grads_land[1, r, :].astype(f32)).astype(bf16)
        grads_cross[row].start()
    arrive([side_q])
    add_in(part_s.at[3, side], far_q)
    begin(plane_q)
    arrive(gain_group)
    gain_land[3] = gain_send[place] + gain_land[0] + gain_land[1] + gain_land[2]
    gain_side.start()
    arrive([grads_core[0]])
    stage[...] = total_s[:rows, :] + grads_land[0].astype(f32)
    stage_out.start()
    sums = [finish(piece) for piece in pieces]
    for at in range(5):
        weight_outs[3 + at][...] = sums[0][at * deep : (at + 1) * deep, :]
    for at in range(sums[1].shape[0] // deep):
        weight_outs[8][:, at * PAIR : (at + 1) * PAIR] = sums[1][at * deep : (at + 1) * deep, :]
    for at in range(sums[2].shape[0] // PAIR):
        r = slice(at * PAIR, (at + 1) * PAIR)
        weight_outs[9][r, :] = sums[2][r, :].T
    arrive([gain_side])
    gain_planes[plane] = gain_land[3] + gain_far[...]
    begin(gain_last)
    arrive(plane_q)
    value = part_s[3, side, plane].astype(f32)
    for at in range(planes - 1):
        value = value + planes_q[at].astype(f32)
    for at in range(3):
        weight_outs[at][...] = value[at * deep : (at + 1) * deep, :]
    arrive(gain_last)
    value = gain_planes[0]
    for at in range(1, planes):
        value = value + gain_planes[at]
    gain_out[...] = value
    arrive([rows_cross, source_cross, *grads_cross])
    for copy in (stage_out, source_own):
        copy.wait()
    for copy in semaphores.sent:
        copy.wait_send()


def hand_over_kernel(planes, *refs):
    (rows_any, rows_far, grad_own, grad_far, source_own, source_far, *plain) = refs[:17]
    (decoder_out, grad_out, source_out, *plain_outs) = refs[17:31]
    (rows_s, grad_s, grad_low, source_s, source_low, *plain_s) = refs[31:-2]
    load, store = refs[-2:]
    chip = Where(planes).chip
    rows = rows_s.shape[1]
    moves = [
        (rows_any.at[:rows], rows_s.at[0], rows_s.at[0], decoder_out.at[chip]),
        (rows_far, rows_s.at[1], rows_s.at[1], decoder_out.at[1 - chip]),
        (grad_own, grad_s.at[0], grad_s.at[0], grad_out.at[chip]),
        (grad_far, grad_low, grad_s.at[1], grad_out.at[1 - chip]),
        (source_own, source_s.at[0], source_s.at[0], source_out.at[chip]),
        (source_far, source_low, source_s.at[1], source_out.at[1 - chip]),
    ]
    moves += [
        (one, held, held.at[: other.shape[0]], other)
        for one, held, other in zip(plain, plain_s, plain_outs)
    ]
    loads = [pltpu.make_async_copy(m[0], m[1], load.at[at]) for at, m in enumerate(moves)]
    stores = [pltpu.make_async_copy(m[2], m[3], store.at[at]) for at, m in enumerate(moves)]
    for copy in loads:
        copy.start()
    for at, (one, other) in enumerate(zip(loads, stores)):
        one.wait()
        if at == 3:
            for row in range(grad_low.shape[0]):
                size = grad_low.shape[1]
                grad_s[1, row * size : (row + 1) * size, :] = grad_low[row].astype(f32)
        if at == 5:
            source_s[1] = source_low[...].astype(f32)
        other.start()
    for copy in stores:
        copy.wait()


def call(kernel, outs, *operands, scratch=(), smem=0, params=PARAMS, spaces=None, out_space=VMEM, out_spaces=None):
    spaces = spaces or {}
    out_spaces = out_spaces or {}
    return pl.pallas_call(
        kernel,
        out_shape=[jax.ShapeDtypeStruct(shape, kind) for shape, kind in outs],
        in_specs=[
            pl.BlockSpec(memory_space=pltpu.SMEM if at < smem else spaces.get(at, VMEM))
            for at in range(len(operands))
        ],
        out_specs=[
            pl.BlockSpec(memory_space=out_spaces.get(at, out_space)) for at in range(len(outs))
        ],
        scratch_shapes=list(scratch),
        compiler_params=params,
    )(*operands)


def swapped(value, axis, bit):
    pairs = [(source, source ^ bit) for source in range(lax.axis_size(axis))]
    return lax.ppermute(value, axis, pairs)


def as_blocks(weight, chunks=1):
    height, width = weight.shape
    deep = height // 8
    cut = weight.reshape(4, 2, deep, 4, chunks, PAIR).transpose(3, 1, 0, 4, 2, 5)
    return cut.reshape(4, 2, 4, chunks * deep, PAIR)


def from_blocks(blocks, chunks=1):
    height = blocks.shape[3] // chunks
    cut = blocks.reshape(4, 2, 4, chunks, height, PAIR).transpose(2, 1, 4, 0, 3, 5)
    return cut.reshape(8 * height, 4 * chunks * PAIR)


def gather_plain(arguments, seq_size, dp_size):
    (decoder_in, source_states, out_grad, narrow, ffn_expand, ffn_reduce, norm_gains) = arguments
    chip = lax.axis_index("seq") // 2
    rows_dec = decoder_in.shape[1]
    own = 2 * rows_dec
    outgoing = jnp.concatenate([decoder_in[1 - chip], source_states[1 - chip]], axis=0)
    arrived = swapped(outgoing, "seq", 2)
    own_rows = jnp.concatenate(
        [decoder_in[chip], arrived[:rows_dec], source_states[chip], arrived[rows_dec:]], axis=0
    )
    other_rows = swapped(own_rows, "seq", 1)
    x_all = jnp.concatenate([own_rows[:own], other_rows[:own]], axis=0)
    source_all = jnp.concatenate([own_rows[own:], other_rows[own:]], axis=0)
    cotangent = swapped(out_grad[1 - chip], "seq", 2)

    def whole(weight):
        weight = lax.all_gather(weight, "seq", axis=1, tiled=True)
        return lax.all_gather(weight, "dp", axis=0, tiled=True)

    blocks = [as_blocks(whole(weight)) for weight in narrow]
    qkv = jnp.concatenate(blocks[:3], axis=3)
    later_a = jnp.concatenate(blocks[3:], axis=3)
    later_b = as_blocks(whole(ffn_expand), ffn_expand.shape[1] // PAIR)
    later_c = as_blocks(whole(ffn_reduce))
    gain_block = jnp.pad(norm_gains.astype(f32), ((0, 5), (0, 0)))
    gains = lax.all_gather(gain_block, "seq", axis=0)
    return x_all, source_all, cotangent, qkv, later_a, later_b, later_c, gains


def body(
    decoder_in,
    source_states,
    source_len,
    upsample,
    send_counts,
    self_query,
    self_key,
    self_value,
    self_output,
    cross_query,
    cross_key,
    cross_value,
    cross_output,
    ffn_expand,
    ffn_reduce,
    norm_gains,
    out_grad,
):
    seq_size = lax.axis_size("seq")
    dp_size = lax.axis_size("dp")
    planes = dp_size // 2
    place = lax.axis_index("seq")
    chip = place // 2
    home_count, rows_dec, width = decoder_in.shape
    rows_src = source_states.shape[1]
    pairs = width // PAIR
    own = 2 * rows_dec
    total = 4 * rows_dec
    deep = self_query.shape[0]
    deep_two = ffn_reduce.shape[0]
    wide = ffn_expand.shape[1] // PAIR
    hidden_width = wide * PAIR * seq_size
    all_src = 4 * rows_src
    comm = dp_size == 8

    def pair_rows(rows):
        return (pairs, rows, PAIR)

    narrow = (self_query, self_key, self_value, self_output)
    narrow += (cross_query, cross_key, cross_value, cross_output)
    rows_outs = [
        (pair_rows(own), bf16),
        (pair_rows(total), bf16),
        (pair_rows(total), bf16),
        (pair_rows(own), bf16),
        ((pairs, 2, own, PAIR), bf16),
    ]
    buffers = [VMEM(shape, kind) for shape, kind in rows_outs]
    work = [
        VMEM((total, width), bf16),
        VMEM((width, 3 * PAIR), bf16),
        VMEM((total, PAIR), bf16),
        *buffers,
    ]
    semaphores = [pltpu.SemaphoreType.DMA((96,)), pltpu.SemaphoreType.DMA((96,))]
    if comm:
        cut = (seq_size, 2, planes)
        gathered = [
            ((total, width), bf16),
            ((all_src, width), bf16),
            ((rows_dec, width), bf16),
            (cut + (3 * deep, PAIR), bf16),
            (cut + (5 * deep, PAIR), bf16),
            (cut + (wide * deep, PAIR), bf16),
            (cut + (deep_two, PAIR), bf16),
            ((seq_size, 8, PAIR), f32),
        ]
        operands = (source_len, upsample, decoder_in, source_states, out_grad)
        operands += (*narrow, ffn_expand, ffn_reduce, norm_gains)
        (
            x_all, source_all, cotangent, qkv, later_a, later_b, later_c, gains,
            q, k, v, mixed, query_extra,
        ) = call(
            partial(open_kernel, True, planes, deep),
            gathered + rows_outs,
            *operands,
            scratch=[
                VMEM((total, width), bf16),
                VMEM(cut + (3 * deep, PAIR), bf16),
                VMEM((seq_size, 8, PAIR), f32),
                *work,
                *semaphores,
                VMEM((5 * deep, PAIR), bf16),
                VMEM((wide * deep, PAIR), bf16),
                VMEM((deep_two, PAIR), bf16),
                VMEM((rows_src, width), bf16),
                VMEM((8, PAIR), f32),
            ],
            smem=2,
            spaces={at: pl.ANY for at in range(2, len(operands) - 1)},
            out_space=pl.ANY,
            params=pltpu.CompilerParams(
                vmem_limit_bytes=VMEM_LIMIT, collective_id=0, has_side_effects=True
            ),
        )
    else:
        x_all, source_all, cotangent, qkv, later_a, later_b, later_c, gains = gather_plain(
            (decoder_in, source_states, out_grad, narrow, ffn_expand, ffn_reduce, norm_gains),
            seq_size,
            dp_size,
        )
        q, k, v, mixed, query_extra = call(
            partial(open_kernel, False, planes, deep),
            rows_outs,
            source_len,
            upsample,
            x_all,
            qkv,
            gains,
            scratch=[*work, *semaphores],
            smem=2,
            out_space=pl.ANY,
        )
    square = VMEM((width, width), f32)
    parts = [
        ((seq_size, 2, 4, 5 * width // 8, PAIR), bf16),
        ((seq_size, 2, 4, hidden_width // 8, PAIR), bf16),
        ((seq_size, 2, 4, hidden_width // 8, PAIR), bf16),
    ]
    out_rows, grad_mixed, grad_self, part_a, part_b, part_c, grad_source, dgain = call(
        partial(middle_kernel, planes),
        [
            ((own, width), bf16),
            (pair_rows(own), bf16),
            ((own, width), f32),
            *parts,
            ((all_src, width), bf16),
            ((8, width), f32),
        ],
        source_len,
        upsample,
        send_counts,
        x_all,
        mixed,
        out_grad,
        cotangent,
        source_all,
        later_a,
        later_b,
        later_c,
        gains,
        scratch=[
            *[square] * 3,
            *[VMEM((width, hidden_width), f32)] * 2,
            *[square] * 2,
            VMEM((own, width), bf16),
            *[VMEM((width, width), bf16)] * 5,
            VMEM((width, hidden_width), bf16),
            VMEM((hidden_width, width), bf16),
            VMEM(pair_rows(all_src), bf16),
            VMEM(pair_rows(all_src), bf16),
            VMEM((pairs, PAIR, all_src), bf16),
            VMEM((all_src, PAIR), bf16),
            VMEM(pair_rows(all_src), f32),
            VMEM(pair_rows(all_src), f32),
            pltpu.SemaphoreType.DMA((3,)),
            VMEM((own, width), bf16),
            VMEM((pairs, BLOCK, PAIR), bf16),
            VMEM((2 * pairs, BLOCK, PAIR), bf16),
            VMEM((pairs, PAIR, BLOCK), bf16),
            VMEM((pairs, BLOCK, PAIR), bf16),
            VMEM((pairs, BLOCK, PAIR), bf16),
            VMEM((pairs, BLOCK, PAIR), bf16),
        ],
        smem=3,
        spaces={3: pl.ANY, 5: pl.ANY, 6: pl.ANY},
    )
    part_q = ((seq_size, 2, 4, 3 * width // 8, PAIR), bf16)
    operands = (source_len, upsample, q, k, v, mixed, grad_mixed, query_extra)
    operands += (x_all, qkv, gains, grad_self, dgain)
    work = [
        VMEM((2, own, PAIR), bf16),
        VMEM((2, total, PAIR), bf16),
        VMEM((2, total, PAIR), bf16),
        VMEM((2, own, PAIR), bf16),
        VMEM((2, own, PAIR), bf16),
        VMEM((2, 2, own, PAIR), bf16),
        VMEM((total, width), bf16),
        VMEM(qkv.shape, bf16),
        VMEM(gains.shape, f32),
        VMEM((own, width), f32),
        VMEM((8, width), f32),
        VMEM((total, PAIR), f32),
        VMEM((total, PAIR), f32),
        VMEM((total, 2 * PAIR), bf16),
        VMEM((total, 2 * PAIR), bf16),
        VMEM((PAIR, total), bf16),
        VMEM((width, total), bf16),
        VMEM((total, width), f32),
        VMEM((pairs, total, 2 * PAIR), bf16),
        VMEM((pairs, own, PAIR), bf16),
        VMEM((pairs, width, 3 * PAIR), bf16),
        VMEM(*part_q),
        pltpu.SemaphoreType.DMA((2, 6)),
        *semaphores,
    ]
    everywhere = {at: pl.ANY for at in range(2, 18)}
    if comm:
        heights = [shape[3] for shape, _ in parts]

        def per_piece(lead):
            return [VMEM((*lead, height, PAIR), bf16) for height in heights]

        work += [
            *per_piece((2, 2, planes)),
            *per_piece((2, 2, planes)),
            *per_piece((2, planes)),
            *per_piece((planes,)),
            *per_piece((2, planes - 1)),
            VMEM((3, 2, planes, 3 * deep, PAIR), bf16),
            VMEM((planes, 3 * deep, PAIR), bf16),
            VMEM((planes - 1, 3 * deep, PAIR), bf16),
            VMEM((pairs, 8, PAIR), f32),
            VMEM((4, 8, PAIR), f32),
            VMEM((8, PAIR), f32),
            VMEM((planes, 8, PAIR), f32),
            VMEM((2, rows_dec, width), bf16),
            VMEM((2, rows_dec, width), bf16),
            VMEM((rows_dec // BLOCK, BLOCK, width), bf16),
            VMEM((rows_dec, width), f32),
            VMEM((2 * rows_src, width), bf16),
            VMEM((2 * rows_src, width), bf16),
            VMEM((rows_src, width), f32),
        ]
        small = ((deep, PAIR), f32)
        plain = [small] * 8 + [(ffn_expand.shape, f32), (ffn_reduce.shape, f32), ((8, PAIR), f32)]
        outs = call(
            partial(last_kernel, True, planes),
            [
                ((rows_dec, width), bf16),
                ((rows_dec, width), f32),
                ((rows_dec // BLOCK, BLOCK, width), bf16),
                ((rows_src, width), f32),
                ((rows_src, width), bf16),
                *plain,
            ],
            *operands,
            part_a,
            part_b,
            part_c,
            grad_source,
            out_rows,
            scratch=work,
            smem=2,
            spaces=everywhere,
            out_spaces={at: pl.ANY for at in range(5)},
            params=pltpu.CompilerParams(
                vmem_limit_bytes=VMEM_LIMIT, collective_id=1, has_side_effects=True
            ),
        )
        outs = call(
            partial(hand_over_kernel, planes),
            [
                (decoder_in.shape, bf16),
                (decoder_in.shape, f32),
                (source_states.shape, f32),
                *plain[:-1],
                (norm_gains.shape, f32),
            ],
            out_rows,
            *outs,
            scratch=[
                VMEM(decoder_in.shape, bf16),
                VMEM(decoder_in.shape, f32),
                VMEM((rows_dec // BLOCK, BLOCK, width), bf16),
                VMEM(source_states.shape, f32),
                VMEM((rows_src, width), bf16),
                *[VMEM(shape, kind) for shape, kind in plain],
                *[pltpu.SemaphoreType.DMA((17,))] * 2,
            ],
            spaces={at: pl.ANY for at in range(17)},
            out_space=pl.ANY,
        )
        (decoder_out, grad_decoder, grad_src, dwq, dwk, dwv, *rest, dw1, dw2, dgains) = outs
        dwo, dwcq, dwck, dwcv, dwco = rest
    else:
        own_grad, other_grad, part_qkv, dgains = call(
            partial(last_kernel, False, planes),
            [((own, width), f32), ((own, width), bf16), part_q, ((8, width), f32)],
            *operands,
            scratch=work,
            smem=2,
            spaces=everywhere,
        )
        crossing = jnp.concatenate([other_grad, grad_source[2 * rows_src :]], axis=0)
        returned = swapped(crossing, "seq", 1).astype(f32)
        grad_rows = own_grad + returned[:own]
        source_rows = grad_source[: 2 * rows_src].astype(f32) + returned[own:]
        homeward = [grad_rows[rows_dec:].astype(bf16), source_rows[rows_src:].astype(bf16)]
        came = swapped(jnp.concatenate([out_rows[rows_dec:], *homeward], axis=0), "seq", 2)

        def both_sentences(mine, theirs):
            theirs = theirs.astype(mine.dtype)
            return jnp.where(chip == 0, jnp.stack([mine, theirs]), jnp.stack([theirs, mine]))

        decoder_out = both_sentences(out_rows[:rows_dec], came[:rows_dec])
        grad_decoder = both_sentences(grad_rows[:rows_dec], came[rows_dec : 2 * rows_dec])
        grad_src = both_sentences(source_rows[:rows_src], came[2 * rows_dec :])

        def summed(blocks, start, count, chunks=1):
            grad = from_blocks(blocks[:, :, :, start : start + chunks * count], chunks)
            grad = lax.psum_scatter(grad.astype(f32), "dp", scatter_dimension=0, tiled=True)
            return lax.psum_scatter(grad, "seq", scatter_dimension=1, tiled=True)

        step = width // 8
        dwq, dwk, dwv = [summed(part_qkv, at * step, step) for at in range(3)]
        dwo, dwcq, dwck, dwcv, dwco = [summed(part_a, at * step, step) for at in range(5)]
        dw1 = summed(part_b, 0, step, hidden_width // width)
        tall = part_c.reshape(seq_size, 2, 4, hidden_width // 8 // PAIR, PAIR, PAIR)
        dw2 = summed(tall.swapaxes(4, 5).reshape(part_c.shape), 0, hidden_width // 8)
        dgains = lax.psum(dgains, "dp")
        dgains = lax.psum_scatter(dgains, "seq", scatter_dimension=1, tiled=True)
    return (
        decoder_out,
        grad_decoder,
        grad_src,
        dwq,
        dwk,
        dwv,
        dwo,
        dwcq,
        dwck,
        dwcv,
        dwco,
        dw1,
        dw2,
        dgains[:3],
    )


def solution(mesh):
    rows = P("dp", "seq", None)
    weight = P("dp", "seq")
    placed = (rows, rows, P(), P(), P()) + (weight,) * 10 + (P(None, "seq"), rows)
    return jax.shard_map(
        body,
        mesh=mesh,
        in_specs=placed,
        out_specs=(rows, rows, rows) + (weight,) * 10 + (P(None, "seq"),),
        check_vma=False,
    )
```

```python
from functools import partial

import jax
import jax.numpy as jnp
from jax import lax
from jax.experimental import pallas as pl
from jax.experimental.pallas import tpu as pltpu
from jax.sharding import PartitionSpec as P

HEADS = 8
EPSILON = 1e-05
NEGATIVE = -1000000000.0
LOG2E = 1.4426950408889634
LN2 = 0.6931471805599453
GELU_IN = 0.7978845608028654
GELU_CUBE = 0.044715
BLOCK = 256
PAIR = 128

bf16 = jnp.bfloat16
f32 = jnp.float32
VMEM = pltpu.VMEM
VMEM_LIMIT = 60 * 1024 * 1024
PARAMS = pltpu.CompilerParams(vmem_limit_bytes=VMEM_LIMIT)


def dot(left, right):
    return jnp.dot(left, right, preferred_element_type=f32)


def dot_nt(left, right):
    return lax.dot_general(left, right, (((1,), (1,)), ((), ())), preferred_element_type=f32)


def block_at(index, size):
    return pl.ds(pl.multiple_of(index * size, size), size)


def repeat(start, stop, todo, group):
    def step(at, _):
        for part in range(group):
            todo(start + at * group + part)
        return 0

    count, rest = divmod(stop - start, group)
    if count == 1:
        step(0, 0)
    elif count:
        lax.fori_loop(0, count, step, 0)
    for part in range(rest):
        todo(start + count * group + part)


def row_mean(values):
    return jnp.mean(values, axis=-1, keepdims=True)


def normalize(values):
    centred = values - row_mean(values)
    inverse = lax.rsqrt(row_mean(centred * centred) + EPSILON)
    return centred * inverse, inverse


def norm_back(upstream, scaled, inverse, gain):
    inner = upstream * gain
    back = inverse * (inner - row_mean(inner) - scaled * row_mean(inner * scaled))
    return back, jnp.sum(upstream * scaled, axis=0, keepdims=True)


def three_parts(column, lane, last):
    high = column.astype(bf16).astype(f32)
    middle = (column - high).astype(bf16).astype(f32)
    low = column - high - middle
    rest = jnp.where(lane == 3, last, 0.0)
    return jnp.where(
        lane == 0, high, jnp.where(lane == 1, middle, jnp.where(lane == 2, low, rest))
    ).astype(bf16)


def one_head(values, first, head):
    zero = jnp.zeros_like(values)
    return jnp.where(first, values, zero) if head == 0 else jnp.where(first, zero, values)


def attend_pair(query, keys, key_extra, values, lane):
    first = lane < 64
    ones = jnp.where(lane == 3, 1.0, 0.0).astype(bf16)
    keys = jnp.concatenate([keys, key_extra], axis=1)
    values = jnp.concatenate([values, jnp.ones_like(values)], axis=1)
    scores = [
        dot_nt(jnp.concatenate([one_head(query, first, head), ones], axis=1), keys)
        for head in (0, 1)
    ]
    mixed, extras = [], []
    for head in (0, 1):
        peak = jnp.max(scores[head], axis=1, keepdims=True)
        exps = jnp.exp2(scores[head] - peak)
        both = dot(exps.astype(bf16), values)
        total = both[:, PAIR : PAIR + 1]
        mixed.append(both[:, :PAIR] * (1.0 / total))
        extras.append(three_parts(-(peak + jnp.log2(total)), lane, 1.0))
    return jnp.where(first, mixed[0], mixed[1]).astype(bf16), extras


def attend_pair_back(
    query, grad, mixed, query_extra, key_at, value_at, key_columns_at, chunks, put_key, put_value
):
    lane = lax.broadcasted_iota(jnp.int32, query.shape, 1)
    first = lane < 64
    product = grad.astype(f32) * mixed.astype(f32)
    queries = [one_head(query, first, head) for head in (0, 1)]
    grads = [one_head(grad, first, head) for head in (0, 1)]
    long_queries = [jnp.concatenate([queries[h], query_extra[h]], axis=1) for h in (0, 1)]
    long_grads = []
    for head in (0, 1):
        delta = jnp.sum(one_head(product, first, head), axis=1, keepdims=True)
        long_grads.append(
            jnp.concatenate([grads[head], three_parts(-delta, lane, 0.0)], axis=1)
        )
    both_queries = jnp.concatenate(queries, axis=0)
    both_grads = jnp.concatenate(grads, axis=0)
    query_grads = [None, None]
    for chunk in range(chunks):
        keys, values = key_at(chunk), value_at(chunk)
        probs, score_grads = [], []
        for head in (0, 1):
            prob = jnp.exp2(dot_nt(keys, long_queries[head]))
            score_grad = (prob * dot_nt(values, long_grads[head])).astype(bf16)
            probs.append(prob.astype(bf16))
            score_grads.append(score_grad)
            term = dot(key_columns_at(chunk, head), score_grad)
            query_grads[head] = term if chunk == 0 else query_grads[head] + term
        put_value(chunk, dot(jnp.concatenate(probs, axis=1), both_grads))
        put_key(chunk, dot(jnp.concatenate(score_grads, axis=1), both_queries))
    return (jnp.concatenate(query_grads, axis=0) * 0.125).astype(bf16)


def copy_to(source, target, send, receive, partner):
    return pltpu.make_async_remote_copy(
        src_ref=source,
        dst_ref=target,
        send_sem=send,
        recv_sem=receive,
        device_id=partner,
        device_id_type=pl.DeviceIdType.MESH,
    )


def greet(partners):
    for partner in partners:
        pl.semaphore_signal(
            pltpu.get_barrier_semaphore(),
            inc=1,
            device_id=partner,
            device_id_type=pl.DeviceIdType.MESH,
        )


def await_greetings(partners):
    pl.semaphore_wait(pltpu.get_barrier_semaphore(), len(partners))


class Where:
    def __init__(self, planes):
        group, self.place = lax.axis_index("dp"), lax.axis_index("seq")
        self.group = group
        self.chip, self.core = self.place // 2, self.place % 2
        self.plane, self.side = group // 2, group % 2
        self.planes = planes
        self.other_core = self.at(self.chip, 1 - self.core)
        self.other_chip = self.at(1 - self.chip, self.core)
        self.diagonal = self.at(1 - self.chip, 1 - self.core)
        self.other_side = {"dp": self.plane * 2 + 1 - self.side}
        self.other_planes = [
            {"dp": (self.plane + step) % planes * 2 + self.side} for step in range(1, planes)
        ]

    def at(self, chip, core):
        return {"seq": chip * 2 + core}

    def column(self, step):
        return (self.chip + step // 2) % 2 * 2 + (self.core + step % 2) % 2

    def everyone(self):
        return [self.other_core, self.other_chip, self.diagonal, self.other_side] + self.other_planes


class Semaphores:
    def __init__(self, send, receive):
        self.send, self.receive, self.count = send, receive, 0
        self.sent = []

    def remote(self, source, target, partner):
        at = self.count
        self.count += 1
        copy = copy_to(source, target, self.send.at[at], self.receive.at[at], partner)
        self.sent.append(copy)
        return copy

    def local(self, source, target):
        at = self.count
        self.count += 1
        return pltpu.make_async_copy(source, target, self.send.at[at])


def block_places(where_chip, where_core, rows, offset, index, size):
    per = rows // size
    slot = index // per
    block = (where_chip + slot % 2) % 2 * 2 + (where_core + slot // 2) % 2
    return block * rows + index % per * size + offset


def mask_columns(where_chip, where_core, rows, count, size, length, ref):
    lane = lax.broadcasted_iota(jnp.int32, (size, PAIR), 1)
    offset = lax.broadcasted_iota(jnp.int32, (size, PAIR), 0)

    def step(index, _):
        places = block_places(where_chip, where_core, rows, offset, index, size)
        bias = jnp.where(places < length, 0.0, NEGATIVE)
        ref[block_at(index, size), :] = jnp.where(
            lane < 3, 1.0, jnp.where(lane == 3, bias, 0.0)
        ).astype(bf16)
        return 0

    lax.fori_loop(0, count // size, step, 0)


def open_kernel(
    comm,
    planes,
    deep,
    source_len_ref,
    upsample_ref,
    *refs,
):
    if comm:
        (
            decoder_ref, source_ref, cotangent_ref,
            wq_in, wk_in, wv_in, *later_in, gain_in,
            x_out, source_out, cotangent_out, qkv_out, later_a, later_b, later_c, gain_out,
            q_out, k_out, v_out, mixed_out, extra_out,
            x_ref, qkv_ref, gain_ref, hidden_ref, weight_ref, mask_ref,
            q_ref, k_ref, v_ref, mixed_ref, extra_ref, send, receive,
            stage_a, stage_b, stage_c, stage_s, gain_block,
        ) = refs
    else:
        (
            x_ref, qkv_ref, gain_ref,
            q_out, k_out, v_out, mixed_out, extra_out,
            hidden_ref, weight_ref, mask_ref,
            q_ref, k_ref, v_ref, mixed_ref, extra_ref, send, receive,
        ) = refs
    where = Where(planes)
    place, plane, side, chip, core = where.place, where.plane, where.side, where.chip, where.core
    total, width = x_ref.shape
    pairs = width // PAIR
    own = total // 2
    rows = total // 4
    semaphores = Semaphores(send, receive)
    column = where.column

    if comm:
        group = where.group
        x_slots = [x_ref.at[slot * rows : (slot + 1) * rows] for slot in range(4)]
        few = source_ref.shape[1]
        s_slots = [source_out.at[slot * few : (slot + 1) * few] for slot in range(4)]
        local_x = semaphores.local(decoder_ref.at[chip], x_slots[0])
        mine = qkv_ref.at[place, side, plane]
        local_qkv = [
            semaphores.local(ref, mine.at[at * deep : (at + 1) * deep])
            for at, ref in enumerate((wq_in, wk_in, wv_in))
        ]
        first = [local_x, *local_qkv]
        wo_in, wcq_in, wck_in, wcv_in, wco_in, w1_in, w2_in = later_in
        mine_a = later_a.at[place, side, plane]
        mine_b = later_b.at[place, side, plane]
        mine_c = later_c.at[place, side, plane]
        wide = w1_in.shape[1] // PAIR
        local_later = [
            [
                semaphores.local(ref, stage_a.at[at * deep : (at + 1) * deep])
                for at, ref in enumerate((wo_in, wcq_in, wck_in, wcv_in, wco_in))
            ],
            [
                semaphores.local(
                    w1_in.at[:, at * PAIR : (at + 1) * PAIR], stage_b.at[at * deep : (at + 1) * deep]
                )
                for at in range(wide)
            ],
            [semaphores.local(w2_in, stage_c)],
        ]
        stores = [
            semaphores.local(stage_a, mine_a),
            semaphores.local(stage_b, mine_b),
            semaphores.local(stage_c, mine_c),
        ]
        source_load = semaphores.local(source_ref.at[chip], stage_s)
        source_store = semaphores.local(stage_s, s_slots[0])
        greet(where.everyone())
        gain_block[...] = jnp.zeros(gain_block.shape, f32)
        gain_block[0 : gain_in.shape[0], :] = gain_in[...].astype(f32)
        gain_ref[place] = gain_block[...]
        for copy in first + local_later[0] + local_later[1] + local_later[2] + [source_load]:
            copy.start()
        await_greetings(where.everyone())

        x_cross = semaphores.remote(decoder_ref.at[1 - chip], x_slots[1], where.other_chip)
        x_core = semaphores.remote(decoder_ref.at[chip], x_slots[2], where.other_core)
        x_pass = semaphores.remote(x_slots[1], x_slots[3], where.other_core)
        s_cross = semaphores.remote(source_ref.at[1 - chip], s_slots[1], where.other_chip)
        s_core = semaphores.remote(source_ref.at[chip], s_slots[2], where.other_core)
        s_pass = semaphores.remote(s_slots[1], s_slots[3], where.other_core)
        c_cross = semaphores.remote(cotangent_ref.at[1 - chip], cotangent_out, where.other_chip)
        gain_sends = [
            semaphores.remote(gain_block, gain_ref.at[place], partner)
            for partner in (where.other_core, where.other_chip, where.diagonal)
        ]
        qkv_planes = [semaphores.remote(mine, mine, partner) for partner in where.other_planes]
        qkv_side = semaphores.remote(
            qkv_ref.at[place, side], qkv_ref.at[place, side], where.other_side
        )
        qkv_core = semaphores.remote(qkv_ref.at[place], qkv_ref.at[place], where.other_core)
        qkv_chip = semaphores.remote(qkv_ref.at[place], qkv_ref.at[place], where.other_chip)
        across = column(2)
        qkv_pass = semaphores.remote(qkv_ref.at[across], qkv_ref.at[across], where.other_core)
        later = []
        for buffer, stage in ((later_a, stage_a), (later_b, stage_b), (later_c, stage_c)):
            block = buffer.at[place, side, plane]
            mine_side, across_side = buffer.at[place, side], buffer.at[across, side]
            if buffer is later_c:
                first = [semaphores.remote(stage, block, where.other_chip)]
                far = buffer.at[across, side, plane]
                second = [
                    semaphores.remote(stage, block, where.other_side),
                    semaphores.remote(far, far, where.other_side),
                ]
                others = [buffer.at[at, 1 - side, plane] for at in (place, across)]
                kept = [(stage, block), (far, far)] + [(one, one) for one in others]
            else:
                first = [semaphores.remote(mine_side, mine_side, where.other_chip)]
                second = [
                    semaphores.remote(one, one, where.other_side)
                    for one in (mine_side, across_side)
                ]
                kept = [(stage, block)]
            later.append(
                dict(
                    planes=[
                        semaphores.remote(one, other, partner)
                        for one, other in kept
                        for partner in where.other_planes
                    ],
                    first=first,
                    second=second,
                    core=[
                        semaphores.remote(buffer.at[at], buffer.at[at], where.other_core)
                        for at in (place, across)
                    ],
                )
            )

        def begin(copies):
            for copy in copies:
                copy.start()

        def arrive(copies):
            for copy in copies:
                copy.wait_recv()

        begin(gain_sends)
        for copy in local_qkv:
            copy.wait()
        begin(qkv_planes)
        x_cross.start()
        x_core.start()
        begin([s_core])
        for copies in local_later:
            for copy in copies:
                copy.wait()
        source_load.wait()
        begin([*stores, source_store])
        a, b, c = later
        begin(c["first"])
        begin(a["planes"])
        begin(b["planes"])

    length = source_len_ref[where.group * 2 + chip] * upsample_ref[where.group * 2 + chip]
    mask_columns(chip, core, rows, total, BLOCK, length, mask_ref)

    def hide(slot):
        gain = jnp.concatenate([gain_ref[at, 0:1, :] for at in range(pairs)], axis=1)

        def step(index):
            at = pl.ds(index * BLOCK + slot * rows, BLOCK)
            scaled, _ = normalize(x_ref[at, :].astype(f32))
            hidden_ref[at, :] = (scaled * gain).astype(bf16)

        repeat(0, rows // BLOCK, step, rows // BLOCK)

    def take_weights(pair):
        for part in range(3):
            for at in range(8):
                weight_ref[at * 64 : at * 64 + 64, part * PAIR : (part + 1) * PAIR] = qkv_ref[
                    pair, at % 2, at // 2, part * 64 : part * 64 + 64, :
                ]

    def project(pair, slot, count):
        size = 2 * BLOCK
        for index in range(count * rows // size):
            at = pl.ds(slot * rows + index * size, size)
            both = dot(hidden_ref[at, :], weight_ref[:, PAIR:]).astype(bf16)
            k_ref[pair, at, :] = both[:, :PAIR]
            v_ref[pair, at, :] = both[:, PAIR:]
            if slot * rows + index * size < own:
                query = dot(hidden_ref[at, :], weight_ref[:, :PAIR]) * (0.125 * LOG2E)
                q_ref[pair, at, :] = query.astype(bf16)

    if comm:
        local_x.wait()
        arrive(gain_sends)
        hide(0)
        arrive([x_core])
        hide(2)
        arrive(qkv_planes)
        qkv_side.start()
        arrive([qkv_side])
        begin([qkv_core])
        take_weights(place)
        project(place, 0, 1)
        project(place, 2, 1)
        arrive([x_cross])
        x_pass.start()
        arrive(a["planes"])
        for copy in [*stores, source_store]:
            copy.wait()
        begin(a["first"])
        arrive(c["first"])
        begin(c["second"])
        begin([qkv_chip])
        hide(1)
        project(place, 1, 1)
        arrive([x_pass])
        hide(3)
        project(place, 3, 1)
    else:
        for slot in range(4):
            hide(slot)
        take_weights(place)
        project(place, 0, 4)

    size = 2 * BLOCK
    blocks = own // size
    lane = lax.broadcasted_iota(jnp.int32, (size, PAIR), 1)

    def outs_of(pair):
        return [
            (q_ref.at[pair], q_out.at[pair]),
            (k_ref.at[pair], k_out.at[pair]),
            (v_ref.at[pair], v_out.at[pair]),
            (mixed_ref.at[pair], mixed_out.at[pair]),
            (extra_ref.at[pair], extra_out.at[pair]),
        ]

    first_out = semaphores.count

    def out_copies(step, pair):
        return [
            pltpu.make_async_copy(source, target, send.at[first_out + step * 5 + at])
            for at, (source, target) in enumerate(outs_of(pair))
        ]

    if comm:
        x_local = pltpu.make_async_copy(x_ref, x_out, send.at[first_out + 20])
        qkv_local = pltpu.make_async_copy(qkv_ref, qkv_out, send.at[first_out + 21])
        gain_local = pltpu.make_async_copy(gain_ref, gain_out, send.at[first_out + 22])
        begin([x_local, gain_local])

    def step(index, _):
        turn = index // blocks
        pair = column(turn)
        if comm:
            @pl.when(index == 1)
            def _():
                arrive(c["second"])
                begin(c["planes"])
                arrive(b["planes"])
                begin(b["first"])
                begin([s_cross, c_cross])

            @pl.when(index == 2)
            def _():
                arrive([qkv_core])
                arrive(a["first"])
                begin(a["second"])

            @pl.when(index == 4)
            def _():
                arrive([qkv_chip])
                qkv_pass.start()

            @pl.when(index == 5)
            def _():
                arrive(b["first"])
                begin(b["second"])
                arrive(a["second"])
                begin(a["core"])

            @pl.when(index == 6)
            def _():
                arrive([qkv_pass])
                qkv_local.start()
                arrive([s_cross])
                s_pass.start()

            @pl.when(index == 7)
            def _():
                arrive(c["planes"])
                begin(c["core"])

        @pl.when((index % blocks == 0) & (index > 0))
        def _():
            take_weights(pair)
            project(pair, 0, 4)

        at = block_at(index % blocks, size)
        mixed, extras = attend_pair(
            q_ref[pair, at, :], k_ref[pair], mask_ref[...], v_ref[pair], lane
        )
        mixed_ref[pair, at, :] = mixed
        extra_ref[pair, 0, at, :] = extras[0]
        extra_ref[pair, 1, at, :] = extras[1]

        @pl.when(index % blocks == blocks - 1)
        def _():
            for copy in out_copies(turn, pair):
                copy.start()

        return 0

    lax.fori_loop(0, pairs * blocks, step, 0)
    if comm:
        arrive(b["second"])
        begin(b["core"])
        arrive([s_core, s_pass, c_cross])
        for piece in later:
            arrive(piece["core"])
        for copy in semaphores.sent:
            copy.wait_send()
        for copy in (x_local, qkv_local, gain_local):
            copy.wait()
    for turn in range(pairs):
        for copy in out_copies(turn, column(turn)):
            copy.wait()


def whole_weight(ref, blocks, start, count, chunks=1):
    columns, sides, planes = blocks.shape[:3]
    for column in range(columns):
        for side in range(sides):
            for plane in range(planes):
                row = (plane * sides + side) * count
                for chunk in range(chunks):
                    at = (column * chunks + chunk) * PAIR
                    ref[row : row + count, at : at + PAIR] = blocks[
                        column, side, plane, start + chunk * count : start + (chunk + 1) * count, :
                    ]


def to_blocks(blocks, columns, places, start, count, value):
    for column_at, column in enumerate(columns):
        for place_at, (side, plane) in enumerate(places):
            blocks[column, side, plane, start : start + count, :] = value[
                place_at * count : (place_at + 1) * count,
                column_at * PAIR : (column_at + 1) * PAIR,
            ].astype(bf16)


def middle_kernel(
    planes,
    source_len_ref,
    upsample_ref,
    send_ref,
    x_any,
    mixed_any,
    cotangent_any,
    cotangent_far,
    source_any,
    later_a,
    later_b,
    later_c,
    gain_blocks,
    out_rows,
    grad_mixed_out,
    grad_self_out,
    part_a,
    part_b,
    part_c,
    grad_source_ref,
    dgain_ref,
    x_ref,
    mixed_ref,
    cotangent_ref,
    source_ref,
    blocks_a,
    blocks_b,
    blocks_c,
    wo_ref,
    wcq_ref,
    wck_ref,
    wcv_ref,
    wco_ref,
    w1_ref,
    w2_ref,
    ck_ref,
    cv_ref,
    ckt_ref,
    cextra_ref,
    dck_ref,
    dcv_ref,
    after_self_s,
    after_cross_s,
    final_s,
    hidden_grad_s,
    qc_s,
    cm_s,
    gcm_s,
    dq_s,
    extra_s,
    hidden_two_t,
    hidden_three_s,
    hidden_three_t,
    grad_ffn_s,
    grad_ffn_t,
    branch_s,
    load,
    store,
):
    rows_own, width = x_ref.shape
    pairs = mixed_ref.shape[0]
    hidden_width = w1_ref.shape[1]
    chunk = hidden_width // pairs
    where = Where(planes)
    chip, core = where.chip, where.core
    half = rows_own // 2
    size = half
    few = source_ref.shape[0]
    deep = width // 8
    loads = [
        pltpu.make_async_copy(source, target, load.at[at])
        for at, (source, target) in enumerate(
            (
                (x_any.at[:rows_own], x_ref),
                (mixed_any, mixed_ref),
                (later_a, blocks_a),
                (source_any, source_ref),
                (cotangent_any.at[chip], cotangent_ref.at[:half]),
                (cotangent_far, cotangent_ref.at[half:]),
                (later_b, blocks_b),
                (later_c, blocks_c),
            )
        )
    ]
    for copy in loads:
        copy.start()
    stores = [
        pltpu.make_async_copy(source, target, store.at[at])
        for at, (source, target) in enumerate(
            (
                (grad_ffn_s, out_rows),
                (gcm_s, grad_mixed_out),
                (final_s, grad_self_out),
                (blocks_a, part_a),
                (blocks_b, part_b),
                (blocks_c, part_c),
            )
        )
    ]
    gain_rows = jnp.concatenate([gain_blocks[at] for at in range(pairs)], axis=1)
    gain_two = gain_rows[1:2, :]
    gain_three = gain_rows[2:3, :]
    dgain_ref[...] = jnp.zeros(dgain_ref.shape, f32)

    dp_size = planes * 2
    group, half_way = where.group, planes
    sentence = group * 2 + chip
    src_len = source_len_ref[sentence]
    dec_len = src_len * upsample_ref[sentence]
    moved = chip * send_ref[group]
    holder = (group + moved * half_way) % dp_size
    partner = (holder + half_way) % dp_size

    def tokens_of(slot):
        return source_len_ref[slot] * upsample_ref[slot]

    tokens = (
        tokens_of(holder * 2)
        + tokens_of(holder * 2 + 1) * (1 - send_ref[holder])
        + tokens_of(partner * 2 + 1) * send_ref[partner]
    )
    loss_scale = jnp.full((1, 1), rows_own * 2, f32) / jnp.full((1, 1), tokens, jnp.int32).astype(f32)
    mask_columns(chip, core, few // 4, few, few // 4, src_len, cextra_ref)
    offset = lax.broadcasted_iota(jnp.int32, (size, 1), 0)

    def counted(index):
        place = block_places(chip, core, half, offset, index, size)
        return jnp.where(place < dec_len, 1.0, 0.0)

    def side_by_side(ref, rows):
        return jnp.concatenate([ref[pair, rows, :] for pair in range(pairs)], axis=1)

    def apart(ref, rows, value):
        for pair in range(pairs):
            ref[pair, rows, :] = value[:, pair * PAIR : (pair + 1) * PAIR]

    for copy in loads[:4]:
        copy.wait()
    for at, ref in enumerate((wo_ref, wcq_ref, wck_ref, wcv_ref, wco_ref)):
        whole_weight(ref, blocks_a, at * deep, deep)

    key_rows = dot(source_ref[...], wck_ref[...]).astype(bf16)
    every = pl.ds(0, few)
    apart(ck_ref, every, key_rows)
    for pair in range(pairs):
        ckt_ref[pair] = key_rows[:, pair * PAIR : (pair + 1) * PAIR].T
    apart(cv_ref, every, dot(source_ref[...], wcv_ref[...]).astype(bf16))

    def first_part(index):
        rows = pl.ds(index * size, size)
        after_self = x_ref[rows, :].astype(f32) + dot(side_by_side(mixed_ref, rows), wo_ref[...])
        after_self_s[rows, :] = after_self
        scaled, _ = normalize(after_self)
        hidden = (scaled * gain_two).astype(bf16)
        hidden_two_t[:, rows] = hidden.T
        apart(qc_s, rows, (dot(hidden, wcq_ref[...]) * (0.125 * LOG2E)).astype(bf16))

    repeat(0, rows_own // size, first_part, rows_own // size)

    def cross(index):
        pair, rows = index // 2, block_at(index % 2, half)
        mixed, extras = attend_pair(
            qc_s[pair, rows, :], ck_ref[pair], cextra_ref[...], cv_ref[pair],
            lax.broadcasted_iota(jnp.int32, (half, PAIR), 1),
        )
        cm_s[pair, rows, :] = mixed
        extra_s[2 * pair, rows, :] = extras[0]
        extra_s[2 * pair + 1, rows, :] = extras[1]

    repeat(0, 2 * pairs, cross, 4)
    for copy in loads[4:]:
        copy.wait()
    whole_weight(w1_ref, blocks_b, 0, deep, hidden_width // width)
    whole_weight(w2_ref, blocks_c, 0, hidden_width // 8)

    def second_part(index):
        rows = pl.ds(index * size, size)
        after_cross = after_self_s[rows, :] + dot(side_by_side(cm_s, rows), wco_ref[...])
        after_cross_s[rows, :] = after_cross
        scaled, _ = normalize(after_cross)
        hidden = (scaled * gain_three).astype(bf16)
        hidden_three_s[rows, :] = hidden
        hidden_three_t[:, rows] = hidden.T
        grad = (cotangent_ref[rows, :].astype(f32) * (counted(index) * loss_scale)).astype(bf16)
        grad_ffn_s[rows, :] = grad
        grad_ffn_t[:, rows] = grad.T

    repeat(0, rows_own // size, second_part, rows_own // size)

    everyone = [(at % 2, at // 2) for at in range(8)]
    deep_two = hidden_width // 8
    halves = [slice(index * size, (index + 1) * size) for index in range(rows_own // size)]

    def opened(part, rows):
        columns = slice(part * chunk, (part + 1) * chunk)
        return (
            dot(hidden_three_s[rows, :], w1_ref[:, columns]),
            dot_nt(grad_ffn_s[rows, :], w2_ref[columns, :]),
        )

    def bent(expanded, grad_active):
        square = expanded * expanded
        bend = jnp.tanh(expanded * (GELU_IN + (GELU_IN * GELU_CUBE) * square))
        rise = 0.5 + 0.5 * bend
        active = expanded * rise
        slope = rise + active * (1.0 - rise) * (
            2.0 * GELU_IN + (6.0 * GELU_IN * GELU_CUBE) * square
        )
        return active.astype(bf16), (grad_active * slope).astype(bf16)

    def closed(part, rows, active, grad_expanded):
        columns = slice(part * chunk, (part + 1) * chunk)
        final = dot(active, w2_ref[columns, :])
        hidden_grad = dot_nt(grad_expanded, w1_ref[:, columns])
        if part == 0:
            final_s[rows, :] = final
            hidden_grad_s[rows, :] = hidden_grad
        else:
            final_s[rows, :] += final
            hidden_grad_s[rows, :] += hidden_grad

    def weights_of(part, actives, grads):
        value = dot(hidden_three_t[...], jnp.concatenate(grads, axis=0))
        for at in range(chunk // PAIR):
            to_blocks(
                blocks_b, [part], everyone, at * deep, deep, value[:, at * PAIR : (at + 1) * PAIR]
            )
        value = dot(grad_ffn_t[...], jnp.concatenate(actives, axis=0))
        for at in range(chunk // PAIR):
            row = part * chunk + at * PAIR
            index = row // deep_two
            for column in range(pairs):
                blocks_c[
                    column, index % 2, index // 2, row % deep_two : row % deep_two + PAIR, :
                ] = value[column * PAIR : (column + 1) * PAIR, at * PAIR : (at + 1) * PAIR].astype(
                    bf16
                )

    units = [(part, rows) for part in range(hidden_width // chunk) for rows in halves]
    ahead = opened(*units[0])
    done = []
    for at, (part, rows) in enumerate(units):
        now = ahead
        if at + 1 < len(units):
            ahead = opened(*units[at + 1])
        active, grad_expanded = bent(*now)
        closed(part, rows, active, grad_expanded)
        done.append((active, grad_expanded))
        if len(done) == len(halves):
            weights_of(part, [one for one, _ in done], [other for _, other in done])
            done = []
    stores[4].start()
    stores[5].start()

    def third_part(index):
        rows = pl.ds(index * size, size)
        after_cross = after_cross_s[rows, :]
        weight = counted(index)
        grad_final = cotangent_ref[rows, :].astype(f32) * (weight * loss_scale)
        scaled, inverse = normalize(after_cross)
        back, gain_sum = norm_back(hidden_grad_s[rows, :], scaled, inverse, gain_three)
        dgain_ref[2:3, :] += gain_sum
        grad_ffn_s[rows, :] = ((after_cross + final_s[rows, :]) * weight).astype(bf16)
        grad_cross = grad_final + back
        final_s[rows, :] = grad_cross
        branch = grad_cross.astype(bf16)
        hidden_three_s[rows, :] = branch
        apart(gcm_s, rows, dot_nt(branch, wco_ref[...]).astype(bf16))

    repeat(0, rows_own // size, third_part, rows_own // size)
    stores[0].start()

    def cross_back(pair, _):
        def put(ref, factor):
            def keep(_, value):
                ref[pair] = (value * factor).astype(bf16)

            return keep

        extra = cextra_ref[...]
        query_grad = attend_pair_back(
            qc_s[pair],
            gcm_s[pair],
            cm_s[pair],
            [extra_s[2 * pair], extra_s[2 * pair + 1]],
            lambda _: jnp.concatenate([ck_ref[pair], extra], axis=1),
            lambda _: jnp.concatenate([cv_ref[pair], extra], axis=1),
            lambda _, head: ckt_ref[pair, 64 * head : 64 * head + 64, :],
            1,
            put(dck_ref, LN2),
            put(dcv_ref, 1.0),
        )
        dq_s[pair] = query_grad.T
        return 0

    lax.fori_loop(0, pairs, cross_back, 0)

    def last_part(index):
        rows = pl.ds(index * size, size)
        scaled, inverse = normalize(after_self_s[rows, :])
        upstream = dot_nt(side_by_side(dq_s, rows), wcq_ref[...])
        back, gain_sum = norm_back(upstream, scaled, inverse, gain_two)
        dgain_ref[1:2, :] += gain_sum
        grad_self = final_s[rows, :] + back
        final_s[rows, :] = grad_self
        branch = grad_self.astype(bf16)
        branch_s[rows, :] = branch
        apart(gcm_s, rows, dot_nt(branch, wo_ref[...]).astype(bf16))

    repeat(0, rows_own // size, last_part, rows_own // size)
    stores[1].start()
    stores[2].start()

    columns = range(pairs)
    both_sides = [(0, 0), (1, 0)]
    for pair in range(pairs):
        two = [(side, pair) for side, _ in both_sides]
        to_blocks(blocks_a, columns, two, 0, deep, dot(mixed_ref[pair].T, branch_s[...]))
        to_blocks(blocks_a, columns, two, 4 * deep, deep, dot(cm_s[pair].T, hidden_three_s[...]))
    all_rows = pl.ds(0, rows_own)
    to_blocks(
        blocks_a, columns, everyone, deep, deep, dot(hidden_two_t[...], side_by_side(dq_s, all_rows))
    )
    source_t = source_ref[...].T
    key_grad = side_by_side(dck_ref, every)
    value_grad = side_by_side(dcv_ref, every)
    to_blocks(blocks_a, columns, everyone, 2 * deep, deep, dot(source_t, key_grad))
    to_blocks(blocks_a, columns, everyone, 3 * deep, deep, dot(source_t, value_grad))
    stores[3].start()
    grad_source_ref[...] = (
        dot_nt(key_grad, wck_ref[...]) + dot_nt(value_grad, wcv_ref[...])
    ).astype(bf16)
    for copy in stores:
        copy.wait()


def last_kernel(comm, planes, source_len_ref, upsample_ref, *refs):
    (q_any, k_any, v_any, mixed_any, grad_any, extra_any) = refs[:6]
    (x_any, qkv_any, gain_any, grad_self_any, dgain_any) = refs[6:11]
    refs = refs[11:]
    if comm:
        (part_a, part_b, part_c, source_any, rows_any) = refs[:5]
        (rows_land, grad_out, cross_land, source_out, source_far) = refs[5:10]
        (*weight_outs, gain_out) = refs[10:21]
        refs = refs[21:]
    else:
        (own_out, other_out, part_out, gain_out) = refs[:4]
        refs = refs[4:]
    (
        q_s, k_s, v_s, mixed_s, grad_s, extra_s, x_s, qkv_s, gain_s, grad_self_s, dgain_s,
        keys_s, values_s, kt_s, hidden_s, total_s, dkv_s, dq_s, weight_s,
        part_s, load, send, receive,
    ) = refs[:23]
    refs = refs[23:]
    where = Where(planes)
    chip, core, side, plane = where.chip, where.core, where.side, where.plane
    total, width = x_s.shape
    own = total // 2
    rows = total // 4
    pairs = width // PAIR
    deep = width // 8
    chunk = 512
    semaphores = Semaphores(send, receive)
    sentence = where.group * 2 + chip
    length = source_len_ref[sentence] * upsample_ref[sentence]

    def turn_pair(turn):
        return where.column(pairs - 1 - turn)

    def turn_loads(turn):
        pair, slot = turn_pair(turn), turn % 2
        return [
            pltpu.make_async_copy(source.at[pair], target.at[slot], load.at[slot, at])
            for at, (source, target) in enumerate(
                (
                    (q_any, q_s),
                    (k_any, k_s),
                    (v_any, v_s),
                    (mixed_any, mixed_s),
                    (grad_any, grad_s),
                    (extra_any, extra_s),
                )
            )
        ]

    for copy in turn_loads(0):
        copy.start()
    common = [
        semaphores.local(source, target)
        for source, target in (
            (x_any, x_s),
            (qkv_any, qkv_s),
            (gain_any, gain_s),
            (dgain_any, dgain_s),
            (grad_self_any, grad_self_s),
        )
    ]
    for copy in common:
        copy.start()

    def begin(copies):
        for copy in copies:
            copy.start()

    def arrive(copies):
        for copy in copies:
            copy.wait_recv()

    if comm:
        (
            keep_a, keep_b, keep_c, core_a, core_b, core_c, far_a, far_b, far_c,
            near_a, near_b, near_c, planes_a, planes_b, planes_c,
            land_q, far_q, planes_q, gain_send, gain_land, gain_far, gain_planes, grads_send,
            grads_land, cross_send, stage, source_s, source_land, stage_s,
        ) = refs
        place, across = where.place, where.column(2)
        pieces = []
        for part, keep, land, far_land, near_land, land_planes, order in (
            (part_a, keep_a, core_a, far_a, near_a, planes_a, "yxz"),
            (part_b, keep_b, core_b, far_b, near_b, planes_b, "yxz"),
            (part_c, keep_c, core_c, far_c, near_c, planes_c, "xyz"),
        ):
            piece = dict(keep=keep, land=land, order=order)
            piece.update(far_land=far_land, near_land=near_land, planes=land_planes)
            piece["load"] = [
                semaphores.local(part.at[place], keep.at[0]),
                semaphores.local(part.at[across], keep.at[1]),
            ]
            piece["core"] = [
                semaphores.remote(part.at[where.column(1)], land.at[0], where.other_core),
                semaphores.remote(part.at[where.column(3)], land.at[1], where.other_core),
            ]
            if order[0] == "y":
                piece["far"] = [
                    semaphores.remote(keep.at[at, 1 - side], far_land.at[at], where.other_side)
                    for at in (0, 1)
                ]
            else:
                piece["far"] = [
                    semaphores.remote(keep.at[1, at], far_land.at[at], where.other_chip)
                    for at in (0, 1)
                ]
            if order == "yxz":
                near = (keep.at[1, side], near_land, where.other_chip)
            else:
                near = (keep.at[0, 1 - side], near_land, where.other_side)
            piece["near"] = [semaphores.remote(*near)]
            piece["last"] = [
                semaphores.remote(
                    keep.at[0, side, (plane + step) % planes],
                    land_planes.at[step - 1],
                    where.other_planes[step - 1],
                )
                for step in range(1, planes)
            ]
            pieces.append(piece)
        a, b, c = pieces
        owners = (where.diagonal, where.other_chip, where.other_core)
        hops = (where.other_core, where.other_chip, where.other_core)
        send_q = [
            semaphores.remote(part_s.at[turn], land_q.at[turn], hops[turn]) for turn in range(3)
        ]
        side_q = semaphores.remote(part_s.at[3, 1 - side], far_q, where.other_side)
        plane_q = [
            semaphores.remote(
                part_s.at[3, side, (plane + step) % planes],
                planes_q.at[step - 1],
                where.other_planes[step - 1],
            )
            for step in range(1, planes)
        ]
        gain_group = [
            semaphores.remote(gain_send.at[where.column(3 - turn)], gain_land.at[turn], owners[turn])
            for turn in range(3)
        ]
        gain_side = semaphores.remote(gain_land.at[3], gain_far, where.other_side)
        gain_last = [
            semaphores.remote(
                gain_planes.at[plane], gain_planes.at[plane], where.other_planes[step - 1]
            )
            for step in range(1, planes)
        ]
        rows_cross = semaphores.remote(rows_any.at[rows:], rows_land, where.other_chip)
        few = source_any.shape[0] // 4
        source_local = semaphores.local(source_any.at[: 2 * few], source_s)
        source_core = semaphores.remote(source_any.at[2 * few :], source_land, where.other_core)
        source_cross = semaphores.remote(source_s.at[few:], source_far, where.other_chip)
        grads_core = [
            semaphores.remote(grads_send.at[at], grads_land.at[at], where.other_core)
            for at in range(2)
        ]
        grads_cross = [
            semaphores.remote(cross_send.at[at], cross_land.at[at], where.other_chip)
            for at in range(rows // BLOCK)
        ]
        stage_out = semaphores.local(stage, grad_out)
        source_own = semaphores.local(stage_s, source_out)
        for piece in pieces:
            begin(piece["load"])
        begin([source_local])
        greet(where.everyone())

        def add_in(ref, land):
            def add(at, _):
                ref[at] = (ref[at].astype(f32) + land[at].astype(f32)).astype(bf16)
                return 0

            lax.fori_loop(0, planes, add, 0)

        def add_core(piece):
            for copy in piece["load"]:
                copy.wait()
            arrive(piece["core"])
            for at in (0, 1):
                for half in (0, 1):
                    add_in(piece["keep"].at[at, half], piece["land"].at[at, half])
            begin(piece["far"])

        def add_far(piece):
            arrive(piece["far"])
            for at in (0, 1):
                if piece["order"][0] == "y":
                    add_in(piece["keep"].at[at, side], piece["far_land"].at[at])
                else:
                    add_in(piece["keep"].at[0, at], piece["far_land"].at[at])
            begin(piece["near"])

        def add_near(piece):
            arrive(piece["near"])
            add_in(piece["keep"].at[0, side], piece["near_land"])
            begin(piece["last"])

        def finish(piece):
            arrive(piece["last"])
            value = piece["keep"][0, side, plane].astype(f32)
            for step in range(planes - 1):
                value = value + piece["planes"][step].astype(f32)
            return value

    mask_columns(chip, core, rows, total, BLOCK, length, values_s.at[:, PAIR:])
    keys_s[:, PAIR:] = values_s[:, PAIR:]
    for copy in common:
        copy.wait()
    gain = jnp.concatenate([gain_s[at, 0:1, :] for at in range(pairs)], axis=1)

    def hide(index):
        at = block_at(index, BLOCK)
        scaled, _ = normalize(x_s[at, :].astype(f32))
        hidden_s[:, at] = (scaled * gain).astype(bf16).T

    repeat(0, total // BLOCK, hide, 4)
    if comm:
        await_greetings(where.everyone())
        for piece in pieces:
            begin(piece["core"])
        begin([source_core, rows_cross])

    def take_weights(turn, pair):
        for part in range(3):
            for at in range(8):
                weight_s[turn, at * 64 : at * 64 + 64, part * PAIR : (part + 1) * PAIR] = qkv_s[
                    pair, at % 2, at // 2, part * 64 : part * 64 + 64, :
                ]

    def upstream(turns, at, own_rows):
        value = None
        for turn in turns:
            term = dot_nt(dkv_s[turn, at, :], weight_s[turn, :, PAIR:])
            if own_rows:
                term = term + dot_nt(dq_s[turn, at, :], weight_s[turn, :, :PAIR])
            value = term if value is None else value + term
        return value

    def comm_steps(index):
        if not comm:
            return

        @pl.when(index == 1)
        def _():
            add_core(a)
            add_core(c)
            add_core(b)
            source_local.wait()
            arrive([source_core])
            for half in range(2):
                r = slice(half * few, (half + 1) * few)
                value = source_s[r, :].astype(f32) + source_land[r, :].astype(f32)
                source_s[r, :] = value.astype(bf16)
                if half == 0:
                    stage_s[...] = value
            begin([source_cross, source_own])

        @pl.when(index == 3)
        def _():
            add_far(a)
            add_far(c)

        @pl.when(index == 4)
        def _():
            arrive([send_q[0]])
            for half in range(2):
                add_in(part_s.at[1, half], land_q.at[0, half])
            send_q[1].start()

        @pl.when(index == 5)
        def _():
            add_far(b)
            add_near(a)

        @pl.when(index == 6)
        def _():
            add_near(c)

        @pl.when(index == 7)
        def _():
            add_near(b)


    def step(turn, _):
        pair, slot = turn_pair(turn), turn % 2
        for copy in turn_loads(turn):
            copy.wait()

        @pl.when(turn + 1 < pairs)
        def _():
            for copy in turn_loads(turn + 1):
                copy.start()

        keys_s[:, :PAIR] = k_s[slot]
        values_s[:, :PAIR] = v_s[slot]
        kt_s[...] = k_s[slot].T
        take_weights(turn, pair)
        comm_steps(2 * turn)

        def part(ref):
            return lambda part: ref[part * chunk : (part + 1) * chunk, :]

        def put(at, factor):
            def keep(part, value):
                dkv_s[turn, part * chunk : (part + 1) * chunk, at : at + PAIR] = (
                    value * factor
                ).astype(bf16)

            return keep

        query_grad = attend_pair_back(
            q_s[slot],
            grad_s[slot],
            mixed_s[slot],
            [extra_s[slot, head] for head in (0, 1)],
            part(keys_s),
            part(values_s),
            lambda part, head: kt_s[64 * head : 64 * head + 64, part * chunk : (part + 1) * chunk],
            total // chunk,
            put(0, LN2),
            put(PAIR, 1.0),
        )
        dq_s[turn] = query_grad.T
        comm_steps(2 * turn + 1)
        both = dot(hidden_s[...], dkv_s[turn]).astype(bf16)
        query = dot(hidden_s[:, :own], dq_s[turn]).astype(bf16)
        for at in range(8):
            r = slice(at * deep, (at + 1) * deep)
            for part_at, value in enumerate((query[r, :], both[r, :PAIR], both[r, PAIR:])):
                part_s[turn, at % 2, at // 2, part_at * deep : (part_at + 1) * deep, :] = value

        if comm:
            for sent in (0, 2):

                @pl.when(turn == sent)
                def _():
                    send_q[sent].start()

        @pl.when(turn == pairs - 2)
        def _():
            size = 2 * BLOCK
            for row in range(total // size):
                r = pl.ds(row * size, size)
                total_s[r, :] = upstream(range(pairs - 1), r, row * size < own)

        return 0

    lax.fori_loop(0, pairs, step, 0)

    def row_back(row, own_rows):
        r = block_at(row, BLOCK)
        scaled, inverse = normalize(x_s[r, :].astype(f32))
        value = total_s[r, :] + upstream([pairs - 1], r, own_rows)
        back, gain_sum = norm_back(value, scaled, inverse, gain)
        dgain_s[0:1, :] += gain_sum
        return r, back

    per = rows // BLOCK
    if not comm:

        def own_step(row):
            r, back = row_back(row, True)
            grad_self_s[r, :] += back

        def other_step(row):
            r, back = row_back(row, False)
            total_s[r, :] = back

        repeat(0, 2 * per, own_step, per)
        repeat(2 * per, 4 * per, other_step, per)
        own_out[...] = grad_self_s[...]
        other_out[...] = total_s[own:, :].astype(bf16)
        for turn in range(pairs):
            part_out[turn_pair(turn)] = part_s[turn]
        gain_out[...] = dgain_s[...]
        return

    def add_q(at, _):
        for half in range(2):
            value = part_s[3, half, at].astype(f32)
            for turn in (1, 2):
                value = value + land_q[turn, half, at].astype(f32)
            part_s[3, half, at] = value.astype(bf16)
        return 0

    def other_rows(slot):
        def other_step(row):
            _, back = row_back(slot * per + row, False)
            grads_send[slot - 2, pl.ds(row * BLOCK, BLOCK), :] = back.astype(bf16)

        repeat(0, per, other_step, per)
        grads_core[slot - 2].start()

    def own_rows(row):
        r, back = row_back(row, True)
        total_s[r, :] = back + grad_self_s[r, :]

    def cross(row):
        r = slice(row * BLOCK, (row + 1) * BLOCK)
        value = total_s[rows + row * BLOCK : rows + (row + 1) * BLOCK, :]
        cross_send[row] = (value + grads_land[1, r, :].astype(f32)).astype(bf16)
        grads_cross[row].start()

    arrive(send_q[1:])
    lax.fori_loop(0, planes, add_q, 0)
    side_q.start()
    other_rows(3)
    repeat(per, 2 * per, own_rows, per)
    arrive([grads_core[1]])
    cross(0)
    other_rows(2)
    arrive([side_q])
    add_in(part_s.at[3, side], far_q)
    begin(plane_q)
    repeat(0, per, own_rows, per)
    for at in range(pairs):
        gain_send[at] = dgain_s[:, at * PAIR : (at + 1) * PAIR]
    begin(gain_group)
    for row in range(1, per):
        cross(row)
    arrive(gain_group)
    gain_land[3] = gain_send[place] + gain_land[0] + gain_land[1] + gain_land[2]
    gain_side.start()
    arrive([grads_core[0]])
    stage[...] = total_s[:rows, :] + grads_land[0].astype(f32)
    stage_out.start()
    sums = [finish(piece) for piece in pieces]
    for at in range(5):
        weight_outs[3 + at][...] = sums[0][at * deep : (at + 1) * deep, :]
    for at in range(sums[1].shape[0] // deep):
        weight_outs[8][:, at * PAIR : (at + 1) * PAIR] = sums[1][at * deep : (at + 1) * deep, :]
    for at in range(sums[2].shape[0] // PAIR):
        r = slice(at * PAIR, (at + 1) * PAIR)
        weight_outs[9][r, :] = sums[2][r, :].T
    arrive([gain_side])
    gain_planes[plane] = gain_land[3] + gain_far[...]
    begin(gain_last)
    arrive(plane_q)
    value = part_s[3, side, plane].astype(f32)
    for at in range(planes - 1):
        value = value + planes_q[at].astype(f32)
    for at in range(3):
        weight_outs[at][...] = value[at * deep : (at + 1) * deep, :]
    arrive(gain_last)
    value = gain_planes[0]
    for at in range(1, planes):
        value = value + gain_planes[at]
    gain_out[...] = value
    arrive([rows_cross, source_cross, *grads_cross])
    for copy in (stage_out, source_own):
        copy.wait()
    for copy in semaphores.sent:
        copy.wait_send()


def hand_over_kernel(planes, *refs):
    (rows_any, rows_far, grad_own, grad_far, source_own, source_far, *plain) = refs[:17]
    (decoder_out, grad_out, source_out, *plain_outs) = refs[17:31]
    (rows_s, grad_s, grad_low, source_s, source_low, *plain_s) = refs[31:-2]
    load, store = refs[-2:]
    chip = Where(planes).chip
    rows = rows_s.shape[1]
    moves = [
        (rows_any.at[:rows], rows_s.at[0], rows_s.at[0], decoder_out.at[chip]),
        (rows_far, rows_s.at[1], rows_s.at[1], decoder_out.at[1 - chip]),
        (grad_own, grad_s.at[0], grad_s.at[0], grad_out.at[chip]),
        (grad_far, grad_low, grad_s.at[1], grad_out.at[1 - chip]),
        (source_own, source_s.at[0], source_s.at[0], source_out.at[chip]),
        (source_far, source_low, source_s.at[1], source_out.at[1 - chip]),
    ]
    moves += [
        (one, held, held.at[: other.shape[0]], other)
        for one, held, other in zip(plain, plain_s, plain_outs)
    ]
    loads = [pltpu.make_async_copy(m[0], m[1], load.at[at]) for at, m in enumerate(moves)]
    stores = [pltpu.make_async_copy(m[2], m[3], store.at[at]) for at, m in enumerate(moves)]
    for copy in loads:
        copy.start()
    for at, (one, other) in enumerate(zip(loads, stores)):
        one.wait()
        if at == 3:
            for row in range(grad_low.shape[0]):
                size = grad_low.shape[1]
                grad_s[1, row * size : (row + 1) * size, :] = grad_low[row].astype(f32)
        if at == 5:
            source_s[1] = source_low[...].astype(f32)
        other.start()
    for copy in stores:
        copy.wait()


def call(kernel, outs, *operands, scratch=(), smem=0, params=PARAMS, spaces=None, out_space=VMEM, out_spaces=None):
    spaces = spaces or {}
    out_spaces = out_spaces or {}
    return pl.pallas_call(
        kernel,
        out_shape=[jax.ShapeDtypeStruct(shape, kind) for shape, kind in outs],
        in_specs=[
            pl.BlockSpec(memory_space=pltpu.SMEM if at < smem else spaces.get(at, VMEM))
            for at in range(len(operands))
        ],
        out_specs=[
            pl.BlockSpec(memory_space=out_spaces.get(at, out_space)) for at in range(len(outs))
        ],
        scratch_shapes=list(scratch),
        compiler_params=params,
    )(*operands)


def swapped(value, axis, bit):
    pairs = [(source, source ^ bit) for source in range(lax.axis_size(axis))]
    return lax.ppermute(value, axis, pairs)


def as_blocks(weight, chunks=1):
    height, width = weight.shape
    deep = height // 8
    cut = weight.reshape(4, 2, deep, 4, chunks, PAIR).transpose(3, 1, 0, 4, 2, 5)
    return cut.reshape(4, 2, 4, chunks * deep, PAIR)


def from_blocks(blocks, chunks=1):
    height = blocks.shape[3] // chunks
    cut = blocks.reshape(4, 2, 4, chunks, height, PAIR).transpose(2, 1, 4, 0, 3, 5)
    return cut.reshape(8 * height, 4 * chunks * PAIR)


def gather_plain(arguments, seq_size, dp_size):
    (decoder_in, source_states, out_grad, narrow, ffn_expand, ffn_reduce, norm_gains) = arguments
    chip = lax.axis_index("seq") // 2
    rows_dec = decoder_in.shape[1]
    own = 2 * rows_dec
    outgoing = jnp.concatenate([decoder_in[1 - chip], source_states[1 - chip]], axis=0)
    arrived = swapped(outgoing, "seq", 2)
    own_rows = jnp.concatenate(
        [decoder_in[chip], arrived[:rows_dec], source_states[chip], arrived[rows_dec:]], axis=0
    )
    other_rows = swapped(own_rows, "seq", 1)
    x_all = jnp.concatenate([own_rows[:own], other_rows[:own]], axis=0)
    source_all = jnp.concatenate([own_rows[own:], other_rows[own:]], axis=0)
    cotangent = swapped(out_grad[1 - chip], "seq", 2)

    def whole(weight):
        weight = lax.all_gather(weight, "seq", axis=1, tiled=True)
        return lax.all_gather(weight, "dp", axis=0, tiled=True)

    blocks = [as_blocks(whole(weight)) for weight in narrow]
    qkv = jnp.concatenate(blocks[:3], axis=3)
    later_a = jnp.concatenate(blocks[3:], axis=3)
    later_b = as_blocks(whole(ffn_expand), ffn_expand.shape[1] // PAIR)
    later_c = as_blocks(whole(ffn_reduce))
    gain_block = jnp.pad(norm_gains.astype(f32), ((0, 5), (0, 0)))
    gains = lax.all_gather(gain_block, "seq", axis=0)
    return x_all, source_all, cotangent, qkv, later_a, later_b, later_c, gains


def body(
    decoder_in,
    source_states,
    source_len,
    upsample,
    send_counts,
    self_query,
    self_key,
    self_value,
    self_output,
    cross_query,
    cross_key,
    cross_value,
    cross_output,
    ffn_expand,
    ffn_reduce,
    norm_gains,
    out_grad,
):
    seq_size = lax.axis_size("seq")
    dp_size = lax.axis_size("dp")
    planes = dp_size // 2
    place = lax.axis_index("seq")
    chip = place // 2
    home_count, rows_dec, width = decoder_in.shape
    rows_src = source_states.shape[1]
    pairs = width // PAIR
    own = 2 * rows_dec
    total = 4 * rows_dec
    deep = self_query.shape[0]
    deep_two = ffn_reduce.shape[0]
    wide = ffn_expand.shape[1] // PAIR
    hidden_width = wide * PAIR * seq_size
    all_src = 4 * rows_src
    comm = dp_size == 8

    def pair_rows(rows):
        return (pairs, rows, PAIR)

    narrow = (self_query, self_key, self_value, self_output)
    narrow += (cross_query, cross_key, cross_value, cross_output)
    rows_outs = [
        (pair_rows(own), bf16),
        (pair_rows(total), bf16),
        (pair_rows(total), bf16),
        (pair_rows(own), bf16),
        ((pairs, 2, own, PAIR), bf16),
    ]
    buffers = [VMEM(shape, kind) for shape, kind in rows_outs]
    work = [
        VMEM((total, width), bf16),
        VMEM((width, 3 * PAIR), bf16),
        VMEM((total, PAIR), bf16),
        *buffers,
    ]
    semaphores = [pltpu.SemaphoreType.DMA((96,)), pltpu.SemaphoreType.DMA((96,))]
    if comm:
        cut = (seq_size, 2, planes)
        gathered = [
            ((total, width), bf16),
            ((all_src, width), bf16),
            ((rows_dec, width), bf16),
            (cut + (3 * deep, PAIR), bf16),
            (cut + (5 * deep, PAIR), bf16),
            (cut + (wide * deep, PAIR), bf16),
            (cut + (deep_two, PAIR), bf16),
            ((seq_size, 8, PAIR), f32),
        ]
        operands = (source_len, upsample, decoder_in, source_states, out_grad)
        operands += (*narrow, ffn_expand, ffn_reduce, norm_gains)
        (
            x_all, source_all, cotangent, qkv, later_a, later_b, later_c, gains,
            q, k, v, mixed, query_extra,
        ) = call(
            partial(open_kernel, True, planes, deep),
            gathered + rows_outs,
            *operands,
            scratch=[
                VMEM((total, width), bf16),
                VMEM(cut + (3 * deep, PAIR), bf16),
                VMEM((seq_size, 8, PAIR), f32),
                *work,
                *semaphores,
                VMEM((5 * deep, PAIR), bf16),
                VMEM((wide * deep, PAIR), bf16),
                VMEM((deep_two, PAIR), bf16),
                VMEM((rows_src, width), bf16),
                VMEM((8, PAIR), f32),
            ],
            smem=2,
            spaces={at: pl.ANY for at in range(2, len(operands) - 1)},
            out_space=pl.ANY,
            params=pltpu.CompilerParams(
                vmem_limit_bytes=VMEM_LIMIT, collective_id=0, has_side_effects=True
            ),
        )
    else:
        x_all, source_all, cotangent, qkv, later_a, later_b, later_c, gains = gather_plain(
            (decoder_in, source_states, out_grad, narrow, ffn_expand, ffn_reduce, norm_gains),
            seq_size,
            dp_size,
        )
        q, k, v, mixed, query_extra = call(
            partial(open_kernel, False, planes, deep),
            rows_outs,
            source_len,
            upsample,
            x_all,
            qkv,
            gains,
            scratch=[*work, *semaphores],
            smem=2,
            out_space=pl.ANY,
        )
    parts = [
        ((seq_size, 2, 4, 5 * width // 8, PAIR), bf16),
        ((seq_size, 2, 4, hidden_width // 8, PAIR), bf16),
        ((seq_size, 2, 4, hidden_width // 8, PAIR), bf16),
    ]
    out_rows, grad_mixed, grad_self, part_a, part_b, part_c, grad_source, dgain = call(
        partial(middle_kernel, planes),
        [
            ((own, width), bf16),
            (pair_rows(own), bf16),
            ((own, width), f32),
            *parts,
            ((all_src, width), bf16),
            ((8, width), f32),
        ],
        source_len,
        upsample,
        send_counts,
        x_all,
        mixed,
        out_grad,
        cotangent,
        source_all,
        later_a,
        later_b,
        later_c,
        gains,
        scratch=[
            VMEM((own, width), bf16),
            VMEM(pair_rows(own), bf16),
            VMEM((own, width), bf16),
            VMEM((all_src, width), bf16),
            *[VMEM(*part) for part in parts],
            *[VMEM((width, width), bf16)] * 5,
            VMEM((width, hidden_width), bf16),
            VMEM((hidden_width, width), bf16),
            VMEM(pair_rows(all_src), bf16),
            VMEM(pair_rows(all_src), bf16),
            VMEM((pairs, PAIR, all_src), bf16),
            VMEM((all_src, PAIR), bf16),
            *[VMEM(pair_rows(all_src), bf16)] * 2,
            *[VMEM((own, width), f32)] * 4,
            *[VMEM(pair_rows(own), bf16)] * 4,
            VMEM((2 * pairs, own, PAIR), bf16),
            VMEM((width, own), bf16),
            VMEM((own, width), bf16),
            VMEM((width, own), bf16),
            VMEM((own, width), bf16),
            VMEM((width, own), bf16),
            VMEM((own, width), bf16),
            pltpu.SemaphoreType.DMA((8,)),
            pltpu.SemaphoreType.DMA((6,)),
        ],
        smem=3,
        spaces={at: pl.ANY for at in range(3, 11)},
        out_spaces={at: pl.ANY for at in range(6)},
    )
    part_q = ((seq_size, 2, 4, 3 * width // 8, PAIR), bf16)
    operands = (source_len, upsample, q, k, v, mixed, grad_mixed, query_extra)
    operands += (x_all, qkv, gains, grad_self, dgain)
    work = [
        VMEM((2, own, PAIR), bf16),
        VMEM((2, total, PAIR), bf16),
        VMEM((2, total, PAIR), bf16),
        VMEM((2, own, PAIR), bf16),
        VMEM((2, own, PAIR), bf16),
        VMEM((2, 2, own, PAIR), bf16),
        VMEM((total, width), bf16),
        VMEM(qkv.shape, bf16),
        VMEM(gains.shape, f32),
        VMEM((own, width), f32),
        VMEM((8, width), f32),
        VMEM((total, 2 * PAIR), bf16),
        VMEM((total, 2 * PAIR), bf16),
        VMEM((PAIR, total), bf16),
        VMEM((width, total), bf16),
        VMEM((total, width), f32),
        VMEM((pairs, total, 2 * PAIR), bf16),
        VMEM((pairs, own, PAIR), bf16),
        VMEM((pairs, width, 3 * PAIR), bf16),
        VMEM(*part_q),
        pltpu.SemaphoreType.DMA((2, 6)),
        *semaphores,
    ]
    everywhere = {at: pl.ANY for at in range(2, 18)}
    if comm:
        heights = [shape[3] for shape, _ in parts]

        def per_piece(lead):
            return [VMEM((*lead, height, PAIR), bf16) for height in heights]

        work += [
            *per_piece((2, 2, planes)),
            *per_piece((2, 2, planes)),
            *per_piece((2, planes)),
            *per_piece((planes,)),
            *per_piece((planes - 1,)),
            VMEM((3, 2, planes, 3 * deep, PAIR), bf16),
            VMEM((planes, 3 * deep, PAIR), bf16),
            VMEM((planes - 1, 3 * deep, PAIR), bf16),
            VMEM((pairs, 8, PAIR), f32),
            VMEM((4, 8, PAIR), f32),
            VMEM((8, PAIR), f32),
            VMEM((planes, 8, PAIR), f32),
            VMEM((2, rows_dec, width), bf16),
            VMEM((2, rows_dec, width), bf16),
            VMEM((rows_dec // BLOCK, BLOCK, width), bf16),
            VMEM((rows_dec, width), f32),
            VMEM((2 * rows_src, width), bf16),
            VMEM((2 * rows_src, width), bf16),
            VMEM((rows_src, width), f32),
        ]
        small = ((deep, PAIR), f32)
        plain = [small] * 8 + [(ffn_expand.shape, f32), (ffn_reduce.shape, f32), ((8, PAIR), f32)]
        outs = call(
            partial(last_kernel, True, planes),
            [
                ((rows_dec, width), bf16),
                ((rows_dec, width), f32),
                ((rows_dec // BLOCK, BLOCK, width), bf16),
                ((rows_src, width), f32),
                ((rows_src, width), bf16),
                *plain,
            ],
            *operands,
            part_a,
            part_b,
            part_c,
            grad_source,
            out_rows,
            scratch=work,
            smem=2,
            spaces=everywhere,
            out_spaces={at: pl.ANY for at in range(5)},
            params=pltpu.CompilerParams(
                vmem_limit_bytes=VMEM_LIMIT, collective_id=1, has_side_effects=True
            ),
        )
        outs = call(
            partial(hand_over_kernel, planes),
            [
                (decoder_in.shape, bf16),
                (decoder_in.shape, f32),
                (source_states.shape, f32),
                *plain[:-1],
                (norm_gains.shape, f32),
            ],
            out_rows,
            *outs,
            scratch=[
                VMEM(decoder_in.shape, bf16),
                VMEM(decoder_in.shape, f32),
                VMEM((rows_dec // BLOCK, BLOCK, width), bf16),
                VMEM(source_states.shape, f32),
                VMEM((rows_src, width), bf16),
                *[VMEM(shape, kind) for shape, kind in plain],
                *[pltpu.SemaphoreType.DMA((17,))] * 2,
            ],
            spaces={at: pl.ANY for at in range(17)},
            out_space=pl.ANY,
        )
        (decoder_out, grad_decoder, grad_src, dwq, dwk, dwv, *rest, dw1, dw2, dgains) = outs
        dwo, dwcq, dwck, dwcv, dwco = rest
    else:
        own_grad, other_grad, part_qkv, dgains = call(
            partial(last_kernel, False, planes),
            [((own, width), f32), ((own, width), bf16), part_q, ((8, width), f32)],
            *operands,
            scratch=work,
            smem=2,
            spaces=everywhere,
        )
        crossing = jnp.concatenate([other_grad, grad_source[2 * rows_src :]], axis=0)
        returned = swapped(crossing, "seq", 1).astype(f32)
        grad_rows = own_grad + returned[:own]
        source_rows = grad_source[: 2 * rows_src].astype(f32) + returned[own:]
        homeward = [grad_rows[rows_dec:].astype(bf16), source_rows[rows_src:].astype(bf16)]
        came = swapped(jnp.concatenate([out_rows[rows_dec:], *homeward], axis=0), "seq", 2)

        def both_sentences(mine, theirs):
            theirs = theirs.astype(mine.dtype)
            return jnp.where(chip == 0, jnp.stack([mine, theirs]), jnp.stack([theirs, mine]))

        decoder_out = both_sentences(out_rows[:rows_dec], came[:rows_dec])
        grad_decoder = both_sentences(grad_rows[:rows_dec], came[rows_dec : 2 * rows_dec])
        grad_src = both_sentences(source_rows[:rows_src], came[2 * rows_dec :])

        def summed(blocks, start, count, chunks=1):
            grad = from_blocks(blocks[:, :, :, start : start + chunks * count], chunks)
            grad = lax.psum_scatter(grad.astype(f32), "dp", scatter_dimension=0, tiled=True)
            return lax.psum_scatter(grad, "seq", scatter_dimension=1, tiled=True)

        step = width // 8
        dwq, dwk, dwv = [summed(part_qkv, at * step, step) for at in range(3)]
        dwo, dwcq, dwck, dwcv, dwco = [summed(part_a, at * step, step) for at in range(5)]
        dw1 = summed(part_b, 0, step, hidden_width // width)
        tall = part_c.reshape(seq_size, 2, 4, hidden_width // 8 // PAIR, PAIR, PAIR)
        dw2 = summed(tall.swapaxes(4, 5).reshape(part_c.shape), 0, hidden_width // 8)
        dgains = lax.psum(dgains, "dp")
        dgains = lax.psum_scatter(dgains, "seq", scatter_dimension=1, tiled=True)
    return (
        decoder_out,
        grad_decoder,
        grad_src,
        dwq,
        dwk,
        dwv,
        dwo,
        dwcq,
        dwck,
        dwcv,
        dwco,
        dw1,
        dw2,
        dgains[:3],
    )


def solution(mesh):
    rows = P("dp", "seq", None)
    weight = P("dp", "seq")
    placed = (rows, rows, P(), P(), P()) + (weight,) * 10 + (P(None, "seq"), rows)
    return jax.shard_map(
        body,
        mesh=mesh,
        in_specs=placed,
        out_specs=(rows, rows, rows) + (weight,) * 10 + (P(None, "seq"),),
        check_vma=False,
    )
```

```python
from functools import partial

import jax
import jax.numpy as jnp
from jax import lax
from jax.experimental import pallas as pl
from jax.experimental.pallas import tpu as pltpu
from jax.sharding import PartitionSpec as P

HEADS = 8
EPSILON = 1e-05
NEGATIVE = -1000000000.0
LOG2E = 1.4426950408889634
LN2 = 0.6931471805599453
GELU_IN = 0.7978845608028654
GELU_CUBE = 0.044715
BLOCK = 256
PAIR = 128

bf16 = jnp.bfloat16
f32 = jnp.float32
VMEM = pltpu.VMEM
VMEM_LIMIT = 60 * 1024 * 1024
PARAMS = pltpu.CompilerParams(vmem_limit_bytes=VMEM_LIMIT)


def dot(left, right):
    return jnp.dot(left, right, preferred_element_type=f32)


def dot_nt(left, right):
    return lax.dot_general(left, right, (((1,), (1,)), ((), ())), preferred_element_type=f32)


def block_at(index, size):
    return pl.ds(pl.multiple_of(index * size, size), size)


def repeat(start, stop, todo, group):
    def step(at, _):
        for part in range(group):
            todo(start + at * group + part)
        return 0

    count, rest = divmod(stop - start, group)
    if count == 1:
        step(0, 0)
    elif count:
        lax.fori_loop(0, count, step, 0)
    for part in range(rest):
        todo(start + count * group + part)


def row_mean(values):
    return jnp.mean(values, axis=-1, keepdims=True)


def normalize(values):
    centred = values - row_mean(values)
    inverse = lax.rsqrt(row_mean(centred * centred) + EPSILON)
    return centred * inverse, inverse


def norm_back(upstream, scaled, inverse, gain):
    inner = upstream * gain
    back = inverse * (inner - row_mean(inner) - scaled * row_mean(inner * scaled))
    return back, jnp.sum(upstream * scaled, axis=0, keepdims=True)


def three_parts(column, lane, last):
    high = column.astype(bf16).astype(f32)
    middle = (column - high).astype(bf16).astype(f32)
    low = column - high - middle
    rest = jnp.where(lane == 3, last, 0.0)
    return jnp.where(
        lane == 0, high, jnp.where(lane == 1, middle, jnp.where(lane == 2, low, rest))
    ).astype(bf16)


def one_head(values, first, head):
    zero = jnp.zeros_like(values)
    return jnp.where(first, values, zero) if head == 0 else jnp.where(first, zero, values)


def attend_pair(query, keys, key_extra, values, lane):
    first = lane < 64
    ones = jnp.where(lane == 3, 1.0, 0.0).astype(bf16)
    keys = jnp.concatenate([keys, key_extra], axis=1)
    values = jnp.concatenate([values, jnp.ones_like(values)], axis=1)
    scores = [
        dot_nt(jnp.concatenate([one_head(query, first, head), ones], axis=1), keys)
        for head in (0, 1)
    ]
    mixed, extras = [], []
    for head in (0, 1):
        peak = jnp.max(scores[head], axis=1, keepdims=True)
        exps = jnp.exp2(scores[head] - peak)
        both = dot(exps.astype(bf16), values)
        total = both[:, PAIR : PAIR + 1]
        mixed.append(both[:, :PAIR] * (1.0 / total))
        extras.append(three_parts(-(peak + jnp.log2(total)), lane, 1.0))
    return jnp.where(first, mixed[0], mixed[1]).astype(bf16), extras


def attend_pair_back(
    query, grad, mixed, query_extra, key_at, value_at, key_columns_at, chunks, put_key, put_value
):
    lane = lax.broadcasted_iota(jnp.int32, query.shape, 1)
    first = lane < 64
    product = grad.astype(f32) * mixed.astype(f32)
    queries = [one_head(query, first, head) for head in (0, 1)]
    grads = [one_head(grad, first, head) for head in (0, 1)]
    long_queries = [jnp.concatenate([queries[h], query_extra[h]], axis=1) for h in (0, 1)]
    long_grads = []
    for head in (0, 1):
        delta = jnp.sum(one_head(product, first, head), axis=1, keepdims=True)
        long_grads.append(
            jnp.concatenate([grads[head], three_parts(-delta, lane, 0.0)], axis=1)
        )
    both_queries = jnp.concatenate(queries, axis=0)
    both_grads = jnp.concatenate(grads, axis=0)
    query_grads = [None, None]
    for chunk in range(chunks):
        keys, values = key_at(chunk), value_at(chunk)
        probs, score_grads = [], []
        for head in (0, 1):
            prob = jnp.exp2(dot_nt(keys, long_queries[head]))
            score_grad = (prob * dot_nt(values, long_grads[head])).astype(bf16)
            probs.append(prob.astype(bf16))
            score_grads.append(score_grad)
            term = dot(key_columns_at(chunk, head), score_grad)
            query_grads[head] = term if chunk == 0 else query_grads[head] + term
        put_value(chunk, dot(jnp.concatenate(probs, axis=1), both_grads))
        put_key(chunk, dot(jnp.concatenate(score_grads, axis=1), both_queries))
    return (jnp.concatenate(query_grads, axis=0) * 0.125).astype(bf16)


def copy_to(source, target, send, receive, partner):
    return pltpu.make_async_remote_copy(
        src_ref=source,
        dst_ref=target,
        send_sem=send,
        recv_sem=receive,
        device_id=partner,
        device_id_type=pl.DeviceIdType.MESH,
    )


def greet(partners):
    for partner in partners:
        pl.semaphore_signal(
            pltpu.get_barrier_semaphore(),
            inc=1,
            device_id=partner,
            device_id_type=pl.DeviceIdType.MESH,
        )


def await_greetings(partners):
    pl.semaphore_wait(pltpu.get_barrier_semaphore(), len(partners))


class Where:
    def __init__(self, planes):
        group, self.place = lax.axis_index("dp"), lax.axis_index("seq")
        self.group = group
        self.chip, self.core = self.place // 2, self.place % 2
        self.plane, self.side = group // 2, group % 2
        self.planes = planes
        self.other_core = self.at(self.chip, 1 - self.core)
        self.other_chip = self.at(1 - self.chip, self.core)
        self.diagonal = self.at(1 - self.chip, 1 - self.core)
        self.other_side = {"dp": self.plane * 2 + 1 - self.side}
        self.other_planes = [
            {"dp": (self.plane + step) % planes * 2 + self.side} for step in range(1, planes)
        ]

    def at(self, chip, core):
        return {"seq": chip * 2 + core}

    def column(self, step):
        return (self.chip + step // 2) % 2 * 2 + (self.core + step % 2) % 2

    def everyone(self):
        return [self.other_core, self.other_chip, self.diagonal, self.other_side] + self.other_planes


class Semaphores:
    def __init__(self, send, receive):
        self.send, self.receive, self.count = send, receive, 0
        self.sent = []

    def remote(self, source, target, partner):
        at = self.count
        self.count += 1
        copy = copy_to(source, target, self.send.at[at], self.receive.at[at], partner)
        self.sent.append(copy)
        return copy

    def local(self, source, target):
        at = self.count
        self.count += 1
        return pltpu.make_async_copy(source, target, self.send.at[at])


def block_places(where_chip, where_core, rows, offset, index, size):
    per = rows // size
    slot = index // per
    block = (where_chip + slot % 2) % 2 * 2 + (where_core + slot // 2) % 2
    return block * rows + index % per * size + offset


def mask_columns(where_chip, where_core, rows, count, size, length, ref):
    lane = lax.broadcasted_iota(jnp.int32, (size, PAIR), 1)
    offset = lax.broadcasted_iota(jnp.int32, (size, PAIR), 0)

    def step(index, _):
        places = block_places(where_chip, where_core, rows, offset, index, size)
        bias = jnp.where(places < length, 0.0, NEGATIVE)
        ref[block_at(index, size), :] = jnp.where(
            lane < 3, 1.0, jnp.where(lane == 3, bias, 0.0)
        ).astype(bf16)
        return 0

    lax.fori_loop(0, count // size, step, 0)


def open_kernel(
    comm,
    planes,
    deep,
    source_len_ref,
    upsample_ref,
    *refs,
):
    if comm:
        (
            decoder_ref, source_ref,
            wq_in, wk_in, wv_in, *later_in, gain_in,
            x_out, source_out, qkv_out, later_a, later_b, later_c, gain_out,
            q_out, k_out, v_out, mixed_out, extra_out,
            x_ref, qkv_ref, gain_ref, hidden_ref, weight_ref, mask_ref,
            q_ref, k_ref, v_ref, mixed_ref, extra_ref, send, receive,
            stage_a, stage_b, stage_c, stage_s, gain_block,
        ) = refs
    else:
        (
            x_ref, qkv_ref, gain_ref,
            q_out, k_out, v_out, mixed_out, extra_out,
            hidden_ref, weight_ref, mask_ref,
            q_ref, k_ref, v_ref, mixed_ref, extra_ref, send, receive,
        ) = refs
    where = Where(planes)
    place, plane, side, chip, core = where.place, where.plane, where.side, where.chip, where.core
    total, width = x_ref.shape
    pairs = width // PAIR
    own = total // 2
    rows = total // 4
    semaphores = Semaphores(send, receive)
    column = where.column

    if comm:
        group = where.group
        x_slots = [x_ref.at[slot * rows : (slot + 1) * rows] for slot in range(4)]
        few = source_ref.shape[1]
        s_slots = [source_out.at[slot * few : (slot + 1) * few] for slot in range(4)]
        local_x = semaphores.local(decoder_ref.at[chip], x_slots[0])
        mine = qkv_ref.at[place, side, plane]
        local_qkv = [
            semaphores.local(ref, mine.at[at * deep : (at + 1) * deep])
            for at, ref in enumerate((wq_in, wk_in, wv_in))
        ]
        first = [local_x, *local_qkv]
        wo_in, wcq_in, wck_in, wcv_in, wco_in, w1_in, w2_in = later_in
        mine_a = later_a.at[place, side, plane]
        mine_b = later_b.at[place, side, plane]
        mine_c = later_c.at[place, side, plane]
        wide = w1_in.shape[1] // PAIR
        local_later = [
            [
                semaphores.local(ref, stage_a.at[at * deep : (at + 1) * deep])
                for at, ref in enumerate((wo_in, wcq_in, wck_in, wcv_in, wco_in))
            ],
            [
                semaphores.local(
                    w1_in.at[:, at * PAIR : (at + 1) * PAIR], stage_b.at[at * deep : (at + 1) * deep]
                )
                for at in range(wide)
            ],
            [semaphores.local(w2_in, stage_c)],
        ]
        stores = [
            semaphores.local(stage_a, mine_a),
            semaphores.local(stage_b, mine_b),
            semaphores.local(stage_c, mine_c),
        ]
        source_load = semaphores.local(source_ref.at[chip], stage_s)
        source_store = semaphores.local(stage_s, s_slots[0])
        greet(where.everyone())
        gain_block[...] = jnp.zeros(gain_block.shape, f32)
        gain_block[0 : gain_in.shape[0], :] = gain_in[...].astype(f32)
        gain_ref[place] = gain_block[...]
        for copy in first + local_later[0] + local_later[1] + local_later[2] + [source_load]:
            copy.start()
        await_greetings(where.everyone())

        x_cross = semaphores.remote(decoder_ref.at[1 - chip], x_slots[1], where.other_chip)
        x_core = semaphores.remote(decoder_ref.at[chip], x_slots[2], where.other_core)
        x_pass = semaphores.remote(x_slots[1], x_slots[3], where.other_core)
        s_cross = semaphores.remote(source_ref.at[1 - chip], s_slots[1], where.other_chip)
        s_core = semaphores.remote(source_ref.at[chip], s_slots[2], where.other_core)
        s_pass = semaphores.remote(s_slots[1], s_slots[3], where.other_core)
        gain_sends = [
            semaphores.remote(gain_block, gain_ref.at[place], partner)
            for partner in (where.other_core, where.other_chip, where.diagonal)
        ]
        qkv_planes = [semaphores.remote(mine, mine, partner) for partner in where.other_planes]
        qkv_side = semaphores.remote(
            qkv_ref.at[place, side], qkv_ref.at[place, side], where.other_side
        )
        qkv_core = semaphores.remote(qkv_ref.at[place], qkv_ref.at[place], where.other_core)
        qkv_chip = semaphores.remote(qkv_ref.at[place], qkv_ref.at[place], where.other_chip)
        across = column(2)
        qkv_pass = semaphores.remote(qkv_ref.at[across], qkv_ref.at[across], where.other_core)
        later = []
        for buffer, stage in ((later_a, stage_a), (later_b, stage_b), (later_c, stage_c)):
            block = buffer.at[place, side, plane]
            mine_side, across_side = buffer.at[place, side], buffer.at[across, side]
            if buffer is later_c:
                first = [semaphores.remote(stage, block, where.other_chip)]
                far = buffer.at[across, side, plane]
                second = [
                    semaphores.remote(stage, block, where.other_side),
                    semaphores.remote(far, far, where.other_side),
                ]
                others = [buffer.at[at, 1 - side, plane] for at in (place, across)]
                kept = [(stage, block), (far, far)] + [(one, one) for one in others]
            else:
                first = [semaphores.remote(mine_side, mine_side, where.other_chip)]
                second = []
                if buffer is later_a:
                    second = [
                        semaphores.remote(one, one, where.other_side)
                        for one in (mine_side, across_side)
                    ]
                kept = [(stage, block)]
            later.append(
                dict(
                    planes=[
                        semaphores.remote(one, other, partner)
                        for one, other in kept
                        for partner in where.other_planes
                    ],
                    first=first,
                    second=second,
                    core=[
                        semaphores.remote(buffer.at[at], buffer.at[at], where.other_core)
                        for at in (() if buffer is later_b else (place, across))
                    ],
                )
            )

        def begin(copies):
            for copy in copies:
                copy.start()

        def arrive(copies):
            for copy in copies:
                copy.wait_recv()

        begin(gain_sends)
        for copy in local_qkv:
            copy.wait()
        begin(qkv_planes)
        x_cross.start()
        x_core.start()
        begin([s_core])
        for copies in local_later:
            for copy in copies:
                copy.wait()
        source_load.wait()
        begin([*stores, source_store])
        a, b, c = later
        begin(c["first"])
        begin(a["planes"])
        begin(b["planes"])

    length = source_len_ref[where.group * 2 + chip] * upsample_ref[where.group * 2 + chip]
    mask_columns(chip, core, rows, total, BLOCK, length, mask_ref)

    def hide(slot):
        gain = jnp.concatenate([gain_ref[at, 0:1, :] for at in range(pairs)], axis=1)

        def step(index):
            at = pl.ds(index * BLOCK + slot * rows, BLOCK)
            scaled, _ = normalize(x_ref[at, :].astype(f32))
            hidden_ref[at, :] = (scaled * gain).astype(bf16)

        repeat(0, rows // BLOCK, step, rows // BLOCK)

    def take_weights(pair):
        for part in range(3):
            for at in range(8):
                weight_ref[at * 64 : at * 64 + 64, part * PAIR : (part + 1) * PAIR] = qkv_ref[
                    pair, at % 2, at // 2, part * 64 : part * 64 + 64, :
                ]

    def project(pair, slot, count):
        size = 2 * BLOCK
        for index in range(count * rows // size):
            at = pl.ds(slot * rows + index * size, size)
            both = dot(hidden_ref[at, :], weight_ref[:, PAIR:]).astype(bf16)
            k_ref[pair, at, :] = both[:, :PAIR]
            v_ref[pair, at, :] = both[:, PAIR:]
            if slot * rows + index * size < own:
                query = dot(hidden_ref[at, :], weight_ref[:, :PAIR]) * (0.125 * LOG2E)
                q_ref[pair, at, :] = query.astype(bf16)

    if comm:
        local_x.wait()
        arrive(gain_sends)
        hide(0)
        arrive([x_core])
        hide(2)
        arrive(qkv_planes)
        qkv_side.start()
        arrive([qkv_side])
        begin([qkv_core])
        take_weights(place)
        project(place, 0, 1)
        project(place, 2, 1)
        arrive([x_cross])
        x_pass.start()
        arrive(a["planes"])
        for copy in [*stores, source_store]:
            copy.wait()
        begin(a["first"])
        arrive(c["first"])
        begin(c["second"])
        begin([qkv_chip])
        hide(1)
        project(place, 1, 1)
        arrive([x_pass])
        hide(3)
        project(place, 3, 1)
    else:
        for slot in range(4):
            hide(slot)
        take_weights(place)
        project(place, 0, 4)

    size = 2 * BLOCK
    blocks = own // size
    lane = lax.broadcasted_iota(jnp.int32, (size, PAIR), 1)

    def outs_of(pair):
        return [
            (q_ref.at[pair], q_out.at[pair]),
            (k_ref.at[pair], k_out.at[pair]),
            (v_ref.at[pair], v_out.at[pair]),
            (mixed_ref.at[pair], mixed_out.at[pair]),
            (extra_ref.at[pair], extra_out.at[pair]),
        ]

    first_out = semaphores.count

    def out_copies(step, pair):
        return [
            pltpu.make_async_copy(source, target, send.at[first_out + step * 5 + at])
            for at, (source, target) in enumerate(outs_of(pair))
        ]

    if comm:
        x_local = pltpu.make_async_copy(x_ref, x_out, send.at[first_out + 20])
        qkv_local = pltpu.make_async_copy(qkv_ref, qkv_out, send.at[first_out + 21])
        gain_local = pltpu.make_async_copy(gain_ref, gain_out, send.at[first_out + 22])
        begin([x_local, gain_local])

    def step(index, _):
        turn = index // blocks
        pair = column(turn)
        if comm:
            @pl.when(index == 1)
            def _():
                arrive(c["second"])
                begin(c["planes"])
                arrive(b["planes"])
                begin(b["first"])
                begin([s_cross])

            @pl.when(index == 2)
            def _():
                arrive([qkv_core])
                arrive(a["first"])
                begin(a["second"])

            @pl.when(index == 4)
            def _():
                arrive([qkv_chip])
                qkv_pass.start()

            @pl.when(index == 5)
            def _():
                arrive(b["first"])
                arrive(a["second"])
                begin(a["core"])

            @pl.when(index == 6)
            def _():
                arrive([qkv_pass])
                qkv_local.start()
                arrive([s_cross])
                s_pass.start()

            @pl.when(index == 7)
            def _():
                arrive(c["planes"])
                begin(c["core"])

        @pl.when((index % blocks == 0) & (index > 0))
        def _():
            take_weights(pair)
            project(pair, 0, 4)

        at = block_at(index % blocks, size)
        mixed, extras = attend_pair(
            q_ref[pair, at, :], k_ref[pair], mask_ref[...], v_ref[pair], lane
        )
        mixed_ref[pair, at, :] = mixed
        extra_ref[pair, 0, at, :] = extras[0]
        extra_ref[pair, 1, at, :] = extras[1]

        @pl.when(index % blocks == blocks - 1)
        def _():
            for copy in out_copies(turn, pair):
                copy.start()

        return 0

    lax.fori_loop(0, pairs * blocks, step, 0)
    if comm:
        arrive([s_core, s_pass])
        for piece in later:
            arrive(piece["core"])
        for copy in semaphores.sent:
            copy.wait_send()
        for copy in (x_local, qkv_local, gain_local):
            copy.wait()
    for turn in range(pairs):
        for copy in out_copies(turn, column(turn)):
            copy.wait()


def whole_weight(ref, blocks, start, count, chunks=1):
    columns, sides, planes = blocks.shape[:3]
    for column in range(columns):
        for side in range(sides):
            for plane in range(planes):
                row = (plane * sides + side) * count
                for chunk in range(chunks):
                    at = (column * chunks + chunk) * PAIR
                    ref[row : row + count, at : at + PAIR] = blocks[
                        column, side, plane, start + chunk * count : start + (chunk + 1) * count, :
                    ]


def to_blocks(blocks, columns, places, start, count, value):
    for column_at, column in enumerate(columns):
        for place_at, (side, plane) in enumerate(places):
            blocks[column, side, plane, start : start + count, :] = value[
                place_at * count : (place_at + 1) * count,
                column_at * PAIR : (column_at + 1) * PAIR,
            ].astype(bf16)


def middle_kernel(
    comm,
    planes,
    source_len_ref,
    upsample_ref,
    send_ref,
    x_any,
    mixed_any,
    cotangent_any,
    cotangent_far,
    source_any,
    later_a,
    later_b,
    later_c,
    gain_blocks,
    out_rows,
    grad_mixed_out,
    grad_self_out,
    part_a,
    part_b,
    part_c,
    grad_source_ref,
    dgain_ref,
    x_ref,
    mixed_ref,
    cotangent_ref,
    source_ref,
    blocks_a,
    blocks_b,
    blocks_c,
    wo_ref,
    wcq_ref,
    wck_ref,
    wcv_ref,
    wco_ref,
    w1_ref,
    w2_ref,
    ck_ref,
    cv_ref,
    ckt_ref,
    cextra_ref,
    dck_ref,
    dcv_ref,
    after_self_s,
    after_cross_s,
    final_s,
    hidden_grad_s,
    qc_s,
    cm_s,
    gcm_s,
    dq_s,
    extra_s,
    hidden_two_t,
    hidden_three_s,
    hidden_three_t,
    grad_ffn_s,
    grad_ffn_t,
    branch_s,
    load,
    store,
    send,
    receive,
):
    rows_own, width = x_ref.shape
    pairs = mixed_ref.shape[0]
    hidden_width = w1_ref.shape[1]
    chunk = hidden_width // pairs
    where = Where(planes)
    chip, core = where.chip, where.core
    half = rows_own // 2
    size = half
    few = source_ref.shape[0]
    deep = width // 8
    place, side, across = where.place, where.side, where.column(2)
    partners = (where.other_core, where.other_chip, where.other_side)
    if comm:
        greet(partners)
    moves = [
        (x_any.at[:rows_own], x_ref),
        (mixed_any, mixed_ref),
        (later_a, blocks_a),
        (source_any, source_ref),
        (cotangent_any.at[chip], cotangent_ref.at[:half]),
        (later_c, blocks_c),
    ]
    if comm:
        moves += [
            (later_b.at[at, side], blocks_b.at[at, side]) for at in (place, across)
        ]
    else:
        moves += [(cotangent_far, cotangent_ref.at[half:]), (later_b, blocks_b)]
    loads = [
        pltpu.make_async_copy(source, target, load.at[at])
        for at, (source, target) in enumerate(moves)
    ]
    for copy in loads:
        copy.start()
    semaphores = Semaphores(send, receive)
    if comm:
        cross_rows = semaphores.remote(
            cotangent_any.at[1 - chip], cotangent_ref.at[half:], where.other_chip
        )
        to_side = [
            semaphores.remote(later_b.at[at, side], blocks_b.at[at, side], where.other_side)
            for at in (place, across)
        ]
        to_core = [
            semaphores.remote(blocks_b.at[at], blocks_b.at[at], where.other_core)
            for at in (place, across)
        ]
    stores = [
        pltpu.make_async_copy(source, target, store.at[at])
        for at, (source, target) in enumerate(
            (
                (grad_ffn_s, out_rows),
                (gcm_s, grad_mixed_out),
                (final_s, grad_self_out),
                (blocks_a, part_a),
                (blocks_b, part_b),
                (blocks_c, part_c),
            )
        )
    ]
    gain_rows = jnp.concatenate([gain_blocks[at] for at in range(pairs)], axis=1)
    gain_two = gain_rows[1:2, :]
    gain_three = gain_rows[2:3, :]
    dgain_ref[...] = jnp.zeros(dgain_ref.shape, f32)

    dp_size = planes * 2
    group, half_way = where.group, planes
    sentence = group * 2 + chip
    src_len = source_len_ref[sentence]
    dec_len = src_len * upsample_ref[sentence]
    moved = chip * send_ref[group]
    holder = (group + moved * half_way) % dp_size
    partner = (holder + half_way) % dp_size

    def tokens_of(slot):
        return source_len_ref[slot] * upsample_ref[slot]

    tokens = (
        tokens_of(holder * 2)
        + tokens_of(holder * 2 + 1) * (1 - send_ref[holder])
        + tokens_of(partner * 2 + 1) * send_ref[partner]
    )
    loss_scale = jnp.full((1, 1), rows_own * 2, f32) / jnp.full((1, 1), tokens, jnp.int32).astype(f32)
    mask_columns(chip, core, few // 4, few, few // 4, src_len, cextra_ref)
    offset = lax.broadcasted_iota(jnp.int32, (size, 1), 0)

    def counted(index):
        place = block_places(chip, core, half, offset, index, size)
        return jnp.where(place < dec_len, 1.0, 0.0)

    def side_by_side(ref, rows):
        return jnp.concatenate([ref[pair, rows, :] for pair in range(pairs)], axis=1)

    def apart(ref, rows, value):
        for pair in range(pairs):
            ref[pair, rows, :] = value[:, pair * PAIR : (pair + 1) * PAIR]

    if comm:
        await_greetings(partners)
        for copy in (*to_side, cross_rows):
            copy.start()
    for copy in loads[:4]:
        copy.wait()
    for at, ref in enumerate((wo_ref, wcq_ref, wck_ref, wcv_ref, wco_ref)):
        whole_weight(ref, blocks_a, at * deep, deep)

    key_rows = dot(source_ref[...], wck_ref[...]).astype(bf16)
    every = pl.ds(0, few)
    apart(ck_ref, every, key_rows)
    for pair in range(pairs):
        ckt_ref[pair] = key_rows[:, pair * PAIR : (pair + 1) * PAIR].T
    apart(cv_ref, every, dot(source_ref[...], wcv_ref[...]).astype(bf16))

    def first_part(index):
        rows = block_at(index, size)
        after_self = x_ref[rows, :].astype(f32) + dot(side_by_side(mixed_ref, rows), wo_ref[...])
        after_self_s[rows, :] = after_self
        scaled, _ = normalize(after_self)
        hidden = (scaled * gain_two).astype(bf16)
        hidden_two_t[:, rows] = hidden.T
        apart(qc_s, rows, (dot(hidden, wcq_ref[...]) * (0.125 * LOG2E)).astype(bf16))

    repeat(0, rows_own // size, first_part, 1)

    def cross(index):
        pair, rows = index // 2, block_at(index % 2, half)
        mixed, extras = attend_pair(
            qc_s[pair, rows, :], ck_ref[pair], cextra_ref[...], cv_ref[pair],
            lax.broadcasted_iota(jnp.int32, (half, PAIR), 1),
        )
        cm_s[pair, rows, :] = mixed
        extra_s[2 * pair, rows, :] = extras[0]
        extra_s[2 * pair + 1, rows, :] = extras[1]

    repeat(0, 2 * pairs, cross, 2)
    for copy in loads[4:]:
        copy.wait()
    if comm:
        for copy in to_side:
            copy.wait_recv()
        for copy in to_core:
            copy.start()
        cross_rows.wait_recv()
    whole_weight(w2_ref, blocks_c, 0, hidden_width // 8)

    def second_part(index):
        rows = block_at(index, size)
        after_cross = after_self_s[rows, :] + dot(side_by_side(cm_s, rows), wco_ref[...])
        after_cross_s[rows, :] = after_cross
        scaled, _ = normalize(after_cross)
        hidden = (scaled * gain_three).astype(bf16)
        hidden_three_s[rows, :] = hidden
        hidden_three_t[:, rows] = hidden.T
        grad = (cotangent_ref[rows, :].astype(f32) * (counted(index) * loss_scale)).astype(bf16)
        grad_ffn_s[rows, :] = grad
        grad_ffn_t[:, rows] = grad.T

    repeat(0, rows_own // size, second_part, 1)
    if comm:
        for copy in to_core:
            copy.wait_recv()
        for copy in semaphores.sent:
            copy.wait_send()
    whole_weight(w1_ref, blocks_b, 0, deep, hidden_width // width)

    everyone = [(at % 2, at // 2) for at in range(8)]
    deep_two = hidden_width // 8
    halves = [slice(index * size, (index + 1) * size) for index in range(rows_own // size)]

    def bent(expanded, grad_active):
        square = expanded * expanded
        bend = jnp.tanh(expanded * (GELU_IN + (GELU_IN * GELU_CUBE) * square))
        rise = 0.5 + 0.5 * bend
        active = expanded * rise
        slope = rise + active * (1.0 - rise) * (
            2.0 * GELU_IN + (6.0 * GELU_IN * GELU_CUBE) * square
        )
        return active.astype(bf16), (grad_active * slope).astype(bf16)

    final_s[...] = jnp.zeros(final_s.shape, f32)
    hidden_grad_s[...] = jnp.zeros(hidden_grad_s.shape, f32)

    def feed(part, _):
        columns = block_at(part, chunk)
        opened = [
            (
                dot(hidden_three_s[rows, :], w1_ref[:, columns]),
                dot_nt(grad_ffn_s[rows, :], w2_ref[columns, :]),
            )
            for rows in halves
        ]
        actives, grads = [], []
        for rows, one in zip(halves, opened):
            active, grad_expanded = bent(*one)
            final_s[rows, :] += dot(active, w2_ref[columns, :])
            hidden_grad_s[rows, :] += dot_nt(grad_expanded, w1_ref[:, columns])
            actives.append(active)
            grads.append(grad_expanded)
        value = dot(hidden_three_t[...], jnp.concatenate(grads, axis=0))
        for at in range(chunk // PAIR):
            to_blocks(
                blocks_b, [part], everyone, at * deep, deep, value[:, at * PAIR : (at + 1) * PAIR]
            )
        value = dot(grad_ffn_t[...], jnp.concatenate(actives, axis=0))
        for at in range(chunk // PAIR):
            index, row = divmod(at * PAIR, deep_two)
            for column in range(pairs):
                blocks_c[column, index, part, row : row + PAIR, :] = value[
                    column * PAIR : (column + 1) * PAIR, at * PAIR : (at + 1) * PAIR
                ].astype(bf16)
        return 0

    lax.fori_loop(0, hidden_width // chunk, feed, 0)
    stores[4].start()
    stores[5].start()

    def third_part(index):
        rows = block_at(index, size)
        after_cross = after_cross_s[rows, :]
        weight = counted(index)
        grad_final = cotangent_ref[rows, :].astype(f32) * (weight * loss_scale)
        scaled, inverse = normalize(after_cross)
        back, gain_sum = norm_back(hidden_grad_s[rows, :], scaled, inverse, gain_three)
        dgain_ref[2:3, :] += gain_sum
        grad_ffn_s[rows, :] = ((after_cross + final_s[rows, :]) * weight).astype(bf16)
        grad_cross = grad_final + back
        final_s[rows, :] = grad_cross
        branch = grad_cross.astype(bf16)
        hidden_three_s[rows, :] = branch
        apart(gcm_s, rows, dot_nt(branch, wco_ref[...]).astype(bf16))

    repeat(0, rows_own // size, third_part, 1)
    stores[0].start()

    def cross_back(pair, _):
        def put(ref, factor):
            def keep(_, value):
                ref[pair] = (value * factor).astype(bf16)

            return keep

        extra = cextra_ref[...]
        query_grad = attend_pair_back(
            qc_s[pair],
            gcm_s[pair],
            cm_s[pair],
            [extra_s[2 * pair], extra_s[2 * pair + 1]],
            lambda _: jnp.concatenate([ck_ref[pair], extra], axis=1),
            lambda _: jnp.concatenate([cv_ref[pair], extra], axis=1),
            lambda _, head: ckt_ref[pair, 64 * head : 64 * head + 64, :],
            1,
            put(dck_ref, LN2),
            put(dcv_ref, 1.0),
        )
        dq_s[pair] = query_grad.T
        return 0

    lax.fori_loop(0, pairs, cross_back, 0)

    def last_part(index):
        rows = block_at(index, size)
        scaled, inverse = normalize(after_self_s[rows, :])
        upstream = dot_nt(side_by_side(dq_s, rows), wcq_ref[...])
        back, gain_sum = norm_back(upstream, scaled, inverse, gain_two)
        dgain_ref[1:2, :] += gain_sum
        grad_self = final_s[rows, :] + back
        final_s[rows, :] = grad_self
        branch = grad_self.astype(bf16)
        branch_s[rows, :] = branch
        apart(gcm_s, rows, dot_nt(branch, wo_ref[...]).astype(bf16))

    repeat(0, rows_own // size, last_part, 1)
    stores[1].start()
    stores[2].start()

    columns = range(pairs)
    both_sides = [(0, 0), (1, 0)]
    for pair in range(pairs):
        two = [(side, pair) for side, _ in both_sides]
        to_blocks(blocks_a, columns, two, 0, deep, dot(mixed_ref[pair].T, branch_s[...]))
        to_blocks(blocks_a, columns, two, 4 * deep, deep, dot(cm_s[pair].T, hidden_three_s[...]))
    all_rows = pl.ds(0, rows_own)
    to_blocks(
        blocks_a, columns, everyone, deep, deep, dot(hidden_two_t[...], side_by_side(dq_s, all_rows))
    )
    source_t = source_ref[...].T
    key_grad = side_by_side(dck_ref, every)
    value_grad = side_by_side(dcv_ref, every)
    to_blocks(blocks_a, columns, everyone, 2 * deep, deep, dot(source_t, key_grad))
    to_blocks(blocks_a, columns, everyone, 3 * deep, deep, dot(source_t, value_grad))
    stores[3].start()
    grad_source_ref[...] = (
        dot_nt(key_grad, wck_ref[...]) + dot_nt(value_grad, wcv_ref[...])
    ).astype(bf16)
    for copy in stores:
        copy.wait()


def last_kernel(comm, planes, source_len_ref, upsample_ref, *refs):
    (q_any, k_any, v_any, mixed_any, grad_any, extra_any) = refs[:6]
    (x_any, qkv_any, gain_any, grad_self_any, dgain_any) = refs[6:11]
    refs = refs[11:]
    if comm:
        (part_a, part_b, part_c, source_any, rows_any) = refs[:5]
        (rows_land, grad_out, cross_land, source_out, source_far) = refs[5:10]
        (*weight_outs, gain_out) = refs[10:21]
        refs = refs[21:]
    else:
        (own_out, other_out, part_out, gain_out) = refs[:4]
        refs = refs[4:]
    (
        q_s, k_s, v_s, mixed_s, grad_s, extra_s, x_s, qkv_s, gain_s, grad_self_s, dgain_s,
        keys_s, values_s, kt_s, hidden_s, total_s, dkv_s, dq_s, weight_s,
        part_s, load, send, receive,
    ) = refs[:23]
    refs = refs[23:]
    where = Where(planes)
    chip, core, side, plane = where.chip, where.core, where.side, where.plane
    total, width = x_s.shape
    own = total // 2
    rows = total // 4
    pairs = width // PAIR
    deep = width // 8
    chunk = 512
    semaphores = Semaphores(send, receive)
    sentence = where.group * 2 + chip
    length = source_len_ref[sentence] * upsample_ref[sentence]

    def turn_pair(turn):
        return where.column(pairs - 1 - turn)

    def turn_loads(turn):
        pair, slot = turn_pair(turn), turn % 2
        return [
            pltpu.make_async_copy(source.at[pair], target.at[slot], load.at[slot, at])
            for at, (source, target) in enumerate(
                (
                    (q_any, q_s),
                    (k_any, k_s),
                    (v_any, v_s),
                    (mixed_any, mixed_s),
                    (grad_any, grad_s),
                    (extra_any, extra_s),
                )
            )
        ]

    for copy in turn_loads(0):
        copy.start()
    common = [
        semaphores.local(source, target)
        for source, target in (
            (x_any, x_s),
            (qkv_any, qkv_s),
            (gain_any, gain_s),
            (dgain_any, dgain_s),
            (grad_self_any, grad_self_s),
        )
    ]
    for copy in common:
        copy.start()

    def begin(copies):
        for copy in copies:
            copy.start()

    def arrive(copies):
        for copy in copies:
            copy.wait_recv()

    if comm:
        (
            keep_a, keep_b, keep_c, core_a, core_b, core_c, far_a, far_b, far_c,
            near_a, near_b, near_c, planes_a, planes_b, planes_c,
            land_q, far_q, planes_q, gain_send, gain_land, gain_far, gain_planes, grads_send,
            grads_land, cross_send, stage, source_s, source_land, stage_s,
        ) = refs
        place, across = where.place, where.column(2)
        pieces = []
        for part, keep, land, far_land, near_land, land_planes, order in (
            (part_a, keep_a, core_a, far_a, near_a, planes_a, "yxz"),
            (part_b, keep_b, core_b, far_b, near_b, planes_b, "yxz"),
            (part_c, keep_c, core_c, far_c, near_c, planes_c, "xyz"),
        ):
            piece = dict(keep=keep, land=land, order=order)
            piece.update(far_land=far_land, near_land=near_land, planes=land_planes)
            piece["load"] = [
                semaphores.local(part.at[place], keep.at[0]),
                semaphores.local(part.at[across], keep.at[1]),
            ]
            piece["core"] = [
                semaphores.remote(part.at[where.column(1)], land.at[0], where.other_core),
                semaphores.remote(part.at[where.column(3)], land.at[1], where.other_core),
            ]
            if order[0] == "y":
                piece["far"] = [
                    semaphores.remote(keep.at[at, 1 - side], far_land.at[at], where.other_side)
                    for at in (0, 1)
                ]
            else:
                piece["far"] = [
                    semaphores.remote(keep.at[1, at], far_land.at[at], where.other_chip)
                    for at in (0, 1)
                ]
            if order == "yxz":
                near = (keep.at[1, side], near_land, where.other_chip)
            else:
                near = (keep.at[0, 1 - side], near_land, where.other_side)
            piece["near"] = [semaphores.remote(*near)]
            piece["last"] = [
                semaphores.remote(
                    keep.at[0, side, (plane + step) % planes],
                    land_planes.at[step - 1],
                    where.other_planes[step - 1],
                )
                for step in range(1, planes)
            ]
            pieces.append(piece)
        a, b, c = pieces
        owners = (where.diagonal, where.other_chip, where.other_core)
        hops = (where.other_core, where.other_chip, where.other_core)
        send_q = [
            semaphores.remote(part_s.at[turn], land_q.at[turn], hops[turn]) for turn in range(3)
        ]
        side_q = semaphores.remote(part_s.at[3, 1 - side], far_q, where.other_side)
        plane_q = [
            semaphores.remote(
                part_s.at[3, side, (plane + step) % planes],
                planes_q.at[step - 1],
                where.other_planes[step - 1],
            )
            for step in range(1, planes)
        ]
        gain_group = [
            semaphores.remote(gain_send.at[where.column(3 - turn)], gain_land.at[turn], owners[turn])
            for turn in range(3)
        ]
        gain_side = semaphores.remote(gain_land.at[3], gain_far, where.other_side)
        gain_last = [
            semaphores.remote(
                gain_planes.at[plane], gain_planes.at[plane], where.other_planes[step - 1]
            )
            for step in range(1, planes)
        ]
        rows_cross = semaphores.remote(rows_any.at[rows:], rows_land, where.other_chip)
        few = source_any.shape[0] // 4
        source_local = semaphores.local(source_any.at[: 2 * few], source_s)
        source_core = semaphores.remote(source_any.at[2 * few :], source_land, where.other_core)
        source_cross = semaphores.remote(source_s.at[few:], source_far, where.other_chip)
        grads_core = [
            semaphores.remote(grads_send.at[at], grads_land.at[at], where.other_core)
            for at in range(2)
        ]
        grads_cross = [
            semaphores.remote(cross_send.at[at], cross_land.at[at], where.other_chip)
            for at in range(rows // BLOCK)
        ]
        stage_out = semaphores.local(stage, grad_out)
        source_own = semaphores.local(stage_s, source_out)
        for piece in pieces:
            begin(piece["load"])
        begin([source_local])
        greet(where.everyone())

        def add_in(ref, land):
            def add(at, _):
                ref[at] = (ref[at].astype(f32) + land[at].astype(f32)).astype(bf16)
                return 0

            lax.fori_loop(0, planes, add, 0)

        def add_core(piece):
            for copy in piece["load"]:
                copy.wait()
            arrive(piece["core"])
            for at in (0, 1):
                for half in (0, 1):
                    add_in(piece["keep"].at[at, half], piece["land"].at[at, half])
            begin(piece["far"])

        def add_far(piece):
            arrive(piece["far"])
            for at in (0, 1):
                if piece["order"][0] == "y":
                    add_in(piece["keep"].at[at, side], piece["far_land"].at[at])
                else:
                    add_in(piece["keep"].at[0, at], piece["far_land"].at[at])
            begin(piece["near"])

        def add_near(piece):
            arrive(piece["near"])
            add_in(piece["keep"].at[0, side], piece["near_land"])
            begin(piece["last"])

        def finish(piece):
            arrive(piece["last"])
            value = piece["keep"][0, side, plane].astype(f32)
            for step in range(planes - 1):
                value = value + piece["planes"][step].astype(f32)
            return value

    mask_columns(chip, core, rows, total, BLOCK, length, values_s.at[:, PAIR:])
    keys_s[:, PAIR:] = values_s[:, PAIR:]
    for copy in common:
        copy.wait()
    gain = jnp.concatenate([gain_s[at, 0:1, :] for at in range(pairs)], axis=1)

    def hide(index):
        at = block_at(index, BLOCK)
        scaled, _ = normalize(x_s[at, :].astype(f32))
        hidden_s[:, at] = (scaled * gain).astype(bf16).T

    repeat(0, total // BLOCK, hide, 2)
    if comm:
        await_greetings(where.everyone())
        for piece in pieces:
            begin(piece["core"])
        begin([source_core, rows_cross])

    def take_weights(turn, pair):
        for part in range(3):
            for at in range(8):
                weight_s[turn, at * 64 : at * 64 + 64, part * PAIR : (part + 1) * PAIR] = qkv_s[
                    pair, at % 2, at // 2, part * 64 : part * 64 + 64, :
                ]

    def upstream(turns, at, own_rows):
        value = None
        for turn in turns:
            term = dot_nt(dkv_s[turn, at, :], weight_s[turn, :, PAIR:])
            if own_rows:
                term = term + dot_nt(dq_s[turn, at, :], weight_s[turn, :, :PAIR])
            value = term if value is None else value + term
        return value

    def comm_steps(index):
        if not comm:
            return

        @pl.when(index == 1)
        def _():
            add_core(a)
            add_core(c)
            add_core(b)
            source_local.wait()
            arrive([source_core])
            for half in range(2):
                r = slice(half * few, (half + 1) * few)
                value = source_s[r, :].astype(f32) + source_land[r, :].astype(f32)
                source_s[r, :] = value.astype(bf16)
                if half == 0:
                    stage_s[...] = value
            begin([source_cross, source_own])

        @pl.when(index == 3)
        def _():
            add_far(a)
            add_far(c)

        @pl.when(index == 4)
        def _():
            arrive([send_q[0]])
            for half in range(2):
                add_in(part_s.at[1, half], land_q.at[0, half])
            send_q[1].start()

        @pl.when(index == 5)
        def _():
            add_far(b)
            add_near(a)

        @pl.when(index == 6)
        def _():
            add_near(c)

        @pl.when(index == 7)
        def _():
            add_near(b)


    def step(turn, _):
        pair, slot = turn_pair(turn), turn % 2
        for copy in turn_loads(turn):
            copy.wait()

        @pl.when(turn + 1 < pairs)
        def _():
            for copy in turn_loads(turn + 1):
                copy.start()

        keys_s[:, :PAIR] = k_s[slot]
        values_s[:, :PAIR] = v_s[slot]
        kt_s[...] = k_s[slot].T
        take_weights(turn, pair)
        comm_steps(2 * turn)

        def part(ref):
            return lambda part: ref[part * chunk : (part + 1) * chunk, :]

        def put(at, factor):
            def keep(part, value):
                dkv_s[turn, part * chunk : (part + 1) * chunk, at : at + PAIR] = (
                    value * factor
                ).astype(bf16)

            return keep

        query_grad = attend_pair_back(
            q_s[slot],
            grad_s[slot],
            mixed_s[slot],
            [extra_s[slot, head] for head in (0, 1)],
            part(keys_s),
            part(values_s),
            lambda part, head: kt_s[64 * head : 64 * head + 64, part * chunk : (part + 1) * chunk],
            total // chunk,
            put(0, LN2),
            put(PAIR, 1.0),
        )
        dq_s[turn] = query_grad.T
        comm_steps(2 * turn + 1)
        both = dot(hidden_s[...], dkv_s[turn]).astype(bf16)
        query = dot(hidden_s[:, :own], dq_s[turn]).astype(bf16)
        for at in range(8):
            r = slice(at * deep, (at + 1) * deep)
            for part_at, value in enumerate((query[r, :], both[r, :PAIR], both[r, PAIR:])):
                part_s[turn, at % 2, at // 2, part_at * deep : (part_at + 1) * deep, :] = value

        if comm:
            for sent in (0, 2):

                @pl.when(turn == sent)
                def _():
                    send_q[sent].start()

        @pl.when(turn == pairs - 2)
        def _():
            size = 2 * BLOCK
            for row in range(total // size):
                r = pl.ds(row * size, size)
                total_s[r, :] = upstream(range(pairs - 1), r, row * size < own)

        return 0

    lax.fori_loop(0, pairs, step, 0)

    def row_back(row, own_rows):
        r = block_at(row, BLOCK)
        scaled, inverse = normalize(x_s[r, :].astype(f32))
        value = total_s[r, :] + upstream([pairs - 1], r, own_rows)
        back, gain_sum = norm_back(value, scaled, inverse, gain)
        dgain_s[0:1, :] += gain_sum
        return r, back

    per = rows // BLOCK
    if not comm:

        def own_step(row):
            r, back = row_back(row, True)
            grad_self_s[r, :] += back

        def other_step(row):
            r, back = row_back(row, False)
            total_s[r, :] = back

        repeat(0, 2 * per, own_step, per)
        repeat(2 * per, 4 * per, other_step, per)
        own_out[...] = grad_self_s[...]
        other_out[...] = total_s[own:, :].astype(bf16)
        for turn in range(pairs):
            part_out[turn_pair(turn)] = part_s[turn]
        gain_out[...] = dgain_s[...]
        return

    def add_q(at, _):
        for half in range(2):
            value = part_s[3, half, at].astype(f32)
            for turn in (1, 2):
                value = value + land_q[turn, half, at].astype(f32)
            part_s[3, half, at] = value.astype(bf16)
        return 0

    def other_rows(slot):
        def other_step(row):
            _, back = row_back(slot * per + row, False)
            grads_send[slot - 2, block_at(row, BLOCK), :] = back.astype(bf16)

        repeat(0, per, other_step, 1)
        grads_core[slot - 2].start()

    def own_rows(row):
        r, back = row_back(row, True)
        total_s[r, :] = back + grad_self_s[r, :]

    def cross(row):
        r = slice(row * BLOCK, (row + 1) * BLOCK)
        value = total_s[rows + row * BLOCK : rows + (row + 1) * BLOCK, :]
        cross_send[row] = (value + grads_land[1, r, :].astype(f32)).astype(bf16)
        grads_cross[row].start()

    arrive(send_q[1:])
    lax.fori_loop(0, planes, add_q, 0)
    side_q.start()
    other_rows(3)
    repeat(per, 2 * per, own_rows, 1)
    arrive([grads_core[1]])
    cross(0)
    other_rows(2)
    arrive([side_q])
    add_in(part_s.at[3, side], far_q)
    begin(plane_q)
    repeat(0, per, own_rows, 1)
    for at in range(pairs):
        gain_send[at] = dgain_s[:, at * PAIR : (at + 1) * PAIR]
    begin(gain_group)
    for row in range(1, per):
        cross(row)
    arrive(gain_group)
    gain_land[3] = gain_send[place] + gain_land[0] + gain_land[1] + gain_land[2]
    gain_side.start()
    arrive([grads_core[0]])
    stage[...] = total_s[:rows, :] + grads_land[0].astype(f32)
    stage_out.start()
    sums = [finish(piece) for piece in pieces]
    for at in range(5):
        weight_outs[3 + at][...] = sums[0][at * deep : (at + 1) * deep, :]
    for at in range(sums[1].shape[0] // deep):
        weight_outs[8][:, at * PAIR : (at + 1) * PAIR] = sums[1][at * deep : (at + 1) * deep, :]
    for at in range(sums[2].shape[0] // PAIR):
        r = slice(at * PAIR, (at + 1) * PAIR)
        weight_outs[9][r, :] = sums[2][r, :].T
    arrive([gain_side])
    gain_planes[plane] = gain_land[3] + gain_far[...]
    begin(gain_last)
    arrive(plane_q)
    value = part_s[3, side, plane].astype(f32)
    for at in range(planes - 1):
        value = value + planes_q[at].astype(f32)
    for at in range(3):
        weight_outs[at][...] = value[at * deep : (at + 1) * deep, :]
    arrive(gain_last)
    value = gain_planes[0]
    for at in range(1, planes):
        value = value + gain_planes[at]
    gain_out[...] = value
    arrive([rows_cross, source_cross, *grads_cross])
    for copy in (stage_out, source_own):
        copy.wait()
    for copy in semaphores.sent:
        copy.wait_send()


def hand_over_kernel(planes, *refs):
    (rows_any, rows_far, grad_own, grad_far, source_own, source_far, *plain) = refs[:17]
    (decoder_out, grad_out, source_out, *plain_outs) = refs[17:31]
    (rows_s, grad_s, grad_low, source_s, source_low, *plain_s) = refs[31:-2]
    load, store = refs[-2:]
    chip = Where(planes).chip
    rows = rows_s.shape[1]
    moves = [
        (rows_any.at[:rows], rows_s.at[0], rows_s.at[0], decoder_out.at[chip]),
        (rows_far, rows_s.at[1], rows_s.at[1], decoder_out.at[1 - chip]),
        (grad_own, grad_s.at[0], grad_s.at[0], grad_out.at[chip]),
        (grad_far, grad_low, grad_s.at[1], grad_out.at[1 - chip]),
        (source_own, source_s.at[0], source_s.at[0], source_out.at[chip]),
        (source_far, source_low, source_s.at[1], source_out.at[1 - chip]),
    ]
    moves += [
        (one, held, held.at[: other.shape[0]], other)
        for one, held, other in zip(plain, plain_s, plain_outs)
    ]
    loads = [pltpu.make_async_copy(m[0], m[1], load.at[at]) for at, m in enumerate(moves)]
    stores = [pltpu.make_async_copy(m[2], m[3], store.at[at]) for at, m in enumerate(moves)]
    for copy in loads:
        copy.start()
    for at, (one, other) in enumerate(zip(loads, stores)):
        one.wait()
        if at == 3:
            for row in range(grad_low.shape[0]):
                size = grad_low.shape[1]
                grad_s[1, row * size : (row + 1) * size, :] = grad_low[row].astype(f32)
        if at == 5:
            source_s[1] = source_low[...].astype(f32)
        other.start()
    for copy in stores:
        copy.wait()


def call(kernel, outs, *operands, scratch=(), smem=0, params=PARAMS, spaces=None, out_space=VMEM, out_spaces=None):
    spaces = spaces or {}
    out_spaces = out_spaces or {}
    return pl.pallas_call(
        kernel,
        out_shape=[jax.ShapeDtypeStruct(shape, kind) for shape, kind in outs],
        in_specs=[
            pl.BlockSpec(memory_space=pltpu.SMEM if at < smem else spaces.get(at, VMEM))
            for at in range(len(operands))
        ],
        out_specs=[
            pl.BlockSpec(memory_space=out_spaces.get(at, out_space)) for at in range(len(outs))
        ],
        scratch_shapes=list(scratch),
        compiler_params=params,
    )(*operands)


def swapped(value, axis, bit):
    pairs = [(source, source ^ bit) for source in range(lax.axis_size(axis))]
    return lax.ppermute(value, axis, pairs)


def as_blocks(weight, chunks=1):
    height, width = weight.shape
    deep = height // 8
    cut = weight.reshape(4, 2, deep, 4, chunks, PAIR).transpose(3, 1, 0, 4, 2, 5)
    return cut.reshape(4, 2, 4, chunks * deep, PAIR)


def from_blocks(blocks, chunks=1):
    height = blocks.shape[3] // chunks
    cut = blocks.reshape(4, 2, 4, chunks, height, PAIR).transpose(2, 1, 4, 0, 3, 5)
    return cut.reshape(8 * height, 4 * chunks * PAIR)


def gather_plain(arguments, seq_size, dp_size):
    (decoder_in, source_states, out_grad, narrow, ffn_expand, ffn_reduce, norm_gains) = arguments
    chip = lax.axis_index("seq") // 2
    rows_dec = decoder_in.shape[1]
    own = 2 * rows_dec
    outgoing = jnp.concatenate([decoder_in[1 - chip], source_states[1 - chip]], axis=0)
    arrived = swapped(outgoing, "seq", 2)
    own_rows = jnp.concatenate(
        [decoder_in[chip], arrived[:rows_dec], source_states[chip], arrived[rows_dec:]], axis=0
    )
    other_rows = swapped(own_rows, "seq", 1)
    x_all = jnp.concatenate([own_rows[:own], other_rows[:own]], axis=0)
    source_all = jnp.concatenate([own_rows[own:], other_rows[own:]], axis=0)
    cotangent = swapped(out_grad[1 - chip], "seq", 2)

    def whole(weight):
        weight = lax.all_gather(weight, "seq", axis=1, tiled=True)
        return lax.all_gather(weight, "dp", axis=0, tiled=True)

    blocks = [as_blocks(whole(weight)) for weight in narrow]
    qkv = jnp.concatenate(blocks[:3], axis=3)
    later_a = jnp.concatenate(blocks[3:], axis=3)
    later_b = as_blocks(whole(ffn_expand), ffn_expand.shape[1] // PAIR)
    later_c = as_blocks(whole(ffn_reduce))
    gain_block = jnp.pad(norm_gains.astype(f32), ((0, 5), (0, 0)))
    gains = lax.all_gather(gain_block, "seq", axis=0)
    return x_all, source_all, cotangent, qkv, later_a, later_b, later_c, gains


def body(
    decoder_in,
    source_states,
    source_len,
    upsample,
    send_counts,
    self_query,
    self_key,
    self_value,
    self_output,
    cross_query,
    cross_key,
    cross_value,
    cross_output,
    ffn_expand,
    ffn_reduce,
    norm_gains,
    out_grad,
):
    seq_size = lax.axis_size("seq")
    dp_size = lax.axis_size("dp")
    planes = dp_size // 2
    place = lax.axis_index("seq")
    chip = place // 2
    home_count, rows_dec, width = decoder_in.shape
    rows_src = source_states.shape[1]
    pairs = width // PAIR
    own = 2 * rows_dec
    total = 4 * rows_dec
    deep = self_query.shape[0]
    deep_two = ffn_reduce.shape[0]
    wide = ffn_expand.shape[1] // PAIR
    hidden_width = wide * PAIR * seq_size
    all_src = 4 * rows_src
    comm = dp_size == 8

    def pair_rows(rows):
        return (pairs, rows, PAIR)

    narrow = (self_query, self_key, self_value, self_output)
    narrow += (cross_query, cross_key, cross_value, cross_output)
    rows_outs = [
        (pair_rows(own), bf16),
        (pair_rows(total), bf16),
        (pair_rows(total), bf16),
        (pair_rows(own), bf16),
        ((pairs, 2, own, PAIR), bf16),
    ]
    buffers = [VMEM(shape, kind) for shape, kind in rows_outs]
    work = [
        VMEM((total, width), bf16),
        VMEM((width, 3 * PAIR), bf16),
        VMEM((total, PAIR), bf16),
        *buffers,
    ]
    semaphores = [pltpu.SemaphoreType.DMA((96,)), pltpu.SemaphoreType.DMA((96,))]
    if comm:
        cut = (seq_size, 2, planes)
        gathered = [
            ((total, width), bf16),
            ((all_src, width), bf16),
            (cut + (3 * deep, PAIR), bf16),
            (cut + (5 * deep, PAIR), bf16),
            (cut + (wide * deep, PAIR), bf16),
            (cut + (deep_two, PAIR), bf16),
            ((seq_size, 8, PAIR), f32),
        ]
        operands = (source_len, upsample, decoder_in, source_states)
        operands += (*narrow, ffn_expand, ffn_reduce, norm_gains)
        (
            x_all, source_all, qkv, later_a, later_b, later_c, gains,
            q, k, v, mixed, query_extra,
        ) = call(
            partial(open_kernel, True, planes, deep),
            gathered + rows_outs,
            *operands,
            scratch=[
                VMEM((total, width), bf16),
                VMEM(cut + (3 * deep, PAIR), bf16),
                VMEM((seq_size, 8, PAIR), f32),
                *work,
                *semaphores,
                VMEM((5 * deep, PAIR), bf16),
                VMEM((wide * deep, PAIR), bf16),
                VMEM((deep_two, PAIR), bf16),
                VMEM((rows_src, width), bf16),
                VMEM((8, PAIR), f32),
            ],
            smem=2,
            spaces={at: pl.ANY for at in range(2, len(operands) - 1)},
            out_space=pl.ANY,
            params=pltpu.CompilerParams(
                vmem_limit_bytes=VMEM_LIMIT, collective_id=0, has_side_effects=True
            ),
        )
    else:
        x_all, source_all, cotangent, qkv, later_a, later_b, later_c, gains = gather_plain(
            (decoder_in, source_states, out_grad, narrow, ffn_expand, ffn_reduce, norm_gains),
            seq_size,
            dp_size,
        )
        q, k, v, mixed, query_extra = call(
            partial(open_kernel, False, planes, deep),
            rows_outs,
            source_len,
            upsample,
            x_all,
            qkv,
            gains,
            scratch=[*work, *semaphores],
            smem=2,
            out_space=pl.ANY,
        )
    parts = [
        ((seq_size, 2, 4, 5 * width // 8, PAIR), bf16),
        ((seq_size, 2, 4, hidden_width // 8, PAIR), bf16),
        ((seq_size, 2, 4, hidden_width // 8, PAIR), bf16),
    ]
    out_rows, grad_mixed, grad_self, part_a, part_b, part_c, grad_source, dgain = call(
        partial(middle_kernel, comm, planes),
        [
            ((own, width), bf16),
            (pair_rows(own), bf16),
            ((own, width), f32),
            *parts,
            ((all_src, width), bf16),
            ((8, width), f32),
        ],
        source_len,
        upsample,
        send_counts,
        x_all,
        mixed,
        out_grad,
        out_grad if comm else cotangent,
        source_all,
        later_a,
        later_b,
        later_c,
        gains,
        scratch=[
            VMEM((own, width), bf16),
            VMEM(pair_rows(own), bf16),
            VMEM((own, width), bf16),
            VMEM((all_src, width), bf16),
            *[VMEM(*part) for part in parts],
            *[VMEM((width, width), bf16)] * 5,
            VMEM((width, hidden_width), bf16),
            VMEM((hidden_width, width), bf16),
            VMEM(pair_rows(all_src), bf16),
            VMEM(pair_rows(all_src), bf16),
            VMEM((pairs, PAIR, all_src), bf16),
            VMEM((all_src, PAIR), bf16),
            *[VMEM(pair_rows(all_src), bf16)] * 2,
            *[VMEM((own, width), f32)] * 4,
            *[VMEM(pair_rows(own), bf16)] * 4,
            VMEM((2 * pairs, own, PAIR), bf16),
            VMEM((width, own), bf16),
            VMEM((own, width), bf16),
            VMEM((width, own), bf16),
            VMEM((own, width), bf16),
            VMEM((width, own), bf16),
            VMEM((own, width), bf16),
            pltpu.SemaphoreType.DMA((8,)),
            pltpu.SemaphoreType.DMA((6,)),
            pltpu.SemaphoreType.DMA((8,)),
            pltpu.SemaphoreType.DMA((8,)),
        ],
        params=pltpu.CompilerParams(
            vmem_limit_bytes=VMEM_LIMIT, collective_id=2, has_side_effects=True
        )
        if comm
        else PARAMS,
        smem=3,
        spaces={at: pl.ANY for at in range(3, 11)},
        out_spaces={at: pl.ANY for at in range(6)},
    )
    part_q = ((seq_size, 2, 4, 3 * width // 8, PAIR), bf16)
    operands = (source_len, upsample, q, k, v, mixed, grad_mixed, query_extra)
    operands += (x_all, qkv, gains, grad_self, dgain)
    work = [
        VMEM((2, own, PAIR), bf16),
        VMEM((2, total, PAIR), bf16),
        VMEM((2, total, PAIR), bf16),
        VMEM((2, own, PAIR), bf16),
        VMEM((2, own, PAIR), bf16),
        VMEM((2, 2, own, PAIR), bf16),
        VMEM((total, width), bf16),
        VMEM(qkv.shape, bf16),
        VMEM(gains.shape, f32),
        VMEM((own, width), f32),
        VMEM((8, width), f32),
        VMEM((total, 2 * PAIR), bf16),
        VMEM((total, 2 * PAIR), bf16),
        VMEM((PAIR, total), bf16),
        VMEM((width, total), bf16),
        VMEM((total, width), f32),
        VMEM((pairs, total, 2 * PAIR), bf16),
        VMEM((pairs, own, PAIR), bf16),
        VMEM((pairs, width, 3 * PAIR), bf16),
        VMEM(*part_q),
        pltpu.SemaphoreType.DMA((2, 6)),
        *semaphores,
    ]
    everywhere = {at: pl.ANY for at in range(2, 18)}
    if comm:
        heights = [shape[3] for shape, _ in parts]

        def per_piece(lead):
            return [VMEM((*lead, height, PAIR), bf16) for height in heights]

        work += [
            *per_piece((2, 2, planes)),
            *per_piece((2, 2, planes)),
            *per_piece((2, planes)),
            *per_piece((planes,)),
            *per_piece((planes - 1,)),
            VMEM((3, 2, planes, 3 * deep, PAIR), bf16),
            VMEM((planes, 3 * deep, PAIR), bf16),
            VMEM((planes - 1, 3 * deep, PAIR), bf16),
            VMEM((pairs, 8, PAIR), f32),
            VMEM((4, 8, PAIR), f32),
            VMEM((8, PAIR), f32),
            VMEM((planes, 8, PAIR), f32),
            VMEM((2, rows_dec, width), bf16),
            VMEM((2, rows_dec, width), bf16),
            VMEM((rows_dec // BLOCK, BLOCK, width), bf16),
            VMEM((rows_dec, width), f32),
            VMEM((2 * rows_src, width), bf16),
            VMEM((2 * rows_src, width), bf16),
            VMEM((rows_src, width), f32),
        ]
        small = ((deep, PAIR), f32)
        plain = [small] * 8 + [(ffn_expand.shape, f32), (ffn_reduce.shape, f32), ((8, PAIR), f32)]
        outs = call(
            partial(last_kernel, True, planes),
            [
                ((rows_dec, width), bf16),
                ((rows_dec, width), f32),
                ((rows_dec // BLOCK, BLOCK, width), bf16),
                ((rows_src, width), f32),
                ((rows_src, width), bf16),
                *plain,
            ],
            *operands,
            part_a,
            part_b,
            part_c,
            grad_source,
            out_rows,
            scratch=work,
            smem=2,
            spaces=everywhere,
            out_spaces={at: pl.ANY for at in range(5)},
            params=pltpu.CompilerParams(
                vmem_limit_bytes=VMEM_LIMIT, collective_id=1, has_side_effects=True
            ),
        )
        outs = call(
            partial(hand_over_kernel, planes),
            [
                (decoder_in.shape, bf16),
                (decoder_in.shape, f32),
                (source_states.shape, f32),
                *plain[:-1],
                (norm_gains.shape, f32),
            ],
            out_rows,
            *outs,
            scratch=[
                VMEM(decoder_in.shape, bf16),
                VMEM(decoder_in.shape, f32),
                VMEM((rows_dec // BLOCK, BLOCK, width), bf16),
                VMEM(source_states.shape, f32),
                VMEM((rows_src, width), bf16),
                *[VMEM(shape, kind) for shape, kind in plain],
                *[pltpu.SemaphoreType.DMA((17,))] * 2,
            ],
            spaces={at: pl.ANY for at in range(17)},
            out_space=pl.ANY,
        )
        (decoder_out, grad_decoder, grad_src, dwq, dwk, dwv, *rest, dw1, dw2, dgains) = outs
        dwo, dwcq, dwck, dwcv, dwco = rest
    else:
        own_grad, other_grad, part_qkv, dgains = call(
            partial(last_kernel, False, planes),
            [((own, width), f32), ((own, width), bf16), part_q, ((8, width), f32)],
            *operands,
            scratch=work,
            smem=2,
            spaces=everywhere,
        )
        crossing = jnp.concatenate([other_grad, grad_source[2 * rows_src :]], axis=0)
        returned = swapped(crossing, "seq", 1).astype(f32)
        grad_rows = own_grad + returned[:own]
        source_rows = grad_source[: 2 * rows_src].astype(f32) + returned[own:]
        homeward = [grad_rows[rows_dec:].astype(bf16), source_rows[rows_src:].astype(bf16)]
        came = swapped(jnp.concatenate([out_rows[rows_dec:], *homeward], axis=0), "seq", 2)

        def both_sentences(mine, theirs):
            theirs = theirs.astype(mine.dtype)
            return jnp.where(chip == 0, jnp.stack([mine, theirs]), jnp.stack([theirs, mine]))

        decoder_out = both_sentences(out_rows[:rows_dec], came[:rows_dec])
        grad_decoder = both_sentences(grad_rows[:rows_dec], came[rows_dec : 2 * rows_dec])
        grad_src = both_sentences(source_rows[:rows_src], came[2 * rows_dec :])

        def summed(blocks, start, count, chunks=1):
            grad = from_blocks(blocks[:, :, :, start : start + chunks * count], chunks)
            grad = lax.psum_scatter(grad.astype(f32), "dp", scatter_dimension=0, tiled=True)
            return lax.psum_scatter(grad, "seq", scatter_dimension=1, tiled=True)

        step = width // 8
        dwq, dwk, dwv = [summed(part_qkv, at * step, step) for at in range(3)]
        dwo, dwcq, dwck, dwcv, dwco = [summed(part_a, at * step, step) for at in range(5)]
        dw1 = summed(part_b, 0, step, hidden_width // width)
        tall = part_c.reshape(seq_size, 2, 4, hidden_width // 8 // PAIR, PAIR, PAIR)
        dw2 = summed(tall.swapaxes(4, 5).reshape(part_c.shape), 0, hidden_width // 8)
        dgains = lax.psum(dgains, "dp")
        dgains = lax.psum_scatter(dgains, "seq", scatter_dimension=1, tiled=True)
    return (
        decoder_out,
        grad_decoder,
        grad_src,
        dwq,
        dwk,
        dwv,
        dwo,
        dwcq,
        dwck,
        dwcv,
        dwco,
        dw1,
        dw2,
        dgains[:3],
    )


def solution(mesh):
    rows = P("dp", "seq", None)
    weight = P("dp", "seq")
    placed = (rows, rows, P(), P(), P()) + (weight,) * 10 + (P(None, "seq"), rows)
    return jax.shard_map(
        body,
        mesh=mesh,
        in_specs=placed,
        out_specs=(rows, rows, rows) + (weight,) * 10 + (P(None, "seq"),),
        check_vma=False,
    )
```

```python
from functools import partial

import jax
import jax.numpy as jnp
from jax import lax
from jax.experimental import pallas as pl
from jax.experimental.pallas import tpu as pltpu
from jax.sharding import PartitionSpec as P

HEADS = 8
EPSILON = 1e-05
NEGATIVE = -1000000000.0
LOG2E = 1.4426950408889634
LN2 = 0.6931471805599453
GELU_IN = 0.7978845608028654
GELU_CUBE = 0.044715
BLOCK = 256
PAIR = 128

bf16 = jnp.bfloat16
f32 = jnp.float32
VMEM = pltpu.VMEM
VMEM_LIMIT = 60 * 1024 * 1024
PARAMS = pltpu.CompilerParams(vmem_limit_bytes=VMEM_LIMIT)


def dot(left, right):
    return jnp.dot(left, right, preferred_element_type=f32)


def dot_nt(left, right):
    return lax.dot_general(left, right, (((1,), (1,)), ((), ())), preferred_element_type=f32)


def block_at(index, size):
    return pl.ds(pl.multiple_of(index * size, size), size)


def repeat(start, stop, todo, group):
    def step(at, _):
        for part in range(group):
            todo(start + at * group + part)
        return 0

    count, rest = divmod(stop - start, group)
    if count == 1:
        step(0, 0)
    elif count:
        lax.fori_loop(0, count, step, 0)
    for part in range(rest):
        todo(start + count * group + part)


def row_mean(values):
    return jnp.mean(values, axis=-1, keepdims=True)


def normalize(values):
    centred = values - row_mean(values)
    inverse = lax.rsqrt(row_mean(centred * centred) + EPSILON)
    return centred * inverse, inverse


def norm_back(upstream, scaled, inverse, gain):
    inner = upstream * gain
    back = inverse * (inner - row_mean(inner) - scaled * row_mean(inner * scaled))
    return back, jnp.sum(upstream * scaled, axis=0, keepdims=True)


def three_parts(column, lane, last):
    high = column.astype(bf16).astype(f32)
    middle = (column - high).astype(bf16).astype(f32)
    low = column - high - middle
    rest = jnp.where(lane == 3, last, 0.0)
    return jnp.where(
        lane == 0, high, jnp.where(lane == 1, middle, jnp.where(lane == 2, low, rest))
    ).astype(bf16)


def one_head(values, first, head):
    zero = jnp.zeros_like(values)
    return jnp.where(first, values, zero) if head == 0 else jnp.where(first, zero, values)


def attend_pair(query, keys, key_extra, values, lane):
    first = lane < 64
    ones = jnp.where(lane == 3, 1.0, 0.0).astype(bf16)
    keys = jnp.concatenate([keys, key_extra], axis=1)
    values = jnp.concatenate([values, jnp.ones_like(values)], axis=1)
    scores = [
        dot_nt(jnp.concatenate([one_head(query, first, head), ones], axis=1), keys)
        for head in (0, 1)
    ]
    mixed, extras = [], []
    for head in (0, 1):
        peak = jnp.max(scores[head], axis=1, keepdims=True)
        exps = jnp.exp2(scores[head] - peak)
        both = dot(exps.astype(bf16), values)
        total = both[:, PAIR : PAIR + 1]
        mixed.append(both[:, :PAIR] * (1.0 / total))
        extras.append(three_parts(-(peak + jnp.log2(total)), lane, 1.0))
    return jnp.where(first, mixed[0], mixed[1]).astype(bf16), extras


def attend_pair_back(
    query, grad, mixed, query_extra, key_at, value_at, key_columns_at, chunks, put_key, put_value
):
    lane = lax.broadcasted_iota(jnp.int32, query.shape, 1)
    first = lane < 64
    product = grad.astype(f32) * mixed.astype(f32)
    queries = [one_head(query, first, head) for head in (0, 1)]
    grads = [one_head(grad, first, head) for head in (0, 1)]
    long_queries = [jnp.concatenate([queries[h], query_extra[h]], axis=1) for h in (0, 1)]
    long_grads = []
    for head in (0, 1):
        delta = jnp.sum(one_head(product, first, head), axis=1, keepdims=True)
        long_grads.append(
            jnp.concatenate([grads[head], three_parts(-delta, lane, 0.0)], axis=1)
        )
    both_queries = jnp.concatenate(queries, axis=0)
    both_grads = jnp.concatenate(grads, axis=0)
    query_grads = [None, None]
    for chunk in range(chunks):
        keys, values = key_at(chunk), value_at(chunk)
        probs, score_grads = [], []
        for head in (0, 1):
            prob = jnp.exp2(dot_nt(keys, long_queries[head]))
            score_grad = (prob * dot_nt(values, long_grads[head])).astype(bf16)
            probs.append(prob.astype(bf16))
            score_grads.append(score_grad)
            term = dot(key_columns_at(chunk, head), score_grad)
            query_grads[head] = term if chunk == 0 else query_grads[head] + term
        put_value(chunk, dot(jnp.concatenate(probs, axis=1), both_grads))
        put_key(chunk, dot(jnp.concatenate(score_grads, axis=1), both_queries))
    return (jnp.concatenate(query_grads, axis=0) * 0.125).astype(bf16)


def copy_to(source, target, send, receive, partner):
    return pltpu.make_async_remote_copy(
        src_ref=source,
        dst_ref=target,
        send_sem=send,
        recv_sem=receive,
        device_id=partner,
        device_id_type=pl.DeviceIdType.MESH,
    )


def greet(partners):
    for partner in partners:
        pl.semaphore_signal(
            pltpu.get_barrier_semaphore(),
            inc=1,
            device_id=partner,
            device_id_type=pl.DeviceIdType.MESH,
        )


def await_greetings(partners):
    pl.semaphore_wait(pltpu.get_barrier_semaphore(), len(partners))


class Where:
    def __init__(self, planes):
        group, self.place = lax.axis_index("dp"), lax.axis_index("seq")
        self.group = group
        self.chip, self.core = self.place // 2, self.place % 2
        self.plane, self.side = group // 2, group % 2
        self.planes = planes
        self.other_core = self.at(self.chip, 1 - self.core)
        self.other_chip = self.at(1 - self.chip, self.core)
        self.diagonal = self.at(1 - self.chip, 1 - self.core)
        self.other_side = {"dp": self.plane * 2 + 1 - self.side}
        self.other_planes = [
            {"dp": (self.plane + step) % planes * 2 + self.side} for step in range(1, planes)
        ]

    def at(self, chip, core):
        return {"seq": chip * 2 + core}

    def column(self, step):
        return (self.chip + step // 2) % 2 * 2 + (self.core + step % 2) % 2

    def everyone(self):
        return [self.other_core, self.other_chip, self.diagonal, self.other_side] + self.other_planes


class Semaphores:
    def __init__(self, send, receive):
        self.send, self.receive, self.count = send, receive, 0
        self.sent = []

    def remote(self, source, target, partner):
        at = self.count
        self.count += 1
        copy = copy_to(source, target, self.send.at[at], self.receive.at[at], partner)
        self.sent.append(copy)
        return copy

    def local(self, source, target):
        at = self.count
        self.count += 1
        return pltpu.make_async_copy(source, target, self.send.at[at])


def block_places(where_chip, where_core, rows, offset, index, size):
    per = rows // size
    slot = index // per
    block = (where_chip + slot % 2) % 2 * 2 + (where_core + slot // 2) % 2
    return block * rows + index % per * size + offset


def mask_columns(where_chip, where_core, rows, count, size, length, ref):
    lane = lax.broadcasted_iota(jnp.int32, (size, PAIR), 1)
    offset = lax.broadcasted_iota(jnp.int32, (size, PAIR), 0)

    def step(index, _):
        places = block_places(where_chip, where_core, rows, offset, index, size)
        bias = jnp.where(places < length, 0.0, NEGATIVE)
        ref[block_at(index, size), :] = jnp.where(
            lane < 3, 1.0, jnp.where(lane == 3, bias, 0.0)
        ).astype(bf16)
        return 0

    lax.fori_loop(0, count // size, step, 0)


def open_kernel(
    comm,
    planes,
    deep,
    source_len_ref,
    upsample_ref,
    *refs,
):
    if comm:
        (
            decoder_ref, source_ref,
            wq_in, wk_in, wv_in, *later_in, gain_in,
            x_out, source_out, qkv_out, later_a, later_b, later_c, gain_out,
            q_out, k_out, v_out, mixed_out, extra_out,
            x_ref, qkv_ref, gain_ref, hidden_ref, weight_ref, mask_ref,
            q_ref, k_ref, v_ref, mixed_ref, extra_ref, send, receive,
            stage_a, stage_b, stage_c, stage_s, gain_block,
        ) = refs
    else:
        (
            x_ref, qkv_ref, gain_ref,
            q_out, k_out, v_out, mixed_out, extra_out,
            hidden_ref, weight_ref, mask_ref,
            q_ref, k_ref, v_ref, mixed_ref, extra_ref, send, receive,
        ) = refs
    where = Where(planes)
    place, plane, side, chip, core = where.place, where.plane, where.side, where.chip, where.core
    total, width = x_ref.shape
    pairs = width // PAIR
    own = total // 2
    rows = total // 4
    semaphores = Semaphores(send, receive)
    column = where.column

    if comm:
        group = where.group
        x_slots = [x_ref.at[slot * rows : (slot + 1) * rows] for slot in range(4)]
        few = source_ref.shape[1]
        s_slots = [source_out.at[slot * few : (slot + 1) * few] for slot in range(4)]
        local_x = semaphores.local(decoder_ref.at[chip], x_slots[0])
        mine = qkv_ref.at[place, side, plane]
        local_qkv = [
            semaphores.local(ref, mine.at[at * deep : (at + 1) * deep])
            for at, ref in enumerate((wq_in, wk_in, wv_in))
        ]
        first = [local_x, *local_qkv]
        wo_in, wcq_in, wck_in, wcv_in, wco_in, w1_in, w2_in = later_in
        mine_a = later_a.at[place, side, plane]
        mine_b = later_b.at[place, side, plane]
        mine_c = later_c.at[place, side, plane]
        wide = w1_in.shape[1] // PAIR
        local_later = [
            [
                semaphores.local(ref, stage_a.at[at * deep : (at + 1) * deep])
                for at, ref in enumerate((wo_in, wcq_in, wck_in, wcv_in, wco_in))
            ],
            [
                semaphores.local(
                    w1_in.at[:, at * PAIR : (at + 1) * PAIR], stage_b.at[at * deep : (at + 1) * deep]
                )
                for at in range(wide)
            ],
            [semaphores.local(w2_in, stage_c)],
        ]
        stores = [
            semaphores.local(stage_a, mine_a),
            semaphores.local(stage_b, mine_b),
            semaphores.local(stage_c, mine_c),
        ]
        source_load = semaphores.local(source_ref.at[chip], stage_s)
        source_store = semaphores.local(stage_s, s_slots[0])
        greet(where.everyone())
        gain_block[...] = jnp.zeros(gain_block.shape, f32)
        gain_block[0 : gain_in.shape[0], :] = gain_in[...].astype(f32)
        gain_ref[place] = gain_block[...]
        for copy in first + local_later[0] + local_later[1] + local_later[2] + [source_load]:
            copy.start()
        await_greetings(where.everyone())

        cuts = [slice(half * rows // 2, (half + 1) * rows // 2) for half in range(2)]
        x_cross = [
            semaphores.remote(decoder_ref.at[1 - chip, cut], x_slots[1].at[cut], where.other_chip)
            for cut in cuts
        ]
        x_core = semaphores.remote(decoder_ref.at[chip], x_slots[2], where.other_core)
        x_pass = [
            semaphores.remote(x_slots[1].at[cut], x_slots[3].at[cut], where.other_core)
            for cut in cuts
        ]
        s_cross = semaphores.remote(source_ref.at[1 - chip], s_slots[1], where.other_chip)
        s_core = semaphores.remote(source_ref.at[chip], s_slots[2], where.other_core)
        s_pass = semaphores.remote(s_slots[1], s_slots[3], where.other_core)
        gain_sends = [
            semaphores.remote(gain_block, gain_ref.at[place], partner)
            for partner in (where.other_core, where.other_chip, where.diagonal)
        ]
        qkv_planes = [semaphores.remote(mine, mine, partner) for partner in where.other_planes]
        qkv_side = semaphores.remote(
            qkv_ref.at[place, side], qkv_ref.at[place, side], where.other_side
        )
        qkv_core = semaphores.remote(qkv_ref.at[place], qkv_ref.at[place], where.other_core)
        qkv_chip = semaphores.remote(qkv_ref.at[place], qkv_ref.at[place], where.other_chip)
        across = column(2)
        qkv_pass = semaphores.remote(qkv_ref.at[across], qkv_ref.at[across], where.other_core)
        later = []
        for buffer, stage in ((later_a, stage_a), (later_b, stage_b), (later_c, stage_c)):
            block = buffer.at[place, side, plane]
            mine_side, across_side = buffer.at[place, side], buffer.at[across, side]
            if buffer is later_c:
                first = [semaphores.remote(stage, block, where.other_chip)]
                far = buffer.at[across, side, plane]
                second = [
                    semaphores.remote(stage, block, where.other_side),
                    semaphores.remote(far, far, where.other_side),
                ]
                others = [buffer.at[at, 1 - side, plane] for at in (place, across)]
                kept = [(stage, block), (far, far)] + [(one, one) for one in others]
            else:
                first = [semaphores.remote(mine_side, mine_side, where.other_chip)]
                second = []
                if buffer is later_a:
                    second = [
                        semaphores.remote(one, one, where.other_side)
                        for one in (mine_side, across_side)
                    ]
                kept = [(stage, block)]
            later.append(
                dict(
                    planes=[
                        semaphores.remote(one, other, partner)
                        for one, other in kept
                        for partner in where.other_planes
                    ],
                    first=first,
                    second=second,
                    core=[
                        semaphores.remote(buffer.at[at], buffer.at[at], where.other_core)
                        for at in (() if buffer is later_b else (place, across))
                    ],
                )
            )

        def begin(copies):
            for copy in copies:
                copy.start()

        def arrive(copies):
            for copy in copies:
                copy.wait_recv()

        begin(gain_sends)
        for copy in local_qkv:
            copy.wait()
        begin(qkv_planes)
        begin(x_cross)
        x_core.start()
        begin([s_core])
        for copies in local_later:
            for copy in copies:
                copy.wait()
        source_load.wait()
        begin([*stores, source_store])
        a, b, c = later
        begin(c["first"])
        begin(a["planes"])
        begin(b["planes"])

    length = source_len_ref[where.group * 2 + chip] * upsample_ref[where.group * 2 + chip]
    mask_columns(chip, core, rows, total, BLOCK, length, mask_ref)

    def hide(slot, start=0, stop=2):
        gain = jnp.concatenate([gain_ref[at, 0:1, :] for at in range(pairs)], axis=1)

        def step(index):
            at = pl.ds(index * BLOCK + slot * rows, BLOCK)
            scaled, _ = normalize(x_ref[at, :].astype(f32))
            hidden_ref[at, :] = (scaled * gain).astype(bf16)

        repeat(start * rows // (2 * BLOCK), stop * rows // (2 * BLOCK), step, 2)

    def take_weights(pair):
        for part in range(3):
            for at in range(8):
                weight_ref[at * 64 : at * 64 + 64, part * PAIR : (part + 1) * PAIR] = qkv_ref[
                    pair, at % 2, at // 2, part * 64 : part * 64 + 64, :
                ]

    def project(pair, slot, count):
        size = 2 * BLOCK

        def one(index, own_rows):
            at = block_at(index, size)
            both = dot(hidden_ref[at, :], weight_ref[:, PAIR:]).astype(bf16)
            k_ref[pair, at, :] = both[:, :PAIR]
            v_ref[pair, at, :] = both[:, PAIR:]
            if own_rows:
                query = dot(hidden_ref[at, :], weight_ref[:, :PAIR]) * (0.125 * LOG2E)
                q_ref[pair, at, :] = query.astype(bf16)

        first, last = slot * rows // size, (slot + count) * rows // size
        middle = min(max(own // size, first), last)
        repeat(first, middle, partial(one, own_rows=True), 1)
        repeat(middle, last, partial(one, own_rows=False), 1)

    if comm:
        local_x.wait()
        arrive(gain_sends)
        hide(0)
        arrive([x_core])
        hide(2)
        arrive(qkv_planes)
        qkv_side.start()
        arrive([qkv_side])
        begin([qkv_core])
        take_weights(place)
        project(place, 0, 1)
        project(place, 2, 1)
        arrive(x_cross[:1])
        x_pass[0].start()
        hide(1, 0, 1)
        arrive(x_cross[1:])
        x_pass[1].start()
        arrive(a["planes"])
        for copy in [*stores, source_store]:
            copy.wait()
        begin(a["first"])
        arrive(c["first"])
        begin(c["second"])
        begin([qkv_chip])
        hide(1, 1, 2)
        project(place, 1, 1)
        arrive(x_pass)
        hide(3)
        project(place, 3, 1)
    else:
        for slot in range(4):
            hide(slot)
        take_weights(place)
        project(place, 0, 4)

    size = 2 * BLOCK
    blocks = own // size
    lane = lax.broadcasted_iota(jnp.int32, (size, PAIR), 1)

    def outs_of(pair):
        return [
            (q_ref.at[pair], q_out.at[pair]),
            (k_ref.at[pair], k_out.at[pair]),
            (v_ref.at[pair], v_out.at[pair]),
            (mixed_ref.at[pair], mixed_out.at[pair]),
            (extra_ref.at[pair], extra_out.at[pair]),
        ]

    first_out = semaphores.count

    def out_copies(step, pair):
        return [
            pltpu.make_async_copy(source, target, send.at[first_out + step * 5 + at])
            for at, (source, target) in enumerate(outs_of(pair))
        ]

    if comm:
        x_local = pltpu.make_async_copy(x_ref, x_out, send.at[first_out + 20])
        qkv_local = pltpu.make_async_copy(qkv_ref, qkv_out, send.at[first_out + 21])
        gain_local = pltpu.make_async_copy(gain_ref, gain_out, send.at[first_out + 22])
        begin([x_local, gain_local])

    def step(index, _):
        turn = index // blocks
        pair = column(turn)
        if comm:
            @pl.when(index == 1)
            def _():
                arrive(c["second"])
                begin(c["planes"])
                arrive(b["planes"])
                begin(b["first"])
                begin([s_cross])

            @pl.when(index == 2)
            def _():
                arrive([qkv_core])
                arrive(a["first"])
                begin(a["second"])

            @pl.when(index == 4)
            def _():
                arrive([qkv_chip])
                qkv_pass.start()

            @pl.when(index == 5)
            def _():
                arrive(b["first"])
                arrive(a["second"])
                begin(a["core"])

            @pl.when(index == 6)
            def _():
                arrive([qkv_pass])
                qkv_local.start()
                arrive([s_cross])
                s_pass.start()

            @pl.when(index == 7)
            def _():
                arrive(c["planes"])
                begin(c["core"])

        @pl.when((index % blocks == 0) & (index > 0))
        def _():
            take_weights(pair)
            project(pair, 0, 4)

        at = block_at(index % blocks, size)
        mixed, extras = attend_pair(
            q_ref[pair, at, :], k_ref[pair], mask_ref[...], v_ref[pair], lane
        )
        mixed_ref[pair, at, :] = mixed
        extra_ref[pair, 0, at, :] = extras[0]
        extra_ref[pair, 1, at, :] = extras[1]

        @pl.when(index % blocks == blocks - 1)
        def _():
            for copy in out_copies(turn, pair):
                copy.start()

        return 0

    lax.fori_loop(0, pairs * blocks, step, 0)
    if comm:
        arrive([s_core, s_pass])
        for piece in later:
            arrive(piece["core"])
        for copy in semaphores.sent:
            copy.wait_send()
        for copy in (x_local, qkv_local, gain_local):
            copy.wait()
    for turn in range(pairs):
        for copy in out_copies(turn, column(turn)):
            copy.wait()


def whole_weight(ref, blocks, start, count, chunks=1):
    columns, sides, planes = blocks.shape[:3]
    for column in range(columns):
        for side in range(sides):
            for plane in range(planes):
                row = (plane * sides + side) * count
                for chunk in range(chunks):
                    at = (column * chunks + chunk) * PAIR
                    ref[row : row + count, at : at + PAIR] = blocks[
                        column, side, plane, start + chunk * count : start + (chunk + 1) * count, :
                    ]


def to_blocks(blocks, columns, places, start, count, value):
    for column_at, column in enumerate(columns):
        for place_at, (side, plane) in enumerate(places):
            blocks[column, side, plane, start : start + count, :] = value[
                place_at * count : (place_at + 1) * count,
                column_at * PAIR : (column_at + 1) * PAIR,
            ].astype(bf16)


def middle_kernel(
    comm,
    planes,
    source_len_ref,
    upsample_ref,
    send_ref,
    x_any,
    mixed_any,
    cotangent_any,
    cotangent_far,
    source_any,
    later_a,
    later_b,
    later_c,
    gain_blocks,
    out_rows,
    grad_mixed_out,
    grad_self_out,
    part_a,
    part_b,
    part_c,
    grad_source_ref,
    dgain_ref,
    x_ref,
    mixed_ref,
    cotangent_ref,
    source_ref,
    blocks_a,
    blocks_b,
    blocks_c,
    wo_ref,
    wcq_ref,
    wck_ref,
    wcv_ref,
    wco_ref,
    w1_ref,
    w2_ref,
    ck_ref,
    cv_ref,
    ckt_ref,
    cextra_ref,
    dck_ref,
    dcv_ref,
    after_self_s,
    after_cross_s,
    final_s,
    hidden_grad_s,
    qc_s,
    cm_s,
    gcm_s,
    dq_s,
    extra_s,
    hidden_two_t,
    hidden_three_s,
    hidden_three_t,
    grad_ffn_s,
    grad_ffn_t,
    branch_s,
    load,
    store,
    send,
    receive,
):
    rows_own, width = x_ref.shape
    pairs = mixed_ref.shape[0]
    hidden_width = w1_ref.shape[1]
    chunk = hidden_width // pairs
    where = Where(planes)
    chip, core = where.chip, where.core
    half = rows_own // 2
    size = half
    few = source_ref.shape[0]
    deep = width // 8
    place, side, across = where.place, where.side, where.column(2)
    partners = (where.other_core, where.other_chip, where.other_side)
    if comm:
        greet(partners)
    moves = [
        (later_a, blocks_a),
        (source_any, source_ref),
        (x_any.at[:rows_own], x_ref),
        (mixed_any, mixed_ref),
        (cotangent_any.at[chip], cotangent_ref.at[:half]),
        (later_c, blocks_c),
    ]
    if comm:
        moves += [
            (later_b.at[at, side], blocks_b.at[at, side]) for at in (place, across)
        ]
    else:
        moves += [(cotangent_far, cotangent_ref.at[half:]), (later_b, blocks_b)]
    loads = [
        pltpu.make_async_copy(source, target, load.at[at])
        for at, (source, target) in enumerate(moves)
    ]
    for copy in loads:
        copy.start()
    semaphores = Semaphores(send, receive)
    if comm:
        cross_rows = semaphores.remote(
            cotangent_any.at[1 - chip], cotangent_ref.at[half:], where.other_chip
        )
        to_side = [
            semaphores.remote(later_b.at[at, side], blocks_b.at[at, side], where.other_side)
            for at in (place, across)
        ]
        to_core = [
            semaphores.remote(blocks_b.at[at], blocks_b.at[at], where.other_core)
            for at in (place, across)
        ]
    stores = [
        pltpu.make_async_copy(source, target, store.at[at])
        for at, (source, target) in enumerate(
            (
                (grad_ffn_s, out_rows),
                (gcm_s, grad_mixed_out),
                (final_s, grad_self_out),
                (blocks_a, part_a),
                (blocks_b, part_b),
                (blocks_c, part_c),
            )
        )
    ]
    gain_rows = jnp.concatenate([gain_blocks[at] for at in range(pairs)], axis=1)
    gain_two = gain_rows[1:2, :]
    gain_three = gain_rows[2:3, :]
    dgain_ref[...] = jnp.zeros(dgain_ref.shape, f32)

    dp_size = planes * 2
    group, half_way = where.group, planes
    sentence = group * 2 + chip
    src_len = source_len_ref[sentence]
    dec_len = src_len * upsample_ref[sentence]
    moved = chip * send_ref[group]
    holder = (group + moved * half_way) % dp_size
    partner = (holder + half_way) % dp_size

    def tokens_of(slot):
        return source_len_ref[slot] * upsample_ref[slot]

    tokens = (
        tokens_of(holder * 2)
        + tokens_of(holder * 2 + 1) * (1 - send_ref[holder])
        + tokens_of(partner * 2 + 1) * send_ref[partner]
    )
    loss_scale = jnp.full((1, 1), rows_own * 2, f32) / jnp.full((1, 1), tokens, jnp.int32).astype(f32)
    mask_columns(chip, core, few // 4, few, few // 4, src_len, cextra_ref)
    offset = lax.broadcasted_iota(jnp.int32, (size, 1), 0)

    def counted(index):
        place = block_places(chip, core, half, offset, index, size)
        return jnp.where(place < dec_len, 1.0, 0.0)

    def side_by_side(ref, rows):
        return jnp.concatenate([ref[pair, rows, :] for pair in range(pairs)], axis=1)

    def apart(ref, rows, value):
        for pair in range(pairs):
            ref[pair, rows, :] = value[:, pair * PAIR : (pair + 1) * PAIR]

    if comm:
        await_greetings(partners)
        for copy in (*to_side, cross_rows):
            copy.start()
    for copy in loads[:2]:
        copy.wait()
    for at, ref in enumerate((wo_ref, wcq_ref, wck_ref, wcv_ref, wco_ref)):
        whole_weight(ref, blocks_a, at * deep, deep)

    key_rows = dot(source_ref[...], wck_ref[...]).astype(bf16)
    every = pl.ds(0, few)
    apart(ck_ref, every, key_rows)
    for pair in range(pairs):
        ckt_ref[pair] = key_rows[:, pair * PAIR : (pair + 1) * PAIR].T
    apart(cv_ref, every, dot(source_ref[...], wcv_ref[...]).astype(bf16))

    for copy in loads[2:4]:
        copy.wait()

    def first_part(index):
        rows = block_at(index, size)
        after_self = x_ref[rows, :].astype(f32) + dot(side_by_side(mixed_ref, rows), wo_ref[...])
        after_self_s[rows, :] = after_self
        scaled, _ = normalize(after_self)
        hidden = (scaled * gain_two).astype(bf16)
        hidden_two_t[:, rows] = hidden.T
        apart(qc_s, rows, (dot(hidden, wcq_ref[...]) * (0.125 * LOG2E)).astype(bf16))

    repeat(0, rows_own // size, first_part, 1)

    def cross(index):
        pair, rows = index // 2, block_at(index % 2, half)
        mixed, extras = attend_pair(
            qc_s[pair, rows, :], ck_ref[pair], cextra_ref[...], cv_ref[pair],
            lax.broadcasted_iota(jnp.int32, (half, PAIR), 1),
        )
        cm_s[pair, rows, :] = mixed
        extra_s[2 * pair, rows, :] = extras[0]
        extra_s[2 * pair + 1, rows, :] = extras[1]

    repeat(0, 2 * pairs, cross, 1)
    for copy in loads[4:]:
        copy.wait()
    if comm:
        for copy in to_side:
            copy.wait_recv()
        for copy in to_core:
            copy.start()
        cross_rows.wait_recv()
    whole_weight(w2_ref, blocks_c, 0, hidden_width // 8)

    def second_part(index):
        rows = block_at(index, size)
        after_cross = after_self_s[rows, :] + dot(side_by_side(cm_s, rows), wco_ref[...])
        after_cross_s[rows, :] = after_cross
        scaled, _ = normalize(after_cross)
        hidden = (scaled * gain_three).astype(bf16)
        hidden_three_s[rows, :] = hidden
        hidden_three_t[:, rows] = hidden.T
        grad = (cotangent_ref[rows, :].astype(f32) * (counted(index) * loss_scale)).astype(bf16)
        grad_ffn_s[rows, :] = grad
        grad_ffn_t[:, rows] = grad.T

    repeat(0, rows_own // size, second_part, 1)
    if comm:
        for copy in to_core:
            copy.wait_recv()
        for copy in semaphores.sent:
            copy.wait_send()
    whole_weight(w1_ref, blocks_b, 0, deep, hidden_width // width)

    everyone = [(at % 2, at // 2) for at in range(8)]
    deep_two = hidden_width // 8
    halves = [slice(index * size, (index + 1) * size) for index in range(rows_own // size)]

    def bent(expanded, grad_active):
        square = expanded * expanded
        bend = jnp.tanh(expanded * (GELU_IN + (GELU_IN * GELU_CUBE) * square))
        rise = 0.5 + 0.5 * bend
        active = expanded * rise
        slope = rise + active * (1.0 - rise) * (
            2.0 * GELU_IN + (6.0 * GELU_IN * GELU_CUBE) * square
        )
        return active.astype(bf16), (grad_active * slope).astype(bf16)

    final_s[...] = jnp.zeros(final_s.shape, f32)
    hidden_grad_s[...] = jnp.zeros(hidden_grad_s.shape, f32)

    def feed(part, _):
        columns = block_at(part, chunk)
        opened = [
            (
                dot(hidden_three_s[rows, :], w1_ref[:, columns]),
                dot_nt(grad_ffn_s[rows, :], w2_ref[columns, :]),
            )
            for rows in halves
        ]
        actives, grads = [], []
        for rows, one in zip(halves, opened):
            active, grad_expanded = bent(*one)
            final_s[rows, :] += dot(active, w2_ref[columns, :])
            hidden_grad_s[rows, :] += dot_nt(grad_expanded, w1_ref[:, columns])
            actives.append(active)
            grads.append(grad_expanded)
        value = dot(hidden_three_t[...], jnp.concatenate(grads, axis=0))
        for at in range(chunk // PAIR):
            to_blocks(
                blocks_b, [part], everyone, at * deep, deep, value[:, at * PAIR : (at + 1) * PAIR]
            )
        value = dot(grad_ffn_t[...], jnp.concatenate(actives, axis=0))
        for at in range(chunk // PAIR):
            index, row = divmod(at * PAIR, deep_two)
            for column in range(pairs):
                blocks_c[column, index, part, row : row + PAIR, :] = value[
                    column * PAIR : (column + 1) * PAIR, at * PAIR : (at + 1) * PAIR
                ].astype(bf16)
        return 0

    lax.fori_loop(0, hidden_width // chunk, feed, 0)
    stores[4].start()
    stores[5].start()

    def third_part(index):
        rows = block_at(index, size)
        after_cross = after_cross_s[rows, :]
        weight = counted(index)
        grad_final = cotangent_ref[rows, :].astype(f32) * (weight * loss_scale)
        scaled, inverse = normalize(after_cross)
        back, gain_sum = norm_back(hidden_grad_s[rows, :], scaled, inverse, gain_three)
        dgain_ref[2:3, :] += gain_sum
        grad_ffn_s[rows, :] = ((after_cross + final_s[rows, :]) * weight).astype(bf16)
        grad_cross = grad_final + back
        final_s[rows, :] = grad_cross
        branch = grad_cross.astype(bf16)
        hidden_three_s[rows, :] = branch
        apart(gcm_s, rows, dot_nt(branch, wco_ref[...]).astype(bf16))

    repeat(0, rows_own // size, third_part, 1)
    stores[0].start()

    def cross_back(pair, _):
        def put(ref, factor):
            def keep(_, value):
                ref[pair] = (value * factor).astype(bf16)

            return keep

        extra = cextra_ref[...]
        query_grad = attend_pair_back(
            qc_s[pair],
            gcm_s[pair],
            cm_s[pair],
            [extra_s[2 * pair], extra_s[2 * pair + 1]],
            lambda _: jnp.concatenate([ck_ref[pair], extra], axis=1),
            lambda _: jnp.concatenate([cv_ref[pair], extra], axis=1),
            lambda _, head: ckt_ref[pair, 64 * head : 64 * head + 64, :],
            1,
            put(dck_ref, LN2),
            put(dcv_ref, 1.0),
        )
        dq_s[pair] = query_grad.T
        return 0

    lax.fori_loop(0, pairs, cross_back, 0)

    def last_part(index):
        rows = block_at(index, size)
        scaled, inverse = normalize(after_self_s[rows, :])
        upstream = dot_nt(side_by_side(dq_s, rows), wcq_ref[...])
        back, gain_sum = norm_back(upstream, scaled, inverse, gain_two)
        dgain_ref[1:2, :] += gain_sum
        grad_self = final_s[rows, :] + back
        final_s[rows, :] = grad_self
        branch = grad_self.astype(bf16)
        branch_s[rows, :] = branch
        apart(gcm_s, rows, dot_nt(branch, wo_ref[...]).astype(bf16))

    repeat(0, rows_own // size, last_part, 1)
    stores[1].start()
    stores[2].start()

    columns = range(pairs)
    both_sides = [(0, 0), (1, 0)]
    for pair in range(pairs):
        two = [(side, pair) for side, _ in both_sides]
        to_blocks(blocks_a, columns, two, 0, deep, dot(mixed_ref[pair].T, branch_s[...]))
        to_blocks(blocks_a, columns, two, 4 * deep, deep, dot(cm_s[pair].T, hidden_three_s[...]))
    all_rows = pl.ds(0, rows_own)
    to_blocks(
        blocks_a, columns, everyone, deep, deep, dot(hidden_two_t[...], side_by_side(dq_s, all_rows))
    )
    source_t = source_ref[...].T
    key_grad = side_by_side(dck_ref, every)
    value_grad = side_by_side(dcv_ref, every)
    to_blocks(blocks_a, columns, everyone, 2 * deep, deep, dot(source_t, key_grad))
    to_blocks(blocks_a, columns, everyone, 3 * deep, deep, dot(source_t, value_grad))
    stores[3].start()
    grad_source_ref[...] = (
        dot_nt(key_grad, wck_ref[...]) + dot_nt(value_grad, wcv_ref[...])
    ).astype(bf16)
    for copy in stores:
        copy.wait()


def last_kernel(comm, planes, source_len_ref, upsample_ref, *refs):
    (q_any, k_any, v_any, mixed_any, grad_any, extra_any) = refs[:6]
    (x_any, qkv_any, gain_any, grad_self_any, dgain_any) = refs[6:11]
    refs = refs[11:]
    if comm:
        (part_a, part_b, part_c, source_any, rows_any) = refs[:5]
        (rows_land, grad_out, cross_land, source_out, source_far) = refs[5:10]
        (*weight_outs, gain_out) = refs[10:21]
        refs = refs[21:]
    else:
        (own_out, other_out, part_out, gain_out) = refs[:4]
        refs = refs[4:]
    (
        q_s, k_s, v_s, mixed_s, grad_s, extra_s, x_s, qkv_s, gain_s, grad_self_s, dgain_s,
        keys_s, values_s, kt_s, hidden_s, total_s, dkv_s, dq_s, weight_s,
        part_s, load, send, receive,
    ) = refs[:23]
    refs = refs[23:]
    where = Where(planes)
    chip, core, side, plane = where.chip, where.core, where.side, where.plane
    total, width = x_s.shape
    own = total // 2
    rows = total // 4
    pairs = width // PAIR
    deep = width // 8
    chunk = 512
    semaphores = Semaphores(send, receive)
    sentence = where.group * 2 + chip
    length = source_len_ref[sentence] * upsample_ref[sentence]

    def turn_pair(turn):
        return where.column(pairs - 1 - turn)

    def turn_loads(turn):
        pair, slot = turn_pair(turn), turn % 2
        return [
            pltpu.make_async_copy(source.at[pair], target.at[slot], load.at[slot, at])
            for at, (source, target) in enumerate(
                (
                    (q_any, q_s),
                    (k_any, k_s),
                    (v_any, v_s),
                    (mixed_any, mixed_s),
                    (grad_any, grad_s),
                    (extra_any, extra_s),
                )
            )
        ]

    common = [
        semaphores.local(source, target)
        for source, target in ((gain_any, gain_s), (x_any, x_s), (qkv_any, qkv_s))
    ]
    for copy in common:
        copy.start()
    for copy in turn_loads(0):
        copy.start()
    late = [
        semaphores.local(source, target)
        for source, target in ((dgain_any, dgain_s), (grad_self_any, grad_self_s))
    ]

    def begin(copies):
        for copy in copies:
            copy.start()

    def arrive(copies):
        for copy in copies:
            copy.wait_recv()

    if comm:
        (
            keep_a, keep_b, keep_c, core_a, core_b, core_c, far_a, far_b, far_c,
            near_a, near_b, near_c, planes_a, planes_b, planes_c,
            land_q, far_q, planes_q, gain_send, gain_land, gain_far, gain_planes, grads_send,
            grads_land, cross_send, stage, source_s, source_land, stage_s,
        ) = refs
        place, across = where.place, where.column(2)
        pieces = []
        for part, keep, land, far_land, near_land, land_planes, order in (
            (part_a, keep_a, core_a, far_a, near_a, planes_a, "yxz"),
            (part_b, keep_b, core_b, far_b, near_b, planes_b, "yxz"),
            (part_c, keep_c, core_c, far_c, near_c, planes_c, "xyz"),
        ):
            piece = dict(keep=keep, land=land, order=order)
            piece.update(far_land=far_land, near_land=near_land, planes=land_planes)
            piece["load"] = [
                semaphores.local(part.at[place], keep.at[0]),
                semaphores.local(part.at[across], keep.at[1]),
            ]
            piece["core"] = [
                semaphores.remote(part.at[where.column(1)], land.at[0], where.other_core),
                semaphores.remote(part.at[where.column(3)], land.at[1], where.other_core),
            ]
            if order[0] == "y":
                piece["far"] = [
                    semaphores.remote(keep.at[at, 1 - side], far_land.at[at], where.other_side)
                    for at in (0, 1)
                ]
            else:
                piece["far"] = [
                    semaphores.remote(keep.at[1, at], far_land.at[at], where.other_chip)
                    for at in (0, 1)
                ]
            if order == "yxz":
                near = (keep.at[1, side], near_land, where.other_chip)
            else:
                near = (keep.at[0, 1 - side], near_land, where.other_side)
            piece["near"] = [semaphores.remote(*near)]
            piece["last"] = [
                semaphores.remote(
                    keep.at[0, side, (plane + step) % planes],
                    land_planes.at[step - 1],
                    where.other_planes[step - 1],
                )
                for step in range(1, planes)
            ]
            pieces.append(piece)
        a, b, c = pieces
        owners = (where.diagonal, where.other_chip, where.other_core)
        hops = (where.other_core, where.other_chip, where.other_core)
        send_q = [
            semaphores.remote(part_s.at[turn], land_q.at[turn], hops[turn]) for turn in range(3)
        ]
        side_q = semaphores.remote(part_s.at[3, 1 - side], far_q, where.other_side)
        plane_q = [
            semaphores.remote(
                part_s.at[3, side, (plane + step) % planes],
                planes_q.at[step - 1],
                where.other_planes[step - 1],
            )
            for step in range(1, planes)
        ]
        gain_group = [
            semaphores.remote(gain_send.at[where.column(3 - turn)], gain_land.at[turn], owners[turn])
            for turn in range(3)
        ]
        gain_side = semaphores.remote(gain_land.at[3], gain_far, where.other_side)
        gain_last = [
            semaphores.remote(
                gain_planes.at[plane], gain_planes.at[plane], where.other_planes[step - 1]
            )
            for step in range(1, planes)
        ]
        rows_cross = semaphores.remote(rows_any.at[rows:], rows_land, where.other_chip)
        few = source_any.shape[0] // 4
        source_local = semaphores.local(source_any.at[: 2 * few], source_s)
        source_core = semaphores.remote(source_any.at[2 * few :], source_land, where.other_core)
        source_cross = semaphores.remote(source_s.at[few:], source_far, where.other_chip)
        grads_core = [
            semaphores.remote(grads_send.at[at], grads_land.at[at], where.other_core)
            for at in range(2)
        ]
        grads_cross = [
            semaphores.remote(cross_send.at[at], cross_land.at[at], where.other_chip)
            for at in range(rows // BLOCK)
        ]
        stage_out = semaphores.local(stage, grad_out)
        source_own = semaphores.local(stage_s, source_out)
        greet(where.everyone())
        for piece in pieces:
            begin(piece["load"])
        begin([source_local])

        def add_in(ref, land):
            def add(at, _):
                ref[at] = (ref[at].astype(f32) + land[at].astype(f32)).astype(bf16)
                return 0

            lax.fori_loop(0, planes, add, 0)

        def add_core(piece):
            for copy in piece["load"]:
                copy.wait()
            arrive(piece["core"])
            for at in (0, 1):
                for half in (0, 1):
                    add_in(piece["keep"].at[at, half], piece["land"].at[at, half])
            begin(piece["far"])

        def add_far(piece):
            arrive(piece["far"])
            for at in (0, 1):
                if piece["order"][0] == "y":
                    add_in(piece["keep"].at[at, side], piece["far_land"].at[at])
                else:
                    add_in(piece["keep"].at[0, at], piece["far_land"].at[at])
            begin(piece["near"])

        def add_near(piece):
            arrive(piece["near"])
            add_in(piece["keep"].at[0, side], piece["near_land"])
            begin(piece["last"])

        def finish(piece):
            arrive(piece["last"])
            value = piece["keep"][0, side, plane].astype(f32)
            for step in range(planes - 1):
                value = value + piece["planes"][step].astype(f32)
            return value

    mask_columns(chip, core, rows, total, BLOCK, length, values_s.at[:, PAIR:])
    keys_s[:, PAIR:] = values_s[:, PAIR:]
    for copy in late:
        copy.start()
    for copy in common:
        copy.wait()
    gain = jnp.concatenate([gain_s[at, 0:1, :] for at in range(pairs)], axis=1)

    def hide(index):
        at = block_at(index, BLOCK)
        scaled, _ = normalize(x_s[at, :].astype(f32))
        hidden_s[:, at] = (scaled * gain).astype(bf16).T

    repeat(0, total // BLOCK, hide, 2)
    if comm:
        await_greetings(where.everyone())
        for piece in pieces:
            begin(piece["core"])
        begin([source_core, rows_cross])

    def take_weights(turn, pair):
        for part in range(3):
            for at in range(8):
                weight_s[turn, at * 64 : at * 64 + 64, part * PAIR : (part + 1) * PAIR] = qkv_s[
                    pair, at % 2, at // 2, part * 64 : part * 64 + 64, :
                ]

    def upstream(turns, at, own_rows):
        value = None
        for turn in turns:
            term = dot_nt(dkv_s[turn, at, :], weight_s[turn, :, PAIR:])
            if own_rows:
                term = term + dot_nt(dq_s[turn, at, :], weight_s[turn, :, :PAIR])
            value = term if value is None else value + term
        return value

    def before_turn(index):
        if not comm:
            return

        @pl.when(index == 4)
        def _():
            arrive([send_q[0]])
            for half in range(2):
                add_in(part_s.at[1, half], land_q.at[0, half])
            send_q[1].start()

        @pl.when(index == 6)
        def _():
            add_near(c)

    def after_turn(index):
        if not comm:
            return

        @pl.when(index == 1)
        def _():
            add_core(a)
            add_core(c)
            add_core(b)
            source_local.wait()
            arrive([source_core])
            for half in range(2):
                r = slice(half * few, (half + 1) * few)
                value = source_s[r, :].astype(f32) + source_land[r, :].astype(f32)
                source_s[r, :] = value.astype(bf16)
                if half == 0:
                    stage_s[...] = value
            begin([source_cross, source_own])

        @pl.when(index == 3)
        def _():
            add_far(a)
            add_far(c)

        @pl.when(index == 5)
        def _():
            add_far(b)
            add_near(a)

        @pl.when(index == 7)
        def _():
            add_near(b)

    def step(turn, _):
        pair, slot = turn_pair(turn), turn % 2
        for copy in turn_loads(turn):
            copy.wait()

        @pl.when(turn + 1 < pairs)
        def _():
            for copy in turn_loads(turn + 1):
                copy.start()

        keys_s[:, :PAIR] = k_s[slot]
        values_s[:, :PAIR] = v_s[slot]
        kt_s[...] = k_s[slot].T
        take_weights(turn, pair)
        before_turn(2 * turn)

        def part(ref):
            return lambda part: ref[part * chunk : (part + 1) * chunk, :]

        def put(at, factor):
            def keep(part, value):
                dkv_s[turn, part * chunk : (part + 1) * chunk, at : at + PAIR] = (
                    value * factor
                ).astype(bf16)

            return keep

        query_grad = attend_pair_back(
            q_s[slot],
            grad_s[slot],
            mixed_s[slot],
            [extra_s[slot, head] for head in (0, 1)],
            part(keys_s),
            part(values_s),
            lambda part, head: kt_s[64 * head : 64 * head + 64, part * chunk : (part + 1) * chunk],
            total // chunk,
            put(0, LN2),
            put(PAIR, 1.0),
        )
        dq_s[turn] = query_grad.T
        after_turn(2 * turn + 1)
        both = dot(hidden_s[...], dkv_s[turn]).astype(bf16)
        query = dot(hidden_s[:, :own], dq_s[turn]).astype(bf16)
        for at in range(8):
            r = slice(at * deep, (at + 1) * deep)
            for part_at, value in enumerate((query[r, :], both[r, :PAIR], both[r, PAIR:])):
                part_s[turn, at % 2, at // 2, part_at * deep : (part_at + 1) * deep, :] = value

        if comm:
            for sent in (0, 2):

                @pl.when(turn == sent)
                def _():
                    send_q[sent].start()

        @pl.when(turn == pairs - 2)
        def _():
            size = 2 * BLOCK

            def early(row, own_rows):
                r = block_at(row, size)
                total_s[r, :] = upstream(range(pairs - 1), r, own_rows)

            repeat(0, own // size, partial(early, own_rows=True), 1)
            repeat(own // size, total // size, partial(early, own_rows=False), 1)

        return 0

    lax.fori_loop(0, pairs, step, 0)

    def row_back(row, own_rows):
        r = block_at(row, BLOCK)
        scaled, inverse = normalize(x_s[r, :].astype(f32))
        value = total_s[r, :] + upstream([pairs - 1], r, own_rows)
        back, gain_sum = norm_back(value, scaled, inverse, gain)
        dgain_s[0:1, :] += gain_sum
        return r, back

    for copy in late:
        copy.wait()
    per = rows // BLOCK
    if not comm:

        def own_step(row):
            r, back = row_back(row, True)
            grad_self_s[r, :] += back

        def other_step(row):
            r, back = row_back(row, False)
            total_s[r, :] = back

        repeat(0, 2 * per, own_step, per)
        repeat(2 * per, 4 * per, other_step, per)
        own_out[...] = grad_self_s[...]
        other_out[...] = total_s[own:, :].astype(bf16)
        for turn in range(pairs):
            part_out[turn_pair(turn)] = part_s[turn]
        gain_out[...] = dgain_s[...]
        return

    def add_q(at, _):
        for half in range(2):
            value = part_s[3, half, at].astype(f32)
            for turn in (1, 2):
                value = value + land_q[turn, half, at].astype(f32)
            part_s[3, half, at] = value.astype(bf16)
        return 0

    def other_rows(slot):
        def other_step(row):
            _, back = row_back(slot * per + row, False)
            grads_send[slot - 2, block_at(row, BLOCK), :] = back.astype(bf16)

        repeat(0, per, other_step, 1)
        grads_core[slot - 2].start()

    def own_rows(row):
        r, back = row_back(row, True)
        total_s[r, :] = back + grad_self_s[r, :]

    def cross(row):
        r = slice(row * BLOCK, (row + 1) * BLOCK)
        value = total_s[rows + row * BLOCK : rows + (row + 1) * BLOCK, :]
        cross_send[row] = (value + grads_land[1, r, :].astype(f32)).astype(bf16)
        grads_cross[row].start()

    arrive(send_q[1:])
    lax.fori_loop(0, planes, add_q, 0)
    side_q.start()
    other_rows(3)
    repeat(per, 2 * per, own_rows, 1)
    arrive([grads_core[1]])
    cross(0)
    other_rows(2)
    arrive([side_q])
    add_in(part_s.at[3, side], far_q)
    begin(plane_q)
    repeat(0, per, own_rows, 1)
    for at in range(pairs):
        gain_send[at] = dgain_s[:, at * PAIR : (at + 1) * PAIR]
    begin(gain_group)
    for row in range(1, per):
        cross(row)
    arrive(gain_group)
    gain_land[3] = gain_send[place] + gain_land[0] + gain_land[1] + gain_land[2]
    gain_side.start()
    arrive([grads_core[0]])
    stage[...] = total_s[:rows, :] + grads_land[0].astype(f32)
    stage_out.start()
    sums = [finish(piece) for piece in pieces]
    for at in range(5):
        weight_outs[3 + at][...] = sums[0][at * deep : (at + 1) * deep, :]
    for at in range(sums[1].shape[0] // deep):
        weight_outs[8][:, at * PAIR : (at + 1) * PAIR] = sums[1][at * deep : (at + 1) * deep, :]
    for at in range(sums[2].shape[0] // PAIR):
        r = slice(at * PAIR, (at + 1) * PAIR)
        weight_outs[9][r, :] = sums[2][r, :].T
    arrive([gain_side])
    gain_planes[plane] = gain_land[3] + gain_far[...]
    begin(gain_last)
    arrive(plane_q)
    value = part_s[3, side, plane].astype(f32)
    for at in range(planes - 1):
        value = value + planes_q[at].astype(f32)
    for at in range(3):
        weight_outs[at][...] = value[at * deep : (at + 1) * deep, :]
    arrive(gain_last)
    value = gain_planes[0]
    for at in range(1, planes):
        value = value + gain_planes[at]
    gain_out[...] = value
    arrive([rows_cross, source_cross, *grads_cross])
    for copy in (stage_out, source_own):
        copy.wait()
    for copy in semaphores.sent:
        copy.wait_send()


def hand_over_kernel(planes, *refs):
    (rows_any, rows_far, grad_own, grad_far, source_own, source_far, *plain) = refs[:17]
    (decoder_out, grad_out, source_out, *plain_outs) = refs[17:31]
    (rows_s, grad_s, grad_low, source_s, source_low, *plain_s) = refs[31:-2]
    load, store = refs[-2:]
    chip = Where(planes).chip
    rows = rows_s.shape[1]
    moves = [
        (rows_any.at[:rows], rows_s.at[0], rows_s.at[0], decoder_out.at[chip]),
        (rows_far, rows_s.at[1], rows_s.at[1], decoder_out.at[1 - chip]),
        (grad_own, grad_s.at[0], grad_s.at[0], grad_out.at[chip]),
        (grad_far, grad_low, grad_s.at[1], grad_out.at[1 - chip]),
        (source_own, source_s.at[0], source_s.at[0], source_out.at[chip]),
        (source_far, source_low, source_s.at[1], source_out.at[1 - chip]),
    ]
    moves += [
        (one, held, held.at[: other.shape[0]], other)
        for one, held, other in zip(plain, plain_s, plain_outs)
    ]
    loads = [pltpu.make_async_copy(m[0], m[1], load.at[at]) for at, m in enumerate(moves)]
    stores = [pltpu.make_async_copy(m[2], m[3], store.at[at]) for at, m in enumerate(moves)]
    for copy in loads:
        copy.start()
    for at, (one, other) in enumerate(zip(loads, stores)):
        one.wait()
        if at == 3:
            for row in range(grad_low.shape[0]):
                size = grad_low.shape[1]
                grad_s[1, row * size : (row + 1) * size, :] = grad_low[row].astype(f32)
        if at == 5:
            source_s[1] = source_low[...].astype(f32)
        other.start()
    for copy in stores:
        copy.wait()


def call(kernel, outs, *operands, scratch=(), smem=0, params=PARAMS, spaces=None, out_space=VMEM, out_spaces=None):
    spaces = spaces or {}
    out_spaces = out_spaces or {}
    return pl.pallas_call(
        kernel,
        out_shape=[jax.ShapeDtypeStruct(shape, kind) for shape, kind in outs],
        in_specs=[
            pl.BlockSpec(memory_space=pltpu.SMEM if at < smem else spaces.get(at, VMEM))
            for at in range(len(operands))
        ],
        out_specs=[
            pl.BlockSpec(memory_space=out_spaces.get(at, out_space)) for at in range(len(outs))
        ],
        scratch_shapes=list(scratch),
        compiler_params=params,
    )(*operands)


def swapped(value, axis, bit):
    pairs = [(source, source ^ bit) for source in range(lax.axis_size(axis))]
    return lax.ppermute(value, axis, pairs)


def as_blocks(weight, chunks=1):
    height, width = weight.shape
    deep = height // 8
    cut = weight.reshape(4, 2, deep, 4, chunks, PAIR).transpose(3, 1, 0, 4, 2, 5)
    return cut.reshape(4, 2, 4, chunks * deep, PAIR)


def from_blocks(blocks, chunks=1):
    height = blocks.shape[3] // chunks
    cut = blocks.reshape(4, 2, 4, chunks, height, PAIR).transpose(2, 1, 4, 0, 3, 5)
    return cut.reshape(8 * height, 4 * chunks * PAIR)


def gather_plain(arguments, seq_size, dp_size):
    (decoder_in, source_states, out_grad, narrow, ffn_expand, ffn_reduce, norm_gains) = arguments
    chip = lax.axis_index("seq") // 2
    rows_dec = decoder_in.shape[1]
    own = 2 * rows_dec
    outgoing = jnp.concatenate([decoder_in[1 - chip], source_states[1 - chip]], axis=0)
    arrived = swapped(outgoing, "seq", 2)
    own_rows = jnp.concatenate(
        [decoder_in[chip], arrived[:rows_dec], source_states[chip], arrived[rows_dec:]], axis=0
    )
    other_rows = swapped(own_rows, "seq", 1)
    x_all = jnp.concatenate([own_rows[:own], other_rows[:own]], axis=0)
    source_all = jnp.concatenate([own_rows[own:], other_rows[own:]], axis=0)
    cotangent = swapped(out_grad[1 - chip], "seq", 2)

    def whole(weight):
        weight = lax.all_gather(weight, "seq", axis=1, tiled=True)
        return lax.all_gather(weight, "dp", axis=0, tiled=True)

    blocks = [as_blocks(whole(weight)) for weight in narrow]
    qkv = jnp.concatenate(blocks[:3], axis=3)
    later_a = jnp.concatenate(blocks[3:], axis=3)
    later_b = as_blocks(whole(ffn_expand), ffn_expand.shape[1] // PAIR)
    later_c = as_blocks(whole(ffn_reduce))
    gain_block = jnp.pad(norm_gains.astype(f32), ((0, 5), (0, 0)))
    gains = lax.all_gather(gain_block, "seq", axis=0)
    return x_all, source_all, cotangent, qkv, later_a, later_b, later_c, gains


def body(
    decoder_in,
    source_states,
    source_len,
    upsample,
    send_counts,
    self_query,
    self_key,
    self_value,
    self_output,
    cross_query,
    cross_key,
    cross_value,
    cross_output,
    ffn_expand,
    ffn_reduce,
    norm_gains,
    out_grad,
):
    seq_size = lax.axis_size("seq")
    dp_size = lax.axis_size("dp")
    planes = dp_size // 2
    place = lax.axis_index("seq")
    chip = place // 2
    home_count, rows_dec, width = decoder_in.shape
    rows_src = source_states.shape[1]
    pairs = width // PAIR
    own = 2 * rows_dec
    total = 4 * rows_dec
    deep = self_query.shape[0]
    deep_two = ffn_reduce.shape[0]
    wide = ffn_expand.shape[1] // PAIR
    hidden_width = wide * PAIR * seq_size
    all_src = 4 * rows_src
    comm = dp_size == 8

    def pair_rows(rows):
        return (pairs, rows, PAIR)

    narrow = (self_query, self_key, self_value, self_output)
    narrow += (cross_query, cross_key, cross_value, cross_output)
    rows_outs = [
        (pair_rows(own), bf16),
        (pair_rows(total), bf16),
        (pair_rows(total), bf16),
        (pair_rows(own), bf16),
        ((pairs, 2, own, PAIR), bf16),
    ]
    buffers = [VMEM(shape, kind) for shape, kind in rows_outs]
    work = [
        VMEM((total, width), bf16),
        VMEM((width, 3 * PAIR), bf16),
        VMEM((total, PAIR), bf16),
        *buffers,
    ]
    semaphores = [pltpu.SemaphoreType.DMA((96,)), pltpu.SemaphoreType.DMA((96,))]
    if comm:
        cut = (seq_size, 2, planes)
        gathered = [
            ((total, width), bf16),
            ((all_src, width), bf16),
            (cut + (3 * deep, PAIR), bf16),
            (cut + (5 * deep, PAIR), bf16),
            (cut + (wide * deep, PAIR), bf16),
            (cut + (deep_two, PAIR), bf16),
            ((seq_size, 8, PAIR), f32),
        ]
        operands = (source_len, upsample, decoder_in, source_states)
        operands += (*narrow, ffn_expand, ffn_reduce, norm_gains)
        (
            x_all, source_all, qkv, later_a, later_b, later_c, gains,
            q, k, v, mixed, query_extra,
        ) = call(
            partial(open_kernel, True, planes, deep),
            gathered + rows_outs,
            *operands,
            scratch=[
                VMEM((total, width), bf16),
                VMEM(cut + (3 * deep, PAIR), bf16),
                VMEM((seq_size, 8, PAIR), f32),
                *work,
                *semaphores,
                VMEM((5 * deep, PAIR), bf16),
                VMEM((wide * deep, PAIR), bf16),
                VMEM((deep_two, PAIR), bf16),
                VMEM((rows_src, width), bf16),
                VMEM((8, PAIR), f32),
            ],
            smem=2,
            spaces={at: pl.ANY for at in range(2, len(operands) - 1)},
            out_space=pl.ANY,
            params=pltpu.CompilerParams(
                vmem_limit_bytes=VMEM_LIMIT, collective_id=0, has_side_effects=True
            ),
        )
    else:
        x_all, source_all, cotangent, qkv, later_a, later_b, later_c, gains = gather_plain(
            (decoder_in, source_states, out_grad, narrow, ffn_expand, ffn_reduce, norm_gains),
            seq_size,
            dp_size,
        )
        q, k, v, mixed, query_extra = call(
            partial(open_kernel, False, planes, deep),
            rows_outs,
            source_len,
            upsample,
            x_all,
            qkv,
            gains,
            scratch=[*work, *semaphores],
            smem=2,
            out_space=pl.ANY,
        )
    parts = [
        ((seq_size, 2, 4, 5 * width // 8, PAIR), bf16),
        ((seq_size, 2, 4, hidden_width // 8, PAIR), bf16),
        ((seq_size, 2, 4, hidden_width // 8, PAIR), bf16),
    ]
    out_rows, grad_mixed, grad_self, part_a, part_b, part_c, grad_source, dgain = call(
        partial(middle_kernel, comm, planes),
        [
            ((own, width), bf16),
            (pair_rows(own), bf16),
            ((own, width), f32),
            *parts,
            ((all_src, width), bf16),
            ((8, width), f32),
        ],
        source_len,
        upsample,
        send_counts,
        x_all,
        mixed,
        out_grad,
        out_grad if comm else cotangent,
        source_all,
        later_a,
        later_b,
        later_c,
        gains,
        scratch=[
            VMEM((own, width), bf16),
            VMEM(pair_rows(own), bf16),
            VMEM((own, width), bf16),
            VMEM((all_src, width), bf16),
            *[VMEM(*part) for part in parts],
            *[VMEM((width, width), bf16)] * 5,
            VMEM((width, hidden_width), bf16),
            VMEM((hidden_width, width), bf16),
            VMEM(pair_rows(all_src), bf16),
            VMEM(pair_rows(all_src), bf16),
            VMEM((pairs, PAIR, all_src), bf16),
            VMEM((all_src, PAIR), bf16),
            *[VMEM(pair_rows(all_src), bf16)] * 2,
            *[VMEM((own, width), f32)] * 4,
            *[VMEM(pair_rows(own), bf16)] * 4,
            VMEM((2 * pairs, own, PAIR), bf16),
            VMEM((width, own), bf16),
            VMEM((own, width), bf16),
            VMEM((width, own), bf16),
            VMEM((own, width), bf16),
            VMEM((width, own), bf16),
            VMEM((own, width), bf16),
            pltpu.SemaphoreType.DMA((8,)),
            pltpu.SemaphoreType.DMA((6,)),
            pltpu.SemaphoreType.DMA((8,)),
            pltpu.SemaphoreType.DMA((8,)),
        ],
        params=pltpu.CompilerParams(
            vmem_limit_bytes=VMEM_LIMIT, collective_id=2, has_side_effects=True
        )
        if comm
        else PARAMS,
        smem=3,
        spaces={at: pl.ANY for at in range(3, 11)},
        out_spaces={at: pl.ANY for at in range(6)},
    )
    part_q = ((seq_size, 2, 4, 3 * width // 8, PAIR), bf16)
    operands = (source_len, upsample, q, k, v, mixed, grad_mixed, query_extra)
    operands += (x_all, qkv, gains, grad_self, dgain)
    work = [
        VMEM((2, own, PAIR), bf16),
        VMEM((2, total, PAIR), bf16),
        VMEM((2, total, PAIR), bf16),
        VMEM((2, own, PAIR), bf16),
        VMEM((2, own, PAIR), bf16),
        VMEM((2, 2, own, PAIR), bf16),
        VMEM((total, width), bf16),
        VMEM(qkv.shape, bf16),
        VMEM(gains.shape, f32),
        VMEM((own, width), f32),
        VMEM((8, width), f32),
        VMEM((total, 2 * PAIR), bf16),
        VMEM((total, 2 * PAIR), bf16),
        VMEM((PAIR, total), bf16),
        VMEM((width, total), bf16),
        VMEM((total, width), f32),
        VMEM((pairs, total, 2 * PAIR), bf16),
        VMEM((pairs, own, PAIR), bf16),
        VMEM((pairs, width, 3 * PAIR), bf16),
        VMEM(*part_q),
        pltpu.SemaphoreType.DMA((2, 6)),
        *semaphores,
    ]
    everywhere = {at: pl.ANY for at in range(2, 18)}
    if comm:
        heights = [shape[3] for shape, _ in parts]

        def per_piece(lead):
            return [VMEM((*lead, height, PAIR), bf16) for height in heights]

        work += [
            *per_piece((2, 2, planes)),
            *per_piece((2, 2, planes)),
            *per_piece((2, planes)),
            *per_piece((planes,)),
            *per_piece((planes - 1,)),
            VMEM((3, 2, planes, 3 * deep, PAIR), bf16),
            VMEM((planes, 3 * deep, PAIR), bf16),
            VMEM((planes - 1, 3 * deep, PAIR), bf16),
            VMEM((pairs, 8, PAIR), f32),
            VMEM((4, 8, PAIR), f32),
            VMEM((8, PAIR), f32),
            VMEM((planes, 8, PAIR), f32),
            VMEM((2, rows_dec, width), bf16),
            VMEM((2, rows_dec, width), bf16),
            VMEM((rows_dec // BLOCK, BLOCK, width), bf16),
            VMEM((rows_dec, width), f32),
            VMEM((2 * rows_src, width), bf16),
            VMEM((2 * rows_src, width), bf16),
            VMEM((rows_src, width), f32),
        ]
        small = ((deep, PAIR), f32)
        plain = [small] * 8 + [(ffn_expand.shape, f32), (ffn_reduce.shape, f32), ((8, PAIR), f32)]
        outs = call(
            partial(last_kernel, True, planes),
            [
                ((rows_dec, width), bf16),
                ((rows_dec, width), f32),
                ((rows_dec // BLOCK, BLOCK, width), bf16),
                ((rows_src, width), f32),
                ((rows_src, width), bf16),
                *plain,
            ],
            *operands,
            part_a,
            part_b,
            part_c,
            grad_source,
            out_rows,
            scratch=work,
            smem=2,
            spaces=everywhere,
            out_spaces={at: pl.ANY for at in range(5)},
            params=pltpu.CompilerParams(
                vmem_limit_bytes=VMEM_LIMIT, collective_id=1, has_side_effects=True
            ),
        )
        outs = call(
            partial(hand_over_kernel, planes),
            [
                (decoder_in.shape, bf16),
                (decoder_in.shape, f32),
                (source_states.shape, f32),
                *plain[:-1],
                (norm_gains.shape, f32),
            ],
            out_rows,
            *outs,
            scratch=[
                VMEM(decoder_in.shape, bf16),
                VMEM(decoder_in.shape, f32),
                VMEM((rows_dec // BLOCK, BLOCK, width), bf16),
                VMEM(source_states.shape, f32),
                VMEM((rows_src, width), bf16),
                *[VMEM(shape, kind) for shape, kind in plain],
                *[pltpu.SemaphoreType.DMA((17,))] * 2,
            ],
            spaces={at: pl.ANY for at in range(17)},
            out_space=pl.ANY,
        )
        (decoder_out, grad_decoder, grad_src, dwq, dwk, dwv, *rest, dw1, dw2, dgains) = outs
        dwo, dwcq, dwck, dwcv, dwco = rest
    else:
        own_grad, other_grad, part_qkv, dgains = call(
            partial(last_kernel, False, planes),
            [((own, width), f32), ((own, width), bf16), part_q, ((8, width), f32)],
            *operands,
            scratch=work,
            smem=2,
            spaces=everywhere,
        )
        crossing = jnp.concatenate([other_grad, grad_source[2 * rows_src :]], axis=0)
        returned = swapped(crossing, "seq", 1).astype(f32)
        grad_rows = own_grad + returned[:own]
        source_rows = grad_source[: 2 * rows_src].astype(f32) + returned[own:]
        homeward = [grad_rows[rows_dec:].astype(bf16), source_rows[rows_src:].astype(bf16)]
        came = swapped(jnp.concatenate([out_rows[rows_dec:], *homeward], axis=0), "seq", 2)

        def both_sentences(mine, theirs):
            theirs = theirs.astype(mine.dtype)
            return jnp.where(chip == 0, jnp.stack([mine, theirs]), jnp.stack([theirs, mine]))

        decoder_out = both_sentences(out_rows[:rows_dec], came[:rows_dec])
        grad_decoder = both_sentences(grad_rows[:rows_dec], came[rows_dec : 2 * rows_dec])
        grad_src = both_sentences(source_rows[:rows_src], came[2 * rows_dec :])

        def summed(blocks, start, count, chunks=1):
            grad = from_blocks(blocks[:, :, :, start : start + chunks * count], chunks)
            grad = lax.psum_scatter(grad.astype(f32), "dp", scatter_dimension=0, tiled=True)
            return lax.psum_scatter(grad, "seq", scatter_dimension=1, tiled=True)

        step = width // 8
        dwq, dwk, dwv = [summed(part_qkv, at * step, step) for at in range(3)]
        dwo, dwcq, dwck, dwcv, dwco = [summed(part_a, at * step, step) for at in range(5)]
        dw1 = summed(part_b, 0, step, hidden_width // width)
        tall = part_c.reshape(seq_size, 2, 4, hidden_width // 8 // PAIR, PAIR, PAIR)
        dw2 = summed(tall.swapaxes(4, 5).reshape(part_c.shape), 0, hidden_width // 8)
        dgains = lax.psum(dgains, "dp")
        dgains = lax.psum_scatter(dgains, "seq", scatter_dimension=1, tiled=True)
    return (
        decoder_out,
        grad_decoder,
        grad_src,
        dwq,
        dwk,
        dwv,
        dwo,
        dwcq,
        dwck,
        dwcv,
        dwco,
        dw1,
        dw2,
        dgains[:3],
    )


def solution(mesh):
    rows = P("dp", "seq", None)
    weight = P("dp", "seq")
    placed = (rows, rows, P(), P(), P()) + (weight,) * 10 + (P(None, "seq"), rows)
    return jax.shard_map(
        body,
        mesh=mesh,
        in_specs=placed,
        out_specs=(rows, rows, rows) + (weight,) * 10 + (P(None, "seq"),),
        check_vma=False,
    )
```

```python
from functools import partial

import jax
import jax.numpy as jnp
from jax import lax
from jax.experimental import pallas as pl
from jax.experimental.pallas import tpu as pltpu
from jax.sharding import PartitionSpec as P

HEADS = 8
EPSILON = 1e-05
NEGATIVE = -1000000000.0
LOG2E = 1.4426950408889634
LN2 = 0.6931471805599453
GELU_IN = 0.7978845608028654
GELU_CUBE = 0.044715
BLOCK = 256
PAIR = 128

bf16 = jnp.bfloat16
f32 = jnp.float32
VMEM = pltpu.VMEM
VMEM_LIMIT = 60 * 1024 * 1024
PARAMS = pltpu.CompilerParams(vmem_limit_bytes=VMEM_LIMIT)


def dot(left, right):
    return jnp.dot(left, right, preferred_element_type=f32)


def dot_nt(left, right):
    return lax.dot_general(left, right, (((1,), (1,)), ((), ())), preferred_element_type=f32)


def block_at(index, size):
    return pl.ds(pl.multiple_of(index * size, size), size)


def repeat(start, stop, todo, group):
    def step(at, _):
        for part in range(group):
            todo(start + at * group + part)
        return 0

    count, rest = divmod(stop - start, group)
    if count == 1:
        step(0, 0)
    elif count:
        lax.fori_loop(0, count, step, 0)
    for part in range(rest):
        todo(start + count * group + part)


def row_mean(values):
    return jnp.mean(values, axis=-1, keepdims=True)


def normalize(values):
    centred = values - row_mean(values)
    inverse = lax.rsqrt(row_mean(centred * centred) + EPSILON)
    return centred * inverse, inverse


def norm_back(upstream, scaled, inverse, gain):
    inner = upstream * gain
    back = inverse * (inner - row_mean(inner) - scaled * row_mean(inner * scaled))
    return back, jnp.sum(upstream * scaled, axis=0, keepdims=True)


def three_parts(column, lane, last):
    high = column.astype(bf16).astype(f32)
    middle = (column - high).astype(bf16).astype(f32)
    low = column - high - middle
    rest = jnp.where(lane == 3, last, 0.0)
    return jnp.where(
        lane == 0, high, jnp.where(lane == 1, middle, jnp.where(lane == 2, low, rest))
    ).astype(bf16)


def one_head(values, first, head):
    zero = jnp.zeros_like(values)
    return jnp.where(first, values, zero) if head == 0 else jnp.where(first, zero, values)


def attend_pair(query, keys, key_extra, values, lane):
    first = lane < 64
    ones = jnp.where(lane == 3, 1.0, 0.0).astype(bf16)
    keys = jnp.concatenate([keys, key_extra], axis=1)
    values = jnp.concatenate([values, jnp.ones_like(values)], axis=1)
    scores = [
        dot_nt(jnp.concatenate([one_head(query, first, head), ones], axis=1), keys)
        for head in (0, 1)
    ]
    mixed, extras = [], []
    for head in (0, 1):
        peak = jnp.max(scores[head], axis=1, keepdims=True)
        exps = jnp.exp2(scores[head] - peak)
        both = dot(exps.astype(bf16), values)
        total = both[:, PAIR : PAIR + 1]
        mixed.append(both[:, :PAIR] * (1.0 / total))
        extras.append(three_parts(-(peak + jnp.log2(total)), lane, 1.0))
    return jnp.where(first, mixed[0], mixed[1]).astype(bf16), extras


def attend_pair_back(
    query, grad, mixed, query_extra, key_at, value_at, key_columns_at, chunks, put_key, put_value
):
    lane = lax.broadcasted_iota(jnp.int32, query.shape, 1)
    first = lane < 64
    product = grad.astype(f32) * mixed.astype(f32)
    queries = [one_head(query, first, head) for head in (0, 1)]
    grads = [one_head(grad, first, head) for head in (0, 1)]
    long_queries = [jnp.concatenate([queries[h], query_extra[h]], axis=1) for h in (0, 1)]
    long_grads = []
    for head in (0, 1):
        delta = jnp.sum(one_head(product, first, head), axis=1, keepdims=True)
        long_grads.append(
            jnp.concatenate([grads[head], three_parts(-delta, lane, 0.0)], axis=1)
        )
    both_queries = jnp.concatenate(queries, axis=0)
    both_grads = jnp.concatenate(grads, axis=0)
    query_grads = [None, None]
    for chunk in range(chunks):
        keys, values = key_at(chunk), value_at(chunk)
        probs, score_grads = [], []
        for head in (0, 1):
            prob = jnp.exp2(dot_nt(keys, long_queries[head]))
            score_grad = (prob * dot_nt(values, long_grads[head])).astype(bf16)
            probs.append(prob.astype(bf16))
            score_grads.append(score_grad)
            term = dot(key_columns_at(chunk, head), score_grad)
            query_grads[head] = term if chunk == 0 else query_grads[head] + term
        put_value(chunk, dot(jnp.concatenate(probs, axis=1), both_grads))
        put_key(chunk, dot(jnp.concatenate(score_grads, axis=1), both_queries))
    return (jnp.concatenate(query_grads, axis=0) * 0.125).astype(bf16)


def copy_to(source, target, send, receive, partner):
    return pltpu.make_async_remote_copy(
        src_ref=source,
        dst_ref=target,
        send_sem=send,
        recv_sem=receive,
        device_id=partner,
        device_id_type=pl.DeviceIdType.MESH,
    )


def greet(partners):
    for partner in partners:
        pl.semaphore_signal(
            pltpu.get_barrier_semaphore(),
            inc=1,
            device_id=partner,
            device_id_type=pl.DeviceIdType.MESH,
        )


def await_greetings(partners):
    pl.semaphore_wait(pltpu.get_barrier_semaphore(), len(partners))


class Where:
    def __init__(self, planes):
        group, self.place = lax.axis_index("dp"), lax.axis_index("seq")
        self.group = group
        self.chip, self.core = self.place // 2, self.place % 2
        self.plane, self.side = group // 2, group % 2
        self.planes = planes
        self.other_core = self.at(self.chip, 1 - self.core)
        self.other_chip = self.at(1 - self.chip, self.core)
        self.diagonal = self.at(1 - self.chip, 1 - self.core)
        self.other_side = {"dp": self.plane * 2 + 1 - self.side}
        self.other_planes = [
            {"dp": (self.plane + step) % planes * 2 + self.side} for step in range(1, planes)
        ]

    def at(self, chip, core):
        return {"seq": chip * 2 + core}

    def column(self, step):
        return (self.chip + step // 2) % 2 * 2 + (self.core + step % 2) % 2

    def everyone(self):
        return [self.other_core, self.other_chip, self.diagonal, self.other_side] + self.other_planes


class Semaphores:
    def __init__(self, send, receive):
        self.send, self.receive, self.count = send, receive, 0
        self.sent = []

    def remote(self, source, target, partner):
        at = self.count
        self.count += 1
        copy = copy_to(source, target, self.send.at[at], self.receive.at[at], partner)
        self.sent.append(copy)
        return copy

    def local(self, source, target):
        at = self.count
        self.count += 1
        return pltpu.make_async_copy(source, target, self.send.at[at])


def block_places(where_chip, where_core, rows, offset, index, size):
    per = rows // size
    slot = index // per
    block = (where_chip + slot % 2) % 2 * 2 + (where_core + slot // 2) % 2
    return block * rows + index % per * size + offset


def mask_columns(where_chip, where_core, rows, count, size, length, ref):
    lane = lax.broadcasted_iota(jnp.int32, (size, PAIR), 1)
    offset = lax.broadcasted_iota(jnp.int32, (size, PAIR), 0)

    def step(index, _):
        places = block_places(where_chip, where_core, rows, offset, index, size)
        bias = jnp.where(places < length, 0.0, NEGATIVE)
        ref[block_at(index, size), :] = jnp.where(
            lane < 3, 1.0, jnp.where(lane == 3, bias, 0.0)
        ).astype(bf16)
        return 0

    lax.fori_loop(0, count // size, step, 0)


def open_kernel(
    comm,
    planes,
    deep,
    source_len_ref,
    upsample_ref,
    *refs,
):
    if comm:
        (
            decoder_ref, source_ref,
            wq_in, wk_in, wv_in, *later_in, gain_in,
            x_out, source_out, qkv_out, later_a, later_b, later_c, gain_out,
            q_out, k_out, v_out, mixed_out, extra_out,
            x_ref, qkv_ref, gain_ref, hidden_ref, weight_ref, mask_ref,
            q_ref, k_ref, v_ref, mixed_ref, extra_ref, send, receive,
            stage_a, stage_b, stage_c, stage_s, gain_block,
        ) = refs
    else:
        (
            x_ref, qkv_ref, gain_ref,
            q_out, k_out, v_out, mixed_out, extra_out,
            hidden_ref, weight_ref, mask_ref,
            q_ref, k_ref, v_ref, mixed_ref, extra_ref, send, receive,
        ) = refs
    where = Where(planes)
    place, plane, side, chip, core = where.place, where.plane, where.side, where.chip, where.core
    total, width = x_ref.shape
    pairs = width // PAIR
    own = total // 2
    rows = total // 4
    semaphores = Semaphores(send, receive)
    column = where.column

    if comm:
        group = where.group
        x_slots = [x_ref.at[slot * rows : (slot + 1) * rows] for slot in range(4)]
        few = source_ref.shape[1]
        s_slots = [source_out.at[slot * few : (slot + 1) * few] for slot in range(4)]
        local_x = semaphores.local(decoder_ref.at[chip], x_slots[0])
        mine = qkv_ref.at[place, side, plane]
        local_qkv = [
            semaphores.local(ref, mine.at[at * deep : (at + 1) * deep])
            for at, ref in enumerate((wq_in, wk_in, wv_in))
        ]
        first = [local_x, *local_qkv]
        wo_in, wcq_in, wck_in, wcv_in, wco_in, w1_in, w2_in = later_in
        mine_a = later_a.at[place, side, plane]
        mine_b = later_b.at[place, side, plane]
        mine_c = later_c.at[place, side, plane]
        wide = w1_in.shape[1] // PAIR
        local_later = [
            [
                semaphores.local(ref, stage_a.at[at * deep : (at + 1) * deep])
                for at, ref in enumerate((wo_in, wcq_in, wck_in, wcv_in, wco_in))
            ],
            [
                semaphores.local(
                    w1_in.at[:, at * PAIR : (at + 1) * PAIR], stage_b.at[at * deep : (at + 1) * deep]
                )
                for at in range(wide)
            ],
            [semaphores.local(w2_in, stage_c)],
        ]
        stores = [
            semaphores.local(stage_a, mine_a),
            semaphores.local(stage_b, mine_b),
            semaphores.local(stage_c, mine_c),
        ]
        source_load = semaphores.local(source_ref.at[chip], stage_s)
        source_store = semaphores.local(stage_s, s_slots[0])
        greet(where.everyone())
        gain_block[...] = jnp.zeros(gain_block.shape, f32)
        gain_block[0 : gain_in.shape[0], :] = gain_in[...].astype(f32)
        gain_ref[place] = gain_block[...]
        for copy in first + local_later[0] + local_later[1] + local_later[2] + [source_load]:
            copy.start()
        await_greetings(where.everyone())

        cuts = [slice(half * rows // 2, (half + 1) * rows // 2) for half in range(2)]
        x_cross = [
            semaphores.remote(decoder_ref.at[1 - chip, cut], x_slots[1].at[cut], where.other_chip)
            for cut in cuts
        ]
        x_core = semaphores.remote(decoder_ref.at[chip], x_slots[2], where.other_core)
        x_pass = [
            semaphores.remote(x_slots[1].at[cut], x_slots[3].at[cut], where.other_core)
            for cut in cuts
        ]
        s_cross = semaphores.remote(source_ref.at[1 - chip], s_slots[1], where.other_chip)
        s_core = semaphores.remote(source_ref.at[chip], s_slots[2], where.other_core)
        s_pass = semaphores.remote(s_slots[1], s_slots[3], where.other_core)
        gain_sends = [
            semaphores.remote(gain_block, gain_ref.at[place], partner)
            for partner in (where.other_core, where.other_chip, where.diagonal)
        ]
        qkv_planes = [semaphores.remote(mine, mine, partner) for partner in where.other_planes]
        qkv_side = semaphores.remote(
            qkv_ref.at[place, side], qkv_ref.at[place, side], where.other_side
        )
        qkv_core = semaphores.remote(qkv_ref.at[place], qkv_ref.at[place], where.other_core)
        qkv_chip = semaphores.remote(qkv_ref.at[place], qkv_ref.at[place], where.other_chip)
        across = column(2)
        qkv_pass = semaphores.remote(qkv_ref.at[across], qkv_ref.at[across], where.other_core)
        later = []
        for buffer, stage in ((later_a, stage_a), (later_b, stage_b), (later_c, stage_c)):
            block = buffer.at[place, side, plane]
            mine_side, across_side = buffer.at[place, side], buffer.at[across, side]
            if buffer is later_c:
                first = [semaphores.remote(stage, block, where.other_chip)]
                far = buffer.at[across, side, plane]
                second = [
                    semaphores.remote(stage, block, where.other_side),
                    semaphores.remote(far, far, where.other_side),
                ]
                others = [buffer.at[at, 1 - side, plane] for at in (place, across)]
                kept = [(stage, block), (far, far)] + [(one, one) for one in others]
            else:
                first = [semaphores.remote(mine_side, mine_side, where.other_chip)]
                second = []
                if buffer is later_a:
                    second = [
                        semaphores.remote(one, one, where.other_side)
                        for one in (mine_side, across_side)
                    ]
                kept = [(stage, block)]
            later.append(
                dict(
                    planes=[
                        semaphores.remote(one, other, partner)
                        for one, other in kept
                        for partner in where.other_planes
                    ],
                    first=first,
                    second=second,
                    core=[
                        semaphores.remote(buffer.at[at], buffer.at[at], where.other_core)
                        for at in (() if buffer is later_b else (place, across))
                    ],
                )
            )

        def begin(copies):
            for copy in copies:
                copy.start()

        def arrive(copies):
            for copy in copies:
                copy.wait_recv()

        begin(gain_sends)
        for copy in local_qkv:
            copy.wait()
        begin(qkv_planes)
        begin(x_cross)
        x_core.start()
        begin([s_core])
        for copies in local_later:
            for copy in copies:
                copy.wait()
        source_load.wait()
        begin([*stores, source_store])
        a, b, c = later
        begin(c["first"])
        begin(a["planes"])
        begin(b["planes"])

    length = source_len_ref[where.group * 2 + chip] * upsample_ref[where.group * 2 + chip]
    mask_columns(chip, core, rows, total, BLOCK, length, mask_ref)

    def hide(slot, start=0, stop=2):
        gain = jnp.concatenate([gain_ref[at, 0:1, :] for at in range(pairs)], axis=1)

        def step(index):
            at = pl.ds(index * BLOCK + slot * rows, BLOCK)
            scaled, _ = normalize(x_ref[at, :].astype(f32))
            hidden_ref[at, :] = (scaled * gain).astype(bf16)

        repeat(start * rows // (2 * BLOCK), stop * rows // (2 * BLOCK), step, 2)

    def take_weights(pair):
        for part in range(3):
            for at in range(8):
                weight_ref[at * 64 : at * 64 + 64, part * PAIR : (part + 1) * PAIR] = qkv_ref[
                    pair, at % 2, at // 2, part * 64 : part * 64 + 64, :
                ]

    def project(pair, slot, count):
        size = 2 * BLOCK
        for index in range(count * rows // size):
            at = pl.ds(slot * rows + index * size, size)
            both = dot(hidden_ref[at, :], weight_ref[:, PAIR:]).astype(bf16)
            k_ref[pair, at, :] = both[:, :PAIR]
            v_ref[pair, at, :] = both[:, PAIR:]
            if slot * rows + index * size < own:
                query = dot(hidden_ref[at, :], weight_ref[:, :PAIR]) * (0.125 * LOG2E)
                q_ref[pair, at, :] = query.astype(bf16)

    if comm:
        local_x.wait()
        arrive(gain_sends)
        hide(0)
        arrive([x_core])
        hide(2)
        arrive(qkv_planes)
        qkv_side.start()
        arrive([qkv_side])
        begin([qkv_core])
        take_weights(place)
        project(place, 0, 1)
        project(place, 2, 1)
        arrive(x_cross[:1])
        x_pass[0].start()
        hide(1, 0, 1)
        arrive(x_cross[1:])
        x_pass[1].start()
        arrive(a["planes"])
        for copy in [*stores, source_store]:
            copy.wait()
        begin(a["first"])
        arrive(c["first"])
        begin(c["second"])
        begin([qkv_chip])
        hide(1, 1, 2)
        project(place, 1, 1)
        arrive(x_pass)
        hide(3)
        project(place, 3, 1)
    else:
        for slot in range(4):
            hide(slot)
        take_weights(place)
        project(place, 0, 4)

    size = 2 * BLOCK
    blocks = own // size
    lane = lax.broadcasted_iota(jnp.int32, (size, PAIR), 1)

    def outs_of(pair):
        return [
            (q_ref.at[pair], q_out.at[pair]),
            (k_ref.at[pair], k_out.at[pair]),
            (v_ref.at[pair], v_out.at[pair]),
            (mixed_ref.at[pair], mixed_out.at[pair]),
            (extra_ref.at[pair], extra_out.at[pair]),
        ]

    first_out = semaphores.count

    def out_copies(step, pair):
        return [
            pltpu.make_async_copy(source, target, send.at[first_out + step * 5 + at])
            for at, (source, target) in enumerate(outs_of(pair))
        ]

    if comm:
        x_local = pltpu.make_async_copy(x_ref, x_out, send.at[first_out + 20])
        qkv_local = pltpu.make_async_copy(qkv_ref, qkv_out, send.at[first_out + 21])
        gain_local = pltpu.make_async_copy(gain_ref, gain_out, send.at[first_out + 22])
        begin([x_local, gain_local])

    def step(index, _):
        turn = index // blocks
        pair = column(turn)
        if comm:
            @pl.when(index == 1)
            def _():
                arrive(c["second"])
                begin(c["planes"])
                arrive(b["planes"])
                begin(b["first"])
                begin([s_cross])

            @pl.when(index == 2)
            def _():
                arrive([qkv_core])
                arrive(a["first"])
                begin(a["second"])

            @pl.when(index == 4)
            def _():
                arrive([qkv_chip])
                qkv_pass.start()

            @pl.when(index == 5)
            def _():
                arrive(b["first"])
                arrive(a["second"])
                begin(a["core"])

            @pl.when(index == 6)
            def _():
                arrive([qkv_pass])
                qkv_local.start()
                arrive([s_cross])
                s_pass.start()

            @pl.when(index == 7)
            def _():
                arrive(c["planes"])
                begin(c["core"])

        @pl.when((index % blocks == 0) & (index > 0))
        def _():
            take_weights(pair)
            project(pair, 0, 4)

        at = block_at(index % blocks, size)
        mixed, extras = attend_pair(
            q_ref[pair, at, :], k_ref[pair], mask_ref[...], v_ref[pair], lane
        )
        mixed_ref[pair, at, :] = mixed
        extra_ref[pair, 0, at, :] = extras[0]
        extra_ref[pair, 1, at, :] = extras[1]

        @pl.when(index % blocks == blocks - 1)
        def _():
            for copy in out_copies(turn, pair):
                copy.start()

        return 0

    lax.fori_loop(0, pairs * blocks, step, 0)
    if comm:
        arrive([s_core, s_pass])
        for piece in later:
            arrive(piece["core"])
        for copy in semaphores.sent:
            copy.wait_send()
        for copy in (x_local, qkv_local, gain_local):
            copy.wait()
    for turn in range(pairs):
        for copy in out_copies(turn, column(turn)):
            copy.wait()


def whole_weight(ref, blocks, start, count, chunks=1):
    columns, sides, planes = blocks.shape[:3]
    for column in range(columns):
        for side in range(sides):
            for plane in range(planes):
                row = (plane * sides + side) * count
                for chunk in range(chunks):
                    at = (column * chunks + chunk) * PAIR
                    ref[row : row + count, at : at + PAIR] = blocks[
                        column, side, plane, start + chunk * count : start + (chunk + 1) * count, :
                    ]


def to_blocks(blocks, columns, places, start, count, value):
    for column_at, column in enumerate(columns):
        for place_at, (side, plane) in enumerate(places):
            blocks[column, side, plane, start : start + count, :] = value[
                place_at * count : (place_at + 1) * count,
                column_at * PAIR : (column_at + 1) * PAIR,
            ].astype(bf16)


def middle_kernel(
    comm,
    planes,
    source_len_ref,
    upsample_ref,
    send_ref,
    x_any,
    mixed_any,
    cotangent_any,
    cotangent_far,
    source_any,
    later_a,
    later_b,
    later_c,
    gain_blocks,
    out_rows,
    grad_mixed_out,
    grad_self_out,
    part_a,
    part_b,
    part_c,
    grad_source_ref,
    dgain_ref,
    x_ref,
    mixed_ref,
    cotangent_ref,
    source_ref,
    blocks_a,
    blocks_b,
    blocks_c,
    wo_ref,
    wcq_ref,
    wck_ref,
    wcv_ref,
    wco_ref,
    w1_ref,
    w2_ref,
    ck_ref,
    cv_ref,
    ckt_ref,
    cextra_ref,
    dck_ref,
    dcv_ref,
    after_self_s,
    after_cross_s,
    final_s,
    hidden_grad_s,
    qc_s,
    cm_s,
    gcm_s,
    dq_s,
    extra_s,
    hidden_two_t,
    hidden_three_s,
    hidden_three_t,
    grad_ffn_s,
    grad_ffn_t,
    branch_s,
    load,
    store,
    send,
    receive,
):
    rows_own, width = x_ref.shape
    pairs = mixed_ref.shape[0]
    hidden_width = w1_ref.shape[1]
    chunk = hidden_width // pairs
    where = Where(planes)
    chip, core = where.chip, where.core
    half = rows_own // 2
    size = half
    few = source_ref.shape[0]
    deep = width // 8
    place, side, across = where.place, where.side, where.column(2)
    partners = (where.other_core, where.other_chip, where.other_side)
    if comm:
        greet(partners)
    moves = [
        (later_a, blocks_a),
        (source_any, source_ref),
        (x_any.at[:rows_own], x_ref),
        (mixed_any, mixed_ref),
        (cotangent_any.at[chip], cotangent_ref.at[:half]),
        (later_c, blocks_c),
    ]
    if comm:
        moves += [
            (later_b.at[at, side], blocks_b.at[at, side]) for at in (place, across)
        ]
    else:
        moves += [(cotangent_far, cotangent_ref.at[half:]), (later_b, blocks_b)]
    loads = [
        pltpu.make_async_copy(source, target, load.at[at])
        for at, (source, target) in enumerate(moves)
    ]
    for copy in loads:
        copy.start()
    semaphores = Semaphores(send, receive)
    if comm:
        cross_rows = semaphores.remote(
            cotangent_any.at[1 - chip], cotangent_ref.at[half:], where.other_chip
        )
        to_side = [
            semaphores.remote(later_b.at[at, side], blocks_b.at[at, side], where.other_side)
            for at in (place, across)
        ]
        to_core = [
            semaphores.remote(blocks_b.at[at], blocks_b.at[at], where.other_core)
            for at in (place, across)
        ]
    stores = [
        pltpu.make_async_copy(source, target, store.at[at])
        for at, (source, target) in enumerate(
            (
                (grad_ffn_s, out_rows),
                (gcm_s, grad_mixed_out),
                (final_s, grad_self_out),
                (blocks_a, part_a),
                (blocks_b, part_b),
                (blocks_c, part_c),
            )
        )
    ]
    gain_rows = jnp.concatenate([gain_blocks[at] for at in range(pairs)], axis=1)
    gain_two = gain_rows[1:2, :]
    gain_three = gain_rows[2:3, :]
    dgain_ref[...] = jnp.zeros(dgain_ref.shape, f32)

    dp_size = planes * 2
    group, half_way = where.group, planes
    sentence = group * 2 + chip
    src_len = source_len_ref[sentence]
    dec_len = src_len * upsample_ref[sentence]
    moved = chip * send_ref[group]
    holder = (group + moved * half_way) % dp_size
    partner = (holder + half_way) % dp_size

    def tokens_of(slot):
        return source_len_ref[slot] * upsample_ref[slot]

    tokens = (
        tokens_of(holder * 2)
        + tokens_of(holder * 2 + 1) * (1 - send_ref[holder])
        + tokens_of(partner * 2 + 1) * send_ref[partner]
    )
    loss_scale = jnp.full((1, 1), rows_own * 2, f32) / jnp.full((1, 1), tokens, jnp.int32).astype(f32)
    mask_columns(chip, core, few // 4, few, few // 4, src_len, cextra_ref)
    offset = lax.broadcasted_iota(jnp.int32, (size, 1), 0)

    def counted(index):
        place = block_places(chip, core, half, offset, index, size)
        return jnp.where(place < dec_len, 1.0, 0.0)

    def side_by_side(ref, rows):
        return jnp.concatenate([ref[pair, rows, :] for pair in range(pairs)], axis=1)

    def apart(ref, rows, value):
        for pair in range(pairs):
            ref[pair, rows, :] = value[:, pair * PAIR : (pair + 1) * PAIR]

    if comm:
        await_greetings(partners)
        for copy in (*to_side, cross_rows):
            copy.start()
    for copy in loads[:2]:
        copy.wait()
    for at, ref in enumerate((wo_ref, wcq_ref, wck_ref, wcv_ref, wco_ref)):
        whole_weight(ref, blocks_a, at * deep, deep)

    key_rows = dot(source_ref[...], wck_ref[...]).astype(bf16)
    every = pl.ds(0, few)
    apart(ck_ref, every, key_rows)
    for pair in range(pairs):
        ckt_ref[pair] = key_rows[:, pair * PAIR : (pair + 1) * PAIR].T
    apart(cv_ref, every, dot(source_ref[...], wcv_ref[...]).astype(bf16))

    for copy in loads[2:4]:
        copy.wait()

    def first_part(index):
        rows = pl.ds(index * size, size)
        after_self = x_ref[rows, :].astype(f32) + dot(side_by_side(mixed_ref, rows), wo_ref[...])
        after_self_s[rows, :] = after_self
        scaled, _ = normalize(after_self)
        hidden = (scaled * gain_two).astype(bf16)
        hidden_two_t[:, rows] = hidden.T
        apart(qc_s, rows, (dot(hidden, wcq_ref[...]) * (0.125 * LOG2E)).astype(bf16))

    repeat(0, rows_own // size, first_part, rows_own // size)

    def cross(index):
        pair, rows = index // 2, block_at(index % 2, half)
        mixed, extras = attend_pair(
            qc_s[pair, rows, :], ck_ref[pair], cextra_ref[...], cv_ref[pair],
            lax.broadcasted_iota(jnp.int32, (half, PAIR), 1),
        )
        cm_s[pair, rows, :] = mixed
        extra_s[2 * pair, rows, :] = extras[0]
        extra_s[2 * pair + 1, rows, :] = extras[1]

    repeat(0, 2 * pairs, cross, 4)
    for copy in loads[4:]:
        copy.wait()
    if comm:
        for copy in to_side:
            copy.wait_recv()
        for copy in to_core:
            copy.start()
        cross_rows.wait_recv()
    whole_weight(w2_ref, blocks_c, 0, hidden_width // 8)

    def second_part(index):
        rows = pl.ds(index * size, size)
        after_cross = after_self_s[rows, :] + dot(side_by_side(cm_s, rows), wco_ref[...])
        after_cross_s[rows, :] = after_cross
        scaled, _ = normalize(after_cross)
        hidden = (scaled * gain_three).astype(bf16)
        hidden_three_s[rows, :] = hidden
        hidden_three_t[:, rows] = hidden.T
        grad = (cotangent_ref[rows, :].astype(f32) * (counted(index) * loss_scale)).astype(bf16)
        grad_ffn_s[rows, :] = grad
        grad_ffn_t[:, rows] = grad.T

    repeat(0, rows_own // size, second_part, rows_own // size)
    if comm:
        for copy in to_core:
            copy.wait_recv()
        for copy in semaphores.sent:
            copy.wait_send()
    whole_weight(w1_ref, blocks_b, 0, deep, hidden_width // width)

    everyone = [(at % 2, at // 2) for at in range(8)]
    deep_two = hidden_width // 8
    halves = [slice(index * size, (index + 1) * size) for index in range(rows_own // size)]

    def opened(part, rows):
        columns = slice(part * chunk, (part + 1) * chunk)
        return (
            dot(hidden_three_s[rows, :], w1_ref[:, columns]),
            dot_nt(grad_ffn_s[rows, :], w2_ref[columns, :]),
        )

    def bent(expanded, grad_active):
        square = expanded * expanded
        bend = jnp.tanh(expanded * (GELU_IN + (GELU_IN * GELU_CUBE) * square))
        rise = 0.5 + 0.5 * bend
        active = expanded * rise
        slope = rise + active * (1.0 - rise) * (
            2.0 * GELU_IN + (6.0 * GELU_IN * GELU_CUBE) * square
        )
        return active.astype(bf16), (grad_active * slope).astype(bf16)

    def closed(part, rows, active, grad_expanded):
        columns = slice(part * chunk, (part + 1) * chunk)
        final = dot(active, w2_ref[columns, :])
        hidden_grad = dot_nt(grad_expanded, w1_ref[:, columns])
        if part == 0:
            final_s[rows, :] = final
            hidden_grad_s[rows, :] = hidden_grad
        else:
            final_s[rows, :] += final
            hidden_grad_s[rows, :] += hidden_grad

    def weights_of(part, actives, grads):
        value = dot(hidden_three_t[...], jnp.concatenate(grads, axis=0))
        for at in range(chunk // PAIR):
            to_blocks(
                blocks_b, [part], everyone, at * deep, deep, value[:, at * PAIR : (at + 1) * PAIR]
            )
        value = dot(grad_ffn_t[...], jnp.concatenate(actives, axis=0))
        for at in range(chunk // PAIR):
            row = part * chunk + at * PAIR
            index = row // deep_two
            for column in range(pairs):
                blocks_c[
                    column, index % 2, index // 2, row % deep_two : row % deep_two + PAIR, :
                ] = value[column * PAIR : (column + 1) * PAIR, at * PAIR : (at + 1) * PAIR].astype(
                    bf16
                )

    units = [(part, rows) for part in range(hidden_width // chunk) for rows in halves]
    ahead = opened(*units[0])
    done = []
    for at, (part, rows) in enumerate(units):
        now = ahead
        if at + 1 < len(units):
            ahead = opened(*units[at + 1])
        active, grad_expanded = bent(*now)
        closed(part, rows, active, grad_expanded)
        done.append((active, grad_expanded))
        if len(done) == len(halves):
            weights_of(part, [one for one, _ in done], [other for _, other in done])
            done = []
    stores[4].start()
    stores[5].start()

    def third_part(index):
        rows = pl.ds(index * size, size)
        after_cross = after_cross_s[rows, :]
        weight = counted(index)
        grad_final = cotangent_ref[rows, :].astype(f32) * (weight * loss_scale)
        scaled, inverse = normalize(after_cross)
        back, gain_sum = norm_back(hidden_grad_s[rows, :], scaled, inverse, gain_three)
        dgain_ref[2:3, :] += gain_sum
        grad_ffn_s[rows, :] = ((after_cross + final_s[rows, :]) * weight).astype(bf16)
        grad_cross = grad_final + back
        final_s[rows, :] = grad_cross
        branch = grad_cross.astype(bf16)
        hidden_three_s[rows, :] = branch
        apart(gcm_s, rows, dot_nt(branch, wco_ref[...]).astype(bf16))

    repeat(0, rows_own // size, third_part, rows_own // size)
    stores[0].start()

    def cross_back(pair, _):
        def put(ref, factor):
            def keep(_, value):
                ref[pair] = (value * factor).astype(bf16)

            return keep

        extra = cextra_ref[...]
        query_grad = attend_pair_back(
            qc_s[pair],
            gcm_s[pair],
            cm_s[pair],
            [extra_s[2 * pair], extra_s[2 * pair + 1]],
            lambda _: jnp.concatenate([ck_ref[pair], extra], axis=1),
            lambda _: jnp.concatenate([cv_ref[pair], extra], axis=1),
            lambda _, head: ckt_ref[pair, 64 * head : 64 * head + 64, :],
            1,
            put(dck_ref, LN2),
            put(dcv_ref, 1.0),
        )
        dq_s[pair] = query_grad.T
        return 0

    lax.fori_loop(0, pairs, cross_back, 0)

    def last_part(index):
        rows = pl.ds(index * size, size)
        scaled, inverse = normalize(after_self_s[rows, :])
        upstream = dot_nt(side_by_side(dq_s, rows), wcq_ref[...])
        back, gain_sum = norm_back(upstream, scaled, inverse, gain_two)
        dgain_ref[1:2, :] += gain_sum
        grad_self = final_s[rows, :] + back
        final_s[rows, :] = grad_self
        branch = grad_self.astype(bf16)
        branch_s[rows, :] = branch
        apart(gcm_s, rows, dot_nt(branch, wo_ref[...]).astype(bf16))

    repeat(0, rows_own // size, last_part, rows_own // size)
    stores[1].start()
    stores[2].start()

    columns = range(pairs)
    both_sides = [(0, 0), (1, 0)]
    for pair in range(pairs):
        two = [(side, pair) for side, _ in both_sides]
        to_blocks(blocks_a, columns, two, 0, deep, dot(mixed_ref[pair].T, branch_s[...]))
        to_blocks(blocks_a, columns, two, 4 * deep, deep, dot(cm_s[pair].T, hidden_three_s[...]))
    all_rows = pl.ds(0, rows_own)
    to_blocks(
        blocks_a, columns, everyone, deep, deep, dot(hidden_two_t[...], side_by_side(dq_s, all_rows))
    )
    source_t = source_ref[...].T
    key_grad = side_by_side(dck_ref, every)
    value_grad = side_by_side(dcv_ref, every)
    to_blocks(blocks_a, columns, everyone, 2 * deep, deep, dot(source_t, key_grad))
    to_blocks(blocks_a, columns, everyone, 3 * deep, deep, dot(source_t, value_grad))
    stores[3].start()
    grad_source_ref[...] = (
        dot_nt(key_grad, wck_ref[...]) + dot_nt(value_grad, wcv_ref[...])
    ).astype(bf16)
    for copy in stores:
        copy.wait()


def last_kernel(comm, planes, source_len_ref, upsample_ref, *refs):
    (q_any, k_any, v_any, mixed_any, grad_any, extra_any) = refs[:6]
    (x_any, qkv_any, gain_any, grad_self_any, dgain_any) = refs[6:11]
    refs = refs[11:]
    if comm:
        (part_a, part_b, part_c, source_any, rows_any) = refs[:5]
        (rows_land, grad_out, cross_land, source_out, source_far) = refs[5:10]
        (*weight_outs, gain_out) = refs[10:21]
        refs = refs[21:]
    else:
        (own_out, other_out, part_out, gain_out) = refs[:4]
        refs = refs[4:]
    (
        q_s, k_s, v_s, mixed_s, grad_s, extra_s, x_s, qkv_s, gain_s, grad_self_s, dgain_s,
        keys_s, values_s, kt_s, hidden_s, total_s, dkv_s, dq_s, weight_s,
        part_s, load, send, receive,
    ) = refs[:23]
    refs = refs[23:]
    where = Where(planes)
    chip, core, side, plane = where.chip, where.core, where.side, where.plane
    total, width = x_s.shape
    own = total // 2
    rows = total // 4
    pairs = width // PAIR
    deep = width // 8
    chunk = 512
    semaphores = Semaphores(send, receive)
    sentence = where.group * 2 + chip
    length = source_len_ref[sentence] * upsample_ref[sentence]

    def turn_pair(turn):
        return where.column(pairs - 1 - turn)

    def turn_loads(turn):
        pair, slot = turn_pair(turn), turn % 2
        return [
            pltpu.make_async_copy(source.at[pair], target.at[slot], load.at[slot, at])
            for at, (source, target) in enumerate(
                (
                    (q_any, q_s),
                    (k_any, k_s),
                    (v_any, v_s),
                    (mixed_any, mixed_s),
                    (grad_any, grad_s),
                    (extra_any, extra_s),
                )
            )
        ]

    common = [
        semaphores.local(source, target)
        for source, target in ((gain_any, gain_s), (x_any, x_s), (qkv_any, qkv_s))
    ]
    for copy in common:
        copy.start()
    for copy in turn_loads(0):
        copy.start()
    late = [
        semaphores.local(source, target)
        for source, target in ((dgain_any, dgain_s), (grad_self_any, grad_self_s))
    ]

    def begin(copies):
        for copy in copies:
            copy.start()

    def arrive(copies):
        for copy in copies:
            copy.wait_recv()

    if comm:
        (
            keep_a, keep_b, keep_c, core_a, core_b, core_c, far_a, far_b, far_c,
            near_a, near_b, near_c, planes_a, planes_b, planes_c,
            land_q, far_q, planes_q, gain_send, gain_land, gain_far, gain_planes, grads_send,
            grads_land, cross_send, stage, source_s, source_land, stage_s,
        ) = refs
        place, across = where.place, where.column(2)
        pieces = []
        for part, keep, land, far_land, near_land, land_planes, order in (
            (part_a, keep_a, core_a, far_a, near_a, planes_a, "yxz"),
            (part_b, keep_b, core_b, far_b, near_b, planes_b, "yxz"),
            (part_c, keep_c, core_c, far_c, near_c, planes_c, "xyz"),
        ):
            piece = dict(keep=keep, land=land, order=order)
            piece.update(far_land=far_land, near_land=near_land, planes=land_planes)
            piece["load"] = [
                semaphores.local(part.at[place], keep.at[0]),
                semaphores.local(part.at[across], keep.at[1]),
            ]
            piece["core"] = [
                semaphores.remote(part.at[where.column(1)], land.at[0], where.other_core),
                semaphores.remote(part.at[where.column(3)], land.at[1], where.other_core),
            ]
            if order[0] == "y":
                piece["far"] = [
                    semaphores.remote(keep.at[at, 1 - side], far_land.at[at], where.other_side)
                    for at in (0, 1)
                ]
            else:
                piece["far"] = [
                    semaphores.remote(keep.at[1, at], far_land.at[at], where.other_chip)
                    for at in (0, 1)
                ]
            if order == "yxz":
                near = (keep.at[1, side], near_land, where.other_chip)
            else:
                near = (keep.at[0, 1 - side], near_land, where.other_side)
            piece["near"] = [semaphores.remote(*near)]
            piece["last"] = [
                semaphores.remote(
                    keep.at[0, side, (plane + step) % planes],
                    land_planes.at[step - 1],
                    where.other_planes[step - 1],
                )
                for step in range(1, planes)
            ]
            pieces.append(piece)
        a, b, c = pieces
        owners = (where.diagonal, where.other_chip, where.other_core)
        hops = (where.other_core, where.other_chip, where.other_core)
        send_q = [
            semaphores.remote(part_s.at[turn], land_q.at[turn], hops[turn]) for turn in range(3)
        ]
        side_q = semaphores.remote(part_s.at[3, 1 - side], far_q, where.other_side)
        plane_q = [
            semaphores.remote(
                part_s.at[3, side, (plane + step) % planes],
                planes_q.at[step - 1],
                where.other_planes[step - 1],
            )
            for step in range(1, planes)
        ]
        gain_group = [
            semaphores.remote(gain_send.at[where.column(3 - turn)], gain_land.at[turn], owners[turn])
            for turn in range(3)
        ]
        gain_side = semaphores.remote(gain_land.at[3], gain_far, where.other_side)
        gain_last = [
            semaphores.remote(
                gain_planes.at[plane], gain_planes.at[plane], where.other_planes[step - 1]
            )
            for step in range(1, planes)
        ]
        rows_cross = semaphores.remote(rows_any.at[rows:], rows_land, where.other_chip)
        few = source_any.shape[0] // 4
        source_local = semaphores.local(source_any.at[: 2 * few], source_s)
        source_core = semaphores.remote(source_any.at[2 * few :], source_land, where.other_core)
        source_cross = semaphores.remote(source_s.at[few:], source_far, where.other_chip)
        grads_core = [
            [
                semaphores.remote(grads_send.at[at, cut], grads_land.at[at, cut], where.other_core)
                for cut in (pl.ds(row * BLOCK, BLOCK) for row in range(rows // BLOCK))
            ]
            for at in range(2)
        ]
        grads_cross = [
            semaphores.remote(cross_send.at[at], cross_land.at[at], where.other_chip)
            for at in range(rows // BLOCK)
        ]
        stage_out = semaphores.local(stage, grad_out)
        source_own = semaphores.local(stage_s, source_out)
        greet(where.everyone())
        for piece in pieces:
            begin(piece["load"])
        begin([source_local])

        def add_in(ref, land):
            def add(at, _):
                ref[at] = (ref[at].astype(f32) + land[at].astype(f32)).astype(bf16)
                return 0

            lax.fori_loop(0, planes, add, 0)

        def add_core(piece):
            for copy in piece["load"]:
                copy.wait()
            arrive(piece["core"])
            for at in (0, 1):
                for half in (0, 1):
                    add_in(piece["keep"].at[at, half], piece["land"].at[at, half])
            begin(piece["far"])

        def add_far(piece):
            arrive(piece["far"])
            for at in (0, 1):
                if piece["order"][0] == "y":
                    add_in(piece["keep"].at[at, side], piece["far_land"].at[at])
                else:
                    add_in(piece["keep"].at[0, at], piece["far_land"].at[at])
            begin(piece["near"])

        def add_near(piece):
            arrive(piece["near"])
            add_in(piece["keep"].at[0, side], piece["near_land"])
            begin(piece["last"])

        def finish(piece):
            arrive(piece["last"])
            value = piece["keep"][0, side, plane].astype(f32)
            for step in range(planes - 1):
                value = value + piece["planes"][step].astype(f32)
            return value

    mask_columns(chip, core, rows, total, BLOCK, length, values_s.at[:, PAIR:])
    keys_s[:, PAIR:] = values_s[:, PAIR:]
    for copy in late:
        copy.start()
    for copy in common:
        copy.wait()
    gain = jnp.concatenate([gain_s[at, 0:1, :] for at in range(pairs)], axis=1)

    def hide(index):
        at = block_at(index, BLOCK)
        scaled, _ = normalize(x_s[at, :].astype(f32))
        hidden_s[:, at] = (scaled * gain).astype(bf16).T

    repeat(0, total // BLOCK, hide, 4)
    if comm:
        await_greetings(where.everyone())
        for piece in pieces:
            begin(piece["core"])
        begin([source_core, rows_cross])

    def take_weights(turn, pair):
        for part in range(3):
            for at in range(8):
                weight_s[turn, at * 64 : at * 64 + 64, part * PAIR : (part + 1) * PAIR] = qkv_s[
                    pair, at % 2, at // 2, part * 64 : part * 64 + 64, :
                ]

    def upstream(turns, at, own_rows):
        value = None
        for turn in turns:
            term = dot_nt(dkv_s[turn, at, :], weight_s[turn, :, PAIR:])
            if own_rows:
                term = term + dot_nt(dq_s[turn, at, :], weight_s[turn, :, :PAIR])
            value = term if value is None else value + term
        return value

    def comm_steps(index):
        if not comm:
            return

        @pl.when(index == 1)
        def _():
            add_core(a)
            add_core(c)
            add_core(b)
            source_local.wait()
            arrive([source_core])
            for half in range(2):
                r = slice(half * few, (half + 1) * few)
                value = source_s[r, :].astype(f32) + source_land[r, :].astype(f32)
                source_s[r, :] = value.astype(bf16)
                if half == 0:
                    stage_s[...] = value
            begin([source_cross, source_own])

        @pl.when(index == 3)
        def _():
            add_far(a)
            add_far(c)

        @pl.when(index == 4)
        def _():
            arrive([send_q[0]])
            for half in range(2):
                add_in(part_s.at[1, half], land_q.at[0, half])
            send_q[1].start()

        @pl.when(index == 5)
        def _():
            add_far(b)
            add_near(a)

        @pl.when(index == 6)
        def _():
            add_near(c)

        @pl.when(index == 7)
        def _():
            add_near(b)


    def step(turn, _):
        pair, slot = turn_pair(turn), turn % 2
        for copy in turn_loads(turn):
            copy.wait()

        @pl.when(turn + 1 < pairs)
        def _():
            for copy in turn_loads(turn + 1):
                copy.start()

        keys_s[:, :PAIR] = k_s[slot]
        values_s[:, :PAIR] = v_s[slot]
        kt_s[...] = k_s[slot].T
        take_weights(turn, pair)
        comm_steps(2 * turn)

        def part(ref):
            return lambda part: ref[part * chunk : (part + 1) * chunk, :]

        def put(at, factor):
            def keep(part, value):
                dkv_s[turn, part * chunk : (part + 1) * chunk, at : at + PAIR] = (
                    value * factor
                ).astype(bf16)

            return keep

        query_grad = attend_pair_back(
            q_s[slot],
            grad_s[slot],
            mixed_s[slot],
            [extra_s[slot, head] for head in (0, 1)],
            part(keys_s),
            part(values_s),
            lambda part, head: kt_s[64 * head : 64 * head + 64, part * chunk : (part + 1) * chunk],
            total // chunk,
            put(0, LN2),
            put(PAIR, 1.0),
        )
        dq_s[turn] = query_grad.T
        comm_steps(2 * turn + 1)
        both = dot(hidden_s[...], dkv_s[turn]).astype(bf16)
        query = dot(hidden_s[:, :own], dq_s[turn]).astype(bf16)
        for at in range(8):
            r = slice(at * deep, (at + 1) * deep)
            for part_at, value in enumerate((query[r, :], both[r, :PAIR], both[r, PAIR:])):
                part_s[turn, at % 2, at // 2, part_at * deep : (part_at + 1) * deep, :] = value

        if comm:
            for sent in (0, 2):

                @pl.when(turn == sent)
                def _():
                    send_q[sent].start()

        @pl.when(turn == pairs - 2)
        def _():
            size = 2 * BLOCK
            for row in range(total // size):
                r = pl.ds(row * size, size)
                total_s[r, :] = upstream(range(pairs - 1), r, row * size < own)

        return 0

    lax.fori_loop(0, pairs, step, 0)

    def row_back(row, own_rows):
        r = block_at(row, BLOCK)
        scaled, inverse = normalize(x_s[r, :].astype(f32))
        value = total_s[r, :] + upstream([pairs - 1], r, own_rows)
        back, gain_sum = norm_back(value, scaled, inverse, gain)
        dgain_s[0:1, :] += gain_sum
        return r, back

    for copy in late:
        copy.wait()
    per = rows // BLOCK
    if not comm:

        def own_step(row):
            r, back = row_back(row, True)
            grad_self_s[r, :] += back

        def other_step(row):
            r, back = row_back(row, False)
            total_s[r, :] = back

        repeat(0, 2 * per, own_step, per)
        repeat(2 * per, 4 * per, other_step, per)
        own_out[...] = grad_self_s[...]
        other_out[...] = total_s[own:, :].astype(bf16)
        for turn in range(pairs):
            part_out[turn_pair(turn)] = part_s[turn]
        gain_out[...] = dgain_s[...]
        return

    def add_q(at, _):
        for half in range(2):
            value = part_s[3, half, at].astype(f32)
            for turn in (1, 2):
                value = value + land_q[turn, half, at].astype(f32)
            part_s[3, half, at] = value.astype(bf16)
        return 0

    def other_rows(slot):
        for row in range(per):
            _, back = row_back(slot * per + row, False)
            grads_send[slot - 2, pl.ds(row * BLOCK, BLOCK), :] = back.astype(bf16)
            grads_core[slot - 2][row].start()

    def own_rows(row):
        r, back = row_back(row, True)
        total_s[r, :] = back + grad_self_s[r, :]

    def cross(row):
        r = slice(row * BLOCK, (row + 1) * BLOCK)
        value = total_s[rows + row * BLOCK : rows + (row + 1) * BLOCK, :]
        cross_send[row] = (value + grads_land[1, r, :].astype(f32)).astype(bf16)
        grads_cross[row].start()

    arrive(send_q[1:])
    lax.fori_loop(0, planes, add_q, 0)
    side_q.start()
    other_rows(3)
    own_rows(per)
    arrive(grads_core[1][:1])
    cross(0)
    repeat(per + 1, 2 * per, own_rows, per)
    other_rows(2)
    arrive([side_q])
    add_in(part_s.at[3, side], far_q)
    begin(plane_q)
    repeat(0, per, own_rows, per)
    for at in range(pairs):
        gain_send[at] = dgain_s[:, at * PAIR : (at + 1) * PAIR]
    begin(gain_group)
    for row in range(1, per):
        arrive(grads_core[1][row : row + 1])
        cross(row)
    arrive(gain_group)
    gain_land[3] = gain_send[place] + gain_land[0] + gain_land[1] + gain_land[2]
    gain_side.start()
    arrive(grads_core[0])
    stage[...] = total_s[:rows, :] + grads_land[0].astype(f32)
    stage_out.start()
    sums = [finish(piece) for piece in pieces]
    for at in range(5):
        weight_outs[3 + at][...] = sums[0][at * deep : (at + 1) * deep, :]
    for at in range(sums[1].shape[0] // deep):
        weight_outs[8][:, at * PAIR : (at + 1) * PAIR] = sums[1][at * deep : (at + 1) * deep, :]
    for at in range(sums[2].shape[0] // PAIR):
        r = slice(at * PAIR, (at + 1) * PAIR)
        weight_outs[9][r, :] = sums[2][r, :].T
    arrive([gain_side])
    gain_planes[plane] = gain_land[3] + gain_far[...]
    begin(gain_last)
    arrive(plane_q)
    value = part_s[3, side, plane].astype(f32)
    for at in range(planes - 1):
        value = value + planes_q[at].astype(f32)
    for at in range(3):
        weight_outs[at][...] = value[at * deep : (at + 1) * deep, :]
    arrive(gain_last)
    value = gain_planes[0]
    for at in range(1, planes):
        value = value + gain_planes[at]
    gain_out[...] = value
    arrive([rows_cross, source_cross, *grads_cross])
    for copy in (stage_out, source_own):
        copy.wait()
    for copy in semaphores.sent:
        copy.wait_send()


def hand_over_kernel(planes, *refs):
    (rows_any, rows_far, grad_own, grad_far, source_own, source_far, *plain) = refs[:17]
    (decoder_out, grad_out, source_out, *plain_outs) = refs[17:31]
    (rows_s, grad_s, grad_low, source_s, source_low, *plain_s) = refs[31:-2]
    load, store = refs[-2:]
    chip = Where(planes).chip
    rows = rows_s.shape[1]
    moves = [
        (rows_any.at[:rows], rows_s.at[0], rows_s.at[0], decoder_out.at[chip]),
        (rows_far, rows_s.at[1], rows_s.at[1], decoder_out.at[1 - chip]),
        (grad_own, grad_s.at[0], grad_s.at[0], grad_out.at[chip]),
        (grad_far, grad_low, grad_s.at[1], grad_out.at[1 - chip]),
        (source_own, source_s.at[0], source_s.at[0], source_out.at[chip]),
        (source_far, source_low, source_s.at[1], source_out.at[1 - chip]),
    ]
    moves += [
        (one, held, held.at[: other.shape[0]], other)
        for one, held, other in zip(plain, plain_s, plain_outs)
    ]
    loads = [pltpu.make_async_copy(m[0], m[1], load.at[at]) for at, m in enumerate(moves)]
    stores = [pltpu.make_async_copy(m[2], m[3], store.at[at]) for at, m in enumerate(moves)]
    for copy in loads:
        copy.start()
    for at, (one, other) in enumerate(zip(loads, stores)):
        one.wait()
        if at == 3:
            for row in range(grad_low.shape[0]):
                size = grad_low.shape[1]
                grad_s[1, row * size : (row + 1) * size, :] = grad_low[row].astype(f32)
        if at == 5:
            source_s[1] = source_low[...].astype(f32)
        other.start()
    for copy in stores:
        copy.wait()


def call(kernel, outs, *operands, scratch=(), smem=0, params=PARAMS, spaces=None, out_space=VMEM, out_spaces=None):
    spaces = spaces or {}
    out_spaces = out_spaces or {}
    return pl.pallas_call(
        kernel,
        out_shape=[jax.ShapeDtypeStruct(shape, kind) for shape, kind in outs],
        in_specs=[
            pl.BlockSpec(memory_space=pltpu.SMEM if at < smem else spaces.get(at, VMEM))
            for at in range(len(operands))
        ],
        out_specs=[
            pl.BlockSpec(memory_space=out_spaces.get(at, out_space)) for at in range(len(outs))
        ],
        scratch_shapes=list(scratch),
        compiler_params=params,
    )(*operands)


def swapped(value, axis, bit):
    pairs = [(source, source ^ bit) for source in range(lax.axis_size(axis))]
    return lax.ppermute(value, axis, pairs)


def as_blocks(weight, chunks=1):
    height, width = weight.shape
    deep = height // 8
    cut = weight.reshape(4, 2, deep, 4, chunks, PAIR).transpose(3, 1, 0, 4, 2, 5)
    return cut.reshape(4, 2, 4, chunks * deep, PAIR)


def from_blocks(blocks, chunks=1):
    height = blocks.shape[3] // chunks
    cut = blocks.reshape(4, 2, 4, chunks, height, PAIR).transpose(2, 1, 4, 0, 3, 5)
    return cut.reshape(8 * height, 4 * chunks * PAIR)


def gather_plain(arguments, seq_size, dp_size):
    (decoder_in, source_states, out_grad, narrow, ffn_expand, ffn_reduce, norm_gains) = arguments
    chip = lax.axis_index("seq") // 2
    rows_dec = decoder_in.shape[1]
    own = 2 * rows_dec
    outgoing = jnp.concatenate([decoder_in[1 - chip], source_states[1 - chip]], axis=0)
    arrived = swapped(outgoing, "seq", 2)
    own_rows = jnp.concatenate(
        [decoder_in[chip], arrived[:rows_dec], source_states[chip], arrived[rows_dec:]], axis=0
    )
    other_rows = swapped(own_rows, "seq", 1)
    x_all = jnp.concatenate([own_rows[:own], other_rows[:own]], axis=0)
    source_all = jnp.concatenate([own_rows[own:], other_rows[own:]], axis=0)
    cotangent = swapped(out_grad[1 - chip], "seq", 2)

    def whole(weight):
        weight = lax.all_gather(weight, "seq", axis=1, tiled=True)
        return lax.all_gather(weight, "dp", axis=0, tiled=True)

    blocks = [as_blocks(whole(weight)) for weight in narrow]
    qkv = jnp.concatenate(blocks[:3], axis=3)
    later_a = jnp.concatenate(blocks[3:], axis=3)
    later_b = as_blocks(whole(ffn_expand), ffn_expand.shape[1] // PAIR)
    later_c = as_blocks(whole(ffn_reduce))
    gain_block = jnp.pad(norm_gains.astype(f32), ((0, 5), (0, 0)))
    gains = lax.all_gather(gain_block, "seq", axis=0)
    return x_all, source_all, cotangent, qkv, later_a, later_b, later_c, gains


def body(
    decoder_in,
    source_states,
    source_len,
    upsample,
    send_counts,
    self_query,
    self_key,
    self_value,
    self_output,
    cross_query,
    cross_key,
    cross_value,
    cross_output,
    ffn_expand,
    ffn_reduce,
    norm_gains,
    out_grad,
):
    seq_size = lax.axis_size("seq")
    dp_size = lax.axis_size("dp")
    planes = dp_size // 2
    place = lax.axis_index("seq")
    chip = place // 2
    home_count, rows_dec, width = decoder_in.shape
    rows_src = source_states.shape[1]
    pairs = width // PAIR
    own = 2 * rows_dec
    total = 4 * rows_dec
    deep = self_query.shape[0]
    deep_two = ffn_reduce.shape[0]
    wide = ffn_expand.shape[1] // PAIR
    hidden_width = wide * PAIR * seq_size
    all_src = 4 * rows_src
    comm = dp_size == 8

    def pair_rows(rows):
        return (pairs, rows, PAIR)

    narrow = (self_query, self_key, self_value, self_output)
    narrow += (cross_query, cross_key, cross_value, cross_output)
    rows_outs = [
        (pair_rows(own), bf16),
        (pair_rows(total), bf16),
        (pair_rows(total), bf16),
        (pair_rows(own), bf16),
        ((pairs, 2, own, PAIR), bf16),
    ]
    buffers = [VMEM(shape, kind) for shape, kind in rows_outs]
    work = [
        VMEM((total, width), bf16),
        VMEM((width, 3 * PAIR), bf16),
        VMEM((total, PAIR), bf16),
        *buffers,
    ]
    semaphores = [pltpu.SemaphoreType.DMA((96,)), pltpu.SemaphoreType.DMA((96,))]
    if comm:
        cut = (seq_size, 2, planes)
        gathered = [
            ((total, width), bf16),
            ((all_src, width), bf16),
            (cut + (3 * deep, PAIR), bf16),
            (cut + (5 * deep, PAIR), bf16),
            (cut + (wide * deep, PAIR), bf16),
            (cut + (deep_two, PAIR), bf16),
            ((seq_size, 8, PAIR), f32),
        ]
        operands = (source_len, upsample, decoder_in, source_states)
        operands += (*narrow, ffn_expand, ffn_reduce, norm_gains)
        (
            x_all, source_all, qkv, later_a, later_b, later_c, gains,
            q, k, v, mixed, query_extra,
        ) = call(
            partial(open_kernel, True, planes, deep),
            gathered + rows_outs,
            *operands,
            scratch=[
                VMEM((total, width), bf16),
                VMEM(cut + (3 * deep, PAIR), bf16),
                VMEM((seq_size, 8, PAIR), f32),
                *work,
                *semaphores,
                VMEM((5 * deep, PAIR), bf16),
                VMEM((wide * deep, PAIR), bf16),
                VMEM((deep_two, PAIR), bf16),
                VMEM((rows_src, width), bf16),
                VMEM((8, PAIR), f32),
            ],
            smem=2,
            spaces={at: pl.ANY for at in range(2, len(operands) - 1)},
            out_space=pl.ANY,
            params=pltpu.CompilerParams(
                vmem_limit_bytes=VMEM_LIMIT, collective_id=0, has_side_effects=True
            ),
        )
    else:
        x_all, source_all, cotangent, qkv, later_a, later_b, later_c, gains = gather_plain(
            (decoder_in, source_states, out_grad, narrow, ffn_expand, ffn_reduce, norm_gains),
            seq_size,
            dp_size,
        )
        q, k, v, mixed, query_extra = call(
            partial(open_kernel, False, planes, deep),
            rows_outs,
            source_len,
            upsample,
            x_all,
            qkv,
            gains,
            scratch=[*work, *semaphores],
            smem=2,
            out_space=pl.ANY,
        )
    parts = [
        ((seq_size, 2, 4, 5 * width // 8, PAIR), bf16),
        ((seq_size, 2, 4, hidden_width // 8, PAIR), bf16),
        ((seq_size, 2, 4, hidden_width // 8, PAIR), bf16),
    ]
    out_rows, grad_mixed, grad_self, part_a, part_b, part_c, grad_source, dgain = call(
        partial(middle_kernel, comm, planes),
        [
            ((own, width), bf16),
            (pair_rows(own), bf16),
            ((own, width), f32),
            *parts,
            ((all_src, width), bf16),
            ((8, width), f32),
        ],
        source_len,
        upsample,
        send_counts,
        x_all,
        mixed,
        out_grad,
        out_grad if comm else cotangent,
        source_all,
        later_a,
        later_b,
        later_c,
        gains,
        scratch=[
            VMEM((own, width), bf16),
            VMEM(pair_rows(own), bf16),
            VMEM((own, width), bf16),
            VMEM((all_src, width), bf16),
            *[VMEM(*part) for part in parts],
            *[VMEM((width, width), bf16)] * 5,
            VMEM((width, hidden_width), bf16),
            VMEM((hidden_width, width), bf16),
            VMEM(pair_rows(all_src), bf16),
            VMEM(pair_rows(all_src), bf16),
            VMEM((pairs, PAIR, all_src), bf16),
            VMEM((all_src, PAIR), bf16),
            *[VMEM(pair_rows(all_src), bf16)] * 2,
            *[VMEM((own, width), f32)] * 4,
            *[VMEM(pair_rows(own), bf16)] * 4,
            VMEM((2 * pairs, own, PAIR), bf16),
            VMEM((width, own), bf16),
            VMEM((own, width), bf16),
            VMEM((width, own), bf16),
            VMEM((own, width), bf16),
            VMEM((width, own), bf16),
            VMEM((own, width), bf16),
            pltpu.SemaphoreType.DMA((8,)),
            pltpu.SemaphoreType.DMA((6,)),
            pltpu.SemaphoreType.DMA((8,)),
            pltpu.SemaphoreType.DMA((8,)),
        ],
        params=pltpu.CompilerParams(
            vmem_limit_bytes=VMEM_LIMIT, collective_id=2, has_side_effects=True
        )
        if comm
        else PARAMS,
        smem=3,
        spaces={at: pl.ANY for at in range(3, 11)},
        out_spaces={at: pl.ANY for at in range(6)},
    )
    part_q = ((seq_size, 2, 4, 3 * width // 8, PAIR), bf16)
    operands = (source_len, upsample, q, k, v, mixed, grad_mixed, query_extra)
    operands += (x_all, qkv, gains, grad_self, dgain)
    work = [
        VMEM((2, own, PAIR), bf16),
        VMEM((2, total, PAIR), bf16),
        VMEM((2, total, PAIR), bf16),
        VMEM((2, own, PAIR), bf16),
        VMEM((2, own, PAIR), bf16),
        VMEM((2, 2, own, PAIR), bf16),
        VMEM((total, width), bf16),
        VMEM(qkv.shape, bf16),
        VMEM(gains.shape, f32),
        VMEM((own, width), f32),
        VMEM((8, width), f32),
        VMEM((total, 2 * PAIR), bf16),
        VMEM((total, 2 * PAIR), bf16),
        VMEM((PAIR, total), bf16),
        VMEM((width, total), bf16),
        VMEM((total, width), f32),
        VMEM((pairs, total, 2 * PAIR), bf16),
        VMEM((pairs, own, PAIR), bf16),
        VMEM((pairs, width, 3 * PAIR), bf16),
        VMEM(*part_q),
        pltpu.SemaphoreType.DMA((2, 6)),
        *semaphores,
    ]
    everywhere = {at: pl.ANY for at in range(2, 18)}
    if comm:
        heights = [shape[3] for shape, _ in parts]

        def per_piece(lead):
            return [VMEM((*lead, height, PAIR), bf16) for height in heights]

        work += [
            *per_piece((2, 2, planes)),
            *per_piece((2, 2, planes)),
            *per_piece((2, planes)),
            *per_piece((planes,)),
            *per_piece((planes - 1,)),
            VMEM((3, 2, planes, 3 * deep, PAIR), bf16),
            VMEM((planes, 3 * deep, PAIR), bf16),
            VMEM((planes - 1, 3 * deep, PAIR), bf16),
            VMEM((pairs, 8, PAIR), f32),
            VMEM((4, 8, PAIR), f32),
            VMEM((8, PAIR), f32),
            VMEM((planes, 8, PAIR), f32),
            VMEM((2, rows_dec, width), bf16),
            VMEM((2, rows_dec, width), bf16),
            VMEM((rows_dec // BLOCK, BLOCK, width), bf16),
            VMEM((rows_dec, width), f32),
            VMEM((2 * rows_src, width), bf16),
            VMEM((2 * rows_src, width), bf16),
            VMEM((rows_src, width), f32),
        ]
        small = ((deep, PAIR), f32)
        plain = [small] * 8 + [(ffn_expand.shape, f32), (ffn_reduce.shape, f32), ((8, PAIR), f32)]
        outs = call(
            partial(last_kernel, True, planes),
            [
                ((rows_dec, width), bf16),
                ((rows_dec, width), f32),
                ((rows_dec // BLOCK, BLOCK, width), bf16),
                ((rows_src, width), f32),
                ((rows_src, width), bf16),
                *plain,
            ],
            *operands,
            part_a,
            part_b,
            part_c,
            grad_source,
            out_rows,
            scratch=work,
            smem=2,
            spaces=everywhere,
            out_spaces={at: pl.ANY for at in range(5)},
            params=pltpu.CompilerParams(
                vmem_limit_bytes=VMEM_LIMIT, collective_id=1, has_side_effects=True
            ),
        )
        outs = call(
            partial(hand_over_kernel, planes),
            [
                (decoder_in.shape, bf16),
                (decoder_in.shape, f32),
                (source_states.shape, f32),
                *plain[:-1],
                (norm_gains.shape, f32),
            ],
            out_rows,
            *outs,
            scratch=[
                VMEM(decoder_in.shape, bf16),
                VMEM(decoder_in.shape, f32),
                VMEM((rows_dec // BLOCK, BLOCK, width), bf16),
                VMEM(source_states.shape, f32),
                VMEM((rows_src, width), bf16),
                *[VMEM(shape, kind) for shape, kind in plain],
                *[pltpu.SemaphoreType.DMA((17,))] * 2,
            ],
            spaces={at: pl.ANY for at in range(17)},
            out_space=pl.ANY,
        )
        (decoder_out, grad_decoder, grad_src, dwq, dwk, dwv, *rest, dw1, dw2, dgains) = outs
        dwo, dwcq, dwck, dwcv, dwco = rest
    else:
        own_grad, other_grad, part_qkv, dgains = call(
            partial(last_kernel, False, planes),
            [((own, width), f32), ((own, width), bf16), part_q, ((8, width), f32)],
            *operands,
            scratch=work,
            smem=2,
            spaces=everywhere,
        )
        crossing = jnp.concatenate([other_grad, grad_source[2 * rows_src :]], axis=0)
        returned = swapped(crossing, "seq", 1).astype(f32)
        grad_rows = own_grad + returned[:own]
        source_rows = grad_source[: 2 * rows_src].astype(f32) + returned[own:]
        homeward = [grad_rows[rows_dec:].astype(bf16), source_rows[rows_src:].astype(bf16)]
        came = swapped(jnp.concatenate([out_rows[rows_dec:], *homeward], axis=0), "seq", 2)

        def both_sentences(mine, theirs):
            theirs = theirs.astype(mine.dtype)
            return jnp.where(chip == 0, jnp.stack([mine, theirs]), jnp.stack([theirs, mine]))

        decoder_out = both_sentences(out_rows[:rows_dec], came[:rows_dec])
        grad_decoder = both_sentences(grad_rows[:rows_dec], came[rows_dec : 2 * rows_dec])
        grad_src = both_sentences(source_rows[:rows_src], came[2 * rows_dec :])

        def summed(blocks, start, count, chunks=1):
            grad = from_blocks(blocks[:, :, :, start : start + chunks * count], chunks)
            grad = lax.psum_scatter(grad.astype(f32), "dp", scatter_dimension=0, tiled=True)
            return lax.psum_scatter(grad, "seq", scatter_dimension=1, tiled=True)

        step = width // 8
        dwq, dwk, dwv = [summed(part_qkv, at * step, step) for at in range(3)]
        dwo, dwcq, dwck, dwcv, dwco = [summed(part_a, at * step, step) for at in range(5)]
        dw1 = summed(part_b, 0, step, hidden_width // width)
        tall = part_c.reshape(seq_size, 2, 4, hidden_width // 8 // PAIR, PAIR, PAIR)
        dw2 = summed(tall.swapaxes(4, 5).reshape(part_c.shape), 0, hidden_width // 8)
        dgains = lax.psum(dgains, "dp")
        dgains = lax.psum_scatter(dgains, "seq", scatter_dimension=1, tiled=True)
    return (
        decoder_out,
        grad_decoder,
        grad_src,
        dwq,
        dwk,
        dwv,
        dwo,
        dwcq,
        dwck,
        dwcv,
        dwco,
        dw1,
        dw2,
        dgains[:3],
    )


def solution(mesh):
    rows = P("dp", "seq", None)
    weight = P("dp", "seq")
    placed = (rows, rows, P(), P(), P()) + (weight,) * 10 + (P(None, "seq"), rows)
    return jax.shard_map(
        body,
        mesh=mesh,
        in_specs=placed,
        out_specs=(rows, rows, rows) + (weight,) * 10 + (P(None, "seq"),),
        check_vma=False,
    )
```

```python
from functools import partial

import jax
import jax.numpy as jnp
from jax import lax
from jax.experimental import pallas as pl
from jax.experimental.pallas import tpu as pltpu
from jax.sharding import PartitionSpec as P

HEADS = 8
EPSILON = 1e-05
NEGATIVE = -1000000000.0
LOG2E = 1.4426950408889634
LN2 = 0.6931471805599453
GELU_IN = 0.7978845608028654
GELU_CUBE = 0.044715
BLOCK = 256
PAIR = 128

bf16 = jnp.bfloat16
f32 = jnp.float32
VMEM = pltpu.VMEM
VMEM_LIMIT = 60 * 1024 * 1024
PARAMS = pltpu.CompilerParams(vmem_limit_bytes=VMEM_LIMIT)


def dot(left, right):
    return jnp.dot(left, right, preferred_element_type=f32)


def dot_nt(left, right):
    return lax.dot_general(left, right, (((1,), (1,)), ((), ())), preferred_element_type=f32)


def block_at(index, size):
    return pl.ds(pl.multiple_of(index * size, size), size)


def repeat(start, stop, todo, group):
    def step(at, _):
        for part in range(group):
            todo(start + at * group + part)
        return 0

    count, rest = divmod(stop - start, group)
    if count == 1:
        step(0, 0)
    elif count:
        lax.fori_loop(0, count, step, 0)
    for part in range(rest):
        todo(start + count * group + part)


def row_mean(values):
    return jnp.mean(values, axis=-1, keepdims=True)


def normalize(values):
    centred = values - row_mean(values)
    inverse = lax.rsqrt(row_mean(centred * centred) + EPSILON)
    return centred * inverse, inverse


def norm_back(upstream, scaled, inverse, gain):
    inner = upstream * gain
    back = inverse * (inner - row_mean(inner) - scaled * row_mean(inner * scaled))
    return back, jnp.sum(upstream * scaled, axis=0, keepdims=True)


def three_parts(column, lane, last):
    high = column.astype(bf16).astype(f32)
    middle = (column - high).astype(bf16).astype(f32)
    low = column - high - middle
    rest = jnp.where(lane == 3, last, 0.0)
    return jnp.where(
        lane == 0, high, jnp.where(lane == 1, middle, jnp.where(lane == 2, low, rest))
    ).astype(bf16)


def one_head(values, first, head):
    zero = jnp.zeros_like(values)
    return jnp.where(first, values, zero) if head == 0 else jnp.where(first, zero, values)


def attend_pair(query, keys, key_extra, values, lane):
    first = lane < 64
    ones = jnp.where(lane == 3, 1.0, 0.0).astype(bf16)
    keys = jnp.concatenate([keys, key_extra], axis=1)
    values = jnp.concatenate([values, jnp.ones_like(values)], axis=1)
    scores = [
        dot_nt(jnp.concatenate([one_head(query, first, head), ones], axis=1), keys)
        for head in (0, 1)
    ]
    mixed, extras = [], []
    for head in (0, 1):
        peak = jnp.max(scores[head], axis=1, keepdims=True)
        exps = jnp.exp2(scores[head] - peak)
        both = dot(exps.astype(bf16), values)
        total = both[:, PAIR : PAIR + 1]
        mixed.append(both[:, :PAIR] * (1.0 / total))
        extras.append(three_parts(-(peak + jnp.log2(total)), lane, 1.0))
    return jnp.where(first, mixed[0], mixed[1]).astype(bf16), extras


def attend_pair_back(
    query, grad, mixed, query_extra, key_at, value_at, key_columns_at, chunks, put_key, put_value
):
    lane = lax.broadcasted_iota(jnp.int32, query.shape, 1)
    first = lane < 64
    product = grad.astype(f32) * mixed.astype(f32)
    queries = [one_head(query, first, head) for head in (0, 1)]
    grads = [one_head(grad, first, head) for head in (0, 1)]
    long_queries = [jnp.concatenate([queries[h], query_extra[h]], axis=1) for h in (0, 1)]
    long_grads = []
    for head in (0, 1):
        delta = jnp.sum(one_head(product, first, head), axis=1, keepdims=True)
        long_grads.append(
            jnp.concatenate([grads[head], three_parts(-delta, lane, 0.0)], axis=1)
        )
    both_queries = jnp.concatenate(queries, axis=0)
    both_grads = jnp.concatenate(grads, axis=0)
    query_grads = [None, None]
    for chunk in range(chunks):
        keys, values = key_at(chunk), value_at(chunk)
        probs, score_grads = [], []
        for head in (0, 1):
            prob = jnp.exp2(dot_nt(keys, long_queries[head]))
            score_grad = (prob * dot_nt(values, long_grads[head])).astype(bf16)
            probs.append(prob.astype(bf16))
            score_grads.append(score_grad)
            term = dot(key_columns_at(chunk, head), score_grad)
            query_grads[head] = term if chunk == 0 else query_grads[head] + term
        put_value(chunk, dot(jnp.concatenate(probs, axis=1), both_grads))
        put_key(chunk, dot(jnp.concatenate(score_grads, axis=1), both_queries))
    return (jnp.concatenate(query_grads, axis=0) * 0.125).astype(bf16)


def copy_to(source, target, send, receive, partner):
    return pltpu.make_async_remote_copy(
        src_ref=source,
        dst_ref=target,
        send_sem=send,
        recv_sem=receive,
        device_id=partner,
        device_id_type=pl.DeviceIdType.MESH,
    )


def greet(partners):
    for partner in partners:
        pl.semaphore_signal(
            pltpu.get_barrier_semaphore(),
            inc=1,
            device_id=partner,
            device_id_type=pl.DeviceIdType.MESH,
        )


def await_greetings(partners):
    pl.semaphore_wait(pltpu.get_barrier_semaphore(), len(partners))


class Where:
    def __init__(self, planes):
        group, self.place = lax.axis_index("dp"), lax.axis_index("seq")
        self.group = group
        self.chip, self.core = self.place // 2, self.place % 2
        self.plane, self.side = group // 2, group % 2
        self.planes = planes
        self.other_core = self.at(self.chip, 1 - self.core)
        self.other_chip = self.at(1 - self.chip, self.core)
        self.diagonal = self.at(1 - self.chip, 1 - self.core)
        self.other_side = {"dp": self.plane * 2 + 1 - self.side}
        self.other_planes = [
            {"dp": (self.plane + step) % planes * 2 + self.side} for step in range(1, planes)
        ]

    def at(self, chip, core):
        return {"seq": chip * 2 + core}

    def column(self, step):
        return (self.chip + step // 2) % 2 * 2 + (self.core + step % 2) % 2

    def everyone(self):
        return [self.other_core, self.other_chip, self.diagonal, self.other_side] + self.other_planes


class Semaphores:
    def __init__(self, send, receive):
        self.send, self.receive, self.count = send, receive, 0
        self.sent = []

    def remote(self, source, target, partner):
        at = self.count
        self.count += 1
        copy = copy_to(source, target, self.send.at[at], self.receive.at[at], partner)
        self.sent.append(copy)
        return copy

    def local(self, source, target):
        at = self.count
        self.count += 1
        return pltpu.make_async_copy(source, target, self.send.at[at])


def block_places(where_chip, where_core, rows, offset, index, size):
    per = rows // size
    slot = index // per
    block = (where_chip + slot % 2) % 2 * 2 + (where_core + slot // 2) % 2
    return block * rows + index % per * size + offset


def mask_columns(where_chip, where_core, rows, count, size, length, ref):
    lane = lax.broadcasted_iota(jnp.int32, (size, PAIR), 1)
    offset = lax.broadcasted_iota(jnp.int32, (size, PAIR), 0)

    def step(index, _):
        places = block_places(where_chip, where_core, rows, offset, index, size)
        bias = jnp.where(places < length, 0.0, NEGATIVE)
        ref[block_at(index, size), :] = jnp.where(
            lane < 3, 1.0, jnp.where(lane == 3, bias, 0.0)
        ).astype(bf16)
        return 0

    lax.fori_loop(0, count // size, step, 0)


def open_kernel(
    comm,
    planes,
    deep,
    source_len_ref,
    upsample_ref,
    *refs,
):
    if comm:
        (
            decoder_ref, source_ref,
            wq_in, wk_in, wv_in, *later_in, gain_in,
            x_out, source_out, qkv_out, later_a, later_b, later_c, gain_out,
            q_out, k_out, v_out, mixed_out, extra_out,
            x_ref, qkv_ref, gain_ref, hidden_ref, weight_ref, mask_ref,
            q_ref, k_ref, v_ref, mixed_ref, extra_ref, send, receive,
            stage_a, stage_b, stage_c, stage_s, gain_block,
        ) = refs
    else:
        (
            x_ref, qkv_ref, gain_ref,
            q_out, k_out, v_out, mixed_out, extra_out,
            hidden_ref, weight_ref, mask_ref,
            q_ref, k_ref, v_ref, mixed_ref, extra_ref, send, receive,
        ) = refs
    where = Where(planes)
    place, plane, side, chip, core = where.place, where.plane, where.side, where.chip, where.core
    total, width = x_ref.shape
    pairs = width // PAIR
    own = total // 2
    rows = total // 4
    semaphores = Semaphores(send, receive)
    column = where.column

    if comm:
        group = where.group
        x_slots = [x_ref.at[slot * rows : (slot + 1) * rows] for slot in range(4)]
        few = source_ref.shape[1]
        s_slots = [source_out.at[slot * few : (slot + 1) * few] for slot in range(4)]
        local_x = semaphores.local(decoder_ref.at[chip], x_slots[0])
        mine = qkv_ref.at[place, side, plane]
        local_qkv = [
            semaphores.local(ref, mine.at[at * deep : (at + 1) * deep])
            for at, ref in enumerate((wq_in, wk_in, wv_in))
        ]
        first = [local_x, *local_qkv]
        wo_in, wcq_in, wck_in, wcv_in, wco_in, w1_in, w2_in = later_in
        mine_a = later_a.at[place, side, plane]
        mine_b = later_b.at[place, side, plane]
        mine_c = later_c.at[place, side, plane]
        wide = w1_in.shape[1] // PAIR
        local_later = [
            [
                semaphores.local(ref, stage_a.at[at * deep : (at + 1) * deep])
                for at, ref in enumerate((wo_in, wcq_in, wck_in, wcv_in, wco_in))
            ],
            [
                semaphores.local(
                    w1_in.at[:, at * PAIR : (at + 1) * PAIR], stage_b.at[at * deep : (at + 1) * deep]
                )
                for at in range(wide)
            ],
            [semaphores.local(w2_in, stage_c)],
        ]
        stores = [
            semaphores.local(stage_a, mine_a),
            semaphores.local(stage_b, mine_b),
            semaphores.local(stage_c, mine_c),
        ]
        source_load = semaphores.local(source_ref.at[chip], stage_s)
        source_store = semaphores.local(stage_s, s_slots[0])
        greet(where.everyone())
        gain_block[...] = jnp.zeros(gain_block.shape, f32)
        gain_block[0 : gain_in.shape[0], :] = gain_in[...].astype(f32)
        gain_ref[place] = gain_block[...]
        for copy in first + local_later[0] + local_later[1] + local_later[2] + [source_load]:
            copy.start()
        await_greetings(where.everyone())

        cuts = [slice(half * rows // 2, (half + 1) * rows // 2) for half in range(2)]
        x_cross = [
            semaphores.remote(decoder_ref.at[1 - chip, cut], x_slots[1].at[cut], where.other_chip)
            for cut in cuts
        ]
        x_core = semaphores.remote(decoder_ref.at[chip], x_slots[2], where.other_core)
        x_pass = [
            semaphores.remote(x_slots[1].at[cut], x_slots[3].at[cut], where.other_core)
            for cut in cuts
        ]
        s_cross = semaphores.remote(source_ref.at[1 - chip], s_slots[1], where.other_chip)
        s_core = semaphores.remote(source_ref.at[chip], s_slots[2], where.other_core)
        s_pass = semaphores.remote(s_slots[1], s_slots[3], where.other_core)
        gain_sends = [
            semaphores.remote(gain_block, gain_ref.at[place], partner)
            for partner in (where.other_core, where.other_chip, where.diagonal)
        ]
        qkv_planes = [semaphores.remote(mine, mine, partner) for partner in where.other_planes]
        qkv_side = semaphores.remote(
            qkv_ref.at[place, side], qkv_ref.at[place, side], where.other_side
        )
        qkv_core = semaphores.remote(qkv_ref.at[place], qkv_ref.at[place], where.other_core)
        qkv_chip = semaphores.remote(qkv_ref.at[place], qkv_ref.at[place], where.other_chip)
        across = column(2)
        qkv_pass = semaphores.remote(qkv_ref.at[across], qkv_ref.at[across], where.other_core)
        later = []
        for buffer, stage in ((later_a, stage_a), (later_b, stage_b), (later_c, stage_c)):
            block = buffer.at[place, side, plane]
            mine_side, across_side = buffer.at[place, side], buffer.at[across, side]
            if buffer is later_c:
                first = [semaphores.remote(stage, block, where.other_chip)]
                far = buffer.at[across, side, plane]
                second = [
                    semaphores.remote(stage, block, where.other_side),
                    semaphores.remote(far, far, where.other_side),
                ]
                others = [buffer.at[at, 1 - side, plane] for at in (place, across)]
                kept = [(stage, block), (far, far)] + [(one, one) for one in others]
            else:
                first = [semaphores.remote(mine_side, mine_side, where.other_chip)]
                second = []
                if buffer is later_a:
                    second = [
                        semaphores.remote(one, one, where.other_side)
                        for one in (mine_side, across_side)
                    ]
                kept = [(stage, block)]
            later.append(
                dict(
                    planes=[
                        semaphores.remote(one, other, partner)
                        for one, other in kept
                        for partner in where.other_planes
                    ],
                    first=first,
                    second=second,
                    core=[
                        semaphores.remote(buffer.at[at], buffer.at[at], where.other_core)
                        for at in (() if buffer is later_b else (place, across))
                    ],
                )
            )

        def begin(copies):
            for copy in copies:
                copy.start()

        def arrive(copies):
            for copy in copies:
                copy.wait_recv()

        begin(gain_sends)
        for copy in local_qkv:
            copy.wait()
        begin(qkv_planes)
        begin(x_cross)
        x_core.start()
        begin([s_core])
        for copies in local_later:
            for copy in copies:
                copy.wait()
        source_load.wait()
        begin([*stores, source_store])
        a, b, c = later
        begin(c["first"])
        begin(a["planes"])
        begin(b["planes"])

    length = source_len_ref[where.group * 2 + chip] * upsample_ref[where.group * 2 + chip]
    mask_columns(chip, core, rows, total, BLOCK, length, mask_ref)

    def hide(slot, start=0, stop=2):
        gain = jnp.concatenate([gain_ref[at, 0:1, :] for at in range(pairs)], axis=1)

        def step(index):
            at = pl.ds(index * BLOCK + slot * rows, BLOCK)
            scaled, _ = normalize(x_ref[at, :].astype(f32))
            hidden_ref[at, :] = (scaled * gain).astype(bf16)

        repeat(start * rows // (2 * BLOCK), stop * rows // (2 * BLOCK), step, 2)

    def take_weights(pair):
        for part in range(3):
            for at in range(8):
                weight_ref[at * 64 : at * 64 + 64, part * PAIR : (part + 1) * PAIR] = qkv_ref[
                    pair, at % 2, at // 2, part * 64 : part * 64 + 64, :
                ]

    def project(pair, slot, count):
        size = 2 * BLOCK
        for index in range(count * rows // size):
            at = pl.ds(slot * rows + index * size, size)
            both = dot(hidden_ref[at, :], weight_ref[:, PAIR:]).astype(bf16)
            k_ref[pair, at, :] = both[:, :PAIR]
            v_ref[pair, at, :] = both[:, PAIR:]
            if slot * rows + index * size < own:
                query = dot(hidden_ref[at, :], weight_ref[:, :PAIR]) * (0.125 * LOG2E)
                q_ref[pair, at, :] = query.astype(bf16)

    if comm:
        local_x.wait()
        arrive(gain_sends)
        hide(0)
        arrive([x_core])
        hide(2)
        arrive(qkv_planes)
        qkv_side.start()
        arrive([qkv_side])
        begin([qkv_core])
        take_weights(place)
        project(place, 0, 1)
        project(place, 2, 1)
        arrive(x_cross[:1])
        x_pass[0].start()
        hide(1, 0, 1)
        arrive(x_cross[1:])
        x_pass[1].start()
        arrive(a["planes"])
        for copy in [*stores, source_store]:
            copy.wait()
        begin(a["first"])
        arrive(c["first"])
        begin(c["second"])
        begin([qkv_chip])
        hide(1, 1, 2)
        project(place, 1, 1)
        arrive(x_pass)
        hide(3)
        project(place, 3, 1)
    else:
        for slot in range(4):
            hide(slot)
        take_weights(place)
        project(place, 0, 4)

    size = 2 * BLOCK
    blocks = own // size
    lane = lax.broadcasted_iota(jnp.int32, (size, PAIR), 1)

    def outs_of(pair):
        return [
            (q_ref.at[pair], q_out.at[pair]),
            (k_ref.at[pair], k_out.at[pair]),
            (v_ref.at[pair], v_out.at[pair]),
            (mixed_ref.at[pair], mixed_out.at[pair]),
            (extra_ref.at[pair], extra_out.at[pair]),
        ]

    first_out = semaphores.count

    def out_copies(step, pair):
        return [
            pltpu.make_async_copy(source, target, send.at[first_out + step * 5 + at])
            for at, (source, target) in enumerate(outs_of(pair))
        ]

    if comm:
        x_local = pltpu.make_async_copy(x_ref, x_out, send.at[first_out + 20])
        qkv_local = pltpu.make_async_copy(qkv_ref, qkv_out, send.at[first_out + 21])
        gain_local = pltpu.make_async_copy(gain_ref, gain_out, send.at[first_out + 22])
        begin([x_local, gain_local])

    def step(index, _):
        turn = index // blocks
        pair = column(turn)
        if comm:
            @pl.when(index == 1)
            def _():
                arrive(c["second"])
                begin(c["planes"])
                arrive(b["planes"])
                begin(b["first"])
                begin([s_cross])

            @pl.when(index == 2)
            def _():
                arrive([qkv_core])
                arrive(a["first"])
                begin(a["second"])

            @pl.when(index == 4)
            def _():
                arrive([qkv_chip])
                qkv_pass.start()

            @pl.when(index == 5)
            def _():
                arrive(b["first"])
                arrive(a["second"])
                begin(a["core"])

            @pl.when(index == 6)
            def _():
                arrive([qkv_pass])
                qkv_local.start()
                arrive([s_cross])
                s_pass.start()

            @pl.when(index == 7)
            def _():
                arrive(c["planes"])
                begin(c["core"])

        @pl.when((index % blocks == 0) & (index > 0))
        def _():
            take_weights(pair)
            project(pair, 0, 4)

        at = block_at(index % blocks, size)
        mixed, extras = attend_pair(
            q_ref[pair, at, :], k_ref[pair], mask_ref[...], v_ref[pair], lane
        )
        mixed_ref[pair, at, :] = mixed
        extra_ref[pair, 0, at, :] = extras[0]
        extra_ref[pair, 1, at, :] = extras[1]

        @pl.when(index % blocks == blocks - 1)
        def _():
            for copy in out_copies(turn, pair):
                copy.start()

        return 0

    lax.fori_loop(0, pairs * blocks, step, 0)
    if comm:
        arrive([s_core, s_pass])
        for piece in later:
            arrive(piece["core"])
        for copy in semaphores.sent:
            copy.wait_send()
        for copy in (x_local, qkv_local, gain_local):
            copy.wait()
    for turn in range(pairs):
        for copy in out_copies(turn, column(turn)):
            copy.wait()


def whole_weight(ref, blocks, start, count, chunks=1):
    columns, sides, planes = blocks.shape[:3]
    for column in range(columns):
        for side in range(sides):
            for plane in range(planes):
                row = (plane * sides + side) * count
                for chunk in range(chunks):
                    at = (column * chunks + chunk) * PAIR
                    ref[row : row + count, at : at + PAIR] = blocks[
                        column, side, plane, start + chunk * count : start + (chunk + 1) * count, :
                    ]


def to_blocks(blocks, columns, places, start, count, value):
    for column_at, column in enumerate(columns):
        for place_at, (side, plane) in enumerate(places):
            blocks[column, side, plane, start : start + count, :] = value[
                place_at * count : (place_at + 1) * count,
                column_at * PAIR : (column_at + 1) * PAIR,
            ].astype(bf16)


def middle_kernel(
    comm,
    planes,
    source_len_ref,
    upsample_ref,
    send_ref,
    x_any,
    mixed_any,
    cotangent_any,
    cotangent_far,
    source_any,
    later_a,
    later_b,
    later_c,
    gain_blocks,
    out_rows,
    grad_mixed_out,
    grad_self_out,
    part_a,
    part_b,
    part_c,
    grad_source_ref,
    dgain_ref,
    x_ref,
    mixed_ref,
    cotangent_ref,
    source_ref,
    blocks_a,
    blocks_b,
    blocks_c,
    wo_ref,
    wcq_ref,
    wck_ref,
    wcv_ref,
    wco_ref,
    w1_ref,
    w2_ref,
    ck_ref,
    cv_ref,
    ckt_ref,
    cextra_ref,
    dck_ref,
    dcv_ref,
    after_self_s,
    after_cross_s,
    final_s,
    hidden_grad_s,
    qc_s,
    cm_s,
    gcm_s,
    dq_s,
    extra_s,
    hidden_two_t,
    hidden_three_s,
    hidden_three_t,
    grad_ffn_s,
    grad_ffn_t,
    branch_s,
    load,
    store,
    send,
    receive,
):
    rows_own, width = x_ref.shape
    pairs = mixed_ref.shape[0]
    hidden_width = w1_ref.shape[1]
    chunk = hidden_width // pairs
    where = Where(planes)
    chip, core = where.chip, where.core
    half = rows_own // 2
    size = half
    few = source_ref.shape[0]
    deep = width // 8
    place, side, across = where.place, where.side, where.column(2)
    partners = (where.other_core, where.other_chip, where.other_side)
    if comm:
        greet(partners)
    moves = [
        (later_a, blocks_a),
        (source_any, source_ref),
        (x_any.at[:rows_own], x_ref),
        (mixed_any, mixed_ref),
        (cotangent_any.at[chip], cotangent_ref.at[:half]),
        (later_c, blocks_c),
    ]
    if comm:
        moves += [
            (later_b.at[at, side], blocks_b.at[at, side]) for at in (place, across)
        ]
    else:
        moves += [(cotangent_far, cotangent_ref.at[half:]), (later_b, blocks_b)]
    loads = [
        pltpu.make_async_copy(source, target, load.at[at])
        for at, (source, target) in enumerate(moves)
    ]
    for copy in loads:
        copy.start()
    semaphores = Semaphores(send, receive)
    if comm:
        cross_rows = semaphores.remote(
            cotangent_any.at[1 - chip], cotangent_ref.at[half:], where.other_chip
        )
        to_side = [
            semaphores.remote(later_b.at[at, side], blocks_b.at[at, side], where.other_side)
            for at in (place, across)
        ]
        to_core = [
            semaphores.remote(blocks_b.at[at], blocks_b.at[at], where.other_core)
            for at in (place, across)
        ]
    stores = [
        pltpu.make_async_copy(source, target, store.at[at])
        for at, (source, target) in enumerate(
            (
                (grad_ffn_s, out_rows),
                (gcm_s, grad_mixed_out),
                (final_s, grad_self_out),
                (blocks_a, part_a),
                (blocks_b, part_b),
                (blocks_c, part_c),
            )
        )
    ]
    gain_rows = jnp.concatenate([gain_blocks[at] for at in range(pairs)], axis=1)
    gain_two = gain_rows[1:2, :]
    gain_three = gain_rows[2:3, :]
    dgain_ref[...] = jnp.zeros(dgain_ref.shape, f32)

    dp_size = planes * 2
    group, half_way = where.group, planes
    sentence = group * 2 + chip
    src_len = source_len_ref[sentence]
    dec_len = src_len * upsample_ref[sentence]
    moved = chip * send_ref[group]
    holder = (group + moved * half_way) % dp_size
    partner = (holder + half_way) % dp_size

    def tokens_of(slot):
        return source_len_ref[slot] * upsample_ref[slot]

    tokens = (
        tokens_of(holder * 2)
        + tokens_of(holder * 2 + 1) * (1 - send_ref[holder])
        + tokens_of(partner * 2 + 1) * send_ref[partner]
    )
    loss_scale = jnp.full((1, 1), rows_own * 2, f32) / jnp.full((1, 1), tokens, jnp.int32).astype(f32)
    mask_columns(chip, core, few // 4, few, few // 4, src_len, cextra_ref)
    offset = lax.broadcasted_iota(jnp.int32, (size, 1), 0)

    def counted(index):
        place = block_places(chip, core, half, offset, index, size)
        return jnp.where(place < dec_len, 1.0, 0.0)

    def side_by_side(ref, rows):
        return jnp.concatenate([ref[pair, rows, :] for pair in range(pairs)], axis=1)

    def apart(ref, rows, value):
        for pair in range(pairs):
            ref[pair, rows, :] = value[:, pair * PAIR : (pair + 1) * PAIR]

    if comm:
        await_greetings(partners)
        for copy in (*to_side, cross_rows):
            copy.start()
    for copy in loads[:2]:
        copy.wait()
    for at, ref in enumerate((wo_ref, wcq_ref, wck_ref, wcv_ref, wco_ref)):
        whole_weight(ref, blocks_a, at * deep, deep)

    key_rows = dot(source_ref[...], wck_ref[...]).astype(bf16)
    every = pl.ds(0, few)
    apart(ck_ref, every, key_rows)
    for pair in range(pairs):
        ckt_ref[pair] = key_rows[:, pair * PAIR : (pair + 1) * PAIR].T
    apart(cv_ref, every, dot(source_ref[...], wcv_ref[...]).astype(bf16))

    for copy in loads[2:4]:
        copy.wait()

    def first_part(index):
        rows = pl.ds(index * size, size)
        after_self = x_ref[rows, :].astype(f32) + dot(side_by_side(mixed_ref, rows), wo_ref[...])
        after_self_s[rows, :] = after_self
        scaled, _ = normalize(after_self)
        hidden = (scaled * gain_two).astype(bf16)
        hidden_two_t[:, rows] = hidden.T
        apart(qc_s, rows, (dot(hidden, wcq_ref[...]) * (0.125 * LOG2E)).astype(bf16))

    repeat(0, rows_own // size, first_part, rows_own // size)

    def cross(index):
        pair, rows = index // 2, block_at(index % 2, half)
        mixed, extras = attend_pair(
            qc_s[pair, rows, :], ck_ref[pair], cextra_ref[...], cv_ref[pair],
            lax.broadcasted_iota(jnp.int32, (half, PAIR), 1),
        )
        cm_s[pair, rows, :] = mixed
        extra_s[2 * pair, rows, :] = extras[0]
        extra_s[2 * pair + 1, rows, :] = extras[1]

    repeat(0, 2 * pairs, cross, 4)
    for copy in loads[4:]:
        copy.wait()
    if comm:
        for copy in to_side:
            copy.wait_recv()
        for copy in to_core:
            copy.start()
        cross_rows.wait_recv()
    whole_weight(w2_ref, blocks_c, 0, hidden_width // 8)

    def second_part(index):
        rows = pl.ds(index * size, size)
        after_cross = after_self_s[rows, :] + dot(side_by_side(cm_s, rows), wco_ref[...])
        after_cross_s[rows, :] = after_cross
        scaled, _ = normalize(after_cross)
        hidden = (scaled * gain_three).astype(bf16)
        hidden_three_s[rows, :] = hidden
        hidden_three_t[:, rows] = hidden.T
        grad = (cotangent_ref[rows, :].astype(f32) * (counted(index) * loss_scale)).astype(bf16)
        grad_ffn_s[rows, :] = grad
        grad_ffn_t[:, rows] = grad.T

    repeat(0, rows_own // size, second_part, rows_own // size)
    if comm:
        for copy in to_core:
            copy.wait_recv()
        for copy in semaphores.sent:
            copy.wait_send()
    whole_weight(w1_ref, blocks_b, 0, deep, hidden_width // width)

    everyone = [(at % 2, at // 2) for at in range(8)]
    deep_two = hidden_width // 8
    halves = [slice(index * size, (index + 1) * size) for index in range(rows_own // size)]

    def opened(part, rows):
        columns = slice(part * chunk, (part + 1) * chunk)
        return (
            dot(hidden_three_s[rows, :], w1_ref[:, columns]),
            dot_nt(grad_ffn_s[rows, :], w2_ref[columns, :]),
        )

    def bent(expanded, grad_active):
        square = expanded * expanded
        bend = jnp.tanh(expanded * (GELU_IN + (GELU_IN * GELU_CUBE) * square))
        rise = 0.5 + 0.5 * bend
        active = expanded * rise
        slope = rise + active * (1.0 - rise) * (
            2.0 * GELU_IN + (6.0 * GELU_IN * GELU_CUBE) * square
        )
        return active.astype(bf16), (grad_active * slope).astype(bf16)

    def closed(part, rows, active, grad_expanded):
        columns = slice(part * chunk, (part + 1) * chunk)
        final = dot(active, w2_ref[columns, :])
        hidden_grad = dot_nt(grad_expanded, w1_ref[:, columns])
        if part == 0:
            final_s[rows, :] = final
            hidden_grad_s[rows, :] = hidden_grad
        else:
            final_s[rows, :] += final
            hidden_grad_s[rows, :] += hidden_grad

    def weights_of(part, actives, grads):
        value = dot(hidden_three_t[...], jnp.concatenate(grads, axis=0))
        for at in range(chunk // PAIR):
            to_blocks(
                blocks_b, [part], everyone, at * deep, deep, value[:, at * PAIR : (at + 1) * PAIR]
            )
        value = dot(grad_ffn_t[...], jnp.concatenate(actives, axis=0))
        for at in range(chunk // PAIR):
            row = part * chunk + at * PAIR
            index = row // deep_two
            for column in range(pairs):
                blocks_c[
                    column, index % 2, index // 2, row % deep_two : row % deep_two + PAIR, :
                ] = value[column * PAIR : (column + 1) * PAIR, at * PAIR : (at + 1) * PAIR].astype(
                    bf16
                )

    units = [(part, rows) for part in range(hidden_width // chunk) for rows in halves]
    ahead = opened(*units[0])
    done = []
    for at, (part, rows) in enumerate(units):
        now = ahead
        if at + 1 < len(units):
            ahead = opened(*units[at + 1])
        active, grad_expanded = bent(*now)
        closed(part, rows, active, grad_expanded)
        done.append((active, grad_expanded))
        if len(done) == len(halves):
            weights_of(part, [one for one, _ in done], [other for _, other in done])
            done = []
    stores[4].start()
    stores[5].start()

    def third_part(index):
        rows = pl.ds(index * size, size)
        after_cross = after_cross_s[rows, :]
        weight = counted(index)
        grad_final = cotangent_ref[rows, :].astype(f32) * (weight * loss_scale)
        scaled, inverse = normalize(after_cross)
        back, gain_sum = norm_back(hidden_grad_s[rows, :], scaled, inverse, gain_three)
        dgain_ref[2:3, :] += gain_sum
        grad_ffn_s[rows, :] = ((after_cross + final_s[rows, :]) * weight).astype(bf16)
        grad_cross = grad_final + back
        final_s[rows, :] = grad_cross
        branch = grad_cross.astype(bf16)
        hidden_three_s[rows, :] = branch
        apart(gcm_s, rows, dot_nt(branch, wco_ref[...]).astype(bf16))

    repeat(0, rows_own // size, third_part, rows_own // size)
    stores[0].start()

    def cross_back(pair, _):
        def put(ref, factor):
            def keep(_, value):
                ref[pair] = (value * factor).astype(bf16)

            return keep

        extra = cextra_ref[...]
        query_grad = attend_pair_back(
            qc_s[pair],
            gcm_s[pair],
            cm_s[pair],
            [extra_s[2 * pair], extra_s[2 * pair + 1]],
            lambda _: jnp.concatenate([ck_ref[pair], extra], axis=1),
            lambda _: jnp.concatenate([cv_ref[pair], extra], axis=1),
            lambda _, head: ckt_ref[pair, 64 * head : 64 * head + 64, :],
            1,
            put(dck_ref, LN2),
            put(dcv_ref, 1.0),
        )
        dq_s[pair] = query_grad.T
        return 0

    lax.fori_loop(0, pairs, cross_back, 0)

    def last_part(index):
        rows = pl.ds(index * size, size)
        scaled, inverse = normalize(after_self_s[rows, :])
        upstream = dot_nt(side_by_side(dq_s, rows), wcq_ref[...])
        back, gain_sum = norm_back(upstream, scaled, inverse, gain_two)
        dgain_ref[1:2, :] += gain_sum
        grad_self = final_s[rows, :] + back
        final_s[rows, :] = grad_self
        branch = grad_self.astype(bf16)
        branch_s[rows, :] = branch
        apart(gcm_s, rows, dot_nt(branch, wo_ref[...]).astype(bf16))

    repeat(0, rows_own // size, last_part, rows_own // size)
    stores[1].start()
    stores[2].start()

    columns = range(pairs)
    both_sides = [(0, 0), (1, 0)]
    for pair in range(pairs):
        two = [(side, pair) for side, _ in both_sides]
        to_blocks(blocks_a, columns, two, 0, deep, dot(mixed_ref[pair].T, branch_s[...]))
        to_blocks(blocks_a, columns, two, 4 * deep, deep, dot(cm_s[pair].T, hidden_three_s[...]))
    all_rows = pl.ds(0, rows_own)
    to_blocks(
        blocks_a, columns, everyone, deep, deep, dot(hidden_two_t[...], side_by_side(dq_s, all_rows))
    )
    source_t = source_ref[...].T
    key_grad = side_by_side(dck_ref, every)
    value_grad = side_by_side(dcv_ref, every)
    to_blocks(blocks_a, columns, everyone, 2 * deep, deep, dot(source_t, key_grad))
    to_blocks(blocks_a, columns, everyone, 3 * deep, deep, dot(source_t, value_grad))
    stores[3].start()
    grad_source_ref[...] = (
        dot_nt(key_grad, wck_ref[...]) + dot_nt(value_grad, wcv_ref[...])
    ).astype(bf16)
    for copy in stores:
        copy.wait()


def last_kernel(comm, planes, source_len_ref, upsample_ref, *refs):
    (q_any, k_any, v_any, mixed_any, grad_any, extra_any) = refs[:6]
    (x_any, qkv_any, gain_any, grad_self_any, dgain_any) = refs[6:11]
    refs = refs[11:]
    if comm:
        (part_a, part_b, part_c, source_any, rows_any) = refs[:5]
        (rows_land, grad_out, cross_land, source_out, source_far) = refs[5:10]
        (*weight_outs, gain_out) = refs[10:21]
        refs = refs[21:]
    else:
        (own_out, other_out, part_out, gain_out) = refs[:4]
        refs = refs[4:]
    (
        q_s, k_s, v_s, mixed_s, grad_s, extra_s, x_s, qkv_s, gain_s, grad_self_s, dgain_s,
        keys_s, values_s, kt_s, hidden_s, total_s, dkv_s, dq_s, weight_s,
        part_s, load, send, receive,
    ) = refs[:23]
    refs = refs[23:]
    where = Where(planes)
    chip, core, side, plane = where.chip, where.core, where.side, where.plane
    total, width = x_s.shape
    own = total // 2
    rows = total // 4
    pairs = width // PAIR
    deep = width // 8
    chunk = 512
    semaphores = Semaphores(send, receive)
    sentence = where.group * 2 + chip
    length = source_len_ref[sentence] * upsample_ref[sentence]

    def turn_pair(turn):
        return where.column(pairs - 1 - turn)

    def turn_loads(turn):
        pair, slot = turn_pair(turn), turn % 2
        return [
            pltpu.make_async_copy(source.at[pair], target.at[slot], load.at[slot, at])
            for at, (source, target) in enumerate(
                (
                    (q_any, q_s),
                    (k_any, k_s),
                    (v_any, v_s),
                    (mixed_any, mixed_s),
                    (grad_any, grad_s),
                    (extra_any, extra_s),
                )
            )
        ]

    common = [
        semaphores.local(source, target)
        for source, target in ((gain_any, gain_s), (x_any, x_s), (qkv_any, qkv_s))
    ]
    for copy in common:
        copy.start()
    for copy in turn_loads(0):
        copy.start()
    late = [
        semaphores.local(source, target)
        for source, target in ((dgain_any, dgain_s), (grad_self_any, grad_self_s))
    ]

    def begin(copies):
        for copy in copies:
            copy.start()

    def arrive(copies):
        for copy in copies:
            copy.wait_recv()

    if comm:
        (
            keep_a, keep_b, keep_c, core_a, core_b, core_c, far_a, far_b, far_c,
            near_a, near_b, near_c, planes_a, planes_b, planes_c,
            land_q, far_q, planes_q, gain_send, gain_land, gain_far, gain_planes, grads_send,
            grads_land, cross_send, stage, source_s, source_land, stage_s,
        ) = refs
        place, across = where.place, where.column(2)
        pieces = []
        for part, keep, land, far_land, near_land, land_planes, order in (
            (part_a, keep_a, core_a, far_a, near_a, planes_a, "yxz"),
            (part_b, keep_b, core_b, far_b, near_b, planes_b, "yxz"),
            (part_c, keep_c, core_c, far_c, near_c, planes_c, "xyz"),
        ):
            piece = dict(keep=keep, land=land, order=order)
            piece.update(far_land=far_land, near_land=near_land, planes=land_planes)
            piece["load"] = [
                semaphores.local(part.at[place], keep.at[0]),
                semaphores.local(part.at[across], keep.at[1]),
            ]
            piece["core"] = [
                semaphores.remote(part.at[where.column(1)], land.at[0], where.other_core),
                semaphores.remote(part.at[where.column(3)], land.at[1], where.other_core),
            ]
            if order[0] == "y":
                piece["far"] = [
                    semaphores.remote(keep.at[at, 1 - side], far_land.at[at], where.other_side)
                    for at in (0, 1)
                ]
            else:
                piece["far"] = [
                    semaphores.remote(keep.at[1, at], far_land.at[at], where.other_chip)
                    for at in (0, 1)
                ]
            if order == "yxz":
                near = (keep.at[1, side], near_land, where.other_chip)
            else:
                near = (keep.at[0, 1 - side], near_land, where.other_side)
            piece["near"] = [semaphores.remote(*near)]
            piece["last"] = [
                semaphores.remote(
                    keep.at[0, side, (plane + step) % planes],
                    land_planes.at[step - 1],
                    where.other_planes[step - 1],
                )
                for step in range(1, planes)
            ]
            pieces.append(piece)
        a, b, c = pieces
        owners = (where.diagonal, where.other_chip, where.other_core)
        hops = (where.other_core, where.other_chip, where.other_core)
        send_q = [
            semaphores.remote(part_s.at[turn], land_q.at[turn], hops[turn]) for turn in range(3)
        ]
        side_q = semaphores.remote(part_s.at[3, 1 - side], far_q, where.other_side)
        plane_q = [
            semaphores.remote(
                part_s.at[3, side, (plane + step) % planes],
                planes_q.at[step - 1],
                where.other_planes[step - 1],
            )
            for step in range(1, planes)
        ]
        gain_group = [
            semaphores.remote(gain_send.at[where.column(3 - turn)], gain_land.at[turn], owners[turn])
            for turn in range(3)
        ]
        gain_side = semaphores.remote(gain_land.at[3], gain_far, where.other_side)
        gain_last = [
            semaphores.remote(
                gain_planes.at[plane], gain_planes.at[plane], where.other_planes[step - 1]
            )
            for step in range(1, planes)
        ]
        rows_cross = semaphores.remote(rows_any.at[rows:], rows_land, where.other_chip)
        few = source_any.shape[0] // 4
        source_local = semaphores.local(source_any.at[: 2 * few], source_s)
        source_core = semaphores.remote(source_any.at[2 * few :], source_land, where.other_core)
        source_cross = semaphores.remote(source_s.at[few:], source_far, where.other_chip)
        grads_core = [
            [
                semaphores.remote(grads_send.at[at, cut], grads_land.at[at, cut], where.other_core)
                for cut in (pl.ds(row * BLOCK, BLOCK) for row in range(rows // BLOCK))
            ]
            for at in range(2)
        ]
        grads_cross = [
            semaphores.remote(cross_send.at[at], cross_land.at[at], where.other_chip)
            for at in range(rows // BLOCK)
        ]
        stage_out = semaphores.local(stage, grad_out)
        source_own = semaphores.local(stage_s, source_out)
        greet(where.everyone())
        for piece in pieces:
            begin(piece["load"])
        begin([source_local])

        def add_in(ref, land):
            def add(at, _):
                ref[at] = (ref[at].astype(f32) + land[at].astype(f32)).astype(bf16)
                return 0

            lax.fori_loop(0, planes, add, 0)

        def add_core(piece):
            for copy in piece["load"]:
                copy.wait()
            arrive(piece["core"])
            for at in (0, 1):
                for half in (0, 1):
                    add_in(piece["keep"].at[at, half], piece["land"].at[at, half])
            begin(piece["far"])

        def add_far(piece):
            arrive(piece["far"])
            for at in (0, 1):
                if piece["order"][0] == "y":
                    add_in(piece["keep"].at[at, side], piece["far_land"].at[at])
                else:
                    add_in(piece["keep"].at[0, at], piece["far_land"].at[at])
            begin(piece["near"])

        def add_near(piece):
            arrive(piece["near"])
            add_in(piece["keep"].at[0, side], piece["near_land"])
            begin(piece["last"])

        def finish(piece):
            arrive(piece["last"])
            value = piece["keep"][0, side, plane].astype(f32)
            for step in range(planes - 1):
                value = value + piece["planes"][step].astype(f32)
            return value

    mask_columns(chip, core, rows, total, BLOCK, length, values_s.at[:, PAIR:])
    keys_s[:, PAIR:] = values_s[:, PAIR:]
    for copy in late:
        copy.start()
    for copy in common:
        copy.wait()
    gain = jnp.concatenate([gain_s[at, 0:1, :] for at in range(pairs)], axis=1)

    def hide(index):
        at = block_at(index, BLOCK)
        scaled, _ = normalize(x_s[at, :].astype(f32))
        hidden_s[:, at] = (scaled * gain).astype(bf16).T

    repeat(0, total // BLOCK, hide, 4)
    if comm:
        await_greetings(where.everyone())
        for piece in pieces:
            begin(piece["core"])
        begin([source_core, rows_cross])

    def take_weights(turn, pair):
        for part in range(3):
            for at in range(8):
                weight_s[turn, at * 64 : at * 64 + 64, part * PAIR : (part + 1) * PAIR] = qkv_s[
                    pair, at % 2, at // 2, part * 64 : part * 64 + 64, :
                ]

    def upstream(turns, at, own_rows):
        value = None
        for turn in turns:
            term = dot_nt(dkv_s[turn, at, :], weight_s[turn, :, PAIR:])
            if own_rows:
                term = term + dot_nt(dq_s[turn, at, :], weight_s[turn, :, :PAIR])
            value = term if value is None else value + term
        return value

    def comm_steps(index):
        if not comm:
            return

        @pl.when(index == 1)
        def _():
            add_core(a)
            add_core(c)
            add_core(b)
            source_local.wait()
            arrive([source_core])
            for half in range(2):
                r = slice(half * few, (half + 1) * few)
                value = source_s[r, :].astype(f32) + source_land[r, :].astype(f32)
                source_s[r, :] = value.astype(bf16)
                if half == 0:
                    stage_s[...] = value
            begin([source_cross, source_own])

        @pl.when(index == 3)
        def _():
            add_far(a)
            add_far(c)

        @pl.when(index == 4)
        def _():
            arrive([send_q[0]])
            for half in range(2):
                add_in(part_s.at[1, half], land_q.at[0, half])
            send_q[1].start()

        @pl.when(index == 5)
        def _():
            add_far(b)
            add_near(a)

        @pl.when(index == 6)
        def _():
            add_near(c)

        @pl.when(index == 7)
        def _():
            add_near(b)


    def step(turn, _):
        pair, slot = turn_pair(turn), turn % 2
        for copy in turn_loads(turn):
            copy.wait()

        @pl.when(turn + 1 < pairs)
        def _():
            for copy in turn_loads(turn + 1):
                copy.start()

        keys_s[:, :PAIR] = k_s[slot]
        values_s[:, :PAIR] = v_s[slot]
        kt_s[...] = k_s[slot].T
        take_weights(turn, pair)
        comm_steps(2 * turn)

        def part(ref):
            return lambda part: ref[part * chunk : (part + 1) * chunk, :]

        def put(at, factor):
            def keep(part, value):
                dkv_s[turn, part * chunk : (part + 1) * chunk, at : at + PAIR] = (
                    value * factor
                ).astype(bf16)

            return keep

        query_grad = attend_pair_back(
            q_s[slot],
            grad_s[slot],
            mixed_s[slot],
            [extra_s[slot, head] for head in (0, 1)],
            part(keys_s),
            part(values_s),
            lambda part, head: kt_s[64 * head : 64 * head + 64, part * chunk : (part + 1) * chunk],
            total // chunk,
            put(0, LN2),
            put(PAIR, 1.0),
        )
        dq_s[turn] = query_grad.T
        comm_steps(2 * turn + 1)
        both = dot(hidden_s[...], dkv_s[turn]).astype(bf16)
        query = dot(hidden_s[:, :own], dq_s[turn]).astype(bf16)
        for at in range(8):
            r = slice(at * deep, (at + 1) * deep)
            for part_at, value in enumerate((query[r, :], both[r, :PAIR], both[r, PAIR:])):
                part_s[turn, at % 2, at // 2, part_at * deep : (part_at + 1) * deep, :] = value

        if comm:
            for sent in (0, 2):

                @pl.when(turn == sent)
                def _():
                    send_q[sent].start()

        @pl.when(turn == pairs - 2)
        def _():
            size = 2 * BLOCK
            for row in range(total // size):
                if row * size // rows % 2 == 1:
                    r = pl.ds(row * size, size)
                    total_s[r, :] = upstream(range(pairs - 1), r, row * size < own)

        return 0

    lax.fori_loop(0, pairs, step, 0)

    def row_back(row, own_rows, all_turns):
        r = block_at(row, BLOCK)
        scaled, inverse = normalize(x_s[r, :].astype(f32))
        if all_turns:
            value = upstream(range(pairs), r, own_rows)
        else:
            value = total_s[r, :] + upstream([pairs - 1], r, own_rows)
        back, gain_sum = norm_back(value, scaled, inverse, gain)
        dgain_s[0:1, :] += gain_sum
        return r, back

    for copy in late:
        copy.wait()
    per = rows // BLOCK
    if not comm:

        def own_step(row):
            r, back = row_back(row, True, True)
            grad_self_s[r, :] += back

        def other_step(row):
            r, back = row_back(row, False, True)
            total_s[r, :] = back

        repeat(0, 2 * per, own_step, per)
        repeat(2 * per, 4 * per, other_step, per)
        own_out[...] = grad_self_s[...]
        other_out[...] = total_s[own:, :].astype(bf16)
        for turn in range(pairs):
            part_out[turn_pair(turn)] = part_s[turn]
        gain_out[...] = dgain_s[...]
        return

    def add_q(at, _):
        for half in range(2):
            value = part_s[3, half, at].astype(f32)
            for turn in (1, 2):
                value = value + land_q[turn, half, at].astype(f32)
            part_s[3, half, at] = value.astype(bf16)
        return 0

    def other_rows(slot):
        for row in range(per):
            _, back = row_back(slot * per + row, False, slot % 2 == 0)
            grads_send[slot - 2, pl.ds(row * BLOCK, BLOCK), :] = back.astype(bf16)
            grads_core[slot - 2][row].start()

    def own_rows(row):
        r, back = row_back(row, True, row < per)
        total_s[r, :] = back + grad_self_s[r, :]

    def cross(row):
        r = slice(row * BLOCK, (row + 1) * BLOCK)
        value = total_s[rows + row * BLOCK : rows + (row + 1) * BLOCK, :]
        cross_send[row] = (value + grads_land[1, r, :].astype(f32)).astype(bf16)
        grads_cross[row].start()

    arrive(send_q[1:])
    lax.fori_loop(0, planes, add_q, 0)
    side_q.start()
    other_rows(3)
    own_rows(per)
    arrive(grads_core[1][:1])
    cross(0)
    repeat(per + 1, 2 * per, own_rows, per)
    other_rows(2)
    arrive([side_q])
    add_in(part_s.at[3, side], far_q)
    begin(plane_q)
    repeat(0, per, own_rows, per)
    for at in range(pairs):
        gain_send[at] = dgain_s[:, at * PAIR : (at + 1) * PAIR]
    begin(gain_group)
    for row in range(1, per):
        arrive(grads_core[1][row : row + 1])
        cross(row)
    arrive(gain_group)
    gain_land[3] = gain_send[place] + gain_land[0] + gain_land[1] + gain_land[2]
    gain_side.start()
    arrive(grads_core[0])
    stage[...] = total_s[:rows, :] + grads_land[0].astype(f32)
    stage_out.start()
    sums = [finish(piece) for piece in pieces]
    for at in range(5):
        weight_outs[3 + at][...] = sums[0][at * deep : (at + 1) * deep, :]
    for at in range(sums[1].shape[0] // deep):
        weight_outs[8][:, at * PAIR : (at + 1) * PAIR] = sums[1][at * deep : (at + 1) * deep, :]
    for at in range(sums[2].shape[0] // PAIR):
        r = slice(at * PAIR, (at + 1) * PAIR)
        weight_outs[9][r, :] = sums[2][r, :].T
    arrive([gain_side])
    gain_planes[plane] = gain_land[3] + gain_far[...]
    begin(gain_last)
    arrive(plane_q)
    value = part_s[3, side, plane].astype(f32)
    for at in range(planes - 1):
        value = value + planes_q[at].astype(f32)
    for at in range(3):
        weight_outs[at][...] = value[at * deep : (at + 1) * deep, :]
    arrive(gain_last)
    value = gain_planes[0]
    for at in range(1, planes):
        value = value + gain_planes[at]
    gain_out[...] = value
    arrive([rows_cross, source_cross, *grads_cross])
    for copy in (stage_out, source_own):
        copy.wait()
    for copy in semaphores.sent:
        copy.wait_send()


def hand_over_kernel(planes, *refs):
    (rows_any, rows_far, grad_own, grad_far, source_own, source_far, *plain) = refs[:17]
    (decoder_out, grad_out, source_out, *plain_outs) = refs[17:31]
    (rows_s, grad_s, grad_low, source_s, source_low, *plain_s) = refs[31:-2]
    load, store = refs[-2:]
    chip = Where(planes).chip
    rows = rows_s.shape[1]
    moves = [
        (rows_any.at[:rows], rows_s.at[0], rows_s.at[0], decoder_out.at[chip]),
        (rows_far, rows_s.at[1], rows_s.at[1], decoder_out.at[1 - chip]),
        (grad_own, grad_s.at[0], grad_s.at[0], grad_out.at[chip]),
        (grad_far, grad_low, grad_s.at[1], grad_out.at[1 - chip]),
        (source_own, source_s.at[0], source_s.at[0], source_out.at[chip]),
        (source_far, source_low, source_s.at[1], source_out.at[1 - chip]),
    ]
    moves += [
        (one, held, held.at[: other.shape[0]], other)
        for one, held, other in zip(plain, plain_s, plain_outs)
    ]
    loads = [pltpu.make_async_copy(m[0], m[1], load.at[at]) for at, m in enumerate(moves)]
    stores = [pltpu.make_async_copy(m[2], m[3], store.at[at]) for at, m in enumerate(moves)]
    for copy in loads:
        copy.start()
    for at, (one, other) in enumerate(zip(loads, stores)):
        one.wait()
        if at == 3:
            for row in range(grad_low.shape[0]):
                size = grad_low.shape[1]
                grad_s[1, row * size : (row + 1) * size, :] = grad_low[row].astype(f32)
        if at == 5:
            source_s[1] = source_low[...].astype(f32)
        other.start()
    for copy in stores:
        copy.wait()


def call(kernel, outs, *operands, scratch=(), smem=0, params=PARAMS, spaces=None, out_space=VMEM, out_spaces=None):
    spaces = spaces or {}
    out_spaces = out_spaces or {}
    return pl.pallas_call(
        kernel,
        out_shape=[jax.ShapeDtypeStruct(shape, kind) for shape, kind in outs],
        in_specs=[
            pl.BlockSpec(memory_space=pltpu.SMEM if at < smem else spaces.get(at, VMEM))
            for at in range(len(operands))
        ],
        out_specs=[
            pl.BlockSpec(memory_space=out_spaces.get(at, out_space)) for at in range(len(outs))
        ],
        scratch_shapes=list(scratch),
        compiler_params=params,
    )(*operands)


def swapped(value, axis, bit):
    pairs = [(source, source ^ bit) for source in range(lax.axis_size(axis))]
    return lax.ppermute(value, axis, pairs)


def as_blocks(weight, chunks=1):
    height, width = weight.shape
    deep = height // 8
    cut = weight.reshape(4, 2, deep, 4, chunks, PAIR).transpose(3, 1, 0, 4, 2, 5)
    return cut.reshape(4, 2, 4, chunks * deep, PAIR)


def from_blocks(blocks, chunks=1):
    height = blocks.shape[3] // chunks
    cut = blocks.reshape(4, 2, 4, chunks, height, PAIR).transpose(2, 1, 4, 0, 3, 5)
    return cut.reshape(8 * height, 4 * chunks * PAIR)


def gather_plain(arguments, seq_size, dp_size):
    (decoder_in, source_states, out_grad, narrow, ffn_expand, ffn_reduce, norm_gains) = arguments
    chip = lax.axis_index("seq") // 2
    rows_dec = decoder_in.shape[1]
    own = 2 * rows_dec
    outgoing = jnp.concatenate([decoder_in[1 - chip], source_states[1 - chip]], axis=0)
    arrived = swapped(outgoing, "seq", 2)
    own_rows = jnp.concatenate(
        [decoder_in[chip], arrived[:rows_dec], source_states[chip], arrived[rows_dec:]], axis=0
    )
    other_rows = swapped(own_rows, "seq", 1)
    x_all = jnp.concatenate([own_rows[:own], other_rows[:own]], axis=0)
    source_all = jnp.concatenate([own_rows[own:], other_rows[own:]], axis=0)
    cotangent = swapped(out_grad[1 - chip], "seq", 2)

    def whole(weight):
        weight = lax.all_gather(weight, "seq", axis=1, tiled=True)
        return lax.all_gather(weight, "dp", axis=0, tiled=True)

    blocks = [as_blocks(whole(weight)) for weight in narrow]
    qkv = jnp.concatenate(blocks[:3], axis=3)
    later_a = jnp.concatenate(blocks[3:], axis=3)
    later_b = as_blocks(whole(ffn_expand), ffn_expand.shape[1] // PAIR)
    later_c = as_blocks(whole(ffn_reduce))
    gain_block = jnp.pad(norm_gains.astype(f32), ((0, 5), (0, 0)))
    gains = lax.all_gather(gain_block, "seq", axis=0)
    return x_all, source_all, cotangent, qkv, later_a, later_b, later_c, gains


def body(
    decoder_in,
    source_states,
    source_len,
    upsample,
    send_counts,
    self_query,
    self_key,
    self_value,
    self_output,
    cross_query,
    cross_key,
    cross_value,
    cross_output,
    ffn_expand,
    ffn_reduce,
    norm_gains,
    out_grad,
):
    seq_size = lax.axis_size("seq")
    dp_size = lax.axis_size("dp")
    planes = dp_size // 2
    place = lax.axis_index("seq")
    chip = place // 2
    home_count, rows_dec, width = decoder_in.shape
    rows_src = source_states.shape[1]
    pairs = width // PAIR
    own = 2 * rows_dec
    total = 4 * rows_dec
    deep = self_query.shape[0]
    deep_two = ffn_reduce.shape[0]
    wide = ffn_expand.shape[1] // PAIR
    hidden_width = wide * PAIR * seq_size
    all_src = 4 * rows_src
    comm = dp_size == 8

    def pair_rows(rows):
        return (pairs, rows, PAIR)

    narrow = (self_query, self_key, self_value, self_output)
    narrow += (cross_query, cross_key, cross_value, cross_output)
    rows_outs = [
        (pair_rows(own), bf16),
        (pair_rows(total), bf16),
        (pair_rows(total), bf16),
        (pair_rows(own), bf16),
        ((pairs, 2, own, PAIR), bf16),
    ]
    buffers = [VMEM(shape, kind) for shape, kind in rows_outs]
    work = [
        VMEM((total, width), bf16),
        VMEM((width, 3 * PAIR), bf16),
        VMEM((total, PAIR), bf16),
        *buffers,
    ]
    semaphores = [pltpu.SemaphoreType.DMA((96,)), pltpu.SemaphoreType.DMA((96,))]
    if comm:
        cut = (seq_size, 2, planes)
        gathered = [
            ((total, width), bf16),
            ((all_src, width), bf16),
            (cut + (3 * deep, PAIR), bf16),
            (cut + (5 * deep, PAIR), bf16),
            (cut + (wide * deep, PAIR), bf16),
            (cut + (deep_two, PAIR), bf16),
            ((seq_size, 8, PAIR), f32),
        ]
        operands = (source_len, upsample, decoder_in, source_states)
        operands += (*narrow, ffn_expand, ffn_reduce, norm_gains)
        (
            x_all, source_all, qkv, later_a, later_b, later_c, gains,
            q, k, v, mixed, query_extra,
        ) = call(
            partial(open_kernel, True, planes, deep),
            gathered + rows_outs,
            *operands,
            scratch=[
                VMEM((total, width), bf16),
                VMEM(cut + (3 * deep, PAIR), bf16),
                VMEM((seq_size, 8, PAIR), f32),
                *work,
                *semaphores,
                VMEM((5 * deep, PAIR), bf16),
                VMEM((wide * deep, PAIR), bf16),
                VMEM((deep_two, PAIR), bf16),
                VMEM((rows_src, width), bf16),
                VMEM((8, PAIR), f32),
            ],
            smem=2,
            spaces={at: pl.ANY for at in range(2, len(operands) - 1)},
            out_space=pl.ANY,
            params=pltpu.CompilerParams(
                vmem_limit_bytes=VMEM_LIMIT, collective_id=0, has_side_effects=True
            ),
        )
    else:
        x_all, source_all, cotangent, qkv, later_a, later_b, later_c, gains = gather_plain(
            (decoder_in, source_states, out_grad, narrow, ffn_expand, ffn_reduce, norm_gains),
            seq_size,
            dp_size,
        )
        q, k, v, mixed, query_extra = call(
            partial(open_kernel, False, planes, deep),
            rows_outs,
            source_len,
            upsample,
            x_all,
            qkv,
            gains,
            scratch=[*work, *semaphores],
            smem=2,
            out_space=pl.ANY,
        )
    parts = [
        ((seq_size, 2, 4, 5 * width // 8, PAIR), bf16),
        ((seq_size, 2, 4, hidden_width // 8, PAIR), bf16),
        ((seq_size, 2, 4, hidden_width // 8, PAIR), bf16),
    ]
    out_rows, grad_mixed, grad_self, part_a, part_b, part_c, grad_source, dgain = call(
        partial(middle_kernel, comm, planes),
        [
            ((own, width), bf16),
            (pair_rows(own), bf16),
            ((own, width), f32),
            *parts,
            ((all_src, width), bf16),
            ((8, width), f32),
        ],
        source_len,
        upsample,
        send_counts,
        x_all,
        mixed,
        out_grad,
        out_grad if comm else cotangent,
        source_all,
        later_a,
        later_b,
        later_c,
        gains,
        scratch=[
            VMEM((own, width), bf16),
            VMEM(pair_rows(own), bf16),
            VMEM((own, width), bf16),
            VMEM((all_src, width), bf16),
            *[VMEM(*part) for part in parts],
            *[VMEM((width, width), bf16)] * 5,
            VMEM((width, hidden_width), bf16),
            VMEM((hidden_width, width), bf16),
            VMEM(pair_rows(all_src), bf16),
            VMEM(pair_rows(all_src), bf16),
            VMEM((pairs, PAIR, all_src), bf16),
            VMEM((all_src, PAIR), bf16),
            *[VMEM(pair_rows(all_src), bf16)] * 2,
            *[VMEM((own, width), f32)] * 4,
            *[VMEM(pair_rows(own), bf16)] * 4,
            VMEM((2 * pairs, own, PAIR), bf16),
            VMEM((width, own), bf16),
            VMEM((own, width), bf16),
            VMEM((width, own), bf16),
            VMEM((own, width), bf16),
            VMEM((width, own), bf16),
            VMEM((own, width), bf16),
            pltpu.SemaphoreType.DMA((8,)),
            pltpu.SemaphoreType.DMA((6,)),
            pltpu.SemaphoreType.DMA((8,)),
            pltpu.SemaphoreType.DMA((8,)),
        ],
        params=pltpu.CompilerParams(
            vmem_limit_bytes=VMEM_LIMIT, collective_id=2, has_side_effects=True
        )
        if comm
        else PARAMS,
        smem=3,
        spaces={at: pl.ANY for at in range(3, 11)},
        out_spaces={at: pl.ANY for at in range(6)},
    )
    part_q = ((seq_size, 2, 4, 3 * width // 8, PAIR), bf16)
    operands = (source_len, upsample, q, k, v, mixed, grad_mixed, query_extra)
    operands += (x_all, qkv, gains, grad_self, dgain)
    work = [
        VMEM((2, own, PAIR), bf16),
        VMEM((2, total, PAIR), bf16),
        VMEM((2, total, PAIR), bf16),
        VMEM((2, own, PAIR), bf16),
        VMEM((2, own, PAIR), bf16),
        VMEM((2, 2, own, PAIR), bf16),
        VMEM((total, width), bf16),
        VMEM(qkv.shape, bf16),
        VMEM(gains.shape, f32),
        VMEM((own, width), f32),
        VMEM((8, width), f32),
        VMEM((total, 2 * PAIR), bf16),
        VMEM((total, 2 * PAIR), bf16),
        VMEM((PAIR, total), bf16),
        VMEM((width, total), bf16),
        VMEM((total, width), f32),
        VMEM((pairs, total, 2 * PAIR), bf16),
        VMEM((pairs, own, PAIR), bf16),
        VMEM((pairs, width, 3 * PAIR), bf16),
        VMEM(*part_q),
        pltpu.SemaphoreType.DMA((2, 6)),
        *semaphores,
    ]
    everywhere = {at: pl.ANY for at in range(2, 18)}
    if comm:
        heights = [shape[3] for shape, _ in parts]

        def per_piece(lead):
            return [VMEM((*lead, height, PAIR), bf16) for height in heights]

        work += [
            *per_piece((2, 2, planes)),
            *per_piece((2, 2, planes)),
            *per_piece((2, planes)),
            *per_piece((planes,)),
            *per_piece((planes - 1,)),
            VMEM((3, 2, planes, 3 * deep, PAIR), bf16),
            VMEM((planes, 3 * deep, PAIR), bf16),
            VMEM((planes - 1, 3 * deep, PAIR), bf16),
            VMEM((pairs, 8, PAIR), f32),
            VMEM((4, 8, PAIR), f32),
            VMEM((8, PAIR), f32),
            VMEM((planes, 8, PAIR), f32),
            VMEM((2, rows_dec, width), bf16),
            VMEM((2, rows_dec, width), bf16),
            VMEM((rows_dec // BLOCK, BLOCK, width), bf16),
            VMEM((rows_dec, width), f32),
            VMEM((2 * rows_src, width), bf16),
            VMEM((2 * rows_src, width), bf16),
            VMEM((rows_src, width), f32),
        ]
        small = ((deep, PAIR), f32)
        plain = [small] * 8 + [(ffn_expand.shape, f32), (ffn_reduce.shape, f32), ((8, PAIR), f32)]
        outs = call(
            partial(last_kernel, True, planes),
            [
                ((rows_dec, width), bf16),
                ((rows_dec, width), f32),
                ((rows_dec // BLOCK, BLOCK, width), bf16),
                ((rows_src, width), f32),
                ((rows_src, width), bf16),
                *plain,
            ],
            *operands,
            part_a,
            part_b,
            part_c,
            grad_source,
            out_rows,
            scratch=work,
            smem=2,
            spaces=everywhere,
            out_spaces={at: pl.ANY for at in range(5)},
            params=pltpu.CompilerParams(
                vmem_limit_bytes=VMEM_LIMIT, collective_id=1, has_side_effects=True
            ),
        )
        outs = call(
            partial(hand_over_kernel, planes),
            [
                (decoder_in.shape, bf16),
                (decoder_in.shape, f32),
                (source_states.shape, f32),
                *plain[:-1],
                (norm_gains.shape, f32),
            ],
            out_rows,
            *outs,
            scratch=[
                VMEM(decoder_in.shape, bf16),
                VMEM(decoder_in.shape, f32),
                VMEM((rows_dec // BLOCK, BLOCK, width), bf16),
                VMEM(source_states.shape, f32),
                VMEM((rows_src, width), bf16),
                *[VMEM(shape, kind) for shape, kind in plain],
                *[pltpu.SemaphoreType.DMA((17,))] * 2,
            ],
            spaces={at: pl.ANY for at in range(17)},
            out_space=pl.ANY,
        )
        (decoder_out, grad_decoder, grad_src, dwq, dwk, dwv, *rest, dw1, dw2, dgains) = outs
        dwo, dwcq, dwck, dwcv, dwco = rest
    else:
        own_grad, other_grad, part_qkv, dgains = call(
            partial(last_kernel, False, planes),
            [((own, width), f32), ((own, width), bf16), part_q, ((8, width), f32)],
            *operands,
            scratch=work,
            smem=2,
            spaces=everywhere,
        )
        crossing = jnp.concatenate([other_grad, grad_source[2 * rows_src :]], axis=0)
        returned = swapped(crossing, "seq", 1).astype(f32)
        grad_rows = own_grad + returned[:own]
        source_rows = grad_source[: 2 * rows_src].astype(f32) + returned[own:]
        homeward = [grad_rows[rows_dec:].astype(bf16), source_rows[rows_src:].astype(bf16)]
        came = swapped(jnp.concatenate([out_rows[rows_dec:], *homeward], axis=0), "seq", 2)

        def both_sentences(mine, theirs):
            theirs = theirs.astype(mine.dtype)
            return jnp.where(chip == 0, jnp.stack([mine, theirs]), jnp.stack([theirs, mine]))

        decoder_out = both_sentences(out_rows[:rows_dec], came[:rows_dec])
        grad_decoder = both_sentences(grad_rows[:rows_dec], came[rows_dec : 2 * rows_dec])
        grad_src = both_sentences(source_rows[:rows_src], came[2 * rows_dec :])

        def summed(blocks, start, count, chunks=1):
            grad = from_blocks(blocks[:, :, :, start : start + chunks * count], chunks)
            grad = lax.psum_scatter(grad.astype(f32), "dp", scatter_dimension=0, tiled=True)
            return lax.psum_scatter(grad, "seq", scatter_dimension=1, tiled=True)

        step = width // 8
        dwq, dwk, dwv = [summed(part_qkv, at * step, step) for at in range(3)]
        dwo, dwcq, dwck, dwcv, dwco = [summed(part_a, at * step, step) for at in range(5)]
        dw1 = summed(part_b, 0, step, hidden_width // width)
        tall = part_c.reshape(seq_size, 2, 4, hidden_width // 8 // PAIR, PAIR, PAIR)
        dw2 = summed(tall.swapaxes(4, 5).reshape(part_c.shape), 0, hidden_width // 8)
        dgains = lax.psum(dgains, "dp")
        dgains = lax.psum_scatter(dgains, "seq", scatter_dimension=1, tiled=True)
    return (
        decoder_out,
        grad_decoder,
        grad_src,
        dwq,
        dwk,
        dwv,
        dwo,
        dwcq,
        dwck,
        dwcv,
        dwco,
        dw1,
        dw2,
        dgains[:3],
    )


def solution(mesh):
    rows = P("dp", "seq", None)
    weight = P("dp", "seq")
    placed = (rows, rows, P(), P(), P()) + (weight,) * 10 + (P(None, "seq"), rows)
    return jax.shard_map(
        body,
        mesh=mesh,
        in_specs=placed,
        out_specs=(rows, rows, rows) + (weight,) * 10 + (P(None, "seq"),),
        check_vma=False,
    )
```
